32 devices in a mesh: dp: 2 (over x), stream: 4 (over y, core), head: 4 (over z).
Axes of the slice: x: 2, y: 2, z: 4, core: 2. Of those that a mesh axis runs over, the one named last changes fastest.
Arguments:
- history: bfloat16 [9, 4, 2048, 2048], P(None, 'dp', 'stream', 'head'), may hold values from -6 to 6
- seq_lens: int32 [4, 3], replicated, may hold values from 0 to 2048, as said below
- bucket_slot: int32 [4], replicated, may hold values from 0 to 3, each once
- w_mix_in: bfloat16 [2048, 36], P('head'), may hold values from -0.125 to 0.125
- w_mix_out: bfloat16 [36, 36], replicated, may hold values from -1 to 1
- mix_bias: float32 [4, 9], replicated, may hold values from -3 to 3
- ln_gain: float32 [4, 2048], P(None, 'head'), may hold values from 0.25 to 1.75
- ln_bias: float32 [4, 2048], P(None, 'head'), may hold values from -2 to 2
- w_qkv: bfloat16 [3, 2048, 2048], P(None, ('dp', 'stream'), 'head'), may hold values from -0.125 to 0.125
- w_attn_out: bfloat16 [2048, 2048], P('head', ('dp', 'stream')), may hold values from -3 to 3
- w_up: bfloat16 [2048, 8192], P(('dp', 'stream'), 'head'), may hold values from -0.125 to 0.125
- w_down: bfloat16 [8192, 2048], P('head', ('dp', 'stream')), may hold values from -0.0625 to 0.0625
- cotangent: bfloat16 [4, 2048, 2048], P('dp', 'stream', 'head'), may hold values from -6 to 6
Outputs:
- block_out: bfloat16 [4, 2048, 2048], P('dp', 'stream', 'head')
- mix_weights: float32 [4, 2048, 36], P('dp', 'stream')
- history_grad: float32 [9, 4, 2048, 2048], P(None, 'dp', 'stream', 'head')
- w_mix_in_grad: float32 [2048, 36], P('head')
- w_mix_out_grad: float32 [36, 36], replicated
- mix_bias_grad: float32 [4, 9], replicated
- ln_gain_grad: float32 [4, 2048], P(None, 'head')
- ln_bias_grad: float32 [4, 2048], P(None, 'head')
- w_qkv_grad: float32 [3, 2048, 2048], P(None, ('dp', 'stream'), 'head')
- w_attn_out_grad: float32 [2048, 2048], P('head', ('dp', 'stream'))
- w_up_grad: float32 [2048, 8192], P(('dp', 'stream'), 'head')
- w_down_grad: float32 [8192, 2048], P('head', ('dp', 'stream'))
The draws below stay inside these ranges and needn't reach their ends.
Inputs may be any that keep to these rules, and one draw needn't show every extreme that they name: `seq_lens`: each bucket holds either one sequence of 1024 to 2048 tokens or two sequences of 1024 tokens each, in its first entries; the other entries are 0 and the places after the lengths' sum are padding. Slot k, the bucket of micro-batch k % 2 of dp member k // 2, takes the lengths of bucket bucket_slot[k]; every bucket is taken once.
All inputs are finite; a program needn't handle non-finite values.
Results may differ from the reference program's by a relative error of at most 0.02.
Values may be sent and summed in bfloat16 or wider, within the bound.
A program may use at most 216 MiB of HBM per device.

```python
from functools import partial
import jax
import jax.numpy as jnp
from jax import lax

D = 2048
HEADS = 16
HD = 128
FF = 8192
HIST = 9
MIXH = 36
ROT = 32
BUCKET = 2048
NB = 4


def draw_seq_lens(key, part):
    key = jax.random.fold_in(key, 7)
    mode_key, length_key = jax.random.split(key, 2)
    rows = jnp.arange(NB)
    single = jax.random.randint(length_key, (NB,), BUCKET // 2, BUCKET + 1)
    single = jnp.where(rows == 0, BUCKET, single)
    paired = jax.random.randint(mode_key, (NB,), 0, 4) == 0
    paired = jnp.where(rows == 1, True, jnp.where(rows == 0, False, paired))
    first_len = jnp.where(paired, BUCKET // 2, single)
    second_len = jnp.where(paired, BUCKET // 2, 0)
    third_len = jnp.zeros((NB,), jnp.int32)
    return jnp.stack([first_len, second_len, third_len], axis=1).astype(jnp.int32)


def levels(key, dims, cuts, low, largest):
    gain = 1.0
    for dim, blocks in cuts:
        steps = jax.random.uniform(jax.random.fold_in(jax.random.fold_in(key, 6), dim), (blocks,), jnp.float32, low / len(cuts), largest / len(cuts))
        gain = gain * jnp.repeat(jnp.exp(steps), dims[dim] // blocks).reshape((-1,) + (1,) * (len(dims) - 1 - dim))
    return gain


def bell_draw(stream_key, extent, deviation, limit, cuts=(), kind=jnp.bfloat16):
    result = deviation * jax.random.normal(stream_key, extent, jnp.float32)
    if cuts:
        result = result * levels(stream_key, extent, cuts, -0.22, 0.18)
    return jnp.clip(result, -limit, limit).astype(kind)


def setup_inputs(seed: int = 0) -> dict:
    splits = jax.random.split(jax.random.key(seed), 14)
    return {
        "history": bell_draw(splits[0], (HIST, NB, BUCKET, D), 1.0, 6.0, ((1, 2), (2, 4), (3, 4))),
        "seq_lens": draw_seq_lens(jax.random.fold_in(splits[13], 71), 0),
        "bucket_slot": jax.random.permutation(splits[2], NB).astype(jnp.int32),
        "w_mix_in": bell_draw(splits[3], (D, MIXH), D ** -0.5, 0.125, ((0, 4),)),
        "w_mix_out": bell_draw(splits[4], (MIXH, 4 * HIST), MIXH ** -0.5, 1.0),
        "mix_bias": bell_draw(splits[5], (4, HIST), 0.5, 3.0, (), jnp.float32),
        "ln_gain": jnp.clip(1.0 + 0.15 * jax.random.normal(splits[6], (4, D), jnp.float32), 0.25, 1.75),
        "ln_bias": bell_draw(splits[7], (4, D), 0.3, 2.0, ((1, 4),), jnp.float32),
        "w_qkv": bell_draw(splits[8], (3, D, D), D ** -0.5, 0.125, ((1, 8), (2, 4))),
        "w_attn_out": bell_draw(splits[9], (D, D), (max(D // 512, 1)) ** -0.5, 3.0, ((0, 4), (1, 8))),
        "w_up": bell_draw(splits[10], (D, FF), D ** -0.5, 0.125, ((0, 8), (1, 4))),
        "w_down": bell_draw(splits[11], (FF, D), FF ** -0.5, 0.0625, ((0, 4), (1, 8))),
        "cotangent": bell_draw(splits[12], (NB, BUCKET, D), 1.0, 6.0, ((0, 2), (1, 4), (2, 4))),
    }


EPSILON = 1e-05
HIGHEST = lax.Precision.HIGHEST
MASKED = -1e+30

@jax.custom_vjp
def low(v):
    return lax.optimization_barrier(v.astype(jnp.bfloat16)).astype(jnp.float32)

@jax.custom_vjp
def low_back(v):
    return v

def low_keep(v):
    return (low(v), None)

def low_pass(kept, grad):
    return (grad,)

def back_keep(v):
    return (v, None)

def back_low(kept, grad):
    return (low(grad),)
low.defvjp(low_keep, low_pass)
low_back.defvjp(back_keep, back_low)

def rotate(values_in, cosine, sine_table):
    half_width = cosine.shape[-1]
    first_part = values_in[..., :half_width]
    second = values_in[..., half_width:2 * half_width]
    remain = values_in[..., 2 * half_width:]
    cos_heads = cosine[:, None, :]
    sin_heads = sine_table[:, None, :]
    return jnp.concatenate([first_part * cos_heads - second * sin_heads, second * cos_heads + first_part * sin_heads, remain], axis=-1)

def layout(lengths, length_total):
    bounds = jnp.cumsum(lengths).astype(jnp.int32)
    places = jnp.arange(length_total, dtype=jnp.int32)
    passed = (places[:, None] >= bounds[None, :]).astype(jnp.int32)
    segment = lax.optimization_barrier(jnp.sum(passed, axis=1)).astype(jnp.int32)
    starts = lax.optimization_barrier(jnp.sum(passed * lengths[None, :].astype(jnp.int32), axis=1)).astype(jnp.int32)
    return (segment, places - starts)

def angle_tables(position, rotary_dims):
    freq_index = jnp.arange(rotary_dims // 2, dtype=jnp.float32)
    inverse = 10000.0 ** (-2.0 * freq_index / rotary_dims)
    phases = position.astype(jnp.float32)[..., None] * inverse
    return (jnp.cos(phases), jnp.sin(phases))

def reference(history, seq_lens, bucket_slot, w_mix_in, w_mix_out, mix_bias, ln_gain, ln_bias, w_qkv, w_attn_out, w_up, w_down, cotangent):
    slot_lens = jnp.take(seq_lens, bucket_slot.astype(jnp.int32), axis=0)
    segment, position = jax.vmap(partial(layout, length_total=BUCKET))(slot_lens)
    valid_rows = (segment < 3).astype(jnp.float32)
    cosine, sine_table = angle_tables(position.reshape(-1), ROT)
    places = jnp.arange(BUCKET, dtype=jnp.int32)
    causal = places[None, :] <= places[:, None]
    score_scale = HD ** (-0.5)

    def attend(pieces):
        query_block, key_block, value_block, seg_row = pieces
        scores = low_back(jnp.einsum('qhd,khd->hqk', query_block, key_block, precision=HIGHEST) * score_scale)
        allowed = (seg_row[:, None] == seg_row[None, :]) & causal
        scores = jnp.where(allowed[None], scores, MASKED)
        prob_bf = low(jax.nn.softmax(scores, axis=-1))
        return jnp.einsum('hqk,khd->qhd', prob_bf, value_block, precision=HIGHEST)

    def shaped(array_in):
        return array_in.reshape(NB, BUCKET, HEADS, HD)

    def forward(history, w_mix_in, w_mix_out, mix_bias, ln_gain, ln_bias, w_qkv, w_attn_out, w_up, w_down):
        current = history[HIST - 1]
        rms_scale = lax.rsqrt(lax.optimization_barrier(jnp.mean(current * current, axis=-1, keepdims=True)) + EPSILON)
        mix_pre = jnp.dot(current * rms_scale, w_mix_in, precision=HIGHEST)
        mix_hidden = jax.nn.gelu(mix_pre, approximate=False)
        mix_weights = jnp.dot(mix_hidden, w_mix_out, precision=HIGHEST) + mix_bias.reshape(-1)
        weights_four = mix_weights.reshape(NB, BUCKET, 4, HIST)
        streams = jnp.einsum('nbsj,jnbd->snbd', weights_four, history, precision=HIGHEST)
        row_means = lax.optimization_barrier(jnp.mean(streams, axis=-1, keepdims=True))
        squares = lax.optimization_barrier(jnp.mean(streams * streams, axis=-1, keepdims=True))
        inv_std = lax.rsqrt(squares - row_means * row_means + EPSILON)
        normed = low((streams - row_means) * inv_std * ln_gain[:, None, None, :] + ln_bias[:, None, None, :])
        flat_streams = normed.reshape(4, NB * BUCKET, D)
        query_pre = low_back(jnp.dot(flat_streams[0], w_qkv[0], precision=HIGHEST))
        key_pre = low_back(jnp.dot(flat_streams[1], w_qkv[1], precision=HIGHEST))
        value_pre = low_back(jnp.dot(flat_streams[2], w_qkv[2], precision=HIGHEST))
        up_pre = low_back(jnp.dot(flat_streams[3], w_up, precision=HIGHEST))
        gated_up = low(jax.nn.gelu(up_pre, approximate=False))
        queries = low(rotate(query_pre.reshape(-1, HEADS, HD), cosine, sine_table))
        key_rows = low(rotate(key_pre.reshape(-1, HEADS, HD), cosine, sine_table))
        values = low(value_pre.reshape(-1, HEADS, HD))
        attended = lax.map(jax.checkpoint(attend), (shaped(queries), shaped(key_rows), shaped(values), segment))
        attended = low_back(low(attended * valid_rows[:, :, None, None]))
        combined = jnp.dot(attended.reshape(NB * BUCKET, D), w_attn_out, precision=HIGHEST) + jnp.dot(gated_up, w_down, precision=HIGHEST)
        output = valid_rows[:, :, None] * (streams[3] + combined.reshape(NB, BUCKET, D))
        return (output, mix_weights)
    output, pullback, mix_weights = jax.vjp(forward, history.astype(jnp.float32), w_mix_in.astype(jnp.float32), w_mix_out.astype(jnp.float32), mix_bias.astype(jnp.float32), ln_gain.astype(jnp.float32), ln_bias.astype(jnp.float32), w_qkv.astype(jnp.float32), w_attn_out.astype(jnp.float32), w_up.astype(jnp.float32), w_down.astype(jnp.float32), has_aux=True)
    grads = pullback(cotangent.astype(jnp.float32))
    return (output.astype(jnp.bfloat16), mix_weights, grads[0], grads[1], grads[2], grads[3], grads[4], grads[5], grads[6], grads[7], grads[8], grads[9])
```

```python
import functools

import jax
import jax.numpy as jnp
from jax import lax
from jax.experimental import pallas as pl
from jax.experimental.pallas import tpu as pltpu
from jax.sharding import PartitionSpec as P

HD = 128
HIST = 9
ROT = 32

EPSILON = 1e-05
HIGHEST = lax.Precision.HIGHEST
MASKED = -1e30
F32 = jnp.float32
BF16 = jnp.bfloat16

SWAP_X = [(0, 1), (1, 0)]
SWAP_Y = [(0, 2), (2, 0), (1, 3), (3, 1)]
SWAP_CORE = [(0, 1), (1, 0), (2, 3), (3, 2)]


def dot(a, b):
    return jnp.dot(a, b, preferred_element_type=F32)


def dot_nt(a, b):
    return lax.dot_general(a, b, (((1,), (1,)), ((), ())), preferred_element_type=F32)


def dot_tn(a, b):
    return lax.dot_general(a, b, (((0,), (0,)), ((), ())), preferred_element_type=F32)


def gelu_exact(values_in):
    return jax.nn.gelu(values_in, approximate=False)


def over_x(a):
    return lax.ppermute(a, "dp", SWAP_X)


def over_y(a):
    return lax.ppermute(a, "stream", SWAP_Y)


def over_core(a):
    return lax.ppermute(a, "stream", SWAP_CORE)


def paired():
    return lax.axis_size("dp") == 2 and lax.axis_size("stream") == 4


def gather_weight(shard, axis):
    if not paired():
        return lax.all_gather(shard, ("dp", "stream"), axis=axis, tiled=True)
    place = lax.axis_index("dp") * 4 + lax.axis_index("stream")
    width = shard.shape[axis]
    full_shape = list(shard.shape)
    full_shape[axis] = width * 8
    near_x = over_x(shard)
    near_y = over_y(shard)
    half = shard.shape[-2] // 2
    low = lax.slice_in_dim(near_x, 0, half, axis=shard.ndim - 2)
    high = lax.slice_in_dim(near_y, half, 2 * half, axis=shard.ndim - 2)
    far = jnp.concatenate([over_y(low), over_x(high)], axis=shard.ndim - 2)
    full = jnp.zeros(full_shape, shard.dtype)
    for flip, block in ((0, shard), (4, near_x), (2, near_y), (6, far)):
        full = lax.dynamic_update_slice_in_dim(full, block, (place ^ flip) * width, axis)
        full = lax.dynamic_update_slice_in_dim(
            full, over_core(block), (place ^ flip ^ 1) * width, axis
        )
    return full


def scatter_product(rows, columns):
    if not paired():
        return lax.psum_scatter(
            dot_tn(rows, columns).astype(BF16),
            ("dp", "stream"),
            scatter_dimension=0,
            tiled=True,
        ).astype(F32)
    tokens, model_width = rows.shape
    width = model_width // 8
    stream = lax.axis_index("stream")
    x, y, core = lax.axis_index("dp"), stream // 2, stream % 2
    split = rows.reshape(tokens, 4, 2, width)
    mine = lax.dynamic_index_in_dim(split, core, 2, keepdims=False).reshape(tokens, 4 * width)
    other = lax.dynamic_index_in_dim(split, 1 - core, 2, keepdims=False).reshape(tokens, 4 * width)
    received = over_core(dot_tn(other, columns).astype(BF16))
    chip = (dot_tn(mine, columns) + received.astype(F32)).astype(BF16)
    half = columns.shape[1] // 2
    chip = chip.reshape(2, 2, width, 2 * half)
    first, second = chip[..., :half], chip[..., half:]

    def pick(a, index, axis):
        return lax.dynamic_index_in_dim(a, index, axis, keepdims=False)

    def add(a, b):
        return a.astype(F32) + b.astype(F32)

    first_x = add(pick(first, x, 0), over_x(pick(first, 1 - x, 0))).astype(BF16)
    second_y = add(pick(second, y, 1), over_y(pick(second, 1 - y, 1))).astype(BF16)
    first_out = add(pick(first_x, y, 0), over_y(pick(first_x, 1 - y, 0)))
    second_out = add(pick(second_y, x, 0), over_x(pick(second_y, 1 - x, 0)))
    return jnp.concatenate([first_out, second_out], axis=1)


def attention_kernel(place_ref, q_ref, do_ref, start_ref, *refs):
    blocks = (len(refs) - 4) // 4
    k_refs, v_refs = refs[:blocks], refs[blocks : 2 * blocks]
    o_ref, dq_ref = refs[2 * blocks : 2 * blocks + 2]
    dk_refs = refs[2 * blocks + 2 : 3 * blocks + 2]
    dv_refs = refs[3 * blocks + 2 : 4 * blocks + 2]
    s_ref, dp_ref = refs[4 * blocks + 2 :]
    rows = q_ref.shape[1]
    scale = HD ** (-0.5)
    member = place_ref[0]
    q, d_out = q_ref[0], do_ref[0]
    start = start_ref[0]
    top = jnp.full((rows, 1), MASKED, F32)
    t = member * rows + lax.broadcasted_iota(jnp.int32, (rows, rows), 0)
    for j in range(blocks):
        u = place_ref[j] * rows + lax.broadcasted_iota(jnp.int32, (rows, rows), 1)
        allowed = (u <= t) & (u >= start)
        s_ref[j] = jnp.where(allowed, dot_nt(q, k_refs[j][0]) * scale, MASKED)
        top = jnp.maximum(top, jnp.max(s_ref[j], axis=1, keepdims=True))
    total = jnp.zeros((rows, 1), F32)
    for j in range(blocks):
        e = jnp.exp(s_ref[j] - top)
        s_ref[j] = e
        total = total + jnp.sum(e, axis=1, keepdims=True)
    inverse = 1.0 / total
    out = jnp.zeros((rows, HD), F32)
    delta = jnp.zeros((rows, 1), F32)
    for j in range(blocks):
        p = s_ref[j] * inverse
        s_ref[j] = p
        p_bf = p.astype(BF16)
        out = out + dot(p_bf, v_refs[j][0])
        dv_refs[j][0] = dot_tn(p_bf, d_out).astype(BF16)
        d_p = dot_nt(d_out, v_refs[j][0])
        dp_ref[j] = d_p
        delta = delta + jnp.sum(p * d_p, axis=1, keepdims=True)
    o_ref[0] = out.astype(BF16)
    d_q = jnp.zeros((rows, HD), F32)
    for j in range(blocks):
        d_s = (s_ref[j] * (dp_ref[j] - delta)).astype(BF16)
        d_q = d_q + dot(d_s, k_refs[j][0])
        dk_refs[j][0] = (dot_tn(d_s, q) * scale).astype(BF16)
    dq_ref[0] = d_q * scale


def attention(places, queries, d_attended, starts, keys, values):
    micro, rows, feats = queries.shape
    blocks = len(keys)
    tile = pl.BlockSpec((1, rows, HD), lambda b, h: (b, 0, h))
    like = lambda dtype: jax.ShapeDtypeStruct((micro, rows, feats), dtype)
    return pl.pallas_call(
        attention_kernel,
        grid=(micro, feats // HD),
        in_specs=[pl.BlockSpec(memory_space=pltpu.SMEM), tile, tile]
        + [pl.BlockSpec((1, rows, 1), lambda b, h: (b, 0, 0))]
        + [tile] * (2 * blocks),
        out_specs=[tile] * (2 + 2 * blocks),
        out_shape=[like(BF16), like(F32)] + [like(BF16)] * (2 * blocks),
        scratch_shapes=[
            pltpu.VMEM((blocks, rows, rows), F32),
            pltpu.VMEM((blocks, rows, rows), F32),
        ],
        compiler_params=pltpu.CompilerParams(vmem_limit_bytes=40 * 1024 * 1024),
        cost_estimate=pl.CostEstimate(
            flops=12 * micro * feats * rows * rows * blocks,
            bytes_accessed=micro * rows * feats * 2 * (4 + 4 * blocks),
            transcendentals=micro * rows * rows * blocks * feats // HD,
        ),
        name="attention_both_ways",
    )(places, queries, d_attended, starts, *keys, *values)


def exchange_rows(local):
    if lax.axis_size("stream") != 4:
        raise ValueError("stream")
    across = lax.ppermute(local, "stream", [(0, 2), (1, 3)])
    beside = over_core(local)
    return (local, beside, across, over_core(across))


def reduce_rows(parts):
    add = lambda a, b: a.astype(F32) + b.astype(F32)
    across = add(parts[2], over_core(parts[3])).astype(BF16)
    return add(
        add(parts[0], over_core(parts[1])), lax.ppermute(across, "stream", [(2, 0), (3, 1)])
    )


def rotate(values_in, cosine, sine, sign):
    tokens, feats = values_in.shape
    rest = HD - ROT
    ones, zeros = jnp.ones((tokens, rest), F32), jnp.zeros((tokens, rest), F32)
    none = jnp.zeros_like(sine)
    heads = feats // HD
    keep = jnp.tile(jnp.concatenate([cosine, cosine, ones], axis=1), (1, heads))
    left = jnp.tile(jnp.concatenate([-sign * sine, none, zeros], axis=1), (1, heads))
    right = jnp.tile(jnp.concatenate([none, sign * sine, zeros], axis=1), (1, heads))
    h = ROT // 2
    return (
        values_in * keep
        + jnp.roll(values_in, -h, axis=1) * left
        + jnp.roll(values_in, h, axis=1) * right
    )


def shards(
    history,
    seq_lens,
    bucket_slot,
    w_mix_in,
    w_mix_out,
    mix_bias,
    ln_gain,
    ln_bias,
    w_qkv,
    w_attn_out,
    w_up,
    w_down,
    cotangent,
):
    member = lax.axis_index("stream")
    micro, quarter, feats = history.shape[1:]
    tokens = micro * quarter
    model_width = feats * lax.axis_size("head")
    slot_base = lax.axis_index("dp") * micro
    slot_ids = jnp.arange(bucket_slot.shape[0], dtype=jnp.int32)
    query_places = member * quarter + jnp.arange(quarter, dtype=jnp.int32)
    w_mix_in_f = w_mix_in.astype(F32)
    w_mix_out_f = w_mix_out.astype(F32)

    segments, starts = [], []
    for index in range(micro):
        bucket = jnp.sum(jnp.where(slot_ids == slot_base + index, bucket_slot, 0))
        lengths = jnp.sum(jnp.where(slot_ids[:, None] == bucket, seq_lens, 0), axis=0)
        bounds = jnp.cumsum(lengths)
        passed = (query_places[:, None] >= bounds[None, :]).astype(jnp.int32)
        segments.append(jnp.sum(passed, axis=1))
        starts.append(jnp.sum(passed * lengths[None, :], axis=1))
    valid = (jnp.concatenate(segments) < 3).astype(F32)[:, None]
    starts = jnp.concatenate(starts)
    position = jnp.tile(query_places, micro) - starts
    frequency = jnp.arange(ROT // 2, dtype=F32)
    phases = position.astype(F32)[:, None] * (10000.0 ** (-2.0 * frequency / ROT))
    cosine, sine = jnp.cos(phases), jnp.sin(phases)

    cot_rows = cotangent.reshape(tokens, feats).astype(F32) * valid
    out_full = lax.all_gather(cot_rows.astype(BF16), "head", axis=1, tiled=True)
    wq, wk, wv = (gather_weight(w_qkv[i], 0) for i in range(3))
    w_out_full = gather_weight(w_attn_out, 1)
    up_full = gather_weight(w_up, 0)
    down_full = gather_weight(w_down, 1)

    history = history.reshape(HIST, tokens, feats)
    current = history[HIST - 1]
    current_f = current.astype(F32)
    mix_sum, square_sum = lax.psum(
        (dot(current, w_mix_in), jnp.sum(current_f * current_f, axis=1)), "head"
    )
    rms_scale = lax.rsqrt(square_sum / model_width + EPSILON)[:, None]
    mix_pre = mix_sum * rms_scale
    mix_hidden = gelu_exact(mix_pre)
    mix_weights = jnp.dot(mix_hidden, w_mix_out_f, precision=HIGHEST) + mix_bias.reshape(-1)
    weights_four = mix_weights.reshape(tokens, 4, HIST)
    streams = jnp.zeros((4, tokens, feats), F32)
    for layer in range(HIST):
        streams = (
            streams
            + jnp.transpose(weights_four[:, :, layer])[:, :, None]
            * history[layer].astype(F32)[None]
        )
    stat_sum, stat_square = lax.psum(
        (jnp.sum(streams, axis=2), jnp.sum(streams * streams, axis=2)), "head"
    )
    row_means = (stat_sum / model_width)[:, :, None]
    inv_std = lax.rsqrt(stat_square[:, :, None] / model_width - row_means * row_means + EPSILON)
    centered = (streams - row_means) * inv_std
    normed = (centered * ln_gain[:, None, :] + ln_bias[:, None, :]).astype(BF16)

    def all_features(stream):
        return lax.all_gather(normed[stream], "head", axis=1, tiled=True)

    k_in, v_in, q_in, up_in = all_features(1), all_features(2), all_features(0), all_features(3)

    keys = rotate(dot(k_in, wk), cosine, sine, 1.0).astype(BF16)
    values = dot(v_in, wv).astype(BF16)
    queries = rotate(dot(q_in, wq), cosine, sine, 1.0).astype(BF16)
    d_attended = dot_nt(out_full, w_out_full).astype(BF16) * valid.astype(BF16)
    by_micro = lambda a: a.reshape(micro, quarter, feats)
    key_blocks = exchange_rows(by_micro(keys))
    value_blocks = exchange_rows(by_micro(values))
    places = member ^ jnp.arange(4, dtype=jnp.int32)
    results = attention(
        places,
        by_micro(queries),
        by_micro(d_attended),
        starts.reshape(micro, quarter, 1),
        key_blocks,
        value_blocks,
    )
    attended, d_queries = results[0].reshape(tokens, feats), results[1].reshape(tokens, feats)
    attended = attended * valid.astype(BF16)
    d_keys = reduce_rows(results[2:6]).reshape(tokens, feats)
    d_values = reduce_rows(results[6:10]).reshape(tokens, feats)
    d_query_pre = rotate(d_queries, cosine, sine, -1.0).astype(BF16)
    d_key_pre = rotate(d_keys, cosine, sine, -1.0).astype(BF16)
    d_value_pre = d_values.astype(BF16)

    up_pre = dot(up_in, up_full)
    gated_up = gelu_exact(up_pre).astype(BF16)
    _, gelu_back = jax.vjp(gelu_exact, up_pre)
    d_up = gelu_back(dot_nt(out_full, down_full))[0].astype(BF16)

    def to_owner(partial):
        return lax.psum_scatter(
            partial.astype(BF16), "head", scatter_dimension=1, tiled=True
        ).astype(F32)

    g_up = to_owner(dot_nt(d_up, up_full))
    g_query = to_owner(dot_nt(d_query_pre, wq))
    g_key = to_owner(dot_nt(d_key_pre, wk))
    g_value = to_owner(dot_nt(d_value_pre, wv))
    branch = to_owner(dot(attended, w_out_full) + dot(gated_up, down_full))
    block_out = (valid * (streams[3] + branch)).astype(BF16)

    grad_up = scatter_product(up_in, d_up)
    grad_down = scatter_product(out_full, gated_up).T
    grad_attn_out = scatter_product(out_full, attended).T
    grad_qkv = jnp.stack(
        [
            scatter_product(q_in, d_query_pre),
            scatter_product(k_in, d_key_pre),
            scatter_product(v_in, d_value_pre),
        ]
    )

    stream_grad = jnp.stack([g_query, g_key, g_value, g_up])
    d_centered = stream_grad * ln_gain[:, None, :]
    sum_grad, sum_cross = lax.psum(
        (jnp.sum(d_centered, axis=2), jnp.sum(d_centered * centered, axis=2)), "head"
    )
    d_streams = inv_std * (
        d_centered
        - sum_grad[:, :, None] / model_width
        - centered * sum_cross[:, :, None] / model_width
    )
    grad_gain = jnp.sum(stream_grad * centered, axis=1)
    grad_shift = jnp.sum(stream_grad, axis=1)
    d_streams = jnp.concatenate([d_streams[:3], (d_streams[3] + cot_rows)[None]], axis=0)
    layer_grads = []
    d_mix_parts = []
    for layer in range(HIST):
        layer_f = history[layer].astype(F32)
        layer_grads.append(
            jnp.sum(jnp.transpose(weights_four[:, :, layer])[:, :, None] * d_streams, axis=0)
        )
        d_mix_parts.append(jnp.sum(d_streams * layer_f[None], axis=2))
    d_mix_local = jnp.transpose(jnp.stack(d_mix_parts, axis=-1), (1, 0, 2)).reshape(
        tokens, 4 * HIST
    )
    d_mix = lax.psum(d_mix_local.astype(BF16), "head").astype(F32)
    grad_bias = jnp.sum(d_mix, axis=0)
    grad_w2 = jnp.dot(mix_hidden.T, d_mix, precision=HIGHEST)
    d_hidden = jnp.dot(d_mix, w_mix_out_f.T, precision=HIGHEST)
    _, gelu_mix_back = jax.vjp(gelu_exact, mix_pre)
    d_pre = gelu_mix_back(d_hidden)[0]
    normed_in = current_f * rms_scale
    grad_w1 = jnp.dot(normed_in.T, d_pre, precision=HIGHEST)
    d_normed_in = jnp.dot(d_pre, w_mix_in_f.T, precision=HIGHEST)
    cross = jnp.sum(d_pre * mix_pre, axis=1, keepdims=True)
    layer_grads[HIST - 1] = layer_grads[HIST - 1] + rms_scale * (
        d_normed_in - normed_in * cross / model_width
    )
    history_grad = jnp.stack(layer_grads).reshape(HIST, micro, quarter, feats)
    small = [
        lax.psum(a.astype(BF16), ("dp", "stream")).astype(F32)
        for a in (grad_w1, grad_w2, grad_bias, grad_gain, grad_shift)
    ]
    return (
        block_out.reshape(micro, quarter, feats),
        mix_weights.reshape(micro, quarter, 4 * HIST),
        history_grad,
        small[0],
        small[1],
        small[2].reshape(mix_bias.shape),
        small[3],
        small[4],
        grad_qkv,
        grad_attn_out,
        grad_up,
        grad_down,
    )


def solution(mesh):
    return jax.shard_map(
        shards,
        mesh=mesh,
        in_specs=(
            P(None, "dp", "stream", "head"),
            P(),
            P(),
            P("head", None),
            P(),
            P(),
            P(None, "head"),
            P(None, "head"),
            P(None, ("dp", "stream"), "head"),
            P("head", ("dp", "stream")),
            P(("dp", "stream"), "head"),
            P("head", ("dp", "stream")),
            P("dp", "stream", "head"),
        ),
        out_specs=(
            P("dp", "stream", "head"),
            P("dp", "stream", None),
            P(None, "dp", "stream", "head"),
            P("head", None),
            P(),
            P(),
            P(None, "head"),
            P(None, "head"),
            P(None, ("dp", "stream"), "head"),
            P("head", ("dp", "stream")),
            P(("dp", "stream"), "head"),
            P("head", ("dp", "stream")),
        ),
        check_vma=False,
    )
```

```python
import functools

import jax
import jax.numpy as jnp
from jax import lax
from jax.experimental import pallas as pl
from jax.experimental.pallas import tpu as pltpu
from jax.sharding import PartitionSpec as P

HD = 128
HIST = 9
ROT = 32

EPSILON = 1e-05
HIGHEST = lax.Precision.HIGHEST
MASKED = -1e30
F32 = jnp.float32
BF16 = jnp.bfloat16

SWAP_X = [(0, 1), (1, 0)]
SWAP_Y = [(0, 2), (2, 0), (1, 3), (3, 1)]
SWAP_CORE = [(0, 1), (1, 0), (2, 3), (3, 2)]


def dot(a, b):
    return jnp.dot(a, b, preferred_element_type=F32)


def dot_nt(a, b):
    return lax.dot_general(a, b, (((1,), (1,)), ((), ())), preferred_element_type=F32)


def dot_tn(a, b):
    return lax.dot_general(a, b, (((0,), (0,)), ((), ())), preferred_element_type=F32)


def gelu_exact(values_in):
    return jax.nn.gelu(values_in, approximate=False)


def over_x(a):
    return lax.ppermute(a, "dp", SWAP_X)


def over_y(a):
    return lax.ppermute(a, "stream", SWAP_Y)


def over_core(a):
    return lax.ppermute(a, "stream", SWAP_CORE)


def paired():
    return lax.axis_size("dp") == 2 and lax.axis_size("stream") == 4


def place_kernel(order_ref, near_ref, beside_ref, out_ref):
    step = pl.program_id(0)
    half = pl.num_programs(0) // 2

    @pl.when(step < half)
    def _():
        out_ref[...] = near_ref[0]

    @pl.when(step >= half)
    def _():
        out_ref[...] = beside_ref[0]


def gather_weight(shard, axis):
    if not paired():
        return lax.all_gather(shard, ("dp", "stream"), axis=axis, tiled=True)
    place = lax.axis_index("dp") * 4 + lax.axis_index("stream")
    row = jnp.stack([shard, over_x(shard)])
    near = jnp.concatenate([row, over_y(row)])
    beside = over_core(near)
    flips = jnp.array([0, 4, 2, 6, 1, 5, 3, 7], jnp.int32)
    full_shape = tuple(n * 8 if i == axis else n for i, n in enumerate(shard.shape))
    at = lambda k: tuple(k if i == axis else 0 for i in range(shard.ndim))
    inner = (0,) * shard.ndim
    return pl.pallas_call(
        place_kernel,
        grid_spec=pltpu.PrefetchScalarGridSpec(
            num_scalar_prefetch=1,
            grid=(8,),
            in_specs=[
                pl.BlockSpec((1,) + shard.shape, lambda k, order: (jnp.minimum(k, 3),) + inner),
                pl.BlockSpec((1,) + shard.shape, lambda k, order: (jnp.maximum(k - 4, 0),) + inner),
            ],
            out_specs=pl.BlockSpec(shard.shape, lambda k, order: at(order[k])),
        ),
        out_shape=jax.ShapeDtypeStruct(full_shape, shard.dtype),
        compiler_params=pltpu.CompilerParams(vmem_limit_bytes=40 * 1024 * 1024),
        cost_estimate=pl.CostEstimate(flops=0, bytes_accessed=32 * shard.size, transcendentals=0),
        name="weight_in_order",
    )(place ^ flips, near, beside)


def scatter_sum(partial):
    if not paired():
        return lax.psum_scatter(
            partial, ("dp", "stream"), scatter_dimension=0, tiled=True
        ).astype(F32)
    rows, columns = partial.shape
    stream = lax.axis_index("stream")
    x, y, core = lax.axis_index("dp"), stream // 2, stream % 2

    def pick(a, index, axis):
        return lax.dynamic_index_in_dim(a, index, axis, keepdims=False)

    def add(a, b):
        return a.astype(F32) + b.astype(F32)

    split = partial.reshape(4, 2, rows // 8, columns)
    chip = add(pick(split, core, 1), over_core(pick(split, 1 - core, 1))).astype(BF16)
    chip = chip.reshape(2, 2, rows // 8, columns)
    line = add(pick(chip, x, 0), over_x(pick(chip, 1 - x, 0))).astype(BF16)
    return add(pick(line, y, 0), over_y(pick(line, 1 - y, 0)))


def head_sum_kernel(members, x_ref, out_ref, slots, send_sem, recv_sem):
    z = lax.axis_index("head")
    barrier = pltpu.get_barrier_semaphore()
    for k in range(1, members):
        pl.semaphore_signal(
            barrier,
            inc=1,
            device_id={"head": lax.rem(z + k, members)},
            device_id_type=pl.DeviceIdType.MESH,
        )
    pl.semaphore_wait(barrier, members - 1)
    copies = []
    for k in range(1, members):
        copy = pltpu.make_async_remote_copy(
            src_ref=x_ref,
            dst_ref=slots.at[z],
            send_sem=send_sem.at[k - 1],
            recv_sem=recv_sem.at[k - 1],
            device_id={"head": lax.rem(z + k, members)},
            device_id_type=pl.DeviceIdType.MESH,
        )
        copy.start()
        copies.append(copy)
    slots[z] = x_ref[...]
    for copy in copies:
        copy.wait()
    total = slots[0]
    for k in range(1, members):
        total = total + slots[k]
    out_ref[...] = total


def head_sum(x, collective_id):
    members = lax.axis_size("head")
    return pl.pallas_call(
        functools.partial(head_sum_kernel, members),
        out_shape=jax.ShapeDtypeStruct(x.shape, F32),
        in_specs=[pl.BlockSpec(memory_space=pltpu.VMEM)],
        out_specs=pl.BlockSpec(memory_space=pltpu.VMEM),
        scratch_shapes=[
            pltpu.VMEM((members,) + x.shape, F32),
            pltpu.SemaphoreType.DMA((members - 1,)),
            pltpu.SemaphoreType.DMA((members - 1,)),
        ],
        compiler_params=pltpu.CompilerParams(collective_id=collective_id, has_side_effects=True),
        name="sum_over_head",
    )(x)


def turn(v, keep, left, right):
    h = ROT // 2
    return v * keep + pltpu.roll(v, HD - h, 1) * left + pltpu.roll(v, h, 1) * right


def rotate_kernel(sign, v_ref, keep_ref, left_ref, right_ref, out_ref):
    for head in range(v_ref.shape[1] // HD):
        part = pl.ds(head * HD, HD)
        out_ref[:, part] = turn(
            v_ref[:, part], keep_ref[...], sign * left_ref[...], sign * right_ref[...]
        ).astype(BF16)


def rotate(values_in, tables, sign):
    tokens, feats = values_in.shape
    block = min(tokens, 256)
    table = pl.BlockSpec((block, HD), lambda i: (i, 0))
    wide = pl.BlockSpec((block, feats), lambda i: (i, 0))
    return pl.pallas_call(
        functools.partial(rotate_kernel, sign),
        grid=(tokens // block,),
        in_specs=[wide, table, table, table],
        out_specs=wide,
        out_shape=jax.ShapeDtypeStruct((tokens, feats), BF16),
        cost_estimate=pl.CostEstimate(
            flops=5 * tokens * feats, bytes_accessed=8 * tokens * feats, transcendentals=0
        ),
        name="rotate_heads",
    )(values_in, *tables)


def attention_kernel(
    place_ref, q_ref, do_ref, start_ref, valid_ref, keep_ref, left_ref, right_ref, *refs
):
    blocks = (len(refs) - 4) // 4
    k_refs, v_refs = refs[:blocks], refs[blocks : 2 * blocks]
    o_ref, dq_ref = refs[2 * blocks : 2 * blocks + 2]
    dk_refs = refs[2 * blocks + 2 : 3 * blocks + 2]
    dv_refs = refs[3 * blocks + 2 : 4 * blocks + 2]
    s_ref, dp_ref = refs[4 * blocks + 2 :]
    rows = q_ref.shape[1]
    scale = HD ** (-0.5)
    member = place_ref[0]
    keep, left, right = keep_ref[0], left_ref[0], right_ref[0]
    q = turn(q_ref[0], keep, left, right).astype(BF16)
    d_out = do_ref[0]
    start = start_ref[0]
    top = jnp.full((rows, 1), MASKED, F32)
    t = member * rows + lax.broadcasted_iota(jnp.int32, (rows, rows), 0)
    for j in range(blocks):
        u = place_ref[j] * rows + lax.broadcasted_iota(jnp.int32, (rows, rows), 1)
        allowed = (u <= t) & (u >= start)
        s_ref[j] = jnp.where(allowed, dot_nt(q, k_refs[j][0]) * scale, MASKED)
        top = jnp.maximum(top, jnp.max(s_ref[j], axis=1, keepdims=True))
    total = jnp.zeros((rows, 1), F32)
    for j in range(blocks):
        e = jnp.exp(s_ref[j] - top)
        s_ref[j] = e
        total = total + jnp.sum(e, axis=1, keepdims=True)
    inverse = 1.0 / total
    out = jnp.zeros((rows, HD), F32)
    delta = jnp.zeros((rows, 1), F32)
    for j in range(blocks):
        p = s_ref[j] * inverse
        s_ref[j] = p
        p_bf = p.astype(BF16)
        out = out + dot(p_bf, v_refs[j][0])
        dv_refs[j][0] = dot_tn(p_bf, d_out).astype(BF16)
        d_p = dot_nt(d_out, v_refs[j][0])
        dp_ref[j] = d_p
        delta = delta + jnp.sum(p * d_p, axis=1, keepdims=True)
    o_ref[0] = (out * valid_ref[0]).astype(BF16)
    d_q = jnp.zeros((rows, HD), F32)
    for j in range(blocks):
        d_s = (s_ref[j] * (dp_ref[j] - delta)).astype(BF16)
        d_q = d_q + dot(d_s, k_refs[j][0])
        dk_refs[j][0] = (dot_tn(d_s, q) * scale).astype(BF16)
    dq_ref[0] = turn(d_q * scale, keep, -left, -right).astype(BF16)


def attention(places, queries, d_attended, starts, valid, tables, keys, values):
    micro, rows, feats = queries.shape
    blocks = len(keys)
    tile = pl.BlockSpec((1, rows, HD), lambda b, h: (b, 0, h))
    like = lambda dtype: jax.ShapeDtypeStruct((micro, rows, feats), dtype)
    return pl.pallas_call(
        attention_kernel,
        grid=(micro, feats // HD),
        in_specs=[pl.BlockSpec(memory_space=pltpu.SMEM), tile, tile]
        + [pl.BlockSpec((1, rows, 1), lambda b, h: (b, 0, 0))] * 2
        + [pl.BlockSpec((1, rows, HD), lambda b, h: (b, 0, 0))] * 3
        + [tile] * (2 * blocks),
        out_specs=[tile] * (2 + 2 * blocks),
        out_shape=[like(BF16)] * (2 + 2 * blocks),
        scratch_shapes=[
            pltpu.VMEM((blocks, rows, rows), F32),
            pltpu.VMEM((blocks, rows, rows), F32),
        ],
        compiler_params=pltpu.CompilerParams(vmem_limit_bytes=40 * 1024 * 1024),
        cost_estimate=pl.CostEstimate(
            flops=12 * micro * feats * rows * rows * blocks,
            bytes_accessed=micro * rows * feats * 2 * (4 + 4 * blocks),
            transcendentals=micro * rows * rows * blocks * feats // HD,
        ),
        name="attention_both_ways",
    )(places, queries, d_attended, starts, valid, *tables, *keys, *values)


def exchange_rows(local):
    if lax.axis_size("stream") != 4:
        raise ValueError("stream")
    across = lax.ppermute(local, "stream", [(0, 2), (1, 3)])
    beside = over_core(local)
    return (local, beside, across, over_core(across))


def reduce_rows(parts):
    add = lambda a, b: a.astype(F32) + b.astype(F32)
    across = add(parts[2], over_core(parts[3])).astype(BF16)
    return add(
        add(parts[0], over_core(parts[1])), lax.ppermute(across, "stream", [(2, 0), (3, 1)])
    )


def shards(
    history,
    seq_lens,
    bucket_slot,
    w_mix_in,
    w_mix_out,
    mix_bias,
    ln_gain,
    ln_bias,
    w_qkv,
    w_attn_out,
    w_up,
    w_down,
    cotangent,
):
    member = lax.axis_index("stream")
    micro, quarter, feats = history.shape[1:]
    tokens = micro * quarter
    model_width = feats * lax.axis_size("head")
    slot_base = lax.axis_index("dp") * micro
    slot_ids = jnp.arange(bucket_slot.shape[0], dtype=jnp.int32)
    query_places = member * quarter + jnp.arange(quarter, dtype=jnp.int32)
    w_mix_in_f = w_mix_in.astype(F32)
    w_mix_out_f = w_mix_out.astype(F32)

    segments, starts = [], []
    for index in range(micro):
        bucket = jnp.sum(jnp.where(slot_ids == slot_base + index, bucket_slot, 0))
        lengths = jnp.sum(jnp.where(slot_ids[:, None] == bucket, seq_lens, 0), axis=0)
        bounds = jnp.cumsum(lengths)
        passed = (query_places[:, None] >= bounds[None, :]).astype(jnp.int32)
        segments.append(jnp.sum(passed, axis=1))
        starts.append(jnp.sum(passed * lengths[None, :], axis=1))
    valid = (jnp.concatenate(segments) < 3).astype(F32)[:, None]
    starts = jnp.concatenate(starts)
    position = jnp.tile(query_places, micro) - starts
    frequency = jnp.arange(ROT // 2, dtype=F32)
    phases = position.astype(F32)[:, None] * (10000.0 ** (-2.0 * frequency / ROT))
    cosine, sine = jnp.cos(phases), jnp.sin(phases)
    plain = jnp.zeros((tokens, HD - ROT), F32)
    none = jnp.zeros_like(sine)
    tables = (
        jnp.concatenate([cosine, cosine, plain + 1.0], axis=1),
        jnp.concatenate([-sine, none, plain], axis=1),
        jnp.concatenate([none, sine, plain], axis=1),
    )

    cot_rows = cotangent.reshape(tokens, feats).astype(F32) * valid
    out_full = lax.all_gather(cot_rows.astype(BF16), "head", axis=1, tiled=True)
    wq, wk, wv = gather_weight(w_qkv, 1)
    both_full = gather_weight(jnp.concatenate([w_attn_out, w_down]), 1)
    w_out_full, down_full = both_full[:feats], both_full[feats:]
    up_full = gather_weight(w_up, 0)

    history = history.reshape(HIST, tokens, feats)
    current = history[HIST - 1]
    current_f = current.astype(F32)
    mixed = lax.dot_general(w_mix_in, current, (((0,), (1,)), ((), ())), preferred_element_type=F32)
    square = jnp.sum(current_f * current_f, axis=1)[None]
    mixed = head_sum(jnp.concatenate([mixed, square]), 0).T
    rms_scale = lax.rsqrt(mixed[:, 4 * HIST :] / model_width + EPSILON)
    mix_pre = mixed[:, : 4 * HIST] * rms_scale
    mix_hidden = gelu_exact(mix_pre)
    mix_weights = jnp.dot(mix_hidden, w_mix_out_f, precision=HIGHEST) + mix_bias.reshape(-1)
    weights_four = mix_weights.reshape(tokens, 4, HIST)
    streams = jnp.zeros((4, tokens, feats), F32)
    for layer in range(HIST):
        streams = (
            streams
            + jnp.transpose(weights_four[:, :, layer])[:, :, None]
            * history[layer].astype(F32)[None]
        )
    stats = head_sum(
        jnp.concatenate([jnp.sum(streams, axis=2), jnp.sum(streams * streams, axis=2)]), 1
    )
    stat_sum, stat_square = stats[:4], stats[4:]
    row_means = (stat_sum / model_width)[:, :, None]
    inv_std = lax.rsqrt(stat_square[:, :, None] / model_width - row_means * row_means + EPSILON)
    centered = (streams - row_means) * inv_std
    normed = (centered * ln_gain[:, None, :] + ln_bias[:, None, :]).astype(BF16)

    def all_features(stream):
        return lax.all_gather(normed[stream], "head", axis=1, tiled=True)

    k_in, v_in, q_in, up_in = (all_features(s) for s in (1, 2, 0, 3))

    keys = rotate(dot(k_in, wk), tables, 1.0)
    values = dot(v_in, wv).astype(BF16)
    queries = dot(q_in, wq)
    d_attended = dot_nt(out_full, w_out_full).astype(BF16) * valid.astype(BF16)
    by_micro = lambda a: a.reshape(micro, quarter, feats)
    key_blocks = exchange_rows(by_micro(keys))
    value_blocks = exchange_rows(by_micro(values))
    places = member ^ jnp.arange(4, dtype=jnp.int32)
    results = attention(
        places,
        by_micro(queries),
        by_micro(d_attended),
        starts.reshape(micro, quarter, 1),
        valid.reshape(micro, quarter, 1),
        tuple(a.reshape(micro, quarter, HD) for a in tables),
        key_blocks,
        value_blocks,
    )
    attended, d_query_pre = results[0].reshape(tokens, feats), results[1].reshape(tokens, feats)
    d_keys = reduce_rows(results[2:6]).reshape(tokens, feats)
    d_values = reduce_rows(results[6:10]).reshape(tokens, feats)
    d_key_pre = rotate(d_keys, tables, -1.0)
    d_value_pre = d_values.astype(BF16)

    up_pre = dot(up_in, up_full)
    below = 0.5 * (1.0 + lax.erf(up_pre * 0.5**0.5))
    slope = below + up_pre * jnp.exp(-0.5 * up_pre * up_pre) * (2.0 * jnp.pi) ** -0.5
    gated_up, slope = lax.optimization_barrier(((up_pre * below).astype(BF16), slope))
    d_up = (dot_nt(out_full, down_full) * slope).astype(BF16)

    def to_owner(partial):
        return lax.psum_scatter(
            partial.astype(BF16), "head", scatter_dimension=1, tiled=True
        ).astype(F32)

    g_up = to_owner(dot_nt(d_up, up_full))
    g_query = to_owner(dot_nt(d_query_pre, wq))
    g_key = to_owner(dot_nt(d_key_pre, wk))
    g_value = to_owner(dot_nt(d_value_pre, wv))
    branch = to_owner(dot(attended, w_out_full) + dot(gated_up, down_full))
    block_out = (valid * (streams[3] + branch)).astype(BF16)

    product = lambda a, b: dot_tn(a, b).astype(BF16)
    grad_up = scatter_sum(product(up_in, d_up))
    grad_down = scatter_sum(product(out_full, gated_up)).T
    grads = scatter_sum(
        jnp.concatenate(
            [
                product(q_in, d_query_pre),
                product(k_in, d_key_pre),
                product(v_in, d_value_pre),
                product(out_full, attended),
            ],
            axis=1,
        )
    )
    grad_qkv = jnp.stack([grads[:, i * feats : (i + 1) * feats] for i in range(3)])
    grad_attn_out = grads[:, 3 * feats :].T

    stream_grad = jnp.stack([g_query, g_key, g_value, g_up])
    d_centered = stream_grad * ln_gain[:, None, :]
    sums = head_sum(
        jnp.concatenate([jnp.sum(d_centered, axis=2), jnp.sum(d_centered * centered, axis=2)]), 2
    )
    sum_grad, sum_cross = sums[:4], sums[4:]
    d_streams = inv_std * (
        d_centered
        - sum_grad[:, :, None] / model_width
        - centered * sum_cross[:, :, None] / model_width
    )
    grad_gain = jnp.sum(stream_grad * centered, axis=1)
    grad_shift = jnp.sum(stream_grad, axis=1)
    d_streams = jnp.concatenate([d_streams[:3], (d_streams[3] + cot_rows)[None]], axis=0)
    layer_grads = []
    d_mix_parts = []
    for layer in range(HIST):
        layer_f = history[layer].astype(F32)
        layer_grads.append(
            jnp.sum(jnp.transpose(weights_four[:, :, layer])[:, :, None] * d_streams, axis=0)
        )
        d_mix_parts.append(jnp.sum(d_streams * layer_f[None], axis=2))
    d_mix_local = jnp.transpose(jnp.stack(d_mix_parts, axis=-1), (1, 0, 2)).reshape(
        tokens, 4 * HIST
    )
    d_mix = head_sum(d_mix_local.T, 3).T
    grad_bias = jnp.sum(d_mix, axis=0)
    grad_w2 = jnp.dot(mix_hidden.T, d_mix, precision=HIGHEST)
    d_hidden = jnp.dot(d_mix, w_mix_out_f.T, precision=HIGHEST)
    _, gelu_mix_back = jax.vjp(gelu_exact, mix_pre)
    d_pre = gelu_mix_back(d_hidden)[0]
    normed_in = current_f * rms_scale
    grad_w1 = jnp.dot(normed_in.T, d_pre, precision=HIGHEST)
    d_normed_in = jnp.dot(d_pre, w_mix_in_f.T, precision=HIGHEST)
    cross = jnp.sum(d_pre * mix_pre, axis=1, keepdims=True)
    layer_grads[HIST - 1] = layer_grads[HIST - 1] + rms_scale * (
        d_normed_in - normed_in * cross / model_width
    )
    history_grad = jnp.stack(layer_grads).reshape(HIST, micro, quarter, feats)
    small = [
        lax.psum(a.astype(BF16), ("dp", "stream")).astype(F32)
        for a in (grad_w1, grad_w2, grad_bias, grad_gain, grad_shift)
    ]
    return (
        block_out.reshape(micro, quarter, feats),
        mix_weights.reshape(micro, quarter, 4 * HIST),
        history_grad,
        small[0],
        small[1],
        small[2].reshape(mix_bias.shape),
        small[3],
        small[4],
        grad_qkv,
        grad_attn_out,
        grad_up,
        grad_down,
    )


def solution(mesh):
    return jax.shard_map(
        shards,
        mesh=mesh,
        in_specs=(
            P(None, "dp", "stream", "head"),
            P(),
            P(),
            P("head", None),
            P(),
            P(),
            P(None, "head"),
            P(None, "head"),
            P(None, ("dp", "stream"), "head"),
            P("head", ("dp", "stream")),
            P(("dp", "stream"), "head"),
            P("head", ("dp", "stream")),
            P("dp", "stream", "head"),
        ),
        out_specs=(
            P("dp", "stream", "head"),
            P("dp", "stream", None),
            P(None, "dp", "stream", "head"),
            P("head", None),
            P(),
            P(),
            P(None, "head"),
            P(None, "head"),
            P(None, ("dp", "stream"), "head"),
            P("head", ("dp", "stream")),
            P(("dp", "stream"), "head"),
            P("head", ("dp", "stream")),
        ),
        check_vma=False,
    )
```

```python
import functools

import jax
import jax.numpy as jnp
from jax import lax
from jax.experimental import pallas as pl
from jax.experimental.pallas import tpu as pltpu
from jax.sharding import PartitionSpec as P

HD = 128
HIST = 9
ROT = 32

EPSILON = 1e-05
HIGHEST = lax.Precision.HIGHEST
MASKED = -1e30
F32 = jnp.float32
BF16 = jnp.bfloat16

SWAP_X = [(0, 1), (1, 0)]
SWAP_Y = [(0, 2), (2, 0), (1, 3), (3, 1)]
SWAP_CORE = [(0, 1), (1, 0), (2, 3), (3, 2)]


def dot(a, b):
    return jnp.dot(a, b, preferred_element_type=F32)


def dot_nt(a, b):
    return lax.dot_general(a, b, (((1,), (1,)), ((), ())), preferred_element_type=F32)


def dot_tn(a, b):
    return lax.dot_general(a, b, (((0,), (0,)), ((), ())), preferred_element_type=F32)


def gelu_exact(values_in):
    return jax.nn.gelu(values_in, approximate=False)


def over_x(a):
    return lax.ppermute(a, "dp", SWAP_X)


def over_y(a):
    return lax.ppermute(a, "stream", SWAP_Y)


def over_core(a):
    return lax.ppermute(a, "stream", SWAP_CORE)


def paired():
    return lax.axis_size("dp") == 2 and lax.axis_size("stream") == 4


def place_kernel(order_ref, near_ref, beside_ref, out_ref):
    step = pl.program_id(0)
    half = pl.num_programs(0) // 2

    @pl.when(step < half)
    def _():
        out_ref[...] = near_ref[0]

    @pl.when(step >= half)
    def _():
        out_ref[...] = beside_ref[0]


def gather_weight(shard, near_x, axis):
    if not paired():
        return lax.all_gather(shard, ("dp", "stream"), axis=axis, tiled=True)
    place = lax.axis_index("dp") * 4 + lax.axis_index("stream")
    row = jnp.stack([shard, near_x])
    near = jnp.concatenate([row, over_y(row)])
    beside = over_core(near)
    flips = jnp.array([0, 4, 2, 6, 1, 5, 3, 7], jnp.int32)
    full_shape = tuple(n * 8 if i == axis else n for i, n in enumerate(shard.shape))
    at = lambda k: tuple(k if i == axis else 0 for i in range(shard.ndim))
    inner = (0,) * shard.ndim
    return pl.pallas_call(
        place_kernel,
        grid_spec=pltpu.PrefetchScalarGridSpec(
            num_scalar_prefetch=1,
            grid=(8,),
            in_specs=[
                pl.BlockSpec((1,) + shard.shape, lambda k, order: (jnp.minimum(k, 3),) + inner),
                pl.BlockSpec((1,) + shard.shape, lambda k, order: (jnp.maximum(k - 4, 0),) + inner),
            ],
            out_specs=pl.BlockSpec(shard.shape, lambda k, order: at(order[k])),
        ),
        out_shape=jax.ShapeDtypeStruct(full_shape, shard.dtype),
        compiler_params=pltpu.CompilerParams(vmem_limit_bytes=40 * 1024 * 1024),
        cost_estimate=pl.CostEstimate(flops=0, bytes_accessed=32 * shard.size, transcendentals=0),
        name="weight_in_order",
    )(place ^ flips, near, beside)


def scatter_parts(partial):
    if not paired():
        whole = lax.psum_scatter(partial, ("dp", "stream"), scatter_dimension=1, tiled=True)
        return whole, jnp.zeros_like(whole)
    count, rows, columns = partial.shape
    stream = lax.axis_index("stream")
    x, y, core = lax.axis_index("dp"), stream // 2, stream % 2

    def pick(a, index, axis):
        return lax.dynamic_index_in_dim(a, index, axis, keepdims=False)

    def add(a, b):
        return (a.astype(F32) + b.astype(F32)).astype(BF16)

    split = partial.reshape(count, 4, 2, rows // 8, columns)
    chip = add(pick(split, core, 2), over_core(pick(split, 1 - core, 2)))
    chip = chip.reshape(count, 2, 2, rows // 8, columns)
    line = add(pick(chip, x, 1), over_x(pick(chip, 1 - x, 1)))
    return pick(line, y, 1), over_y(pick(line, 1 - y, 1))


def add_kernel(turned, a_ref, b_ref, out_ref):
    total = a_ref[...].astype(F32) + b_ref[...].astype(F32)
    out_ref[...] = total.T if turned else total


def add_terms(a, b, turned):
    rows, columns = a.shape
    block = min(512, columns)
    return pl.pallas_call(
        functools.partial(add_kernel, turned),
        grid=(columns // block,),
        in_specs=[pl.BlockSpec((rows, block), lambda i: (0, i))] * 2,
        out_specs=pl.BlockSpec((block, rows), lambda i: (i, 0))
        if turned
        else pl.BlockSpec((rows, block), lambda i: (0, i)),
        out_shape=jax.ShapeDtypeStruct((columns, rows) if turned else (rows, columns), F32),
        cost_estimate=pl.CostEstimate(
            flops=rows * columns, bytes_accessed=8 * rows * columns, transcendentals=0
        ),
        name="add_terms",
    )(a, b)


def head_sum_kernel(members, x_ref, out_ref, slots, send_sem, recv_sem):
    z = lax.axis_index("head")
    barrier = pltpu.get_barrier_semaphore()
    for k in range(1, members):
        pl.semaphore_signal(
            barrier,
            inc=1,
            device_id={"head": lax.rem(z + k, members)},
            device_id_type=pl.DeviceIdType.MESH,
        )
    pl.semaphore_wait(barrier, members - 1)
    copies = []
    for k in range(1, members):
        copy = pltpu.make_async_remote_copy(
            src_ref=x_ref,
            dst_ref=slots.at[z],
            send_sem=send_sem.at[k - 1],
            recv_sem=recv_sem.at[k - 1],
            device_id={"head": lax.rem(z + k, members)},
            device_id_type=pl.DeviceIdType.MESH,
        )
        copy.start()
        copies.append(copy)
    slots[z] = x_ref[...]
    for copy in copies:
        copy.wait()
    total = slots[0]
    for k in range(1, members):
        total = total + slots[k]
    out_ref[...] = total


def head_sum(x, collective_id):
    members = lax.axis_size("head")
    return pl.pallas_call(
        functools.partial(head_sum_kernel, members),
        out_shape=jax.ShapeDtypeStruct(x.shape, F32),
        in_specs=[pl.BlockSpec(memory_space=pltpu.VMEM)],
        out_specs=pl.BlockSpec(memory_space=pltpu.VMEM),
        scratch_shapes=[
            pltpu.VMEM((members,) + x.shape, F32),
            pltpu.SemaphoreType.DMA((members - 1,)),
            pltpu.SemaphoreType.DMA((members - 1,)),
        ],
        compiler_params=pltpu.CompilerParams(collective_id=collective_id, has_side_effects=True),
        name="sum_over_head",
    )(x)


def turn(v, keep, left, right):
    h = ROT // 2
    return v * keep + pltpu.roll(v, HD - h, 1) * left + pltpu.roll(v, h, 1) * right


def rotate_kernel(sign, v_ref, keep_ref, left_ref, right_ref, out_ref):
    for head in range(v_ref.shape[1] // HD):
        part = pl.ds(head * HD, HD)
        out_ref[:, part] = turn(
            v_ref[:, part], keep_ref[...], sign * left_ref[...], sign * right_ref[...]
        ).astype(BF16)


def rotate(values_in, tables, sign):
    tokens, feats = values_in.shape
    block = min(tokens, 256)
    table = pl.BlockSpec((block, HD), lambda i: (i, 0))
    wide = pl.BlockSpec((block, feats), lambda i: (i, 0))
    return pl.pallas_call(
        functools.partial(rotate_kernel, sign),
        grid=(tokens // block,),
        in_specs=[wide, table, table, table],
        out_specs=wide,
        out_shape=jax.ShapeDtypeStruct((tokens, feats), BF16),
        cost_estimate=pl.CostEstimate(
            flops=5 * tokens * feats, bytes_accessed=8 * tokens * feats, transcendentals=0
        ),
        name="rotate_heads",
    )(values_in, *tables)


def attention_kernel(
    place_ref, q_ref, do_ref, start_ref, valid_ref, keep_ref, left_ref, right_ref, *refs
):
    blocks = (len(refs) - 4) // 4
    k_refs, v_refs = refs[:blocks], refs[blocks : 2 * blocks]
    o_ref, dq_ref = refs[2 * blocks : 2 * blocks + 2]
    dk_refs = refs[2 * blocks + 2 : 3 * blocks + 2]
    dv_refs = refs[3 * blocks + 2 : 4 * blocks + 2]
    s_ref, dp_ref = refs[4 * blocks + 2 :]
    rows = q_ref.shape[1]
    scale = HD ** (-0.5)
    member = place_ref[0]
    keep, left, right = keep_ref[0], left_ref[0], right_ref[0]
    q = turn(q_ref[0], keep, left, right).astype(BF16)
    d_out = do_ref[0]
    start = start_ref[0]
    top = jnp.full((rows, 1), MASKED, F32)
    t = member * rows + lax.broadcasted_iota(jnp.int32, (rows, rows), 0)
    for j in range(blocks):
        u = place_ref[j] * rows + lax.broadcasted_iota(jnp.int32, (rows, rows), 1)
        allowed = (u <= t) & (u >= start)
        s_ref[j] = jnp.where(allowed, dot_nt(q, k_refs[j][0]) * scale, MASKED)
        top = jnp.maximum(top, jnp.max(s_ref[j], axis=1, keepdims=True))
    total = jnp.zeros((rows, 1), F32)
    for j in range(blocks):
        e = jnp.exp(s_ref[j] - top)
        s_ref[j] = e
        total = total + jnp.sum(e, axis=1, keepdims=True)
    inverse = 1.0 / total
    out = jnp.zeros((rows, HD), F32)
    delta = jnp.zeros((rows, 1), F32)
    for j in range(blocks):
        p = s_ref[j] * inverse
        s_ref[j] = p
        p_bf = p.astype(BF16)
        out = out + dot(p_bf, v_refs[j][0])
        dv_refs[j][0] = dot_tn(p_bf, d_out).astype(BF16)
        d_p = dot_nt(d_out, v_refs[j][0])
        dp_ref[j] = d_p
        delta = delta + jnp.sum(p * d_p, axis=1, keepdims=True)
    o_ref[0] = (out * valid_ref[0]).astype(BF16)
    d_q = jnp.zeros((rows, HD), F32)
    for j in range(blocks):
        d_s = (s_ref[j] * (dp_ref[j] - delta)).astype(BF16)
        d_q = d_q + dot(d_s, k_refs[j][0])
        dk_refs[j][0] = (dot_tn(d_s, q) * scale).astype(BF16)
    dq_ref[0] = turn(d_q * scale, keep, -left, -right).astype(BF16)


def attention(places, queries, d_attended, starts, valid, tables, keys, values):
    micro, rows, feats = queries.shape
    blocks = len(keys)
    tile = pl.BlockSpec((1, rows, HD), lambda b, h: (b, 0, h))
    like = lambda dtype: jax.ShapeDtypeStruct((micro, rows, feats), dtype)
    return pl.pallas_call(
        attention_kernel,
        grid=(micro, feats // HD),
        in_specs=[pl.BlockSpec(memory_space=pltpu.SMEM), tile, tile]
        + [pl.BlockSpec((1, rows, 1), lambda b, h: (b, 0, 0))] * 2
        + [pl.BlockSpec((1, rows, HD), lambda b, h: (b, 0, 0))] * 3
        + [tile] * (2 * blocks),
        out_specs=[tile] * (2 + 2 * blocks),
        out_shape=[like(BF16)] * (2 + 2 * blocks),
        scratch_shapes=[
            pltpu.VMEM((blocks, rows, rows), F32),
            pltpu.VMEM((blocks, rows, rows), F32),
        ],
        compiler_params=pltpu.CompilerParams(vmem_limit_bytes=40 * 1024 * 1024),
        cost_estimate=pl.CostEstimate(
            flops=12 * micro * feats * rows * rows * blocks,
            bytes_accessed=micro * rows * feats * 2 * (4 + 4 * blocks),
            transcendentals=micro * rows * rows * blocks * feats // HD,
        ),
        name="attention_both_ways",
    )(places, queries, d_attended, starts, valid, *tables, *keys, *values)


def exchange_rows(local):
    if lax.axis_size("stream") != 4:
        raise ValueError("stream")
    across = lax.ppermute(local, "stream", [(0, 2), (1, 3)])
    beside = over_core(local)
    return (local, beside, across, over_core(across))


def reduce_rows(parts):
    add = lambda a, b: a.astype(F32) + b.astype(F32)
    across = add(parts[2], over_core(parts[3])).astype(BF16)
    return add(
        add(parts[0], over_core(parts[1])), lax.ppermute(across, "stream", [(2, 0), (3, 1)])
    )


def columns_of(pieces, rows):
    lane = lax.broadcasted_iota(jnp.int32, (rows, 128), 1)
    out = jnp.zeros((rows, 128), F32)
    for index, piece in enumerate(pieces):
        out = jnp.where(lane == index, piece, out)
    return out


def row_sum(a):
    return jnp.sum(a, axis=1, keepdims=True)


def early_kernel(streams_ref, stats_ref, cot_ref, history_ref, out_ref):
    stats = stats_ref[...]
    cot = cot_ref[...].astype(F32)
    plain, crossed, direct = [], [], []
    layers = [history_ref[j].astype(F32) for j in range(HIST)]
    for layer in layers:
        plain.append(row_sum(layer))
        direct.append(row_sum(cot * layer))
    for s in range(4):
        centered = (streams_ref[s] - stats[:, s : s + 1]) * stats[:, 4 + s : 5 + s]
        for layer in layers:
            crossed.append(row_sum(centered * layer))
    out_ref[...] = columns_of(crossed + plain + direct, stats.shape[0])


def early_sums(streams, stats, cot, history):
    _, tokens, feats = streams.shape
    block = min(128, tokens)
    return pl.pallas_call(
        early_kernel,
        grid=(tokens // block,),
        in_specs=[
            pl.BlockSpec((4, block, feats), lambda i: (0, i, 0)),
            pl.BlockSpec((block, 8), lambda i: (i, 0)),
            pl.BlockSpec((block, feats), lambda i: (i, 0)),
            pl.BlockSpec((HIST, block, feats), lambda i: (0, i, 0)),
        ],
        out_specs=pl.BlockSpec((block, 128), lambda i: (i, 0)),
        out_shape=jax.ShapeDtypeStruct((tokens, 128), F32),
        compiler_params=pltpu.CompilerParams(vmem_limit_bytes=40 * 1024 * 1024),
        cost_estimate=pl.CostEstimate(
            flops=110 * tokens * feats, bytes_accessed=36 * tokens * feats, transcendentals=0
        ),
        name="early_sums",
    )(streams, stats, cot, history)


def sums_kernel(g0, g1, g2, g3, streams_ref, stats_ref, gain_ref, history_ref, out_ref, edge_ref):
    stats = stats_ref[...]
    rows = stats.shape[0]

    @pl.when(pl.program_id(0) == 0)
    def _():
        edge_ref[...] = jnp.zeros_like(edge_ref)

    firsts, seconds, dots = [], [], []
    for s, g_ref in enumerate((g0, g1, g2, g3)):
        g = g_ref[...].astype(F32)
        centered = (streams_ref[s] - stats[:, s : s + 1]) * stats[:, 4 + s : 5 + s]
        edge_ref[s : s + 1] += jnp.sum(g * centered, axis=0, keepdims=True)
        edge_ref[4 + s : 5 + s] += jnp.sum(g, axis=0, keepdims=True)
        scaled = g * gain_ref[s : s + 1]
        firsts.append(row_sum(scaled))
        seconds.append(row_sum(scaled * centered))
        for j in range(HIST):
            dots.append(row_sum(scaled * history_ref[j].astype(F32)))
    out_ref[...] = columns_of(dots + firsts + seconds, rows)


def gradient_sums(grads, streams, stats, gain, history):
    _, tokens, feats = streams.shape
    block = min(128, tokens)
    wide = pl.BlockSpec((block, feats), lambda i: (i, 0))
    sums, edges = pl.pallas_call(
        sums_kernel,
        grid=(tokens // block,),
        in_specs=[wide] * 4
        + [
            pl.BlockSpec((4, block, feats), lambda i: (0, i, 0)),
            pl.BlockSpec((block, 8), lambda i: (i, 0)),
            pl.BlockSpec((4, feats), lambda i: (0, 0)),
            pl.BlockSpec((HIST, block, feats), lambda i: (0, i, 0)),
        ],
        out_specs=[
            pl.BlockSpec((block, 128), lambda i: (i, 0)),
            pl.BlockSpec((8, feats), lambda i: (0, 0)),
        ],
        out_shape=[
            jax.ShapeDtypeStruct((tokens, 128), F32),
            jax.ShapeDtypeStruct((8, feats), F32),
        ],
        compiler_params=pltpu.CompilerParams(vmem_limit_bytes=40 * 1024 * 1024),
        cost_estimate=pl.CostEstimate(
            flops=110 * tokens * feats, bytes_accessed=42 * tokens * feats, transcendentals=0
        ),
        name="gradient_sums",
    )(*grads, streams, stats, gain, history)
    return sums[:, : 4 * HIST + 8], edges


def mix_gradient(sums, early, stats, model_width):
    n = 4 * HIST
    first, second = sums[n : n + 4] / model_width, sums[n + 4 : n + 8] / model_width
    spread = lambda a: jnp.repeat(a, HIST, axis=0)
    crossed, plain, direct = early[:n], early[n : n + HIST], early[n + HIST : n + 2 * HIST]
    d_mix = spread(stats.T[4:]) * (
        sums[:n] - spread(first) * jnp.tile(plain, (4, 1)) - spread(second) * crossed
    )
    d_mix = d_mix + jnp.concatenate([jnp.zeros_like(d_mix[: 3 * HIST]), direct])
    return d_mix, jnp.concatenate([first, second])


def history_kernel(
    g0, g1, g2, g3, streams_ref, stats_ref, gain_ref, cot_ref, current_ref, columns_ref, d_ref, w_ref, out_ref
):
    n = 4 * HIST
    stats, columns = stats_ref[...], columns_ref[...]
    column = lambda i: columns[:, i : i + 1]
    d_streams = []
    for s, g_ref in enumerate((g0, g1, g2, g3)):
        inverse = stats[:, 4 + s : 5 + s]
        centered = (streams_ref[s] - stats[:, s : s + 1]) * inverse
        scaled = g_ref[...].astype(F32) * gain_ref[s : s + 1]
        d_streams.append(inverse * (scaled - column(n + s) - centered * column(n + 4 + s)))
    d_streams[3] = d_streams[3] + cot_ref[...].astype(F32)
    for j in range(HIST):
        total = column(j) * d_streams[0]
        for s in range(1, 4):
            total = total + column(s * HIST + j) * d_streams[s]
        if j == HIST - 1:
            total = total + jnp.dot(
                d_ref[...], w_ref[...], precision=HIGHEST, preferred_element_type=F32
            )
            total = total - current_ref[...].astype(F32) * column(n + 9)
        out_ref[j] = total


def history_gradient(grads, streams, stats, gain, cot, current, columns, d_scaled, w_rows):
    _, tokens, feats = streams.shape
    block = min(128, tokens)
    wide = pl.BlockSpec((block, feats), lambda i: (i, 0))
    narrow = lambda a: pl.BlockSpec((block, a.shape[1]), lambda i: (i, 0))
    fixed = lambda a: pl.BlockSpec(a.shape, lambda i: (0, 0))
    return pl.pallas_call(
        history_kernel,
        grid=(tokens // block,),
        in_specs=[wide] * 4
        + [
            pl.BlockSpec((4, block, feats), lambda i: (0, i, 0)),
            narrow(stats),
            fixed(gain),
            wide,
            wide,
            narrow(columns),
            narrow(d_scaled),
            fixed(w_rows),
        ],
        out_specs=pl.BlockSpec((HIST, block, feats), lambda i: (0, i, 0)),
        out_shape=jax.ShapeDtypeStruct((HIST, tokens, feats), F32),
        compiler_params=pltpu.CompilerParams(vmem_limit_bytes=40 * 1024 * 1024),
        cost_estimate=pl.CostEstimate(
            flops=110 * tokens * feats, bytes_accessed=64 * tokens * feats, transcendentals=0
        ),
        name="history_gradient",
    )(*grads, streams, stats, gain, cot, current, columns, d_scaled, w_rows)


def shards(
    history,
    seq_lens,
    bucket_slot,
    w_mix_in,
    w_mix_out,
    mix_bias,
    ln_gain,
    ln_bias,
    w_qkv,
    w_attn_out,
    w_up,
    w_down,
    cotangent,
):
    member = lax.axis_index("stream")
    micro, quarter, feats = history.shape[1:]
    tokens = micro * quarter
    model_width = feats * lax.axis_size("head")
    slot_base = lax.axis_index("dp") * micro
    slot_ids = jnp.arange(bucket_slot.shape[0], dtype=jnp.int32)
    query_places = member * quarter + jnp.arange(quarter, dtype=jnp.int32)
    w_mix_in_f = w_mix_in.astype(F32)
    w_mix_out_f = w_mix_out.astype(F32)

    segments, starts = [], []
    for index in range(micro):
        bucket = jnp.sum(jnp.where(slot_ids == slot_base + index, bucket_slot, 0))
        lengths = jnp.sum(jnp.where(slot_ids[:, None] == bucket, seq_lens, 0), axis=0)
        bounds = jnp.cumsum(lengths)
        passed = (query_places[:, None] >= bounds[None, :]).astype(jnp.int32)
        segments.append(jnp.sum(passed, axis=1))
        starts.append(jnp.sum(passed * lengths[None, :], axis=1))
    valid = (jnp.concatenate(segments) < 3).astype(F32)[:, None]
    starts = jnp.concatenate(starts)
    position = jnp.tile(query_places, micro) - starts
    frequency = jnp.arange(ROT // 2, dtype=F32)
    phases = position.astype(F32)[:, None] * (10000.0 ** (-2.0 * frequency / ROT))
    cosine, sine = jnp.cos(phases), jnp.sin(phases)
    plain = jnp.zeros((tokens, HD - ROT), F32)
    none = jnp.zeros_like(sine)
    tables = (
        jnp.concatenate([cosine, cosine, plain + 1.0], axis=1),
        jnp.concatenate([-sine, none, plain], axis=1),
        jnp.concatenate([none, sine, plain], axis=1),
    )

    cot_rows = cotangent.reshape(tokens, feats).astype(F32) * valid
    out_full = lax.all_gather(cot_rows.astype(BF16), "head", axis=1, tiled=True)
    w_both = jnp.concatenate([w_attn_out, w_down])
    near_x = tuple(over_x(w) if paired() else w[:1] for w in (w_qkv, w_both, w_up))

    history = history.reshape(HIST, tokens, feats)
    current = history[HIST - 1]
    current_f = current.astype(F32)
    mixed = lax.dot_general(w_mix_in, current, (((0,), (1,)), ((), ())), preferred_element_type=F32)
    square = jnp.sum(current_f * current_f, axis=1)[None]
    mixed = head_sum(jnp.concatenate([mixed, square]), 0).T
    rms_scale = lax.rsqrt(mixed[:, 4 * HIST :] / model_width + EPSILON)
    mix_pre = mixed[:, : 4 * HIST] * rms_scale
    mix_hidden = gelu_exact(mix_pre)
    mix_weights = jnp.dot(mix_hidden, w_mix_out_f, precision=HIGHEST) + mix_bias.reshape(-1)
    weights_four = mix_weights.reshape(tokens, 4, HIST)
    streams = jnp.zeros((4, tokens, feats), F32)
    for layer in range(HIST):
        streams = (
            streams
            + jnp.transpose(weights_four[:, :, layer])[:, :, None]
            * history[layer].astype(F32)[None]
        )
    stats = head_sum(
        jnp.concatenate([jnp.sum(streams, axis=2), jnp.sum(streams * streams, axis=2)]), 1
    )
    stat_sum, stat_square = stats[:4], stats[4:]
    stat_sum, stat_square, out_full, near_x = lax.optimization_barrier(
        (stat_sum, stat_square, out_full, near_x)
    )
    row_means = (stat_sum / model_width)[:, :, None]
    inv_std = lax.rsqrt(stat_square[:, :, None] / model_width - row_means * row_means + EPSILON)
    centered = (streams - row_means) * inv_std
    row_stats = jnp.concatenate([row_means[..., 0], inv_std[..., 0]]).T
    early = early_sums(streams, row_stats, cot_rows.astype(BF16), history)
    early = head_sum(early[:, : 6 * HIST].T, 2)
    normed = (centered * ln_gain[:, None, :] + ln_bias[:, None, :]).astype(BF16)

    wq, wk, wv = gather_weight(w_qkv, near_x[0], 1)
    both_full = gather_weight(w_both, near_x[1], 1)
    w_out_full, down_full = both_full[:feats], both_full[feats:]
    up_full = gather_weight(w_up, near_x[2], 0)

    def all_features(stream):
        return lax.all_gather(normed[stream], "head", axis=1, tiled=True)

    k_in, v_in, q_in, up_in = (all_features(s) for s in (1, 2, 0, 3))

    keys = rotate(dot(k_in, wk), tables, 1.0)
    values = dot(v_in, wv).astype(BF16)
    queries = dot(q_in, wq)
    d_attended = dot_nt(out_full, w_out_full).astype(BF16) * valid.astype(BF16)
    by_micro = lambda a: a.reshape(micro, quarter, feats)
    key_blocks = exchange_rows(by_micro(keys))
    value_blocks = exchange_rows(by_micro(values))
    places = member ^ jnp.arange(4, dtype=jnp.int32)
    results = attention(
        places,
        by_micro(queries),
        by_micro(d_attended),
        starts.reshape(micro, quarter, 1),
        valid.reshape(micro, quarter, 1),
        tuple(a.reshape(micro, quarter, HD) for a in tables),
        key_blocks,
        value_blocks,
    )
    attended, d_query_pre = results[0].reshape(tokens, feats), results[1].reshape(tokens, feats)
    d_keys = reduce_rows(results[2:6]).reshape(tokens, feats)
    d_values = reduce_rows(results[6:10]).reshape(tokens, feats)
    d_key_pre = rotate(d_keys, tables, -1.0)
    d_value_pre = d_values.astype(BF16)

    up_pre = dot(up_in, up_full)
    below = 0.5 * (1.0 + lax.erf(up_pre * 0.5**0.5))
    slope = below + up_pre * jnp.exp(-0.5 * up_pre * up_pre) * (2.0 * jnp.pi) ** -0.5
    gated_up, slope = lax.optimization_barrier(((up_pre * below).astype(BF16), slope))
    d_up = (dot_nt(out_full, down_full) * slope).astype(BF16)

    def to_owner(partial):
        return lax.psum_scatter(
            partial.astype(BF16), "head", scatter_dimension=1, tiled=True
        ).astype(F32)

    g_up = to_owner(dot_nt(d_up, up_full))
    g_query = to_owner(dot_nt(d_query_pre, wq))
    g_key = to_owner(dot_nt(d_key_pre, wk))
    g_value = to_owner(dot_nt(d_value_pre, wv))
    branch = to_owner(dot(attended, w_out_full) + dot(gated_up, down_full))
    block_out = (valid * (streams[3] + branch)).astype(BF16)

    product = lambda a, b: dot_tn(a, b).astype(BF16)
    up_terms = scatter_parts(product(up_in, d_up)[None])
    down_terms = scatter_parts(product(out_full, gated_up)[None])
    grad_up = add_terms(up_terms[0][0], up_terms[1][0], False)
    grad_down = add_terms(down_terms[0][0], down_terms[1][0], True)
    terms = scatter_parts(
        jnp.stack(
            [
                product(q_in, d_query_pre),
                product(k_in, d_key_pre),
                product(v_in, d_value_pre),
                product(out_full, attended),
            ]
        )
    )
    grad_qkv = terms[0][:3].astype(F32) + terms[1][:3].astype(F32)
    grad_attn_out = add_terms(terms[0][3], terms[1][3], True)

    grads = (g_query, g_key, g_value, g_up)
    sums, gain_shift = gradient_sums(grads, streams, row_stats, ln_gain, history)
    sums = head_sum(sums.T, 3)
    d_mix, coefs = mix_gradient(sums, early, row_stats, model_width)
    d_hidden = jnp.dot(w_mix_out_f, d_mix, precision=HIGHEST)
    mix_pre_t = mix_pre.T
    below_mix = 0.5 * (1.0 + lax.erf(mix_pre_t * 0.5**0.5))
    density = jnp.exp(-0.5 * mix_pre_t * mix_pre_t) * (2.0 * jnp.pi) ** -0.5
    d_pre = d_hidden * (below_mix + mix_pre_t * density)
    cross = jnp.sum(d_pre * mix_pre_t, axis=0, keepdims=True)
    rms_row = rms_scale.T
    grad_w1 = jnp.dot(d_pre * rms_row, current_f, precision=HIGHEST)
    grad_w2 = jnp.dot(mix_hidden.T, d_mix.T, precision=HIGHEST)
    grad_bias = jnp.sum(d_mix, axis=1)
    wide = lambda a: jnp.pad(a, ((0, 0), (0, feats - a.shape[1])))
    small = jnp.concatenate([grad_w1, gain_shift, wide(grad_w2), wide(grad_bias[None])])
    small = lax.psum(small.astype(BF16), ("dp", "stream")).astype(F32)
    n = 4 * HIST
    columns = jnp.concatenate(
        [mix_weights.T, coefs, rms_row, rms_row * rms_row * cross / model_width]
    ).T
    history_grad = history_gradient(
        grads,
        streams,
        row_stats,
        ln_gain,
        cot_rows.astype(BF16),
        current,
        columns,
        (d_pre * rms_row).T,
        w_mix_in_f.T,
    ).reshape(HIST, micro, quarter, feats)
    return (
        block_out.reshape(micro, quarter, feats),
        mix_weights.reshape(micro, quarter, 4 * HIST),
        history_grad,
        small[:n].T,
        small[n + 8 : 2 * n + 8, :n],
        small[2 * n + 8, :n].reshape(mix_bias.shape),
        small[n : n + 4],
        small[n + 4 : n + 8],
        grad_qkv,
        grad_attn_out,
        grad_up,
        grad_down,
    )


def solution(mesh):
    return jax.shard_map(
        shards,
        mesh=mesh,
        in_specs=(
            P(None, "dp", "stream", "head"),
            P(),
            P(),
            P("head", None),
            P(),
            P(),
            P(None, "head"),
            P(None, "head"),
            P(None, ("dp", "stream"), "head"),
            P("head", ("dp", "stream")),
            P(("dp", "stream"), "head"),
            P("head", ("dp", "stream")),
            P("dp", "stream", "head"),
        ),
        out_specs=(
            P("dp", "stream", "head"),
            P("dp", "stream", None),
            P(None, "dp", "stream", "head"),
            P("head", None),
            P(),
            P(),
            P(None, "head"),
            P(None, "head"),
            P(None, ("dp", "stream"), "head"),
            P("head", ("dp", "stream")),
            P(("dp", "stream"), "head"),
            P("head", ("dp", "stream")),
        ),
        check_vma=False,
    )
```

```python
import functools

import jax
import jax.numpy as jnp
from jax import lax
from jax.experimental import pallas as pl
from jax.experimental.pallas import tpu as pltpu
from jax.sharding import PartitionSpec as P

HD = 128
HIST = 9
ROT = 32

EPSILON = 1e-05
HIGHEST = lax.Precision.HIGHEST
MASKED = -1e30
F32 = jnp.float32
BF16 = jnp.bfloat16

SWAP_X = [(0, 1), (1, 0)]
SWAP_Y = [(0, 2), (2, 0), (1, 3), (3, 1)]
SWAP_CORE = [(0, 1), (1, 0), (2, 3), (3, 2)]


def dot(a, b):
    return jnp.dot(a, b, preferred_element_type=F32)


def dot_nt(a, b):
    return lax.dot_general(a, b, (((1,), (1,)), ((), ())), preferred_element_type=F32)


def dot_tn(a, b):
    return lax.dot_general(a, b, (((0,), (0,)), ((), ())), preferred_element_type=F32)


def gelu_exact(values_in):
    return jax.nn.gelu(values_in, approximate=False)


def over_x(a):
    return lax.ppermute(a, "dp", SWAP_X)


def over_y(a):
    return lax.ppermute(a, "stream", SWAP_Y)


def over_core(a):
    return lax.ppermute(a, "stream", SWAP_CORE)


def paired():
    return lax.axis_size("dp") == 2 and lax.axis_size("stream") == 4


def place_kernel(order_ref, near_ref, beside_ref, out_ref):
    step = pl.program_id(0)
    half = pl.num_programs(0) // 2

    @pl.when(step < half)
    def _():
        out_ref[...] = near_ref[0]

    @pl.when(step >= half)
    def _():
        out_ref[...] = beside_ref[0]


def gather_weight(shard, axis):
    return lax.all_gather(shard, ("dp", "stream"), axis=axis, tiled=True)


def lined():
    return paired() and lax.axis_size("head") == 4


def swap_head(a):
    at = lambda x, y, core, z: (x * 4 + y * 2 + core) * 4 + z
    pairs = [
        (at(x, y, core, z), at(z // 2, z % 2, core, 2 * x + y))
        for x in range(2)
        for y in range(2)
        for core in range(2)
        for z in range(4)
    ]
    return lax.ppermute(a, ("dp", "stream", "head"), pairs)


def row_weight(shard, near):
    place = lax.axis_index("dp") * 4 + lax.axis_index("stream")
    beside = over_core(near)
    flips = jnp.array([0, 4, 2, 6, 1, 5, 3, 7], jnp.int32)
    count, rows, columns = shard.shape
    piece = (1, count, rows, columns)
    inner = (0, 0, 0)
    return pl.pallas_call(
        place_kernel,
        grid_spec=pltpu.PrefetchScalarGridSpec(
            num_scalar_prefetch=1,
            grid=(8,),
            in_specs=[
                pl.BlockSpec(piece, lambda k, order: (jnp.minimum(k, 3),) + inner),
                pl.BlockSpec(piece, lambda k, order: (jnp.maximum(k - 4, 0),) + inner),
            ],
            out_specs=pl.BlockSpec(
                shard.shape,
                lambda k, order: (0, lax.rem(order[k], 2), lax.div(order[k], 2)),
            ),
        ),
        out_shape=jax.ShapeDtypeStruct((count, 2 * rows, 4 * columns), shard.dtype),
        compiler_params=pltpu.CompilerParams(vmem_limit_bytes=40 * 1024 * 1024),
        cost_estimate=pl.CostEstimate(flops=0, bytes_accessed=32 * shard.size, transcendentals=0),
        name="weight_in_order",
    )(place ^ flips, near, beside)


def scatter_parts(partial):
    if not paired():
        whole = lax.psum_scatter(partial, ("dp", "stream"), scatter_dimension=1, tiled=True)
        return whole, jnp.zeros_like(whole)
    count, rows, columns = partial.shape
    stream = lax.axis_index("stream")
    x, y, core = lax.axis_index("dp"), stream // 2, stream % 2

    def pick(a, index, axis):
        return lax.dynamic_index_in_dim(a, index, axis, keepdims=False)

    def add(a, b):
        return (a.astype(F32) + b.astype(F32)).astype(BF16)

    split = partial.reshape(count, 4, 2, rows // 8, columns)
    chip = add(pick(split, core, 2), over_core(pick(split, 1 - core, 2)))
    chip = chip.reshape(count, 2, 2, rows // 8, columns)
    line = add(pick(chip, x, 1), over_x(pick(chip, 1 - x, 1)))
    return pick(line, y, 1), over_y(pick(line, 1 - y, 1))


def add_kernel(turned, a_ref, b_ref, out_ref):
    total = a_ref[...].astype(F32) + b_ref[...].astype(F32)
    out_ref[...] = total.T if turned else total


def add_terms(a, b, turned):
    rows, columns = a.shape
    block = min(512, columns)
    return pl.pallas_call(
        functools.partial(add_kernel, turned),
        grid=(columns // block,),
        in_specs=[pl.BlockSpec((rows, block), lambda i: (0, i))] * 2,
        out_specs=pl.BlockSpec((block, rows), lambda i: (i, 0))
        if turned
        else pl.BlockSpec((rows, block), lambda i: (0, i)),
        out_shape=jax.ShapeDtypeStruct((columns, rows) if turned else (rows, columns), F32),
        cost_estimate=pl.CostEstimate(
            flops=rows * columns, bytes_accessed=8 * rows * columns, transcendentals=0
        ),
        name="add_terms",
    )(a, b)


def exchange_kernel(units, axes, *refs):
    count = len(axes)
    partials, shard_refs = refs[:units], refs[units : units + count]
    outs = refs[units + count : 2 * units + count]
    fulls = refs[2 * units + count : 2 * units + 2 * count]
    held, got, load_sem, send_sem, recv_sem, own_sem, near_send, near_recv = refs[
        2 * units + 2 * count :
    ]
    x, stream, z = lax.axis_index("dp"), lax.axis_index("stream"), lax.axis_index("head")
    core = lax.rem(stream, 2)
    other_x, other_y, other_core = 1 - x, lax.rem(stream + 2, 4), stream + 1 - 2 * core
    line = ({"head": lax.rem(z + 1, 4)}, {"head": lax.rem(z + 3, 4)})
    to_x, to_y, to_core = {"dp": other_x}, {"stream": other_y}, {"stream": other_core}
    place = x * 4 + stream
    place_x, place_y = other_x * 4 + stream, x * 4 + other_y
    place_far = other_x * 4 + other_y
    beside = lambda at: at + 1 - 2 * core

    barrier = pltpu.get_barrier_semaphore()
    peers = line + ((to_x, to_y, to_core) if count else ())
    for peer in peers:
        pl.semaphore_signal(barrier, inc=1, device_id=peer, device_id_type=pl.DeviceIdType.MESH)
    pl.semaphore_wait(barrier, len(peers))

    def region(w, at, part=None):
        full, width = fulls[w], shard_refs[w].shape[axes[w]]
        rows = shard_refs[w].shape[0]
        start, size = (0, rows) if part is None else (part * (rows // 2), rows // 2)
        if axes[w] == 0:
            return full.at[pl.ds(pl.multiple_of(at * width + start, size), size)]
        return full.at[pl.ds(start, size), pl.ds(pl.multiple_of(at * width, width), width)]

    def near(w, index, source, target, peer):
        return pltpu.make_async_remote_copy(
            src_ref=source,
            dst_ref=target,
            send_sem=near_send.at[w, index],
            recv_sem=near_recv.at[w, index],
            device_id=peer,
            device_id_type=pl.DeviceIdType.MESH,
        )

    def pass_on(w, index, at, peer, part=None):
        return near(w, index, region(w, at, part), region(w, at, part), peer)

    def first(w):
        target = region(w, place)
        pltpu.make_async_copy(shard_refs[w], target, own_sem.at[w]).start()
        for index, peer in enumerate((to_x, to_y, to_core)):
            near(w, index, shard_refs[w], target, peer).start()

    def second(w):
        pass_on(w, 0, place_x, to_x).wait_recv()
        pass_on(w, 4, place_x, to_y, 0).start()
        pass_on(w, 3, place_x, to_core).start()
        pass_on(w, 1, place_y, to_y).wait_recv()
        pass_on(w, 6, place_y, to_x, 1).start()
        pass_on(w, 5, place_y, to_core).start()

    def third(w):
        pass_on(w, 4, place_far, to_y, 0).wait_recv()
        pass_on(w, 7, place_far, to_core, 0).start()
        pass_on(w, 6, place_far, to_x, 1).wait_recv()
        pass_on(w, 8, place_far, to_core, 1).start()

    def last(w):
        for index, at, part in (
            (2, place, None),
            (3, place_x, None),
            (5, place_y, None),
            (7, place_far, 0),
            (8, place_far, 1),
        ):
            pass_on(w, index, beside(at), to_core, part).wait_recv()
        pltpu.make_async_copy(shard_refs[w], region(w, place), own_sem.at[w]).wait()
        for index in (0, 1, 2):
            near(w, index, shard_refs[w], region(w, place), to_core).wait_send()
        for index, at, part in (
            (3, place_x, None),
            (4, place_x, 0),
            (5, place_y, None),
            (6, place_y, 1),
            (7, place_far, 0),
            (8, place_far, 1),
        ):
            pass_on(w, index, at, to_core, part).wait_send()

    feats = held.shape[-1]
    chunk = send_sem.shape[-1]
    step_rows = held.shape[2] // chunk

    def load(u, b):
        return pltpu.make_async_copy(
            partials[u].at[:, b * feats : (b + 1) * feats], held.at[u, b], load_sem.at[u, b]
        )

    for u in range(units):
        for b in range(4):
            load(u, b).start()
    for w in range(count):
        first(w)
    for u in range(units):
        for b in range(4):
            load(u, b).wait()

    def part(c):
        return pl.ds(pl.multiple_of(c * step_rows, step_rows), step_rows)

    def hop(way, u, step, block, c):
        return pltpu.make_async_remote_copy(
            src_ref=held.at[u, block, part(c)],
            dst_ref=got.at[way, u, step, part(c)],
            send_sem=send_sem.at[way, u, step, c],
            recv_sem=recv_sem.at[way, u, step, c],
            device_id=line[way],
            device_id_type=pl.DeviceIdType.MESH,
        )

    ways = ((0, z), (1, 3 - z))

    def block_at(way, step):
        return 3 - step + z if way == 0 else step + z - 3

    def line_step(step):
        def body(c, carry):
            for way, rank in ways:

                @pl.when(rank <= step)
                def _():
                    block = block_at(way, step)
                    for u in range(units):
                        if step > 0:

                            @pl.when(rank > 0)
                            def _():
                                hop(way, u, step - 1, block, c).wait_recv()
                                total = held[u, block, part(c)].astype(F32) + got[
                                    way, u, step - 1, part(c)
                                ].astype(F32)
                                held[u, block, part(c)] = total.astype(BF16)

                        hop(way, u, step, block, c).start()

            return carry

        lax.fori_loop(0, chunk, body, 0)

    line_step(0)
    for w in range(min(count, 2)):
        second(w)
    line_step(1)
    for w in range(2, count):
        second(w)
    line_step(2)
    for w in range(count):
        third(w)

    def finish(c, carry):
        for u in range(units):
            outs[u][part(c)] = held[u, z, part(c)].astype(F32)
            for way, rank in ways:

                @pl.when(rank > 0)
                def _():
                    hop(way, u, 2, z, c).wait_recv()
                    outs[u][part(c)] += got[way, u, 2, part(c)].astype(F32)

        return carry

    lax.fori_loop(0, chunk, finish, 0)
    for w in range(count):
        last(w)

    def drain(c, carry):
        for step in range(3):
            for way, rank in ways:

                @pl.when(rank <= step)
                def _():
                    for u in range(units):
                        hop(way, u, step, block_at(way, step), c).wait_send()

        return carry

    lax.fori_loop(0, chunk, drain, 0)


def exchange(partials, shards_in, axes, collective_id):
    units, count = len(partials), len(shards_in)
    tokens, feats = partials[0].shape[0], partials[0].shape[1] // 4
    chunk = 4
    full = [
        jax.ShapeDtypeStruct(tuple(n * 8 if i == axis else n for i, n in enumerate(w.shape)), BF16)
        for w, axis in zip(shards_in, axes)
    ]
    anywhere = pl.BlockSpec(memory_space=pl.ANY)
    sems = pltpu.SemaphoreType.DMA
    results = pl.pallas_call(
        functools.partial(exchange_kernel, units, axes),
        in_specs=[anywhere] * (units + count),
        out_specs=[pl.BlockSpec(memory_space=pltpu.VMEM)] * units + [anywhere] * count,
        out_shape=[jax.ShapeDtypeStruct((tokens, feats), F32)] * units + full,
        scratch_shapes=[
            pltpu.VMEM((units, 4, tokens, feats), BF16),
            pltpu.VMEM((2, units, 3, tokens, feats), BF16),
            sems((units, 4)),
            sems((2, units, 3, chunk)),
            sems((2, units, 3, chunk)),
            sems((max(count, 1),)),
            sems((max(count, 1), 9)),
            sems((max(count, 1), 9)),
        ],
        compiler_params=pltpu.CompilerParams(
            collective_id=collective_id,
            has_side_effects=True,
            vmem_limit_bytes=48 * 1024 * 1024,
        ),
        cost_estimate=pl.CostEstimate(
            flops=0, bytes_accessed=600 * 1024 * 1024, transcendentals=0
        ),
        name="exchange",
    )(*partials, *shards_in)
    return results[:units], results[units:]


def head_sum_kernel(members, x_ref, out_ref, slots, send_sem, recv_sem):
    z = lax.axis_index("head")
    barrier = pltpu.get_barrier_semaphore()
    for k in range(1, members):
        pl.semaphore_signal(
            barrier,
            inc=1,
            device_id={"head": lax.rem(z + k, members)},
            device_id_type=pl.DeviceIdType.MESH,
        )
    pl.semaphore_wait(barrier, members - 1)
    copies = []
    for k in range(1, members):
        copy = pltpu.make_async_remote_copy(
            src_ref=x_ref,
            dst_ref=slots.at[z],
            send_sem=send_sem.at[k - 1],
            recv_sem=recv_sem.at[k - 1],
            device_id={"head": lax.rem(z + k, members)},
            device_id_type=pl.DeviceIdType.MESH,
        )
        copy.start()
        copies.append(copy)
    slots[z] = x_ref[...]
    for copy in copies:
        copy.wait()
    total = slots[0]
    for k in range(1, members):
        total = total + slots[k]
    out_ref[...] = total


def head_sum(x, collective_id):
    members = lax.axis_size("head")
    return pl.pallas_call(
        functools.partial(head_sum_kernel, members),
        out_shape=jax.ShapeDtypeStruct(x.shape, F32),
        in_specs=[pl.BlockSpec(memory_space=pltpu.VMEM)],
        out_specs=pl.BlockSpec(memory_space=pltpu.VMEM),
        scratch_shapes=[
            pltpu.VMEM((members,) + x.shape, F32),
            pltpu.SemaphoreType.DMA((members - 1,)),
            pltpu.SemaphoreType.DMA((members - 1,)),
        ],
        compiler_params=pltpu.CompilerParams(collective_id=collective_id, has_side_effects=True),
        name="sum_over_head",
    )(x)


def turn(v, keep, left, right):
    h = ROT // 2
    return v * keep + pltpu.roll(v, HD - h, 1) * left + pltpu.roll(v, h, 1) * right


def rotate_kernel(sign, v_ref, keep_ref, left_ref, right_ref, out_ref):
    for head in range(v_ref.shape[1] // HD):
        part = pl.ds(head * HD, HD)
        out_ref[:, part] = turn(
            v_ref[:, part], keep_ref[...], sign * left_ref[...], sign * right_ref[...]
        ).astype(BF16)


def rotate(values_in, tables, sign):
    tokens, feats = values_in.shape
    block = min(tokens, 256)
    table = pl.BlockSpec((block, HD), lambda i: (i, 0))
    wide = pl.BlockSpec((block, feats), lambda i: (i, 0))
    return pl.pallas_call(
        functools.partial(rotate_kernel, sign),
        grid=(tokens // block,),
        in_specs=[wide, table, table, table],
        out_specs=wide,
        out_shape=jax.ShapeDtypeStruct((tokens, feats), BF16),
        cost_estimate=pl.CostEstimate(
            flops=5 * tokens * feats, bytes_accessed=8 * tokens * feats, transcendentals=0
        ),
        name="rotate_heads",
    )(values_in, *tables)


def attention_kernel(
    place_ref, q_ref, do_ref, start_ref, valid_ref, keep_ref, left_ref, right_ref, *refs
):
    blocks = (len(refs) - 4) // 4
    k_refs, v_refs = refs[:blocks], refs[blocks : 2 * blocks]
    o_ref, dq_ref = refs[2 * blocks : 2 * blocks + 2]
    dk_refs = refs[2 * blocks + 2 : 3 * blocks + 2]
    dv_refs = refs[3 * blocks + 2 : 4 * blocks + 2]
    s_ref, dp_ref = refs[4 * blocks + 2 :]
    rows = q_ref.shape[1]
    scale = HD ** (-0.5)
    member = place_ref[0]
    keep, left, right = keep_ref[0], left_ref[0], right_ref[0]
    q = turn(q_ref[0], keep, left, right).astype(BF16)
    d_out = do_ref[0]
    start = start_ref[0]
    top = jnp.full((rows, 1), MASKED, F32)
    t = member * rows + lax.broadcasted_iota(jnp.int32, (rows, rows), 0)
    for j in range(blocks):
        u = place_ref[j] * rows + lax.broadcasted_iota(jnp.int32, (rows, rows), 1)
        allowed = (u <= t) & (u >= start)
        s_ref[j] = jnp.where(allowed, dot_nt(q, k_refs[j][0]) * scale, MASKED)
        top = jnp.maximum(top, jnp.max(s_ref[j], axis=1, keepdims=True))
    total = jnp.zeros((rows, 1), F32)
    for j in range(blocks):
        e = jnp.exp(s_ref[j] - top)
        s_ref[j] = e
        total = total + jnp.sum(e, axis=1, keepdims=True)
    inverse = 1.0 / total
    out = jnp.zeros((rows, HD), F32)
    delta = jnp.zeros((rows, 1), F32)
    for j in range(blocks):
        p = s_ref[j] * inverse
        s_ref[j] = p
        p_bf = p.astype(BF16)
        out = out + dot(p_bf, v_refs[j][0])
        dv_refs[j][0] = dot_tn(p_bf, d_out).astype(BF16)
        d_p = dot_nt(d_out, v_refs[j][0])
        dp_ref[j] = d_p
        delta = delta + jnp.sum(p * d_p, axis=1, keepdims=True)
    o_ref[0] = (out * valid_ref[0]).astype(BF16)
    d_q = jnp.zeros((rows, HD), F32)
    for j in range(blocks):
        d_s = (s_ref[j] * (dp_ref[j] - delta)).astype(BF16)
        d_q = d_q + dot(d_s, k_refs[j][0])
        dk_refs[j][0] = (dot_tn(d_s, q) * scale).astype(BF16)
    dq_ref[0] = turn(d_q * scale, keep, -left, -right).astype(BF16)


def attention(places, queries, d_attended, starts, valid, tables, keys, values):
    micro, rows, feats = queries.shape
    blocks = len(keys)
    tile = pl.BlockSpec((1, rows, HD), lambda b, h: (b, 0, h))
    like = lambda dtype: jax.ShapeDtypeStruct((micro, rows, feats), dtype)
    return pl.pallas_call(
        attention_kernel,
        grid=(micro, feats // HD),
        in_specs=[pl.BlockSpec(memory_space=pltpu.SMEM), tile, tile]
        + [pl.BlockSpec((1, rows, 1), lambda b, h: (b, 0, 0))] * 2
        + [pl.BlockSpec((1, rows, HD), lambda b, h: (b, 0, 0))] * 3
        + [tile] * (2 * blocks),
        out_specs=[tile] * (2 + 2 * blocks),
        out_shape=[like(BF16)] * (2 + 2 * blocks),
        scratch_shapes=[
            pltpu.VMEM((blocks, rows, rows), F32),
            pltpu.VMEM((blocks, rows, rows), F32),
        ],
        compiler_params=pltpu.CompilerParams(vmem_limit_bytes=40 * 1024 * 1024),
        cost_estimate=pl.CostEstimate(
            flops=12 * micro * feats * rows * rows * blocks,
            bytes_accessed=micro * rows * feats * 2 * (4 + 4 * blocks),
            transcendentals=micro * rows * rows * blocks * feats // HD,
        ),
        name="attention_both_ways",
    )(places, queries, d_attended, starts, valid, *tables, *keys, *values)


def exchange_rows(local):
    if lax.axis_size("stream") != 4:
        raise ValueError("stream")
    across = lax.ppermute(local, "stream", [(0, 2), (1, 3)])
    beside = over_core(local)
    return (local, beside, across, over_core(across))


def reduce_rows(parts):
    add = lambda a, b: a.astype(F32) + b.astype(F32)
    across = add(parts[2], over_core(parts[3])).astype(BF16)
    return add(
        add(parts[0], over_core(parts[1])), lax.ppermute(across, "stream", [(2, 0), (3, 1)])
    )


def columns_of(pieces, rows):
    lane = lax.broadcasted_iota(jnp.int32, (rows, 128), 1)
    out = jnp.zeros((rows, 128), F32)
    for index, piece in enumerate(pieces):
        out = jnp.where(lane == index, piece, out)
    return out


def row_sum(a):
    return jnp.sum(a, axis=1, keepdims=True)


def early_kernel(streams_ref, cot_ref, history_ref, out_ref):
    cot = cot_ref[...].astype(F32)
    plain, crossed, direct = [], [], []
    layers = [history_ref[j].astype(F32) for j in range(HIST)]
    for layer in layers:
        plain.append(row_sum(layer))
        direct.append(row_sum(cot * layer))
    for s in range(4):
        for layer in layers:
            crossed.append(row_sum(streams_ref[s] * layer))
    out_ref[...] = columns_of(crossed + plain + direct, cot.shape[0])


def early_sums(streams, cot, history):
    _, tokens, feats = streams.shape
    block = min(128, tokens)
    return pl.pallas_call(
        early_kernel,
        grid=(tokens // block,),
        in_specs=[
            pl.BlockSpec((4, block, feats), lambda i: (0, i, 0)),
            pl.BlockSpec((block, feats), lambda i: (i, 0)),
            pl.BlockSpec((HIST, block, feats), lambda i: (0, i, 0)),
        ],
        out_specs=pl.BlockSpec((block, 128), lambda i: (i, 0)),
        out_shape=jax.ShapeDtypeStruct((tokens, 128), F32),
        compiler_params=pltpu.CompilerParams(vmem_limit_bytes=40 * 1024 * 1024),
        cost_estimate=pl.CostEstimate(
            flops=110 * tokens * feats, bytes_accessed=36 * tokens * feats, transcendentals=0
        ),
        name="early_sums",
    )(streams, cot, history)


def sums_kernel(g0, g1, g2, g3, streams_ref, stats_ref, gain_ref, history_ref, out_ref, edge_ref):
    stats = stats_ref[...]
    rows = stats.shape[0]

    @pl.when(pl.program_id(0) == 0)
    def _():
        edge_ref[...] = jnp.zeros_like(edge_ref)

    firsts, seconds, dots = [], [], []
    for s, g_ref in enumerate((g0, g1, g2, g3)):
        g = g_ref[...].astype(F32)
        centered = (streams_ref[s] - stats[:, s : s + 1]) * stats[:, 4 + s : 5 + s]
        edge_ref[s : s + 1] += jnp.sum(g * centered, axis=0, keepdims=True)
        edge_ref[4 + s : 5 + s] += jnp.sum(g, axis=0, keepdims=True)
        scaled = g * gain_ref[s : s + 1]
        firsts.append(row_sum(scaled))
        seconds.append(row_sum(scaled * centered))
        for j in range(HIST):
            dots.append(row_sum(scaled * history_ref[j].astype(F32)))
    out_ref[...] = columns_of(dots + firsts + seconds, rows)


def gradient_sums(grads, streams, stats, gain, history):
    _, tokens, feats = streams.shape
    block = min(128, tokens)
    wide = pl.BlockSpec((block, feats), lambda i: (i, 0))
    sums, edges = pl.pallas_call(
        sums_kernel,
        grid=(tokens // block,),
        in_specs=[wide] * 4
        + [
            pl.BlockSpec((4, block, feats), lambda i: (0, i, 0)),
            pl.BlockSpec((block, 8), lambda i: (i, 0)),
            pl.BlockSpec((4, feats), lambda i: (0, 0)),
            pl.BlockSpec((HIST, block, feats), lambda i: (0, i, 0)),
        ],
        out_specs=[
            pl.BlockSpec((block, 128), lambda i: (i, 0)),
            pl.BlockSpec((8, feats), lambda i: (0, 0)),
        ],
        out_shape=[
            jax.ShapeDtypeStruct((tokens, 128), F32),
            jax.ShapeDtypeStruct((8, feats), F32),
        ],
        compiler_params=pltpu.CompilerParams(vmem_limit_bytes=40 * 1024 * 1024),
        cost_estimate=pl.CostEstimate(
            flops=110 * tokens * feats, bytes_accessed=42 * tokens * feats, transcendentals=0
        ),
        name="gradient_sums",
    )(*grads, streams, stats, gain, history)
    return sums[:, : 4 * HIST + 8], edges


def mix_gradient(sums, early, stats, model_width):
    n = 4 * HIST
    first, second = sums[n : n + 4] / model_width, sums[n + 4 : n + 8] / model_width
    spread = lambda a: jnp.repeat(a, HIST, axis=0)
    crossed, plain, direct = early[:n], early[n : n + HIST], early[n + HIST : n + 2 * HIST]
    means, inverse = spread(stats.T[:4]), spread(stats.T[4:])
    plain = jnp.tile(plain, (4, 1))
    crossed = (crossed - means * plain) * inverse
    d_mix = inverse * (sums[:n] - spread(first) * plain - spread(second) * crossed)
    d_mix = d_mix + jnp.concatenate([jnp.zeros_like(d_mix[: 3 * HIST]), direct])
    return d_mix, jnp.concatenate([first, second])


def history_kernel(
    g0, g1, g2, g3, streams_ref, stats_ref, gain_ref, cot_ref, current_ref, columns_ref, d_ref, w_ref, out_ref
):
    n = 4 * HIST
    stats, columns = stats_ref[...], columns_ref[...]
    column = lambda i: columns[:, i : i + 1]
    d_streams = []
    for s, g_ref in enumerate((g0, g1, g2, g3)):
        inverse = stats[:, 4 + s : 5 + s]
        centered = (streams_ref[s] - stats[:, s : s + 1]) * inverse
        scaled = g_ref[...].astype(F32) * gain_ref[s : s + 1]
        d_streams.append(inverse * (scaled - column(n + s) - centered * column(n + 4 + s)))
    d_streams[3] = d_streams[3] + cot_ref[...].astype(F32)
    for j in range(HIST):
        total = column(j) * d_streams[0]
        for s in range(1, 4):
            total = total + column(s * HIST + j) * d_streams[s]
        if j == HIST - 1:
            total = total + jnp.dot(
                d_ref[...], w_ref[...], precision=HIGHEST, preferred_element_type=F32
            )
            total = total - current_ref[...].astype(F32) * column(n + 9)
        out_ref[j] = total


def history_gradient(grads, streams, stats, gain, cot, current, columns, d_scaled, w_rows):
    _, tokens, feats = streams.shape
    block = min(128, tokens)
    wide = pl.BlockSpec((block, feats), lambda i: (i, 0))
    narrow = lambda a: pl.BlockSpec((block, a.shape[1]), lambda i: (i, 0))
    fixed = lambda a: pl.BlockSpec(a.shape, lambda i: (0, 0))
    return pl.pallas_call(
        history_kernel,
        grid=(tokens // block,),
        in_specs=[wide] * 4
        + [
            pl.BlockSpec((4, block, feats), lambda i: (0, i, 0)),
            narrow(stats),
            fixed(gain),
            wide,
            wide,
            narrow(columns),
            narrow(d_scaled),
            fixed(w_rows),
        ],
        out_specs=pl.BlockSpec((HIST, block, feats), lambda i: (0, i, 0)),
        out_shape=jax.ShapeDtypeStruct((HIST, tokens, feats), F32),
        compiler_params=pltpu.CompilerParams(vmem_limit_bytes=40 * 1024 * 1024),
        cost_estimate=pl.CostEstimate(
            flops=110 * tokens * feats, bytes_accessed=64 * tokens * feats, transcendentals=0
        ),
        name="history_gradient",
    )(*grads, streams, stats, gain, cot, current, columns, d_scaled, w_rows)


def shards(
    history,
    seq_lens,
    bucket_slot,
    w_mix_in,
    w_mix_out,
    mix_bias,
    ln_gain,
    ln_bias,
    w_qkv,
    w_attn_out,
    w_up,
    w_down,
    cotangent,
):
    member = lax.axis_index("stream")
    micro, quarter, feats = history.shape[1:]
    tokens = micro * quarter
    model_width = feats * lax.axis_size("head")
    slot_base = lax.axis_index("dp") * micro
    slot_ids = jnp.arange(bucket_slot.shape[0], dtype=jnp.int32)
    query_places = member * quarter + jnp.arange(quarter, dtype=jnp.int32)
    w_mix_in_f = w_mix_in.astype(F32)
    w_mix_out_f = w_mix_out.astype(F32)

    segments, starts = [], []
    for index in range(micro):
        bucket = jnp.sum(jnp.where(slot_ids == slot_base + index, bucket_slot, 0))
        lengths = jnp.sum(jnp.where(slot_ids[:, None] == bucket, seq_lens, 0), axis=0)
        bounds = jnp.cumsum(lengths)
        passed = (query_places[:, None] >= bounds[None, :]).astype(jnp.int32)
        segments.append(jnp.sum(passed, axis=1))
        starts.append(jnp.sum(passed * lengths[None, :], axis=1))
    valid = (jnp.concatenate(segments) < 3).astype(F32)[:, None]
    starts = jnp.concatenate(starts)
    position = jnp.tile(query_places, micro) - starts
    frequency = jnp.arange(ROT // 2, dtype=F32)
    phases = position.astype(F32)[:, None] * (10000.0 ** (-2.0 * frequency / ROT))
    cosine, sine = jnp.cos(phases), jnp.sin(phases)
    plain = jnp.zeros((tokens, HD - ROT), F32)
    none = jnp.zeros_like(sine)
    tables = (
        jnp.concatenate([cosine, cosine, plain + 1.0], axis=1),
        jnp.concatenate([-sine, none, plain], axis=1),
        jnp.concatenate([none, sine, plain], axis=1),
    )

    cot_rows = cotangent.reshape(tokens, feats).astype(F32) * valid
    out_full = lax.all_gather(cot_rows.astype(BF16), "head", axis=1, tiled=True)
    w_both = jnp.concatenate([w_attn_out, w_down])
    duplex = lined()
    kv_near = swap_head(w_qkv[1:]) if duplex else w_qkv[:1]

    history = history.reshape(HIST, tokens, feats)
    current = history[HIST - 1]
    current_f = current.astype(F32)
    mixed = lax.dot_general(w_mix_in, current, (((0,), (1,)), ((), ())), preferred_element_type=F32)
    square = jnp.sum(current_f * current_f, axis=1)[None]
    mixed = head_sum(jnp.concatenate([mixed, square]), 0).T
    mixed, kv_near = lax.optimization_barrier((mixed, kv_near))
    if duplex:
        kv_near = jnp.stack([kv_near, over_x(kv_near)])
        kv_near = jnp.concatenate([kv_near, over_y(kv_near)])
    rms_scale = lax.rsqrt(mixed[:, 4 * HIST :] / model_width + EPSILON)
    mix_pre = mixed[:, : 4 * HIST] * rms_scale
    mix_hidden = gelu_exact(mix_pre)
    mix_weights = jnp.dot(mix_hidden, w_mix_out_f, precision=HIGHEST) + mix_bias.reshape(-1)
    weights_four = mix_weights.reshape(tokens, 4, HIST)
    streams = jnp.zeros((4, tokens, feats), F32)
    for layer in range(HIST):
        streams = (
            streams
            + jnp.transpose(weights_four[:, :, layer])[:, :, None]
            * history[layer].astype(F32)[None]
        )
    stats = head_sum(
        jnp.concatenate([jnp.sum(streams, axis=2), jnp.sum(streams * streams, axis=2)]), 1
    )
    stat_sum, stat_square = stats[:4], stats[4:]
    early = early_sums(streams, cot_rows.astype(BF16), history)
    stat_sum, stat_square, out_full, kv_near, early = lax.optimization_barrier(
        (stat_sum, stat_square, out_full, kv_near, early)
    )
    row_means = (stat_sum / model_width)[:, :, None]
    inv_std = lax.rsqrt(stat_square[:, :, None] / model_width - row_means * row_means + EPSILON)
    centered = (streams - row_means) * inv_std
    row_stats = jnp.concatenate([row_means[..., 0], inv_std[..., 0]]).T
    early = lax.psum(early[:, : 6 * HIST].T, "head")
    normed = (centered * ln_gain[:, None, :] + ln_bias[:, None, :]).astype(BF16)

    def all_features(stream):
        return lax.all_gather(normed[stream], "head", axis=1, tiled=True)

    if duplex:
        w_kv = row_weight(w_qkv[1:], kv_near)
        k_in, v_in, up_in, q_in = normed[1], normed[2], all_features(3), all_features(0)
        (key_pre, value_pre), (wq, up_full, both_full) = exchange(
            [dot(k_in, w_kv[0]).astype(BF16), dot(v_in, w_kv[1]).astype(BF16)],
            [w_qkv[0], w_up, w_both],
            (0, 0, 1),
            4,
        )
    else:
        wq, wk, wv = gather_weight(w_qkv, 1)
        both_full = gather_weight(w_both, 1)
        up_full = gather_weight(w_up, 0)
        k_in, v_in, q_in, up_in = (all_features(s) for s in (1, 2, 0, 3))
        key_pre, value_pre = dot(k_in, wk), dot(v_in, wv)
    w_out_full, down_full = both_full[:feats], both_full[feats:]

    keys = rotate(key_pre, tables, 1.0)
    values = value_pre.astype(BF16)
    queries = dot(q_in, wq)
    d_attended = dot_nt(out_full, w_out_full).astype(BF16) * valid.astype(BF16)
    by_micro = lambda a: a.reshape(micro, quarter, feats)
    key_blocks = exchange_rows(by_micro(keys))
    value_blocks = exchange_rows(by_micro(values))
    places = member ^ jnp.arange(4, dtype=jnp.int32)
    results = attention(
        places,
        by_micro(queries),
        by_micro(d_attended),
        starts.reshape(micro, quarter, 1),
        valid.reshape(micro, quarter, 1),
        tuple(a.reshape(micro, quarter, HD) for a in tables),
        key_blocks,
        value_blocks,
    )
    attended, d_query_pre = results[0].reshape(tokens, feats), results[1].reshape(tokens, feats)
    d_keys = reduce_rows(results[2:6]).reshape(tokens, feats)
    d_values = reduce_rows(results[6:10]).reshape(tokens, feats)
    d_key_pre = rotate(d_keys, tables, -1.0)
    d_value_pre = d_values.astype(BF16)

    up_pre = dot(up_in, up_full)
    below = 0.5 * (1.0 + lax.erf(up_pre * 0.5**0.5))
    slope = below + up_pre * jnp.exp(-0.5 * up_pre * up_pre) * (2.0 * jnp.pi) ** -0.5
    gated_up, slope = lax.optimization_barrier(((up_pre * below).astype(BF16), slope))
    d_up = (dot_nt(out_full, down_full) * slope).astype(BF16)

    def to_owner(partial):
        return lax.psum_scatter(
            partial.astype(BF16), "head", scatter_dimension=1, tiled=True
        ).astype(F32)

    g_up = to_owner(dot_nt(d_up, up_full))
    combined = dot(attended, w_out_full) + dot(gated_up, down_full)
    if duplex:
        partials = [dot_nt(d_query_pre, wq).astype(BF16), combined.astype(BF16)]
        partials, d_key_pre, d_value_pre = lax.optimization_barrier(
            (partials, d_key_pre, d_value_pre)
        )
        (g_query, branch), _ = exchange(partials, [], (), 5)
        d_key_full = lax.all_gather(d_key_pre, "head", axis=1, tiled=True)
        d_value_full = lax.all_gather(d_value_pre, "head", axis=1, tiled=True)
        g_key, g_value = dot_nt(d_key_full, w_kv[0]), dot_nt(d_value_full, w_kv[1])
    else:
        g_query = to_owner(dot_nt(d_query_pre, wq))
        g_key = to_owner(dot_nt(d_key_pre, wk))
        g_value = to_owner(dot_nt(d_value_pre, wv))
        branch = to_owner(combined)
    block_out = (valid * (streams[3] + branch)).astype(BF16)

    product = lambda a, b: dot_tn(a, b).astype(BF16)
    up_terms = scatter_parts(product(up_in, d_up)[None])
    down_terms = scatter_parts(product(out_full, gated_up)[None])
    grad_up = add_terms(up_terms[0][0], up_terms[1][0], False)
    grad_down = add_terms(down_terms[0][0], down_terms[1][0], True)
    if duplex:
        by_head = lambda a, b: jnp.concatenate(
            [product(a, b[:, i * feats : (i + 1) * feats]) for i in range(4)]
        )
        terms = scatter_parts(
            jnp.stack([by_head(k_in, d_key_full), by_head(v_in, d_value_full)])
        )
        kv = swap_head((terms[0].astype(F32) + terms[1].astype(F32)).astype(BF16)).astype(F32)
        terms = scatter_parts(jnp.stack([product(q_in, d_query_pre), product(out_full, attended)]))
        grad_query = terms[0][:1].astype(F32) + terms[1][:1].astype(F32)
        grad_qkv = jnp.concatenate([grad_query, kv])
    else:
        terms = scatter_parts(
            jnp.stack(
                [
                    product(q_in, d_query_pre),
                    product(k_in, d_key_pre),
                    product(v_in, d_value_pre),
                    product(out_full, attended),
                ]
            )
        )
        grad_qkv = terms[0][:3].astype(F32) + terms[1][:3].astype(F32)
    grad_attn_out = add_terms(terms[0][-1], terms[1][-1], True)

    grads = (g_query, g_key, g_value, g_up)
    sums, gain_shift = gradient_sums(grads, streams, row_stats, ln_gain, history)
    sums = head_sum(sums.T, 3)
    d_mix, coefs = mix_gradient(sums, early, row_stats, model_width)
    d_hidden = jnp.dot(w_mix_out_f, d_mix, precision=HIGHEST)
    mix_pre_t = mix_pre.T
    below_mix = 0.5 * (1.0 + lax.erf(mix_pre_t * 0.5**0.5))
    density = jnp.exp(-0.5 * mix_pre_t * mix_pre_t) * (2.0 * jnp.pi) ** -0.5
    d_pre = d_hidden * (below_mix + mix_pre_t * density)
    cross = jnp.sum(d_pre * mix_pre_t, axis=0, keepdims=True)
    rms_row = rms_scale.T
    grad_w1 = jnp.dot(d_pre * rms_row, current_f, precision=HIGHEST)
    grad_w2 = jnp.dot(mix_hidden.T, d_mix.T, precision=HIGHEST)
    grad_bias = jnp.sum(d_mix, axis=1)
    wide = lambda a: jnp.pad(a, ((0, 0), (0, feats - a.shape[1])))
    small = jnp.concatenate([grad_w1, gain_shift, wide(grad_w2), wide(grad_bias[None])])
    small = lax.psum(small.astype(BF16), ("dp", "stream")).astype(F32)
    n = 4 * HIST
    columns = jnp.concatenate(
        [mix_weights.T, coefs, rms_row, rms_row * rms_row * cross / model_width]
    ).T
    history_grad = history_gradient(
        grads,
        streams,
        row_stats,
        ln_gain,
        cot_rows.astype(BF16),
        current,
        columns,
        (d_pre * rms_row).T,
        w_mix_in_f.T,
    ).reshape(HIST, micro, quarter, feats)
    return (
        block_out.reshape(micro, quarter, feats),
        mix_weights.reshape(micro, quarter, 4 * HIST),
        history_grad,
        small[:n].T,
        small[n + 8 : 2 * n + 8, :n],
        small[2 * n + 8, :n].reshape(mix_bias.shape),
        small[n : n + 4],
        small[n + 4 : n + 8],
        grad_qkv,
        grad_attn_out,
        grad_up,
        grad_down,
    )


def solution(mesh):
    return jax.shard_map(
        shards,
        mesh=mesh,
        in_specs=(
            P(None, "dp", "stream", "head"),
            P(),
            P(),
            P("head", None),
            P(),
            P(),
            P(None, "head"),
            P(None, "head"),
            P(None, ("dp", "stream"), "head"),
            P("head", ("dp", "stream")),
            P(("dp", "stream"), "head"),
            P("head", ("dp", "stream")),
            P("dp", "stream", "head"),
        ),
        out_specs=(
            P("dp", "stream", "head"),
            P("dp", "stream", None),
            P(None, "dp", "stream", "head"),
            P("head", None),
            P(),
            P(),
            P(None, "head"),
            P(None, "head"),
            P(None, ("dp", "stream"), "head"),
            P("head", ("dp", "stream")),
            P(("dp", "stream"), "head"),
            P("head", ("dp", "stream")),
        ),
        check_vma=False,
    )
```

```python
import functools

import jax
import jax.numpy as jnp
from jax import lax
from jax.experimental import pallas as pl
from jax.experimental.pallas import tpu as pltpu
from jax.sharding import PartitionSpec as P

HD = 128
HIST = 9
ROT = 32

EPSILON = 1e-05
HIGHEST = lax.Precision.HIGHEST
MASKED = -1e30
F32 = jnp.float32
BF16 = jnp.bfloat16

SWAP_X = [(0, 1), (1, 0)]
SWAP_Y = [(0, 2), (2, 0), (1, 3), (3, 1)]
SWAP_CORE = [(0, 1), (1, 0), (2, 3), (3, 2)]


def dot(a, b):
    return jnp.dot(a, b, preferred_element_type=F32)


def dot_nt(a, b):
    return lax.dot_general(a, b, (((1,), (1,)), ((), ())), preferred_element_type=F32)


def dot_tn(a, b):
    return lax.dot_general(a, b, (((0,), (0,)), ((), ())), preferred_element_type=F32)


def gelu_exact(values_in):
    return jax.nn.gelu(values_in, approximate=False)


def over_x(a):
    return lax.ppermute(a, "dp", SWAP_X)


def over_y(a):
    return lax.ppermute(a, "stream", SWAP_Y)


def over_core(a):
    return lax.ppermute(a, "stream", SWAP_CORE)


def paired():
    return lax.axis_size("dp") == 2 and lax.axis_size("stream") == 4


def place_kernel(order_ref, near_ref, beside_ref, out_ref):
    step = pl.program_id(0)
    half = pl.num_programs(0) // 2

    @pl.when(step < half)
    def _():
        out_ref[...] = near_ref[0]

    @pl.when(step >= half)
    def _():
        out_ref[...] = beside_ref[0]


def gather_weight(shard, axis):
    return lax.all_gather(shard, ("dp", "stream"), axis=axis, tiled=True)


def lined():
    return paired() and lax.axis_size("head") == 4


def swap_head(a):
    at = lambda x, y, core, z: (x * 4 + y * 2 + core) * 4 + z
    pairs = [
        (at(x, y, core, z), at(z // 2, z % 2, core, 2 * x + y))
        for x in range(2)
        for y in range(2)
        for core in range(2)
        for z in range(4)
    ]
    return lax.ppermute(a, ("dp", "stream", "head"), pairs)


def row_weight(shard, near):
    place = lax.axis_index("dp") * 4 + lax.axis_index("stream")
    beside = over_core(near)
    flips = jnp.array([0, 4, 2, 6, 1, 5, 3, 7], jnp.int32)
    count, rows, columns = shard.shape
    piece = (1, count, rows, columns)
    inner = (0, 0, 0)
    return pl.pallas_call(
        place_kernel,
        grid_spec=pltpu.PrefetchScalarGridSpec(
            num_scalar_prefetch=1,
            grid=(8,),
            in_specs=[
                pl.BlockSpec(piece, lambda k, order: (jnp.minimum(k, 3),) + inner),
                pl.BlockSpec(piece, lambda k, order: (jnp.maximum(k - 4, 0),) + inner),
            ],
            out_specs=pl.BlockSpec(
                shard.shape,
                lambda k, order: (0, lax.rem(order[k], 2), lax.div(order[k], 2)),
            ),
        ),
        out_shape=jax.ShapeDtypeStruct((count, 2 * rows, 4 * columns), shard.dtype),
        compiler_params=pltpu.CompilerParams(vmem_limit_bytes=40 * 1024 * 1024),
        cost_estimate=pl.CostEstimate(flops=0, bytes_accessed=32 * shard.size, transcendentals=0),
        name="weight_in_order",
    )(place ^ flips, near, beside)


def scatter_parts(partial):
    if not paired():
        whole = lax.psum_scatter(partial, ("dp", "stream"), scatter_dimension=1, tiled=True)
        return whole, jnp.zeros_like(whole)
    count, rows, columns = partial.shape
    stream = lax.axis_index("stream")
    x, y, core = lax.axis_index("dp"), stream // 2, stream % 2

    def pick(a, index, axis):
        return lax.dynamic_index_in_dim(a, index, axis, keepdims=False)

    def add(a, b):
        return (a.astype(F32) + b.astype(F32)).astype(BF16)

    split = partial.reshape(count, 4, 2, rows // 8, columns)
    chip = add(pick(split, core, 2), over_core(pick(split, 1 - core, 2)))
    chip = chip.reshape(count, 2, 2, rows // 8, columns)
    line = add(pick(chip, x, 1), over_x(pick(chip, 1 - x, 1)))
    return pick(line, y, 1), over_y(pick(line, 1 - y, 1))


def add_kernel(turned, a_ref, b_ref, out_ref):
    total = a_ref[...].astype(F32) + b_ref[...].astype(F32)
    out_ref[...] = total.T if turned else total


def add_terms(a, b, turned):
    rows, columns = a.shape
    block = min(512, columns)
    return pl.pallas_call(
        functools.partial(add_kernel, turned),
        grid=(columns // block,),
        in_specs=[pl.BlockSpec((rows, block), lambda i: (0, i))] * 2,
        out_specs=pl.BlockSpec((block, rows), lambda i: (i, 0))
        if turned
        else pl.BlockSpec((rows, block), lambda i: (0, i)),
        out_shape=jax.ShapeDtypeStruct((columns, rows) if turned else (rows, columns), F32),
        cost_estimate=pl.CostEstimate(
            flops=rows * columns, bytes_accessed=8 * rows * columns, transcendentals=0
        ),
        name="add_terms",
    )(a, b)


def exchange_kernel(units, whole, axes, *refs):
    count = len(axes)
    inputs, refs = refs[: units + whole + count], refs[units + whole + count :]
    partials, pieces, shard_refs = inputs[:units], inputs[units : units + whole], inputs[units + whole :]
    outputs, refs = refs[: units + whole + count], refs[units + whole + count :]
    outs, wides, fulls = outputs[:units], outputs[units : units + whole], outputs[units + whole :]
    held, got, load_sem, send_sem, recv_sem, own_sem, near_send, near_recv = refs[:8]
    piece_own, piece_send, piece_recv = refs[8:]
    x, stream, z = lax.axis_index("dp"), lax.axis_index("stream"), lax.axis_index("head")
    core = lax.rem(stream, 2)
    other_x, other_y, other_core = 1 - x, lax.rem(stream + 2, 4), stream + 1 - 2 * core
    line = ({"head": lax.rem(z + 1, 4)}, {"head": lax.rem(z + 3, 4)})
    to_x, to_y, to_core = {"dp": other_x}, {"stream": other_y}, {"stream": other_core}
    place = x * 4 + stream
    place_x, place_y = other_x * 4 + stream, x * 4 + other_y
    place_far = other_x * 4 + other_y
    beside = lambda at: at + 1 - 2 * core

    barrier = pltpu.get_barrier_semaphore()
    peers = line + ((to_x, to_y, to_core) if count else ())
    for peer in peers:
        pl.semaphore_signal(barrier, inc=1, device_id=peer, device_id_type=pl.DeviceIdType.MESH)
    pl.semaphore_wait(barrier, len(peers))

    def region(w, at, part=None):
        full, width = fulls[w], shard_refs[w].shape[axes[w]]
        rows = shard_refs[w].shape[0]
        start, size = (0, rows) if part is None else (part * (rows // 2), rows // 2)
        if axes[w] == 0:
            return full.at[pl.ds(pl.multiple_of(at * width + start, size), size)]
        return full.at[pl.ds(start, size), pl.ds(pl.multiple_of(at * width, width), width)]

    def near(w, index, source, target, peer):
        return pltpu.make_async_remote_copy(
            src_ref=source,
            dst_ref=target,
            send_sem=near_send.at[w, index],
            recv_sem=near_recv.at[w, index],
            device_id=peer,
            device_id_type=pl.DeviceIdType.MESH,
        )

    def pass_on(w, index, at, peer, part=None):
        return near(w, index, region(w, at, part), region(w, at, part), peer)

    def first(w):
        target = region(w, place)
        pltpu.make_async_copy(shard_refs[w], target, own_sem.at[w]).start()
        for index, peer in enumerate((to_x, to_y, to_core)):
            near(w, index, shard_refs[w], target, peer).start()

    def second(w):
        pass_on(w, 0, place_x, to_x).wait_recv()
        pass_on(w, 4, place_x, to_y, 0).start()
        pass_on(w, 3, place_x, to_core).start()
        pass_on(w, 1, place_y, to_y).wait_recv()
        pass_on(w, 6, place_y, to_x, 1).start()
        pass_on(w, 5, place_y, to_core).start()

    def third(w):
        pass_on(w, 4, place_far, to_y, 0).wait_recv()
        pass_on(w, 7, place_far, to_core, 0).start()
        pass_on(w, 6, place_far, to_x, 1).wait_recv()
        pass_on(w, 8, place_far, to_core, 1).start()

    def last(w):
        for index, at, part in (
            (2, place, None),
            (3, place_x, None),
            (5, place_y, None),
            (7, place_far, 0),
            (8, place_far, 1),
        ):
            pass_on(w, index, beside(at), to_core, part).wait_recv()
        pltpu.make_async_copy(shard_refs[w], region(w, place), own_sem.at[w]).wait()
        for index in (0, 1, 2):
            near(w, index, shard_refs[w], region(w, place), to_core).wait_send()
        for index, at, part in (
            (3, place_x, None),
            (4, place_x, 0),
            (5, place_y, None),
            (6, place_y, 1),
            (7, place_far, 0),
            (8, place_far, 1),
        ):
            pass_on(w, index, at, to_core, part).wait_send()

    feats = held.shape[-1]
    chunk = send_sem.shape[-1]
    step_rows = held.shape[2] // chunk

    def load(u, b):
        return pltpu.make_async_copy(
            partials[u].at[:, b * feats : (b + 1) * feats], held.at[u, b], load_sem.at[u, b]
        )

    for u in range(units):
        for b in range(4):
            load(u, b).start()
    for w in range(count):
        first(w)

    def columns(block):
        return pl.ds(pl.multiple_of(block * feats, feats), feats)

    def keep(v):
        return pltpu.make_async_copy(pieces[v], wides[v].at[:, columns(z)], piece_own.at[v])

    for v in range(whole):
        keep(v).start()
    for u in range(units):
        for b in range(4):
            load(u, b).wait()

    def part(c):
        return pl.ds(pl.multiple_of(c * step_rows, step_rows), step_rows)

    def hop(way, u, step, block, c):
        return pltpu.make_async_remote_copy(
            src_ref=held.at[u, block, part(c)],
            dst_ref=got.at[way, u, step, part(c)],
            send_sem=send_sem.at[way, u, step, c],
            recv_sem=recv_sem.at[way, u, step, c],
            device_id=line[way],
            device_id_type=pl.DeviceIdType.MESH,
        )

    ways = ((0, z), (1, 3 - z))

    def relay(way, v, step, block, c):
        target = wides[v].at[part(c), columns(block)]
        return pltpu.make_async_remote_copy(
            src_ref=pieces[v].at[part(c)] if step == 0 else target,
            dst_ref=target,
            send_sem=piece_send.at[way, v, step, c],
            recv_sem=piece_recv.at[way, v, step, c],
            device_id=line[way],
            device_id_type=pl.DeviceIdType.MESH,
        )

    def piece_at(way, step):
        return z - step if way == 0 else z + step

    def block_at(way, step):
        return 3 - step + z if way == 0 else step + z - 3

    def line_step(step):
        def body(c, carry):
            for way, rank in ways:

                @pl.when(rank <= step)
                def _():
                    block = block_at(way, step)
                    for u in range(units):
                        if step > 0:

                            @pl.when(rank > 0)
                            def _():
                                hop(way, u, step - 1, block, c).wait_recv()
                                total = held[u, block, part(c)].astype(F32) + got[
                                    way, u, step - 1, part(c)
                                ].astype(F32)
                                held[u, block, part(c)] = total.astype(BF16)

                        hop(way, u, step, block, c).start()

                @pl.when((rank >= step) & (rank < 3))
                def _():
                    block = piece_at(way, step)
                    for v in range(whole):
                        if step > 0:
                            relay(way, v, step - 1, block, c).wait_recv()
                        relay(way, v, step, block, c).start()

            return carry

        lax.fori_loop(0, chunk, body, 0)

    line_step(0)
    for w in range(min(count, 2)):
        second(w)
    line_step(1)
    for w in range(2, count):
        second(w)
    line_step(2)
    for w in range(count):
        third(w)

    def finish(c, carry):
        for u in range(units):
            outs[u][part(c)] = held[u, z, part(c)].astype(F32)
            for way, rank in ways:

                @pl.when(rank > 0)
                def _():
                    hop(way, u, 2, z, c).wait_recv()
                    outs[u][part(c)] += got[way, u, 2, part(c)].astype(F32)

        for way, rank in ways:

            @pl.when(rank == 3)
            def _():
                for v in range(whole):
                    for step in range(3):
                        relay(way, v, step, piece_at(way, step + 1), c).wait_recv()

        return carry

    lax.fori_loop(0, chunk, finish, 0)
    for w in range(count):
        last(w)

    def drain(c, carry):
        for step in range(3):
            for way, rank in ways:

                @pl.when(rank <= step)
                def _():
                    for u in range(units):
                        hop(way, u, step, block_at(way, step), c).wait_send()

                @pl.when((rank >= step) & (rank < 3))
                def _():
                    for v in range(whole):
                        relay(way, v, step, piece_at(way, step), c).wait_send()

        return carry

    lax.fori_loop(0, chunk, drain, 0)
    for v in range(whole):
        keep(v).wait()


def exchange(partials, pieces, shards_in, axes, collective_id):
    units, whole, count = len(partials), len(pieces), len(shards_in)
    tokens, feats = partials[0].shape[0], partials[0].shape[1] // 4
    chunk = 4
    full = [
        jax.ShapeDtypeStruct(tuple(n * 8 if i == axis else n for i, n in enumerate(w.shape)), BF16)
        for w, axis in zip(shards_in, axes)
    ]
    anywhere = pl.BlockSpec(memory_space=pl.ANY)
    sems = pltpu.SemaphoreType.DMA
    results = pl.pallas_call(
        functools.partial(exchange_kernel, units, whole, axes),
        in_specs=[anywhere] * (units + whole + count),
        out_specs=[pl.BlockSpec(memory_space=pltpu.VMEM)] * units + [anywhere] * (whole + count),
        out_shape=[jax.ShapeDtypeStruct((tokens, feats), F32)] * units
        + [jax.ShapeDtypeStruct((tokens, 4 * feats), BF16)] * whole
        + full,
        scratch_shapes=[
            pltpu.VMEM((units, 4, tokens, feats), BF16),
            pltpu.VMEM((2, units, 3, tokens, feats), BF16),
            sems((units, 4)),
            sems((2, units, 3, chunk)),
            sems((2, units, 3, chunk)),
            sems((max(count, 1),)),
            sems((max(count, 1), 9)),
            sems((max(count, 1), 9)),
            sems((whole,)),
            sems((2, whole, 3, chunk)),
            sems((2, whole, 3, chunk)),
        ],
        compiler_params=pltpu.CompilerParams(
            collective_id=collective_id,
            has_side_effects=True,
            vmem_limit_bytes=48 * 1024 * 1024,
        ),
        cost_estimate=pl.CostEstimate(
            flops=0, bytes_accessed=600 * 1024 * 1024, transcendentals=0
        ),
        name="exchange",
    )(*partials, *pieces, *shards_in)
    return results[:units], results[units : units + whole], results[units + whole :]


def head_sum_kernel(members, x_ref, out_ref, slots, send_sem, recv_sem):
    z = lax.axis_index("head")
    barrier = pltpu.get_barrier_semaphore()
    for k in range(1, members):
        pl.semaphore_signal(
            barrier,
            inc=1,
            device_id={"head": lax.rem(z + k, members)},
            device_id_type=pl.DeviceIdType.MESH,
        )
    pl.semaphore_wait(barrier, members - 1)
    copies = []
    for k in range(1, members):
        copy = pltpu.make_async_remote_copy(
            src_ref=x_ref,
            dst_ref=slots.at[z],
            send_sem=send_sem.at[k - 1],
            recv_sem=recv_sem.at[k - 1],
            device_id={"head": lax.rem(z + k, members)},
            device_id_type=pl.DeviceIdType.MESH,
        )
        copy.start()
        copies.append(copy)
    slots[z] = x_ref[...]
    for copy in copies:
        copy.wait()
    total = slots[0]
    for k in range(1, members):
        total = total + slots[k]
    out_ref[...] = total


def head_sum(x, collective_id):
    members = lax.axis_size("head")
    return pl.pallas_call(
        functools.partial(head_sum_kernel, members),
        out_shape=jax.ShapeDtypeStruct(x.shape, F32),
        in_specs=[pl.BlockSpec(memory_space=pltpu.VMEM)],
        out_specs=pl.BlockSpec(memory_space=pltpu.VMEM),
        scratch_shapes=[
            pltpu.VMEM((members,) + x.shape, F32),
            pltpu.SemaphoreType.DMA((members - 1,)),
            pltpu.SemaphoreType.DMA((members - 1,)),
        ],
        compiler_params=pltpu.CompilerParams(collective_id=collective_id, has_side_effects=True),
        name="sum_over_head",
    )(x)


def plane_sum_kernel(x_ref, out_ref, got, send_sem, recv_sem):
    x, stream = lax.axis_index("dp"), lax.axis_index("stream")
    peers = (
        {"stream": stream + 1 - 2 * lax.rem(stream, 2)},
        {"stream": lax.rem(stream + 2, 4)},
        {"dp": 1 - x},
    )
    barrier = pltpu.get_barrier_semaphore()
    for peer in peers:
        pl.semaphore_signal(barrier, inc=1, device_id=peer, device_id_type=pl.DeviceIdType.MESH)
    pl.semaphore_wait(barrier, 3)
    out_ref[...] = x_ref[...]
    for step, peer in enumerate(peers):
        copy = pltpu.make_async_remote_copy(
            src_ref=out_ref,
            dst_ref=got.at[step],
            send_sem=send_sem.at[step],
            recv_sem=recv_sem.at[step],
            device_id=peer,
            device_id_type=pl.DeviceIdType.MESH,
        )
        copy.start()
        copy.wait()
        out_ref[...] += got[step]


def plane_sum(x, collective_id):
    if not paired():
        return lax.psum(x.astype(BF16), ("dp", "stream")).astype(F32)
    return pl.pallas_call(
        plane_sum_kernel,
        out_shape=jax.ShapeDtypeStruct(x.shape, F32),
        in_specs=[pl.BlockSpec(memory_space=pltpu.VMEM)],
        out_specs=pl.BlockSpec(memory_space=pltpu.VMEM),
        scratch_shapes=[
            pltpu.VMEM((3,) + x.shape, F32),
            pltpu.SemaphoreType.DMA((3,)),
            pltpu.SemaphoreType.DMA((3,)),
        ],
        compiler_params=pltpu.CompilerParams(collective_id=collective_id, has_side_effects=True),
        name="sum_over_plane",
    )(x)


def turn(v, keep, left, right):
    h = ROT // 2
    return v * keep + pltpu.roll(v, HD - h, 1) * left + pltpu.roll(v, h, 1) * right


def rotate_kernel(sign, v_ref, keep_ref, left_ref, right_ref, out_ref):
    for head in range(v_ref.shape[1] // HD):
        part = pl.ds(head * HD, HD)
        out_ref[:, part] = turn(
            v_ref[:, part], keep_ref[...], sign * left_ref[...], sign * right_ref[...]
        ).astype(BF16)


def rotate(values_in, tables, sign):
    tokens, feats = values_in.shape
    block = min(tokens, 256)
    table = pl.BlockSpec((block, HD), lambda i: (i, 0))
    wide = pl.BlockSpec((block, feats), lambda i: (i, 0))
    return pl.pallas_call(
        functools.partial(rotate_kernel, sign),
        grid=(tokens // block,),
        in_specs=[wide, table, table, table],
        out_specs=wide,
        out_shape=jax.ShapeDtypeStruct((tokens, feats), BF16),
        cost_estimate=pl.CostEstimate(
            flops=5 * tokens * feats, bytes_accessed=8 * tokens * feats, transcendentals=0
        ),
        name="rotate_heads",
    )(values_in, *tables)


def attention_kernel(
    place_ref, q_ref, do_ref, start_ref, valid_ref, keep_ref, left_ref, right_ref, *refs
):
    blocks = (len(refs) - 4) // 4
    k_refs, v_refs = refs[:blocks], refs[blocks : 2 * blocks]
    o_ref, dq_ref = refs[2 * blocks : 2 * blocks + 2]
    dk_refs = refs[2 * blocks + 2 : 3 * blocks + 2]
    dv_refs = refs[3 * blocks + 2 : 4 * blocks + 2]
    s_ref, dp_ref = refs[4 * blocks + 2 :]
    rows = q_ref.shape[1]
    scale = HD ** (-0.5)
    member = place_ref[0]
    keep, left, right = keep_ref[0], left_ref[0], right_ref[0]
    q = turn(q_ref[0], keep, left, right).astype(BF16)
    d_out = do_ref[0]
    start = start_ref[0]
    top = jnp.full((rows, 1), MASKED, F32)
    t = member * rows + lax.broadcasted_iota(jnp.int32, (rows, rows), 0)
    for j in range(blocks):
        u = place_ref[j] * rows + lax.broadcasted_iota(jnp.int32, (rows, rows), 1)
        allowed = (u <= t) & (u >= start)
        s_ref[j] = jnp.where(allowed, dot_nt(q, k_refs[j][0]) * scale, MASKED)
        top = jnp.maximum(top, jnp.max(s_ref[j], axis=1, keepdims=True))
    total = jnp.zeros((rows, 1), F32)
    for j in range(blocks):
        e = jnp.exp(s_ref[j] - top)
        s_ref[j] = e
        total = total + jnp.sum(e, axis=1, keepdims=True)
    inverse = 1.0 / total
    out = jnp.zeros((rows, HD), F32)
    delta = jnp.zeros((rows, 1), F32)
    for j in range(blocks):
        p = s_ref[j] * inverse
        s_ref[j] = p
        p_bf = p.astype(BF16)
        out = out + dot(p_bf, v_refs[j][0])
        dv_refs[j][0] = dot_tn(p_bf, d_out).astype(BF16)
        d_p = dot_nt(d_out, v_refs[j][0])
        dp_ref[j] = d_p
        delta = delta + jnp.sum(p * d_p, axis=1, keepdims=True)
    o_ref[0] = (out * valid_ref[0]).astype(BF16)
    d_q = jnp.zeros((rows, HD), F32)
    for j in range(blocks):
        d_s = (s_ref[j] * (dp_ref[j] - delta)).astype(BF16)
        d_q = d_q + dot(d_s, k_refs[j][0])
        dk_refs[j][0] = (dot_tn(d_s, q) * scale).astype(BF16)
    dq_ref[0] = turn(d_q * scale, keep, -left, -right).astype(BF16)


def attention(places, queries, d_attended, starts, valid, tables, keys, values):
    micro, rows, feats = queries.shape
    blocks = len(keys)
    tile = pl.BlockSpec((1, rows, HD), lambda b, h: (b, 0, h))
    like = lambda dtype: jax.ShapeDtypeStruct((micro, rows, feats), dtype)
    return pl.pallas_call(
        attention_kernel,
        grid=(micro, feats // HD),
        in_specs=[pl.BlockSpec(memory_space=pltpu.SMEM), tile, tile]
        + [pl.BlockSpec((1, rows, 1), lambda b, h: (b, 0, 0))] * 2
        + [pl.BlockSpec((1, rows, HD), lambda b, h: (b, 0, 0))] * 3
        + [tile] * (2 * blocks),
        out_specs=[tile] * (2 + 2 * blocks),
        out_shape=[like(BF16)] * (2 + 2 * blocks),
        scratch_shapes=[
            pltpu.VMEM((blocks, rows, rows), F32),
            pltpu.VMEM((blocks, rows, rows), F32),
        ],
        compiler_params=pltpu.CompilerParams(vmem_limit_bytes=40 * 1024 * 1024),
        cost_estimate=pl.CostEstimate(
            flops=12 * micro * feats * rows * rows * blocks,
            bytes_accessed=micro * rows * feats * 2 * (4 + 4 * blocks),
            transcendentals=micro * rows * rows * blocks * feats // HD,
        ),
        name="attention_both_ways",
    )(places, queries, d_attended, starts, valid, *tables, *keys, *values)


def exchange_rows(local):
    if lax.axis_size("stream") != 4:
        raise ValueError("stream")
    across = lax.ppermute(local, "stream", [(0, 2), (1, 3)])
    beside = over_core(local)
    return (local, beside, across, over_core(across))


def reduce_rows(parts):
    add = lambda a, b: a.astype(F32) + b.astype(F32)
    across = add(parts[2], over_core(parts[3])).astype(BF16)
    return add(
        add(parts[0], over_core(parts[1])), lax.ppermute(across, "stream", [(2, 0), (3, 1)])
    )


def columns_of(pieces, rows):
    lane = lax.broadcasted_iota(jnp.int32, (rows, 128), 1)
    out = jnp.zeros((rows, 128), F32)
    for index, piece in enumerate(pieces):
        out = jnp.where(lane == index, piece, out)
    return out


def row_sum(a):
    return jnp.sum(a, axis=1, keepdims=True)


def streams_kernel(weights_ref, history_ref, streams_ref, stats_ref):
    weights = weights_ref[...]
    layers = [history_ref[j].astype(F32) for j in range(HIST)]
    sums, squares = [], []
    for s in range(4):
        total = weights[:, s * HIST : s * HIST + 1] * layers[0]
        for j in range(1, HIST):
            total = total + weights[:, s * HIST + j : s * HIST + j + 1] * layers[j]
        streams_ref[s] = total
        sums.append(row_sum(total))
        squares.append(row_sum(total * total))
    stats_ref[...] = columns_of(sums + squares, weights.shape[0])


def mix_streams(weights, history):
    _, tokens, feats = history.shape
    block = min(128, tokens)
    return pl.pallas_call(
        streams_kernel,
        grid=(tokens // block,),
        in_specs=[
            pl.BlockSpec((block, weights.shape[1]), lambda i: (i, 0)),
            pl.BlockSpec((HIST, block, feats), lambda i: (0, i, 0)),
        ],
        out_specs=[
            pl.BlockSpec((4, block, feats), lambda i: (0, i, 0)),
            pl.BlockSpec((block, 128), lambda i: (i, 0)),
        ],
        out_shape=[
            jax.ShapeDtypeStruct((4, tokens, feats), F32),
            jax.ShapeDtypeStruct((tokens, 128), F32),
        ],
        compiler_params=pltpu.CompilerParams(vmem_limit_bytes=40 * 1024 * 1024),
        cost_estimate=pl.CostEstimate(
            flops=80 * tokens * feats, bytes_accessed=34 * tokens * feats, transcendentals=0
        ),
        name="mix_streams",
    )(weights, history)


def early_kernel(streams_ref, cot_ref, history_ref, out_ref):
    cot = cot_ref[...].astype(F32)
    plain, crossed, direct = [], [], []
    layers = [history_ref[j].astype(F32) for j in range(HIST)]
    for layer in layers:
        plain.append(row_sum(layer))
        direct.append(row_sum(cot * layer))
    for s in range(4):
        for layer in layers:
            crossed.append(row_sum(streams_ref[s] * layer))
    out_ref[...] = columns_of(crossed + plain + direct, cot.shape[0])


def early_sums(streams, cot, history):
    _, tokens, feats = streams.shape
    block = min(128, tokens)
    return pl.pallas_call(
        early_kernel,
        grid=(tokens // block,),
        in_specs=[
            pl.BlockSpec((4, block, feats), lambda i: (0, i, 0)),
            pl.BlockSpec((block, feats), lambda i: (i, 0)),
            pl.BlockSpec((HIST, block, feats), lambda i: (0, i, 0)),
        ],
        out_specs=pl.BlockSpec((block, 128), lambda i: (i, 0)),
        out_shape=jax.ShapeDtypeStruct((tokens, 128), F32),
        compiler_params=pltpu.CompilerParams(vmem_limit_bytes=40 * 1024 * 1024),
        cost_estimate=pl.CostEstimate(
            flops=110 * tokens * feats, bytes_accessed=36 * tokens * feats, transcendentals=0
        ),
        name="early_sums",
    )(streams, cot, history)


def sums_kernel(g0, g1, g2, g3, streams_ref, stats_ref, gain_ref, history_ref, out_ref, edge_ref):
    stats = stats_ref[...]
    rows = stats.shape[0]

    @pl.when(pl.program_id(0) == 0)
    def _():
        edge_ref[...] = jnp.zeros_like(edge_ref)

    firsts, seconds, dots = [], [], []
    for s, g_ref in enumerate((g0, g1, g2, g3)):
        g = g_ref[...].astype(F32)
        centered = (streams_ref[s] - stats[:, s : s + 1]) * stats[:, 4 + s : 5 + s]
        edge_ref[s : s + 1] += jnp.sum(g * centered, axis=0, keepdims=True)
        edge_ref[4 + s : 5 + s] += jnp.sum(g, axis=0, keepdims=True)
        scaled = g * gain_ref[s : s + 1]
        firsts.append(row_sum(scaled))
        seconds.append(row_sum(scaled * centered))
        for j in range(HIST):
            dots.append(row_sum(scaled * history_ref[j].astype(F32)))
    out_ref[...] = columns_of(dots + firsts + seconds, rows)


def gradient_sums(grads, streams, stats, gain, history):
    _, tokens, feats = streams.shape
    block = min(128, tokens)
    wide = pl.BlockSpec((block, feats), lambda i: (i, 0))
    sums, edges = pl.pallas_call(
        sums_kernel,
        grid=(tokens // block,),
        in_specs=[wide] * 4
        + [
            pl.BlockSpec((4, block, feats), lambda i: (0, i, 0)),
            pl.BlockSpec((block, 8), lambda i: (i, 0)),
            pl.BlockSpec((4, feats), lambda i: (0, 0)),
            pl.BlockSpec((HIST, block, feats), lambda i: (0, i, 0)),
        ],
        out_specs=[
            pl.BlockSpec((block, 128), lambda i: (i, 0)),
            pl.BlockSpec((8, feats), lambda i: (0, 0)),
        ],
        out_shape=[
            jax.ShapeDtypeStruct((tokens, 128), F32),
            jax.ShapeDtypeStruct((8, feats), F32),
        ],
        compiler_params=pltpu.CompilerParams(vmem_limit_bytes=40 * 1024 * 1024),
        cost_estimate=pl.CostEstimate(
            flops=110 * tokens * feats, bytes_accessed=42 * tokens * feats, transcendentals=0
        ),
        name="gradient_sums",
    )(*grads, streams, stats, gain, history)
    return sums[:, : 4 * HIST + 8], edges


def mix_gradient(sums, early, stats, model_width):
    n = 4 * HIST
    first, second = sums[n : n + 4] / model_width, sums[n + 4 : n + 8] / model_width
    spread = lambda a: jnp.repeat(a, HIST, axis=0)
    crossed, plain, direct = early[:n], early[n : n + HIST], early[n + HIST : n + 2 * HIST]
    means, inverse = spread(stats.T[:4]), spread(stats.T[4:])
    plain = jnp.tile(plain, (4, 1))
    crossed = (crossed - means * plain) * inverse
    d_mix = inverse * (sums[:n] - spread(first) * plain - spread(second) * crossed)
    d_mix = d_mix + jnp.concatenate([jnp.zeros_like(d_mix[: 3 * HIST]), direct])
    return d_mix, jnp.concatenate([first, second])


def history_kernel(
    g0, g1, g2, g3, streams_ref, stats_ref, gain_ref, cot_ref, current_ref, columns_ref, d_ref, w_ref, out_ref
):
    n = 4 * HIST
    stats, columns = stats_ref[...], columns_ref[...]
    column = lambda i: columns[:, i : i + 1]
    d_streams = []
    for s, g_ref in enumerate((g0, g1, g2, g3)):
        inverse = stats[:, 4 + s : 5 + s]
        centered = (streams_ref[s] - stats[:, s : s + 1]) * inverse
        scaled = g_ref[...].astype(F32) * gain_ref[s : s + 1]
        d_streams.append(inverse * (scaled - column(n + s) - centered * column(n + 4 + s)))
    d_streams[3] = d_streams[3] + cot_ref[...].astype(F32)
    for j in range(HIST):
        total = column(j) * d_streams[0]
        for s in range(1, 4):
            total = total + column(s * HIST + j) * d_streams[s]
        if j == HIST - 1:
            total = total + jnp.dot(
                d_ref[...], w_ref[...], precision=HIGHEST, preferred_element_type=F32
            )
            total = total - current_ref[...].astype(F32) * column(n + 9)
        out_ref[j] = total


def history_gradient(grads, streams, stats, gain, cot, current, columns, d_scaled, w_rows):
    _, tokens, feats = streams.shape
    block = min(128, tokens)
    wide = pl.BlockSpec((block, feats), lambda i: (i, 0))
    narrow = lambda a: pl.BlockSpec((block, a.shape[1]), lambda i: (i, 0))
    fixed = lambda a: pl.BlockSpec(a.shape, lambda i: (0, 0))
    return pl.pallas_call(
        history_kernel,
        grid=(tokens // block,),
        in_specs=[wide] * 4
        + [
            pl.BlockSpec((4, block, feats), lambda i: (0, i, 0)),
            narrow(stats),
            fixed(gain),
            wide,
            wide,
            narrow(columns),
            narrow(d_scaled),
            fixed(w_rows),
        ],
        out_specs=pl.BlockSpec((HIST, block, feats), lambda i: (0, i, 0)),
        out_shape=jax.ShapeDtypeStruct((HIST, tokens, feats), F32),
        compiler_params=pltpu.CompilerParams(vmem_limit_bytes=40 * 1024 * 1024),
        cost_estimate=pl.CostEstimate(
            flops=110 * tokens * feats, bytes_accessed=64 * tokens * feats, transcendentals=0
        ),
        name="history_gradient",
    )(*grads, streams, stats, gain, cot, current, columns, d_scaled, w_rows)


def shards(
    history,
    seq_lens,
    bucket_slot,
    w_mix_in,
    w_mix_out,
    mix_bias,
    ln_gain,
    ln_bias,
    w_qkv,
    w_attn_out,
    w_up,
    w_down,
    cotangent,
):
    member = lax.axis_index("stream")
    micro, quarter, feats = history.shape[1:]
    tokens = micro * quarter
    model_width = feats * lax.axis_size("head")
    slot_base = lax.axis_index("dp") * micro
    slot_ids = jnp.arange(bucket_slot.shape[0], dtype=jnp.int32)
    query_places = member * quarter + jnp.arange(quarter, dtype=jnp.int32)
    w_mix_in_f = w_mix_in.astype(F32)
    w_mix_out_f = w_mix_out.astype(F32)

    segments, starts = [], []
    for index in range(micro):
        bucket = jnp.sum(jnp.where(slot_ids == slot_base + index, bucket_slot, 0))
        lengths = jnp.sum(jnp.where(slot_ids[:, None] == bucket, seq_lens, 0), axis=0)
        bounds = jnp.cumsum(lengths)
        passed = (query_places[:, None] >= bounds[None, :]).astype(jnp.int32)
        segments.append(jnp.sum(passed, axis=1))
        starts.append(jnp.sum(passed * lengths[None, :], axis=1))
    valid = (jnp.concatenate(segments) < 3).astype(F32)[:, None]
    starts = jnp.concatenate(starts)
    position = jnp.tile(query_places, micro) - starts
    frequency = jnp.arange(ROT // 2, dtype=F32)
    phases = position.astype(F32)[:, None] * (10000.0 ** (-2.0 * frequency / ROT))
    cosine, sine = jnp.cos(phases), jnp.sin(phases)
    plain = jnp.zeros((tokens, HD - ROT), F32)
    none = jnp.zeros_like(sine)
    tables = (
        jnp.concatenate([cosine, cosine, plain + 1.0], axis=1),
        jnp.concatenate([-sine, none, plain], axis=1),
        jnp.concatenate([none, sine, plain], axis=1),
    )

    cot_rows = cotangent.reshape(tokens, feats).astype(F32) * valid
    cot_bf = cot_rows.astype(BF16)
    w_both = jnp.concatenate([w_attn_out, w_down])
    duplex = lined()
    kv_near = swap_head(w_qkv[1:]) if duplex else w_qkv[:1]

    history = history.reshape(HIST, tokens, feats)
    current = history[HIST - 1]
    current_f = current.astype(F32)
    mixed = lax.dot_general(w_mix_in, current, (((0,), (1,)), ((), ())), preferred_element_type=F32)
    square = jnp.sum(current_f * current_f, axis=1)[None]
    mixed = head_sum(jnp.concatenate([mixed, square]), 0).T
    mixed, kv_near, cot_bf = lax.optimization_barrier((mixed, kv_near, cot_bf))
    out_full = lax.all_gather(cot_bf, "head", axis=1, tiled=True)
    if duplex:
        kv_near = jnp.stack([kv_near, over_x(kv_near)])
        kv_near = jnp.concatenate([kv_near, over_y(kv_near)])
    rms_scale = lax.rsqrt(mixed[:, 4 * HIST :] / model_width + EPSILON)
    mix_pre = mixed[:, : 4 * HIST] * rms_scale
    mix_hidden = gelu_exact(mix_pre)
    mix_weights = jnp.dot(mix_hidden, w_mix_out_f, precision=HIGHEST) + mix_bias.reshape(-1)
    streams, stats = mix_streams(mix_weights, history)
    stats = head_sum(stats[:, :8].T, 1)
    stat_sum, stat_square = stats[:4], stats[4:]
    early = early_sums(streams, cot_bf, history)
    stat_sum, stat_square, kv_near = lax.optimization_barrier((stat_sum, stat_square, kv_near))
    row_means = (stat_sum / model_width)[:, :, None]
    inv_std = lax.rsqrt(stat_square[:, :, None] / model_width - row_means * row_means + EPSILON)
    centered = (streams - row_means) * inv_std
    row_stats = jnp.concatenate([row_means[..., 0], inv_std[..., 0]]).T
    early = lax.psum(early[:, : 6 * HIST].T, "head")
    normed = (centered * ln_gain[:, None, :] + ln_bias[:, None, :]).astype(BF16)

    def all_features(stream):
        return lax.all_gather(normed[stream], "head", axis=1, tiled=True)

    if duplex:
        w_kv = row_weight(w_qkv[1:], kv_near)
        k_in, v_in = normed[1], normed[2]
        partials = [dot(k_in, w_kv[0]).astype(BF16), dot(v_in, w_kv[1]).astype(BF16)]
        partials, out_full = lax.optimization_barrier((partials, out_full))
        (key_pre, value_pre), (up_in, q_in), (wq, up_full, both_full) = exchange(
            partials,
            [normed[3], normed[0]],
            [w_qkv[0], w_up, w_both],
            (0, 0, 1),
            4,
        )
    else:
        wq, wk, wv = gather_weight(w_qkv, 1)
        both_full = gather_weight(w_both, 1)
        up_full = gather_weight(w_up, 0)
        k_in, v_in, q_in, up_in = (all_features(s) for s in (1, 2, 0, 3))
        key_pre, value_pre = dot(k_in, wk), dot(v_in, wv)
    w_out_full, down_full = both_full[:feats], both_full[feats:]

    keys = rotate(key_pre, tables, 1.0)
    values = value_pre.astype(BF16)
    queries = dot(q_in, wq)
    d_attended = dot_nt(out_full, w_out_full).astype(BF16) * valid.astype(BF16)
    by_micro = lambda a: a.reshape(micro, quarter, feats)
    key_blocks = exchange_rows(by_micro(keys))
    value_blocks = exchange_rows(by_micro(values))
    places = member ^ jnp.arange(4, dtype=jnp.int32)

    def to_owner(partial):
        return lax.psum_scatter(
            partial.astype(BF16), "head", scatter_dimension=1, tiled=True
        ).astype(F32)

    up_pre = dot(up_in, up_full)
    below = 0.5 * (1.0 + lax.erf(up_pre * 0.5**0.5))
    slope = below + up_pre * jnp.exp(-0.5 * up_pre * up_pre) * (2.0 * jnp.pi) ** -0.5
    gated_up, slope = lax.optimization_barrier(((up_pre * below).astype(BF16), slope))
    d_up = (dot_nt(out_full, down_full) * slope).astype(BF16)
    d_up_in = dot_nt(d_up, up_full).astype(BF16)
    queries, d_up, gated_up, d_up_in = lax.optimization_barrier((queries, d_up, gated_up, d_up_in))
    g_up = to_owner(d_up_in)

    results = attention(
        places,
        by_micro(queries),
        by_micro(d_attended),
        starts.reshape(micro, quarter, 1),
        valid.reshape(micro, quarter, 1),
        tuple(a.reshape(micro, quarter, HD) for a in tables),
        key_blocks,
        value_blocks,
    )
    attended, d_query_pre = results[0].reshape(tokens, feats), results[1].reshape(tokens, feats)
    d_keys = reduce_rows(results[2:6]).reshape(tokens, feats)
    d_values = reduce_rows(results[6:10]).reshape(tokens, feats)
    d_key_pre = rotate(d_keys, tables, -1.0)
    d_value_pre = d_values.astype(BF16)

    combined = dot(attended, w_out_full) + dot(gated_up, down_full)
    if duplex:
        partials = [dot_nt(d_query_pre, wq).astype(BF16), combined.astype(BF16)]
        (g_query, branch), (d_key_full, d_value_full), _ = exchange(
            partials, [d_key_pre, d_value_pre], [], (), 5
        )
        g_key, g_value = dot_nt(d_key_full, w_kv[0]), dot_nt(d_value_full, w_kv[1])
    else:
        g_query = to_owner(dot_nt(d_query_pre, wq))
        g_key = to_owner(dot_nt(d_key_pre, wk))
        g_value = to_owner(dot_nt(d_value_pre, wv))
        branch = to_owner(combined)
    block_out = (valid * (streams[3] + branch)).astype(BF16)

    product = lambda a, b: dot_tn(a, b).astype(BF16)
    up_terms = scatter_parts(product(up_in, d_up)[None])
    down_terms = scatter_parts(product(out_full, gated_up)[None])
    grad_up = add_terms(up_terms[0][0], up_terms[1][0], False)
    grad_down = add_terms(down_terms[0][0], down_terms[1][0], True)
    if duplex:
        by_head = lambda a, b: jnp.concatenate(
            [product(a, b[:, i * feats : (i + 1) * feats]) for i in range(4)]
        )
        terms = scatter_parts(
            jnp.stack([by_head(k_in, d_key_full), by_head(v_in, d_value_full)])
        )
        kv = swap_head((terms[0].astype(F32) + terms[1].astype(F32)).astype(BF16)).astype(F32)
        terms = scatter_parts(jnp.stack([product(q_in, d_query_pre), product(out_full, attended)]))
        grad_query = terms[0][:1].astype(F32) + terms[1][:1].astype(F32)
        grad_qkv = jnp.concatenate([grad_query, kv])
    else:
        terms = scatter_parts(
            jnp.stack(
                [
                    product(q_in, d_query_pre),
                    product(k_in, d_key_pre),
                    product(v_in, d_value_pre),
                    product(out_full, attended),
                ]
            )
        )
        grad_qkv = terms[0][:3].astype(F32) + terms[1][:3].astype(F32)
    grad_attn_out = add_terms(terms[0][-1], terms[1][-1], True)

    grads = (g_query, g_key, g_value, g_up)
    sums, gain_shift = gradient_sums(grads, streams, row_stats, ln_gain, history)
    sums = head_sum(sums.T, 3)
    d_mix, coefs = mix_gradient(sums, early, row_stats, model_width)
    d_hidden = jnp.dot(w_mix_out_f, d_mix, precision=HIGHEST)
    mix_pre_t = mix_pre.T
    below_mix = 0.5 * (1.0 + lax.erf(mix_pre_t * 0.5**0.5))
    density = jnp.exp(-0.5 * mix_pre_t * mix_pre_t) * (2.0 * jnp.pi) ** -0.5
    d_pre = d_hidden * (below_mix + mix_pre_t * density)
    cross = jnp.sum(d_pre * mix_pre_t, axis=0, keepdims=True)
    rms_row = rms_scale.T
    grad_w1 = jnp.dot(d_pre * rms_row, current_f, precision=HIGHEST)
    grad_w2 = jnp.dot(mix_hidden.T, d_mix.T, precision=HIGHEST)
    grad_bias = jnp.sum(d_mix, axis=1)
    wide = lambda a: jnp.pad(a, ((0, 0), (0, feats - a.shape[1])))
    small = jnp.concatenate([grad_w1, gain_shift, wide(grad_w2), wide(grad_bias[None])])
    small = plane_sum(small, 6)
    n = 4 * HIST
    columns = jnp.concatenate(
        [mix_weights.T, coefs, rms_row, rms_row * rms_row * cross / model_width]
    ).T
    history_grad = history_gradient(
        grads,
        streams,
        row_stats,
        ln_gain,
        cot_bf,
        current,
        columns,
        (d_pre * rms_row).T,
        w_mix_in_f.T,
    ).reshape(HIST, micro, quarter, feats)
    return (
        block_out.reshape(micro, quarter, feats),
        mix_weights.reshape(micro, quarter, 4 * HIST),
        history_grad,
        small[:n].T,
        small[n + 8 : 2 * n + 8, :n],
        small[2 * n + 8, :n].reshape(mix_bias.shape),
        small[n : n + 4],
        small[n + 4 : n + 8],
        grad_qkv,
        grad_attn_out,
        grad_up,
        grad_down,
    )


def solution(mesh):
    return jax.shard_map(
        shards,
        mesh=mesh,
        in_specs=(
            P(None, "dp", "stream", "head"),
            P(),
            P(),
            P("head", None),
            P(),
            P(),
            P(None, "head"),
            P(None, "head"),
            P(None, ("dp", "stream"), "head"),
            P("head", ("dp", "stream")),
            P(("dp", "stream"), "head"),
            P("head", ("dp", "stream")),
            P("dp", "stream", "head"),
        ),
        out_specs=(
            P("dp", "stream", "head"),
            P("dp", "stream", None),
            P(None, "dp", "stream", "head"),
            P("head", None),
            P(),
            P(),
            P(None, "head"),
            P(None, "head"),
            P(None, ("dp", "stream"), "head"),
            P("head", ("dp", "stream")),
            P(("dp", "stream"), "head"),
            P("head", ("dp", "stream")),
        ),
        check_vma=False,
    )
```

```python
import functools

import jax
import jax.numpy as jnp
from jax import lax
from jax.experimental import pallas as pl
from jax.experimental.pallas import tpu as pltpu
from jax.sharding import PartitionSpec as P

HD = 128
HIST = 9
ROT = 32

EPSILON = 1e-05
HIGHEST = lax.Precision.HIGHEST
MASKED = -1e30
F32 = jnp.float32
BF16 = jnp.bfloat16

SWAP_X = [(0, 1), (1, 0)]
SWAP_Y = [(0, 2), (2, 0), (1, 3), (3, 1)]
SWAP_CORE = [(0, 1), (1, 0), (2, 3), (3, 2)]


def dot(a, b):
    return jnp.dot(a, b, preferred_element_type=F32)


def dot_nt(a, b):
    return lax.dot_general(a, b, (((1,), (1,)), ((), ())), preferred_element_type=F32)


def dot_tn(a, b):
    return lax.dot_general(a, b, (((0,), (0,)), ((), ())), preferred_element_type=F32)


def gelu_exact(values_in):
    return jax.nn.gelu(values_in, approximate=False)


def over_x(a):
    return lax.ppermute(a, "dp", SWAP_X)


def over_y(a):
    return lax.ppermute(a, "stream", SWAP_Y)


def over_core(a):
    return lax.ppermute(a, "stream", SWAP_CORE)


def paired():
    return lax.axis_size("dp") == 2 and lax.axis_size("stream") == 4


def gather_weight(shard, axis):
    return lax.all_gather(shard, ("dp", "stream"), axis=axis, tiled=True)


def lined():
    return paired() and lax.axis_size("head") == 4


def take(a, index, axis):
    return lax.dynamic_index_in_dim(a, index, axis, keepdims=False)


def add_bf(a, b):
    return (a.astype(F32) + b.astype(F32)).astype(BF16)


def chip_parts(partial):
    count, rows, columns = partial.shape
    core, x = lax.axis_index("stream") % 2, lax.axis_index("dp")
    split = partial.reshape(count, 4, 2, rows // 8, columns)
    chip = add_bf(take(split, core, 2), over_core(take(split, 1 - core, 2)))
    chip = chip.reshape(count, 2, 2, rows // 8, columns)
    return take(chip, x, 1), take(chip, 1 - x, 1)


def plane_parts(stays, leaves):
    y = lax.axis_index("stream") // 2
    line = add_bf(stays, over_x(leaves))
    return take(line, y, 1), over_y(take(line, 1 - y, 1))


def scatter_parts(partial):
    if not paired():
        whole = lax.psum_scatter(partial, ("dp", "stream"), scatter_dimension=1, tiled=True)
        return whole, jnp.zeros_like(whole)
    return plane_parts(*chip_parts(partial))


def add_kernel(turned, a_ref, b_ref, out_ref):
    total = a_ref[...].astype(F32) + b_ref[...].astype(F32)
    out_ref[...] = total.T if turned else total


def add_terms(a, b, turned):
    rows, columns = a.shape
    block = min(512, columns)
    return pl.pallas_call(
        functools.partial(add_kernel, turned),
        grid=(columns // block,),
        in_specs=[pl.BlockSpec((rows, block), lambda i: (0, i))] * 2,
        out_specs=pl.BlockSpec((block, rows), lambda i: (i, 0))
        if turned
        else pl.BlockSpec((rows, block), lambda i: (0, i)),
        out_shape=jax.ShapeDtypeStruct((columns, rows) if turned else (rows, columns), F32),
        cost_estimate=pl.CostEstimate(
            flops=rows * columns, bytes_accessed=8 * rows * columns, transcendentals=0
        ),
        name="add_terms",
    )(a, b)


def exchange_kernel(units, whole, axes, *refs):
    count = len(axes)
    inputs, refs = refs[: units + whole + count], refs[units + whole + count :]
    partials, pieces, shard_refs = inputs[:units], inputs[units : units + whole], inputs[units + whole :]
    outputs, refs = refs[: units + whole + count], refs[units + whole + count :]
    outs, wides, fulls = outputs[:units], outputs[units : units + whole], outputs[units + whole :]
    held, got, load_sem, send_sem, recv_sem, own_sem, near_send, near_recv = refs[:8]
    piece_own, piece_send, piece_recv = refs[8:]
    x, stream, z = lax.axis_index("dp"), lax.axis_index("stream"), lax.axis_index("head")
    core = lax.rem(stream, 2)
    other_x, other_y, other_core = 1 - x, lax.rem(stream + 2, 4), stream + 1 - 2 * core
    line = ({"head": lax.rem(z + 1, 4)}, {"head": lax.rem(z + 3, 4)})
    to_x, to_y, to_core = {"dp": other_x}, {"stream": other_y}, {"stream": other_core}
    place = x * 4 + stream
    place_x, place_y = other_x * 4 + stream, x * 4 + other_y
    place_far = other_x * 4 + other_y
    beside = lambda at: at + 1 - 2 * core

    barrier = pltpu.get_barrier_semaphore()
    peers = (line if units else ()) + ((to_x, to_y, to_core) if count else ())
    for peer in peers:
        pl.semaphore_signal(barrier, inc=1, device_id=peer, device_id_type=pl.DeviceIdType.MESH)
    pl.semaphore_wait(barrier, len(peers))

    def region(w, at, part=None):
        full, width = fulls[w], shard_refs[w].shape[min(axes[w], 1)]
        rows, columns = shard_refs[w].shape
        start, size = (0, rows) if part is None else (part * (rows // 2), rows // 2)
        if axes[w] == 0:
            return full.at[pl.ds(pl.multiple_of(at * width + start, size), size)]
        column = at * width
        if axes[w] == 2:
            start = lax.rem(at, 2) * rows + start
            start, column = pl.multiple_of(start, size), lax.div(at, 2) * width
        return full.at[pl.ds(start, size), pl.ds(pl.multiple_of(column, width), width)]

    def near(w, index, source, target, peer):
        return pltpu.make_async_remote_copy(
            src_ref=source,
            dst_ref=target,
            send_sem=near_send.at[w, index],
            recv_sem=near_recv.at[w, index],
            device_id=peer,
            device_id_type=pl.DeviceIdType.MESH,
        )

    def pass_on(w, index, at, peer, part=None):
        return near(w, index, region(w, at, part), region(w, at, part), peer)

    def first(w):
        target = region(w, place)
        pltpu.make_async_copy(shard_refs[w], target, own_sem.at[w]).start()
        for index, peer in enumerate((to_x, to_y, to_core)):
            near(w, index, shard_refs[w], target, peer).start()

    def second(w):
        pass_on(w, 0, place_x, to_x).wait_recv()
        pass_on(w, 4, place_x, to_y, 0).start()
        pass_on(w, 3, place_x, to_core).start()
        pass_on(w, 1, place_y, to_y).wait_recv()
        pass_on(w, 6, place_y, to_x, 1).start()
        pass_on(w, 5, place_y, to_core).start()

    def third(w):
        pass_on(w, 4, place_far, to_y, 0).wait_recv()
        pass_on(w, 7, place_far, to_core, 0).start()
        pass_on(w, 6, place_far, to_x, 1).wait_recv()
        pass_on(w, 8, place_far, to_core, 1).start()

    def last(w):
        for index, at, part in (
            (2, place, None),
            (3, place_x, None),
            (5, place_y, None),
            (7, place_far, 0),
            (8, place_far, 1),
        ):
            pass_on(w, index, beside(at), to_core, part).wait_recv()
        pltpu.make_async_copy(shard_refs[w], region(w, place), own_sem.at[w]).wait()
        for index in (0, 1, 2):
            near(w, index, shard_refs[w], region(w, place), to_core).wait_send()
        for index, at, part in (
            (3, place_x, None),
            (4, place_x, 0),
            (5, place_y, None),
            (6, place_y, 1),
            (7, place_far, 0),
            (8, place_far, 1),
        ):
            pass_on(w, index, at, to_core, part).wait_send()

    feats = held.shape[-1]
    chunk = send_sem.shape[-1]
    step_rows = held.shape[2] // chunk

    def load(u, b):
        return pltpu.make_async_copy(
            partials[u].at[:, b * feats : (b + 1) * feats], held.at[u, b], load_sem.at[u, b]
        )

    for u in range(units):
        for b in range(4):
            load(u, b).start()
    for w in range(count):
        first(w)

    def columns(block):
        return pl.ds(pl.multiple_of(block * feats, feats), feats)

    def keep(v):
        return pltpu.make_async_copy(pieces[v], wides[v].at[:, columns(z)], piece_own.at[v])

    for v in range(whole):
        keep(v).start()
    for u in range(units):
        for b in range(4):
            load(u, b).wait()

    def part(c):
        return pl.ds(pl.multiple_of(c * step_rows, step_rows), step_rows)

    def hop(way, u, step, block, c):
        return pltpu.make_async_remote_copy(
            src_ref=held.at[u, block, part(c)],
            dst_ref=got.at[way, u, step, part(c)],
            send_sem=send_sem.at[way, u, step, c],
            recv_sem=recv_sem.at[way, u, step, c],
            device_id=line[way],
            device_id_type=pl.DeviceIdType.MESH,
        )

    ways = ((0, z), (1, 3 - z))

    def relay(way, v, step, block, c):
        target = wides[v].at[part(c), columns(block)]
        return pltpu.make_async_remote_copy(
            src_ref=pieces[v].at[part(c)] if step == 0 else target,
            dst_ref=target,
            send_sem=piece_send.at[way, v, step, c],
            recv_sem=piece_recv.at[way, v, step, c],
            device_id=line[way],
            device_id_type=pl.DeviceIdType.MESH,
        )

    def piece_at(way, step):
        return z - step if way == 0 else z + step

    def block_at(way, step):
        return 3 - step + z if way == 0 else step + z - 3

    def line_step(step):
        if not units:
            return

        def body(c, carry):
            for way, rank in ways:

                @pl.when(rank <= step)
                def _():
                    block = block_at(way, step)
                    for u in range(units):
                        if step > 0:

                            @pl.when(rank > 0)
                            def _():
                                hop(way, u, step - 1, block, c).wait_recv()
                                total = held[u, block, part(c)].astype(F32) + got[
                                    way, u, step - 1, part(c)
                                ].astype(F32)
                                held[u, block, part(c)] = total.astype(BF16)

                        hop(way, u, step, block, c).start()

                @pl.when((rank >= step) & (rank < 3))
                def _():
                    block = piece_at(way, step)
                    for v in range(whole):
                        if step > 0:
                            relay(way, v, step - 1, block, c).wait_recv()
                        relay(way, v, step, block, c).start()

            return carry

        lax.fori_loop(0, chunk, body, 0)

    line_step(0)
    for w in range(min(count, 2)):
        second(w)
    line_step(1)
    for w in range(2, count):
        second(w)
    line_step(2)
    for w in range(count):
        third(w)

    def finish(c, carry):
        for u in range(units):
            outs[u][part(c)] = held[u, z, part(c)].astype(F32)
            for way, rank in ways:

                @pl.when(rank > 0)
                def _():
                    hop(way, u, 2, z, c).wait_recv()
                    outs[u][part(c)] += got[way, u, 2, part(c)].astype(F32)

        for way, rank in ways:

            @pl.when(rank == 3)
            def _():
                for v in range(whole):
                    for step in range(3):
                        relay(way, v, step, piece_at(way, step + 1), c).wait_recv()

        return carry

    if units:
        lax.fori_loop(0, chunk, finish, 0)
    for w in range(count):
        last(w)

    def drain(c, carry):
        for step in range(3):
            for way, rank in ways:

                @pl.when(rank <= step)
                def _():
                    for u in range(units):
                        hop(way, u, step, block_at(way, step), c).wait_send()

                @pl.when((rank >= step) & (rank < 3))
                def _():
                    for v in range(whole):
                        relay(way, v, step, piece_at(way, step), c).wait_send()

        return carry

    if units:
        lax.fori_loop(0, chunk, drain, 0)
    for v in range(whole):
        keep(v).wait()


def exchange(partials, pieces, shards_in, axes, collective_id):
    units, whole, count = len(partials), len(pieces), len(shards_in)
    tokens, feats = (partials[0].shape[0], partials[0].shape[1] // 4) if units else (64, 128)
    chunk = 4
    grown = ((8, 1), (1, 8), (2, 4))
    full = [
        jax.ShapeDtypeStruct(tuple(n * k for n, k in zip(w.shape, grown[axis])), BF16)
        for w, axis in zip(shards_in, axes)
    ]
    anywhere = pl.BlockSpec(memory_space=pl.ANY)
    sems = pltpu.SemaphoreType.DMA
    results = pl.pallas_call(
        functools.partial(exchange_kernel, units, whole, axes),
        in_specs=[anywhere] * (units + whole + count),
        out_specs=[pl.BlockSpec(memory_space=pltpu.VMEM)] * units + [anywhere] * (whole + count),
        out_shape=[jax.ShapeDtypeStruct((tokens, feats), F32)] * units
        + [jax.ShapeDtypeStruct((tokens, 4 * feats), BF16)] * whole
        + full,
        scratch_shapes=[
            pltpu.VMEM((max(units, 1), 4, tokens, feats), BF16),
            pltpu.VMEM((2, max(units, 1), 3, tokens, feats), BF16),
            sems((max(units, 1), 4)),
            sems((2, max(units, 1), 3, chunk)),
            sems((2, max(units, 1), 3, chunk)),
            sems((max(count, 1),)),
            sems((max(count, 1), 9)),
            sems((max(count, 1), 9)),
            sems((max(whole, 1),)),
            sems((2, max(whole, 1), 3, chunk)),
            sems((2, max(whole, 1), 3, chunk)),
        ],
        compiler_params=pltpu.CompilerParams(
            collective_id=collective_id,
            has_side_effects=True,
            vmem_limit_bytes=48 * 1024 * 1024,
        ),
        cost_estimate=pl.CostEstimate(
            flops=0, bytes_accessed=(1 if units else 240) * 1024 * 1024, transcendentals=0
        ),
        name="exchange",
    )(*partials, *pieces, *shards_in)
    return results[:units], results[units : units + whole], results[units + whole :]


def head_sum_kernel(members, x_ref, out_ref, slots, send_sem, recv_sem):
    z = lax.axis_index("head")
    barrier = pltpu.get_barrier_semaphore()
    for k in range(1, members):
        pl.semaphore_signal(
            barrier,
            inc=1,
            device_id={"head": lax.rem(z + k, members)},
            device_id_type=pl.DeviceIdType.MESH,
        )
    pl.semaphore_wait(barrier, members - 1)
    copies = []
    for k in range(1, members):
        copy = pltpu.make_async_remote_copy(
            src_ref=x_ref,
            dst_ref=slots.at[z],
            send_sem=send_sem.at[k - 1],
            recv_sem=recv_sem.at[k - 1],
            device_id={"head": lax.rem(z + k, members)},
            device_id_type=pl.DeviceIdType.MESH,
        )
        copy.start()
        copies.append(copy)
    slots[z] = x_ref[...]
    for copy in copies:
        copy.wait()
    total = slots[0]
    for k in range(1, members):
        total = total + slots[k]
    out_ref[...] = total


def head_sum(x, collective_id):
    members = lax.axis_size("head")
    return pl.pallas_call(
        functools.partial(head_sum_kernel, members),
        out_shape=jax.ShapeDtypeStruct(x.shape, F32),
        in_specs=[pl.BlockSpec(memory_space=pltpu.VMEM)],
        out_specs=pl.BlockSpec(memory_space=pltpu.VMEM),
        scratch_shapes=[
            pltpu.VMEM((members,) + x.shape, F32),
            pltpu.SemaphoreType.DMA((members - 1,)),
            pltpu.SemaphoreType.DMA((members - 1,)),
        ],
        compiler_params=pltpu.CompilerParams(collective_id=collective_id, has_side_effects=True),
        name="sum_over_head",
    )(x)


def turn(v, keep, left, right):
    h = ROT // 2
    return v * keep + pltpu.roll(v, HD - h, 1) * left + pltpu.roll(v, h, 1) * right


def rotate_kernel(sign, v_ref, keep_ref, left_ref, right_ref, out_ref):
    for head in range(v_ref.shape[1] // HD):
        part = pl.ds(head * HD, HD)
        out_ref[:, part] = turn(
            v_ref[:, part], keep_ref[...], sign * left_ref[...], sign * right_ref[...]
        ).astype(BF16)


def rotate(values_in, tables, sign):
    tokens, feats = values_in.shape
    block = min(tokens, 256)
    table = pl.BlockSpec((block, HD), lambda i: (i, 0))
    wide = pl.BlockSpec((block, feats), lambda i: (i, 0))
    return pl.pallas_call(
        functools.partial(rotate_kernel, sign),
        grid=(tokens // block,),
        in_specs=[wide, table, table, table],
        out_specs=wide,
        out_shape=jax.ShapeDtypeStruct((tokens, feats), BF16),
        cost_estimate=pl.CostEstimate(
            flops=5 * tokens * feats, bytes_accessed=8 * tokens * feats, transcendentals=0
        ),
        name="rotate_heads",
    )(values_in, *tables)


def feed_kernel(x_ref, d_ref, up_ref, down_ref, gated_ref, d_up_ref, grad_up_ref, grad_down_ref):
    tokens, model_width = x_ref.shape
    step = min(256, tokens)
    for r in range(0, tokens, step):
        rows = slice(r, r + step)
        up_pre = dot(x_ref[rows], up_ref[...])
        d_gated = dot_nt(d_ref[rows], down_ref[...])
        below = 0.5 * (1.0 + lax.erf(up_pre * 0.5**0.5))
        density = jnp.exp(-0.5 * up_pre * up_pre) * (2.0 * jnp.pi) ** -0.5
        gated_ref[rows] = (up_pre * below).astype(BF16)
        d_up_ref[rows] = (d_gated * (below + up_pre * density)).astype(BF16)
    wide = min(512, model_width)
    for c in range(0, model_width, wide):
        part = slice(c, c + wide)
        grad_up_ref[part] = dot_tn(x_ref[:, part], d_up_ref[...]).astype(BF16)
        grad_down_ref[part] = dot_tn(d_ref[:, part], gated_ref[...]).astype(BF16)


def feed_forward(x, d_out, up, down):
    tokens, model_width = x.shape
    hidden = up.shape[1]
    block = min(512, hidden)
    fixed = pl.BlockSpec((tokens, model_width), lambda i: (0, 0), pipeline_mode=pl.Buffered(1))
    narrow = pl.BlockSpec((tokens, block), lambda i: (0, i))
    column = pl.BlockSpec((model_width, block), lambda i: (0, i))
    shape = lambda rows: jax.ShapeDtypeStruct((rows, hidden), BF16)
    return pl.pallas_call(
        feed_kernel,
        grid=(hidden // block,),
        in_specs=[fixed, fixed, column, pl.BlockSpec((block, model_width), lambda i: (i, 0))],
        out_specs=[narrow, narrow, column, column],
        out_shape=[shape(tokens), shape(tokens), shape(model_width), shape(model_width)],
        compiler_params=pltpu.CompilerParams(vmem_limit_bytes=56 * 1024 * 1024),
        cost_estimate=pl.CostEstimate(
            flops=8 * tokens * model_width * hidden,
            bytes_accessed=4 * model_width * (2 * hidden + tokens),
            transcendentals=0,
        ),
        name="feed_forward",
    )(x, d_out, up, down)


def attention_kernel(
    place_ref, q_ref, do_ref, start_ref, valid_ref, keep_ref, left_ref, right_ref, *refs
):
    blocks = (len(refs) - 6) // 2
    k_refs, v_refs = refs[:blocks], refs[blocks : 2 * blocks]
    o_ref, dq_ref, near_ref, beside_ref, s_ref, dp_ref = refs[2 * blocks :]
    grad_ref = lambda j: (beside_ref if j % 2 else near_ref).at[j // 2]
    rows = q_ref.shape[1]
    scale = HD ** (-0.5)
    member = place_ref[0]
    keep, left, right = keep_ref[0], left_ref[0], right_ref[0]
    q = turn(q_ref[0], keep, left, right).astype(BF16)
    d_out = do_ref[0]
    start = start_ref[0]
    top = jnp.full((rows, 1), MASKED, F32)
    t = member * rows + lax.broadcasted_iota(jnp.int32, (rows, rows), 0)
    for j in range(blocks):
        u = place_ref[j] * rows + lax.broadcasted_iota(jnp.int32, (rows, rows), 1)
        allowed = (u <= t) & (u >= start)
        s_ref[j] = jnp.where(allowed, dot_nt(q, k_refs[j][0]) * scale, MASKED)
        top = jnp.maximum(top, jnp.max(s_ref[j], axis=1, keepdims=True))
    total = jnp.zeros((rows, 1), F32)
    for j in range(blocks):
        e = jnp.exp(s_ref[j] - top)
        s_ref[j] = e
        total = total + jnp.sum(e, axis=1, keepdims=True)
    inverse = 1.0 / total
    out = jnp.zeros((rows, HD), F32)
    delta = jnp.zeros((rows, 1), F32)
    for j in range(blocks):
        p = s_ref[j] * inverse
        s_ref[j] = p
        p_bf = p.astype(BF16)
        out = out + dot(p_bf, v_refs[j][0])
        grad_ref(j)[1] = dot_tn(p_bf, d_out).astype(BF16)
        d_p = dot_nt(d_out, v_refs[j][0])
        dp_ref[j] = d_p
        delta = delta + jnp.sum(p * d_p, axis=1, keepdims=True)
    o_ref[0] = (out * valid_ref[0]).astype(BF16)
    d_q = jnp.zeros((rows, HD), F32)
    for j in range(blocks):
        d_s = (s_ref[j] * (dp_ref[j] - delta)).astype(BF16)
        d_q = d_q + dot(d_s, k_refs[j][0])
        grad_ref(j)[0] = (dot_tn(d_s, q) * scale).astype(BF16)
    dq_ref[0] = turn(d_q * scale, keep, -left, -right).astype(BF16)


def attention(index, places, queries, d_attended, starts, valid, tables, keys, values):
    _, rows, feats = queries.shape
    blocks = len(keys)
    tile = pl.BlockSpec((1, rows, HD), lambda h: (index, 0, h))
    fixed = lambda width: pl.BlockSpec((1, rows, width), lambda h: (index, 0, 0))
    out_tile = pl.BlockSpec((1, rows, HD), lambda h: (0, 0, h))
    grad_tile = pl.BlockSpec((blocks // 2, 2, rows, HD), lambda h: (0, 0, 0, h))
    shape = lambda *lead: jax.ShapeDtypeStruct(lead + (rows, feats), BF16)
    return pl.pallas_call(
        attention_kernel,
        grid=(feats // HD,),
        in_specs=[pl.BlockSpec(memory_space=pltpu.SMEM), tile, tile]
        + [fixed(1)] * 2
        + [fixed(HD)] * 3
        + [tile] * (2 * blocks),
        out_specs=[out_tile] * 2 + [grad_tile] * 2,
        out_shape=[shape(1)] * 2 + [shape(blocks // 2, 2)] * 2,
        scratch_shapes=[
            pltpu.VMEM((blocks, rows, rows), F32),
            pltpu.VMEM((blocks, rows, rows), F32),
        ],
        compiler_params=pltpu.CompilerParams(vmem_limit_bytes=40 * 1024 * 1024),
        cost_estimate=pl.CostEstimate(
            flops=0,
            bytes_accessed=1024,
            transcendentals=0,
        ),
        name="attention_both_ways",
    )(places, queries, d_attended, starts, valid, *tables, *keys, *values)


def exchange_rows(local):
    if lax.axis_size("stream") != 4:
        raise ValueError("stream")
    across = lax.ppermute(local, "stream", [(0, 2), (1, 3)])
    beside = over_core(local)
    return (local, beside, across, over_core(across))


def add_f32(a, b):
    return a.astype(F32) + b.astype(F32)


def over_line(a):
    return lax.ppermute(a, "stream", [(2, 0), (3, 1)])


def columns_of(pieces, rows):
    lane = lax.broadcasted_iota(jnp.int32, (rows, 128), 1)
    out = jnp.zeros((rows, 128), F32)
    for index, piece in enumerate(pieces):
        out = jnp.where(lane == index, piece, out)
    return out


def row_sum(a):
    return jnp.sum(a, axis=1, keepdims=True)


def streams_kernel(weights_ref, history_ref, streams_ref, stats_ref):
    weights = weights_ref[...]
    layers = [history_ref[j].astype(F32) for j in range(HIST)]
    sums, squares = [], []
    for s in range(4):
        total = weights[:, s * HIST : s * HIST + 1] * layers[0]
        for j in range(1, HIST):
            total = total + weights[:, s * HIST + j : s * HIST + j + 1] * layers[j]
        streams_ref[s] = total
        sums.append(row_sum(total))
        squares.append(row_sum(total * total))
    stats_ref[...] = columns_of(sums + squares, weights.shape[0]).T[:8]


def mix_streams(weights, history):
    _, tokens, feats = history.shape
    block = min(128, tokens)
    return pl.pallas_call(
        streams_kernel,
        grid=(tokens // block,),
        in_specs=[
            pl.BlockSpec((block, weights.shape[1]), lambda i: (i, 0)),
            pl.BlockSpec((HIST, block, feats), lambda i: (0, i, 0)),
        ],
        out_specs=[
            pl.BlockSpec((4, block, feats), lambda i: (0, i, 0)),
            pl.BlockSpec((8, block), lambda i: (0, i)),
        ],
        out_shape=[
            jax.ShapeDtypeStruct((4, tokens, feats), F32),
            jax.ShapeDtypeStruct((8, tokens), F32),
        ],
        compiler_params=pltpu.CompilerParams(vmem_limit_bytes=40 * 1024 * 1024),
        cost_estimate=pl.CostEstimate(
            flops=80 * tokens * feats, bytes_accessed=34 * tokens * feats, transcendentals=0
        ),
        name="mix_streams",
    )(weights, history)


def early_kernel(streams_ref, cot_ref, history_ref, out_ref):
    cot = cot_ref[...].astype(F32)
    plain, crossed, direct = [], [], []
    layers = [history_ref[j].astype(F32) for j in range(HIST)]
    for layer in layers:
        plain.append(row_sum(layer))
        direct.append(row_sum(cot * layer))
    for s in range(4):
        for layer in layers:
            crossed.append(row_sum(streams_ref[s] * layer))
    out_ref[...] = columns_of(crossed + plain + direct, cot.shape[0]).T[:56]


def early_sums(streams, cot, history):
    _, tokens, feats = streams.shape
    block = min(128, tokens)
    return pl.pallas_call(
        early_kernel,
        grid=(tokens // block,),
        in_specs=[
            pl.BlockSpec((4, block, feats), lambda i: (0, i, 0)),
            pl.BlockSpec((block, feats), lambda i: (i, 0)),
            pl.BlockSpec((HIST, block, feats), lambda i: (0, i, 0)),
        ],
        out_specs=pl.BlockSpec((56, block), lambda i: (0, i)),
        out_shape=jax.ShapeDtypeStruct((56, tokens), F32),
        compiler_params=pltpu.CompilerParams(vmem_limit_bytes=40 * 1024 * 1024),
        cost_estimate=pl.CostEstimate(
            flops=110 * tokens * feats, bytes_accessed=36 * tokens * feats, transcendentals=0
        ),
        name="early_sums",
    )(streams, cot, history)


def sums_kernel(g0, g1, g2, g3, streams_ref, stats_ref, gain_ref, history_ref, out_ref, edge_ref):
    stats = stats_ref[...]
    rows = stats.shape[0]

    @pl.when(pl.program_id(0) == 0)
    def _():
        edge_ref[...] = jnp.zeros_like(edge_ref)

    firsts, seconds, dots = [], [], []
    for s, g_ref in enumerate((g0, g1, g2, g3)):
        g = g_ref[...].astype(F32)
        centered = (streams_ref[s] - stats[:, s : s + 1]) * stats[:, 4 + s : 5 + s]
        edge_ref[s : s + 1] += jnp.sum(g * centered, axis=0, keepdims=True)
        edge_ref[4 + s : 5 + s] += jnp.sum(g, axis=0, keepdims=True)
        scaled = g * gain_ref[s : s + 1]
        firsts.append(row_sum(scaled))
        seconds.append(row_sum(scaled * centered))
        for j in range(HIST):
            dots.append(row_sum(scaled * history_ref[j].astype(F32)))
    out_ref[...] = columns_of(dots + firsts + seconds, rows).T[:48]


def gradient_sums(grads, streams, stats, gain, history):
    _, tokens, feats = streams.shape
    block = min(128, tokens)
    wide = pl.BlockSpec((block, feats), lambda i: (i, 0))
    return pl.pallas_call(
        sums_kernel,
        grid=(tokens // block,),
        in_specs=[wide] * 4
        + [
            pl.BlockSpec((4, block, feats), lambda i: (0, i, 0)),
            pl.BlockSpec((block, 8), lambda i: (i, 0)),
            pl.BlockSpec((4, feats), lambda i: (0, 0)),
            pl.BlockSpec((HIST, block, feats), lambda i: (0, i, 0)),
        ],
        out_specs=[
            pl.BlockSpec((48, block), lambda i: (0, i)),
            pl.BlockSpec((8, feats), lambda i: (0, 0)),
        ],
        out_shape=[
            jax.ShapeDtypeStruct((48, tokens), F32),
            jax.ShapeDtypeStruct((8, feats), F32),
        ],
        compiler_params=pltpu.CompilerParams(vmem_limit_bytes=40 * 1024 * 1024),
        cost_estimate=pl.CostEstimate(
            flops=110 * tokens * feats, bytes_accessed=42 * tokens * feats, transcendentals=0
        ),
        name="gradient_sums",
    )(*grads, streams, stats, gain, history)


def small_kernel(
    members,
    plane,
    sums_ref,
    early_ref,
    stats_ref,
    pre_ref,
    slope_ref,
    hidden_ref,
    rms_ref,
    w_ref,
    current_ref,
    edge_ref,
    small_ref,
    scaled_ref,
    coef_ref,
    slots,
    got,
    d_mix_ref,
    rows_ref,
    send_sem,
    recv_sem,
    plane_send,
    plane_recv,
):
    x, stream, z = lax.axis_index("dp"), lax.axis_index("stream"), lax.axis_index("head")
    line = [{"head": lax.rem(z + k, members)} for k in range(1, members)]
    near = (
        {"stream": stream + 1 - 2 * lax.rem(stream, 2)},
        {"stream": lax.rem(stream + 2, 4)},
        {"dp": 1 - x},
    )
    near = near if plane else ()
    barrier = pltpu.get_barrier_semaphore()
    for peer in line + list(near):
        pl.semaphore_signal(barrier, inc=1, device_id=peer, device_id_type=pl.DeviceIdType.MESH)
    pl.semaphore_wait(barrier, len(line) + len(near))
    copies = []
    for k, peer in enumerate(line):
        copy = pltpu.make_async_remote_copy(
            src_ref=sums_ref,
            dst_ref=slots.at[z],
            send_sem=send_sem.at[k],
            recv_sem=recv_sem.at[k],
            device_id=peer,
            device_id_type=pl.DeviceIdType.MESH,
        )
        copy.start()
        copies.append(copy)
    slots[z] = sums_ref[...]
    for copy in copies:
        copy.wait()
    total = slots[0]
    for k in range(1, members):
        total = total + slots[k]
    slots[0] = total
    n = 4 * HIST
    model_width = members * small_ref.shape[1]
    plain = early_ref[n : n + HIST]
    rows_ref[...] = jnp.zeros_like(rows_ref)
    rows_ref[0:8] = slots[0, n : n + 8] / model_width
    for s in range(4):
        part = slice(s * HIST, (s + 1) * HIST)
        mean, inverse = stats_ref[s : s + 1], stats_ref[4 + s : 5 + s]
        crossed = (early_ref[part] - mean * plain) * inverse
        d_part = inverse * (
            slots[0, part] - rows_ref[s : s + 1] * plain - rows_ref[4 + s : 5 + s] * crossed
        )
        if s == 3:
            d_part = d_part + early_ref[n + HIST : n + 2 * HIST]
        d_mix_ref[part] = d_part
    d_mix = d_mix_ref[...]
    high = dict(precision=HIGHEST, preferred_element_type=F32)
    d_pre = jnp.dot(w_ref[...], d_mix, **high) * slope_ref[...]
    rms = rms_ref[...]
    cross = jnp.sum(d_pre * pre_ref[...], axis=0, keepdims=True)
    rows_ref[8:9] = rms * rms * cross / model_width
    coef_ref[...] = rows_ref[...].T
    scaled = d_pre * rms
    scaled_ref[...] = scaled
    small_ref[...] = jnp.zeros_like(small_ref)
    small_ref[0:n] = jnp.dot(scaled, current_ref[...].astype(F32), **high)
    small_ref[n : n + 8] = edge_ref[...]
    small_ref[n + 8 : 2 * n + 8, 0:n] = lax.dot_general(
        hidden_ref[...], d_mix, (((1,), (1,)), ((), ())), **high
    )
    small_ref[n + 8 : 2 * n + 8, n : n + 1] = jnp.sum(d_mix, axis=1, keepdims=True)
    for step, peer in enumerate(near):
        copy = pltpu.make_async_remote_copy(
            src_ref=small_ref,
            dst_ref=got.at[step],
            send_sem=plane_send.at[step],
            recv_sem=plane_recv.at[step],
            device_id=peer,
            device_id_type=pl.DeviceIdType.MESH,
        )
        copy.start()
        copy.wait()
        small_ref[...] += got[step]


def small_gradients(sums, early, stats, pre, slope, hidden, rms, w_out, current, edges):
    members, plane = lax.axis_size("head"), paired()
    tokens, feats = current.shape
    n = 4 * HIST
    shape = jax.ShapeDtypeStruct
    sems = pltpu.SemaphoreType.DMA
    small, scaled, coefs = pl.pallas_call(
        functools.partial(small_kernel, members, plane),
        in_specs=[pl.BlockSpec(memory_space=pltpu.VMEM)] * 10,
        out_specs=[pl.BlockSpec(memory_space=pltpu.VMEM)] * 3,
        out_shape=[shape((80, feats), F32), shape((n, tokens), F32), shape((tokens, 128), F32)],
        scratch_shapes=[
            pltpu.VMEM((members, 48, tokens), F32),
            pltpu.VMEM((3, 80, feats), F32),
            pltpu.VMEM((n, tokens), F32),
            pltpu.VMEM((128, tokens), F32),
            sems((members - 1,)),
            sems((members - 1,)),
            sems((3,)),
            sems((3,)),
        ],
        compiler_params=pltpu.CompilerParams(
            collective_id=3, has_side_effects=True, vmem_limit_bytes=40 * 1024 * 1024
        ),
        name="small_gradients",
    )(sums, early, stats, pre, slope, hidden, rms, w_out, current, edges)
    if not plane:
        small = lax.psum(small.astype(BF16), ("dp", "stream")).astype(F32)
    return small, scaled, coefs


def history_kernel(
    g0, g1, g2, g3, streams_ref, stats_ref, gain_ref, cot_ref, current_ref, weights_ref, coef_ref, d_ref, w_ref, out_ref
):
    stats, weights, coefs = stats_ref[...], weights_ref[...], coef_ref[...]
    d_streams = []
    for s, g_ref in enumerate((g0, g1, g2, g3)):
        inverse = stats[:, 4 + s : 5 + s]
        centered = (streams_ref[s] - stats[:, s : s + 1]) * inverse
        scaled = g_ref[...].astype(F32) * gain_ref[s : s + 1]
        d_streams.append(
            inverse * (scaled - coefs[:, s : s + 1] - centered * coefs[:, 4 + s : 5 + s])
        )
    d_streams[3] = d_streams[3] + cot_ref[...].astype(F32)
    for j in range(HIST):
        total = weights[:, j : j + 1] * d_streams[0]
        for s in range(1, 4):
            total = total + weights[:, s * HIST + j : s * HIST + j + 1] * d_streams[s]
        if j == HIST - 1:
            total = total + lax.dot_general(
                d_ref[...],
                w_ref[...],
                (((0,), (0,)), ((), ())),
                precision=HIGHEST,
                preferred_element_type=F32,
            )
            total = total - current_ref[...].astype(F32) * coefs[:, 8:9]
        out_ref[j] = total


def history_gradient(grads, streams, stats, gain, cot, current, weights, coefs, d_scaled, w_rows):
    _, tokens, feats = streams.shape
    block = min(128, tokens)
    wide = pl.BlockSpec((block, feats), lambda i: (i, 0))
    narrow = lambda a: pl.BlockSpec((block, a.shape[1]), lambda i: (i, 0))
    fixed = lambda a: pl.BlockSpec(a.shape, lambda i: (0, 0))
    return pl.pallas_call(
        history_kernel,
        grid=(tokens // block,),
        in_specs=[wide] * 4
        + [
            pl.BlockSpec((4, block, feats), lambda i: (0, i, 0)),
            narrow(stats),
            fixed(gain),
            wide,
            wide,
            narrow(weights),
            narrow(coefs),
            pl.BlockSpec((d_scaled.shape[0], block), lambda i: (0, i)),
            fixed(w_rows),
        ],
        out_specs=pl.BlockSpec((HIST, block, feats), lambda i: (0, i, 0)),
        out_shape=jax.ShapeDtypeStruct((HIST, tokens, feats), F32),
        compiler_params=pltpu.CompilerParams(vmem_limit_bytes=40 * 1024 * 1024),
        cost_estimate=pl.CostEstimate(
            flops=110 * tokens * feats, bytes_accessed=64 * tokens * feats, transcendentals=0
        ),
        name="history_gradient",
    )(*grads, streams, stats, gain, cot, current, weights, coefs, d_scaled, w_rows)


def shards(
    history,
    seq_lens,
    bucket_slot,
    w_mix_in,
    w_mix_out,
    mix_bias,
    ln_gain,
    ln_bias,
    w_qkv,
    w_attn_out,
    w_up,
    w_down,
    cotangent,
):
    member = lax.axis_index("stream")
    micro, quarter, feats = history.shape[1:]
    tokens = micro * quarter
    model_width = feats * lax.axis_size("head")
    slot_base = lax.axis_index("dp") * micro
    slot_ids = jnp.arange(bucket_slot.shape[0], dtype=jnp.int32)
    query_places = member * quarter + jnp.arange(quarter, dtype=jnp.int32)
    w_mix_in_f = w_mix_in.astype(F32)
    w_mix_out_f = w_mix_out.astype(F32)

    segments, starts = [], []
    for index in range(micro):
        bucket = jnp.sum(jnp.where(slot_ids == slot_base + index, bucket_slot, 0))
        lengths = jnp.sum(jnp.where(slot_ids[:, None] == bucket, seq_lens, 0), axis=0)
        bounds = jnp.cumsum(lengths)
        passed = (query_places[:, None] >= bounds[None, :]).astype(jnp.int32)
        segments.append(jnp.sum(passed, axis=1))
        starts.append(jnp.sum(passed * lengths[None, :], axis=1))
    valid = (jnp.concatenate(segments) < 3).astype(F32)[:, None]
    starts = jnp.concatenate(starts)
    position = jnp.tile(query_places, micro) - starts
    frequency = jnp.arange(ROT // 2, dtype=F32)
    phases = position.astype(F32)[:, None] * (10000.0 ** (-2.0 * frequency / ROT))
    cosine, sine = jnp.cos(phases), jnp.sin(phases)
    plain = jnp.zeros((tokens, HD - ROT), F32)
    none = jnp.zeros_like(sine)
    tables = (
        jnp.concatenate([cosine, cosine, plain + 1.0], axis=1),
        jnp.concatenate([-sine, none, plain], axis=1),
        jnp.concatenate([none, sine, plain], axis=1),
    )

    cot_rows = cotangent.reshape(tokens, feats).astype(F32) * valid
    cot_bf = cot_rows.astype(BF16)
    duplex = lined()

    history = history.reshape(HIST, tokens, feats)
    current = history[HIST - 1]
    current_f = current.astype(F32)
    mixed = lax.dot_general(w_mix_in, current, (((0,), (1,)), ((), ())), preferred_element_type=F32)
    square = jnp.sum(current_f * current_f, axis=1)[None]
    mixed = head_sum(jnp.concatenate([mixed, square]), 0).T
    mixed, cot_bf, w_up = lax.optimization_barrier((mixed, cot_bf, w_up))
    out_full = lax.all_gather(cot_bf, "head", axis=1, tiled=True)
    if duplex:
        _, _, (up_full, wk) = exchange([], [], [w_up, w_qkv[1]], (0, 0), 4)
        mixed, up_full = lax.optimization_barrier((mixed, up_full))
    rms_scale = lax.rsqrt(mixed[:, 4 * HIST :] / model_width + EPSILON)
    mix_pre = mixed[:, : 4 * HIST] * rms_scale
    below_mix = 0.5 * (1.0 + lax.erf(mix_pre * 0.5**0.5))
    mix_hidden = gelu_exact(mix_pre)
    slope_mix = below_mix + mix_pre * jnp.exp(-0.5 * mix_pre * mix_pre) * (2.0 * jnp.pi) ** -0.5
    mix_weights = jnp.dot(mix_hidden, w_mix_out_f, precision=HIGHEST) + mix_bias.reshape(-1)
    streams, stats = mix_streams(mix_weights, history)
    stats = head_sum(stats, 1)
    stat_sum, stat_square = stats[:4], stats[4:]
    row_means = (stat_sum / model_width)[:, :, None]
    inv_std = lax.rsqrt(stat_square[:, :, None] / model_width - row_means * row_means + EPSILON)
    centered = (streams - row_means) * inv_std
    row_stats = jnp.concatenate([row_means[..., 0], inv_std[..., 0]]).T
    normed = (centered * ln_gain[:, None, :] + ln_bias[:, None, :]).astype(BF16)

    def all_features(a):
        return lax.all_gather(a, "head", axis=1, tiled=True)

    if duplex:
        w_down, normed = lax.optimization_barrier((w_down, normed))
        _, _, (down_full, w_out_full, wv, wq) = exchange(
            [], [], [w_down, w_attn_out, w_qkv[2], w_qkv[0]], (1, 1, 0, 0), 6
        )
    else:
        wq, wk, wv = gather_weight(w_qkv, 1)
        w_out_full, down_full = gather_weight(w_attn_out, 1), gather_weight(w_down, 1)
        up_full = gather_weight(w_up, 0)

    def to_owner(partial):
        return lax.psum_scatter(
            partial.astype(BF16), "head", scatter_dimension=1, tiled=True
        ).astype(F32)

    up_out, out_full = lax.optimization_barrier((normed[3], out_full))
    up_in, k_out, down_full = lax.optimization_barrier(
        (all_features(up_out), normed[1], down_full)
    )
    k_in, v_out = lax.optimization_barrier((all_features(k_out), normed[2]))
    gated_up, d_up, product_up, product_down = feed_forward(up_in, out_full, up_full, down_full)
    feed_products = [product_up[None], product_down[None]]
    feed_parts = [chip_parts(a) if paired() else a for a in feed_products]
    streams_late, v_out, d_up, feed_parts = lax.optimization_barrier(
        (streams, v_out, d_up, feed_parts)
    )
    early = head_sum(early_sums(streams_late, cot_bf, history), 2)
    v_in, q_out, early = lax.optimization_barrier((all_features(v_out), normed[0], early))
    key_pre, value_pre = dot(k_in, wk), dot(v_in, wv)
    d_up_in = dot_nt(d_up, up_full).astype(BF16)
    q_in, d_up_in = lax.optimization_barrier((all_features(q_out), d_up_in))
    g_up = to_owner(d_up_in)
    product = lambda a, b: dot_tn(a, b).astype(BF16)
    feed = dot(gated_up, down_full).astype(BF16)
    d_attended = dot_nt(out_full, w_out_full).astype(BF16) * valid.astype(BF16)
    feed_terms = [plane_parts(*a) if paired() else scatter_parts(a) for a in feed_parts]
    grad_up = add_terms(feed_terms[0][0][0], feed_terms[0][1][0], False)
    grad_down = add_terms(feed_terms[1][0][0], feed_terms[1][1][0], True)

    keys = rotate(key_pre, tables, 1.0)
    values = value_pre.astype(BF16)
    queries = dot(q_in, wq)
    if duplex:
        place = lax.axis_index("dp") * 4 + member
        own = lambda w: take(w.reshape(4, 8, feats // 8, feats), place, 1)
        shares = lax.all_to_all(jnp.stack([own(wk), own(wv)], axis=1), "head", 0, 0)
        shares = [shares[:, i].transpose(1, 0, 2).reshape(feats // 8, 4 * feats) for i in range(2)]
        queries, feed, d_attended, grad_up, grad_down, early, shares = lax.optimization_barrier(
            (queries, feed, d_attended, grad_up, grad_down, early, shares)
        )
    by_micro = lambda a: a.reshape((micro, quarter) + a.shape[1:])
    key_blocks = exchange_rows(by_micro(keys))
    value_blocks = exchange_rows(by_micro(values))
    places = member ^ jnp.arange(4, dtype=jnp.int32)
    attended, d_query_pre, d_rows = [], [], []
    queries = by_micro(queries)
    for index in range(micro):
        results = attention(
            index,
            places,
            queries,
            by_micro(d_attended),
            by_micro(starts[:, None]),
            by_micro(valid),
            tuple(by_micro(a) for a in tables),
            key_blocks,
            value_blocks,
        )
        attended.append(results[0][0])
        d_query_pre.append(results[1][0])
        chip = add_f32(results[2], over_core(results[3]))
        across = chip[1].astype(BF16)
        queries, across = lax.optimization_barrier((queries, across))
        d_rows.append(add_f32(chip[0], over_line(across)))
    attended, d_query_pre = jnp.concatenate(attended), jnp.concatenate(d_query_pre)
    d_key_pre = rotate(jnp.concatenate([a[0] for a in d_rows]), tables, -1.0)
    d_value_pre = jnp.concatenate([a[1] for a in d_rows]).astype(BF16)

    combined = dot(attended, w_out_full) + feed
    products = jnp.stack([product(q_in, d_query_pre), product(out_full, attended)])
    if duplex:
        partials = [dot_nt(d_query_pre, wq).astype(BF16), combined.astype(BF16)]
        parts = chip_parts(products)
        kv = jnp.stack([product(k_in, d_key_pre), product(v_in, d_value_pre)])
        partials, parts, kv, g_up = lax.optimization_barrier((partials, parts, kv, g_up))
        (g_query, branch), (d_key_full, d_value_full), (wk_rows, wv_rows) = exchange(
            partials, [d_key_pre, d_value_pre], shares, (0, 0), 5
        )
        g_key, g_value = dot_nt(d_key_full, wk_rows), dot_nt(d_value_full, wv_rows)
        kv_terms = scatter_parts(kv)
        terms = plane_parts(*parts)
    else:
        g_query = to_owner(dot_nt(d_query_pre, wq))
        g_key = to_owner(dot_nt(d_key_pre, wk))
        g_value = to_owner(dot_nt(d_value_pre, wv))
        branch = to_owner(combined)
        terms = scatter_parts(products)
        kv_terms = scatter_parts(
            jnp.stack([product(k_in, d_key_pre), product(v_in, d_value_pre)])
        )
    block_out = (valid * (streams[3] + branch)).astype(BF16)
    grad_query = terms[0][:1].astype(F32) + terms[1][:1].astype(F32)
    grad_attn_out = add_terms(terms[0][1], terms[1][1], True)

    grads = (g_query, g_key, g_value, g_up)
    sums, edges = gradient_sums(grads, streams, row_stats, ln_gain, history)
    small, d_scaled, coefs = small_gradients(
        sums, early, row_stats.T, mix_pre.T, slope_mix.T, mix_hidden.T, rms_scale.T, w_mix_out_f, current, edges
    )
    history_grad = history_gradient(
        grads, streams, row_stats, ln_gain, cot_bf, current, mix_weights, coefs, d_scaled, w_mix_in_f.T
    ).reshape(HIST, micro, quarter, feats)
    grad_qkv = jnp.concatenate([grad_query, kv_terms[0].astype(F32) + kv_terms[1].astype(F32)])
    n = 4 * HIST
    return (
        block_out.reshape(micro, quarter, feats),
        mix_weights.reshape(micro, quarter, 4 * HIST),
        history_grad,
        small[:n].T,
        small[n + 8 : 2 * n + 8, :n],
        small[n + 8 : 2 * n + 8, n].reshape(mix_bias.shape),
        small[n : n + 4],
        small[n + 4 : n + 8],
        grad_qkv,
        grad_attn_out,
        grad_up,
        grad_down,
    )


def solution(mesh):
    return jax.shard_map(
        shards,
        mesh=mesh,
        in_specs=(
            P(None, "dp", "stream", "head"),
            P(),
            P(),
            P("head", None),
            P(),
            P(),
            P(None, "head"),
            P(None, "head"),
            P(None, ("dp", "stream"), "head"),
            P("head", ("dp", "stream")),
            P(("dp", "stream"), "head"),
            P("head", ("dp", "stream")),
            P("dp", "stream", "head"),
        ),
        out_specs=(
            P("dp", "stream", "head"),
            P("dp", "stream", None),
            P(None, "dp", "stream", "head"),
            P("head", None),
            P(),
            P(),
            P(None, "head"),
            P(None, "head"),
            P(None, ("dp", "stream"), "head"),
            P("head", ("dp", "stream")),
            P(("dp", "stream"), "head"),
            P("head", ("dp", "stream")),
        ),
        check_vma=False,
    )
```

```python
import functools

import jax
import jax.numpy as jnp
from jax import lax
from jax.experimental import pallas as pl
from jax.experimental.pallas import tpu as pltpu
from jax.sharding import PartitionSpec as P

HD = 128
HIST = 9
ROT = 32

EPSILON = 1e-05
HIGHEST = lax.Precision.HIGHEST
MASKED = -1e30
F32 = jnp.float32
BF16 = jnp.bfloat16

SWAP_X = [(0, 1), (1, 0)]
SWAP_Y = [(0, 2), (2, 0), (1, 3), (3, 1)]
SWAP_CORE = [(0, 1), (1, 0), (2, 3), (3, 2)]


def dot(a, b):
    return jnp.dot(a, b, preferred_element_type=F32)


def dot_nt(a, b):
    return lax.dot_general(a, b, (((1,), (1,)), ((), ())), preferred_element_type=F32)


def dot_tn(a, b):
    return lax.dot_general(a, b, (((0,), (0,)), ((), ())), preferred_element_type=F32)


def gelu_exact(values_in):
    return jax.nn.gelu(values_in, approximate=False)


def over_x(a):
    return lax.ppermute(a, "dp", SWAP_X)


def over_y(a):
    return lax.ppermute(a, "stream", SWAP_Y)


def over_core(a):
    return lax.ppermute(a, "stream", SWAP_CORE)


def paired():
    return lax.axis_size("dp") == 2 and lax.axis_size("stream") == 4


def gather_weight(shard, axis):
    return lax.all_gather(shard, ("dp", "stream"), axis=axis, tiled=True)


def lined():
    return paired() and lax.axis_size("head") == 4


def take(a, index, axis):
    return lax.dynamic_index_in_dim(a, index, axis, keepdims=False)


def add_bf(a, b):
    return (a.astype(F32) + b.astype(F32)).astype(BF16)


def chip_parts(partial):
    count, rows, columns = partial.shape
    core, x = lax.axis_index("stream") % 2, lax.axis_index("dp")
    split = partial.reshape(count, 4, 2, rows // 8, columns)
    chip = add_bf(take(split, core, 2), over_core(take(split, 1 - core, 2)))
    chip = chip.reshape(count, 2, 2, rows // 8, columns)
    return take(chip, x, 1), take(chip, 1 - x, 1)


def line_parts(stays, leaves):
    return add_bf(stays, over_x(leaves))


def last_parts(line):
    y = lax.axis_index("stream") // 2
    return take(line, y, 1), over_y(take(line, 1 - y, 1))


def plane_parts(stays, leaves):
    return last_parts(line_parts(stays, leaves))


def scatter_parts(partial):
    if not paired():
        whole = lax.psum_scatter(partial, ("dp", "stream"), scatter_dimension=1, tiled=True)
        return whole, jnp.zeros_like(whole)
    return plane_parts(*chip_parts(partial))


def add_kernel(turned, a_ref, b_ref, out_ref):
    total = a_ref[...].astype(F32) + b_ref[...].astype(F32)
    out_ref[...] = total.T if turned else total


def add_terms(a, b, turned):
    rows, columns = a.shape
    block = min(512, columns)
    return pl.pallas_call(
        functools.partial(add_kernel, turned),
        grid=(columns // block,),
        in_specs=[pl.BlockSpec((rows, block), lambda i: (0, i))] * 2,
        out_specs=pl.BlockSpec((block, rows), lambda i: (i, 0))
        if turned
        else pl.BlockSpec((rows, block), lambda i: (0, i)),
        out_shape=jax.ShapeDtypeStruct((columns, rows) if turned else (rows, columns), F32),
        cost_estimate=pl.CostEstimate(
            flops=rows * columns, bytes_accessed=8 * rows * columns, transcendentals=0
        ),
        name="add_terms",
    )(a, b)


def exchange_kernel(units, spread, axes, *refs):
    count, whole = len(axes), 2 if units else 0
    inputs, refs = refs[: units + count], refs[units + count :]
    partials, shard_refs = inputs[:units], inputs[units:]
    if units:
        done_in, near_in, beside_in = refs[:2], refs[2], refs[3]
        keep_ref, left_ref, right_ref = refs[4:7]
        refs = refs[7:]
    outputs, refs = refs[: units + whole + count], refs[units + whole + count :]
    outs, wides, fulls = outputs[:units], outputs[units : units + whole], outputs[units + whole :]
    shares, refs = refs[:spread], refs[spread:]
    own_sem, near_send, near_recv = refs[:3]
    if units:
        held, got, load_sem, send_sem, recv_sem = refs[3:8]
        mine, theirs, below, pieces, piece_own, piece_send, piece_recv = refs[8:15]
        mine_sem, done_sem, core_send, core_recv, y_send, y_recv = refs[15:]
    x, stream, z = lax.axis_index("dp"), lax.axis_index("stream"), lax.axis_index("head")
    core = lax.rem(stream, 2)
    other_x, other_y, other_core = 1 - x, lax.rem(stream + 2, 4), stream + 1 - 2 * core
    line = ({"head": lax.rem(z + 1, 4)}, {"head": lax.rem(z + 3, 4)})
    to_x, to_y, to_core = {"dp": other_x}, {"stream": other_y}, {"stream": other_core}
    place = x * 4 + stream
    place_x, place_y = other_x * 4 + stream, x * 4 + other_y
    place_far = other_x * 4 + other_y
    beside = lambda at: at + 1 - 2 * core

    barrier = pltpu.get_barrier_semaphore()
    peers = (line if units or spread else ()) + ((to_x, to_y, to_core) if count else ())
    peers = peers + (({"head": lax.rem(z + 2, 4)},) if spread else ())
    for peer in peers:
        pl.semaphore_signal(barrier, inc=1, device_id=peer, device_id_type=pl.DeviceIdType.MESH)
    pl.semaphore_wait(barrier, len(peers))

    def region(w, at, part=None):
        full, width = fulls[w], shard_refs[w].shape[min(axes[w], 1)]
        rows, columns = shard_refs[w].shape
        start, size = (0, rows) if part is None else (part * (rows // 2), rows // 2)
        if axes[w] == 0:
            return full.at[pl.ds(pl.multiple_of(at * width + start, size), size)]
        column = at * width
        if axes[w] == 2:
            start = lax.rem(at, 2) * rows + start
            start, column = pl.multiple_of(start, size), lax.div(at, 2) * width
        return full.at[pl.ds(start, size), pl.ds(pl.multiple_of(column, width), width)]

    def near(w, index, source, target, peer):
        return pltpu.make_async_remote_copy(
            src_ref=source,
            dst_ref=target,
            send_sem=near_send.at[w, index],
            recv_sem=near_recv.at[w, index],
            device_id=peer,
            device_id_type=pl.DeviceIdType.MESH,
        )

    def pass_on(w, index, at, peer, part=None):
        return near(w, index, region(w, at, part), region(w, at, part), peer)

    def first(w):
        target = region(w, place)
        pltpu.make_async_copy(shard_refs[w], target, own_sem.at[w]).start()
        for index, peer in enumerate((to_x, to_y, to_core)):
            near(w, index, shard_refs[w], target, peer).start()

    def second(w):
        pass_on(w, 0, place_x, to_x).wait_recv()
        pass_on(w, 4, place_x, to_y, 0).start()
        pass_on(w, 3, place_x, to_core).start()
        pass_on(w, 1, place_y, to_y).wait_recv()
        pass_on(w, 6, place_y, to_x, 1).start()
        pass_on(w, 5, place_y, to_core).start()

    def third(w):
        pass_on(w, 4, place_far, to_y, 0).wait_recv()
        pass_on(w, 7, place_far, to_core, 0).start()
        pass_on(w, 6, place_far, to_x, 1).wait_recv()
        pass_on(w, 8, place_far, to_core, 1).start()

    def last(w):
        for index, at, part in (
            (2, place, None),
            (3, place_x, None),
            (5, place_y, None),
            (7, place_far, 0),
            (8, place_far, 1),
        ):
            pass_on(w, index, beside(at), to_core, part).wait_recv()
        pltpu.make_async_copy(shard_refs[w], region(w, place), own_sem.at[w]).wait()
        for index in (0, 1, 2):
            near(w, index, shard_refs[w], region(w, place), to_core).wait_send()
        for index, at, part in (
            (3, place_x, None),
            (4, place_x, 0),
            (5, place_y, None),
            (6, place_y, 1),
            (7, place_far, 0),
            (8, place_far, 1),
        ):
            pass_on(w, index, at, to_core, part).wait_send()

    for w in range(count):
        first(w)
    if not units:
        moves = []
        for i in range(spread):
            second(i)
        for i in range(spread):
            third(i)
        for i in range(spread):
            last(i)
            spread_own, spread_send, spread_recv = refs[3:6]
            rows, columns = shares[i].shape[0], fulls[i].shape[1]
            target = shares[i].at[:, pl.ds(pl.multiple_of(z * columns, columns), columns)]

            def source(at):
                start = (at * 8 + place) * rows
                return fulls[i].at[pl.ds(pl.multiple_of(start, rows), rows)]

            moves.append(pltpu.make_async_copy(source(z), target, spread_own.at[i]))
            for k in range(1, 4):
                to = lax.rem(z + k, 4)
                moves.append(
                    pltpu.make_async_remote_copy(
                        src_ref=source(to),
                        dst_ref=target,
                        send_sem=spread_send.at[i, k - 1],
                        recv_sem=spread_recv.at[i, k - 1],
                        device_id={"head": to},
                        device_id_type=pl.DeviceIdType.MESH,
                    )
                )
        for move in moves:
            move.start()
        for w in range(spread, count):
            second(w)
        for w in range(spread, count):
            third(w)
        for w in range(spread, count):
            last(w)
        for move in moves:
            move.wait()
        return

    feats = held.shape[-1]
    chunk = send_sem.shape[-1]
    tokens = held.shape[2]
    step_rows = tokens // chunk
    y = lax.div(stream, 2)

    def load(u, b):
        return pltpu.make_async_copy(
            partials[u].at[:, b * feats : (b + 1) * feats], held.at[u, b], load_sem.at[u, b]
        )

    def to_beside(v):
        return pltpu.make_async_remote_copy(
            src_ref=beside_in.at[:, v],
            dst_ref=theirs.at[v],
            send_sem=core_send.at[v],
            recv_sem=core_recv.at[v],
            device_id=to_core,
            device_id_type=pl.DeviceIdType.MESH,
        )

    def load_done(v):
        return pltpu.make_async_copy(
            done_in[v], pieces.at[v, pl.ds(0, done_in[v].shape[0])], done_sem.at[v]
        )

    def load_mine(v):
        return pltpu.make_async_copy(near_in.at[:, v], mine.at[v], mine_sem.at[v])

    def to_below(v):
        return pltpu.make_async_remote_copy(
            src_ref=mine.at[v, 1],
            dst_ref=below.at[v],
            send_sem=y_send.at[v],
            recv_sem=y_recv.at[v],
            device_id=to_y,
            device_id_type=pl.DeviceIdType.MESH,
        )

    for v in range(2):
        to_beside(v).start()
        load_mine(v).start()
        load_done(v).start()
    for u in range(units):
        for b in range(4):
            load(u, b).start()
    for u in range(units):
        for b in range(4):
            load(u, b).wait()

    def columns(block):
        return pl.ds(pl.multiple_of(block * feats, feats), feats)

    def part(c):
        return pl.ds(pl.multiple_of(c * step_rows, step_rows), step_rows)

    def hop(way, u, step, block, c):
        return pltpu.make_async_remote_copy(
            src_ref=held.at[u, block, part(c)],
            dst_ref=got.at[way, u, step, part(c)],
            send_sem=send_sem.at[way, u, step, c],
            recv_sem=recv_sem.at[way, u, step, c],
            device_id=line[way],
            device_id_type=pl.DeviceIdType.MESH,
        )

    ways = ((0, z), (1, 3 - z))

    def relay(way, v, step, block, c):
        target = wides[v].at[part(c), columns(block)]
        return pltpu.make_async_remote_copy(
            src_ref=pieces.at[v, part(c)] if step == 0 else target,
            dst_ref=target,
            send_sem=piece_send.at[way, v, step, c],
            recv_sem=piece_recv.at[way, v, step, c],
            device_id=line[way],
            device_id_type=pl.DeviceIdType.MESH,
        )

    def piece_at(way, step):
        return z - step if way == 0 else z + step

    def block_at(way, step):
        return 3 - step + z if way == 0 else step + z - 3

    def keep(v):
        return pltpu.make_async_copy(pieces.at[v], wides[v].at[:, columns(z)], piece_own.at[v])

    def over_parts(body, start=0, stop=None):
        def step(c, carry):
            body(c)
            return carry

        lax.fori_loop(start, chunk if stop is None else stop, step, 0)

    ready = done_in[0].shape[0] // step_rows
    early, late = (0, ready), (ready, chunk)

    def sum_step(step):
        def body(c):
            for way, rank in ways:

                @pl.when(rank <= step)
                def _():
                    block = block_at(way, step)
                    for u in range(units):
                        if step > 0:

                            @pl.when(rank > 0)
                            def _():
                                hop(way, u, step - 1, block, c).wait_recv()
                                total = held[u, block, part(c)].astype(F32) + got[
                                    way, u, step - 1, part(c)
                                ].astype(F32)
                                held[u, block, part(c)] = total.astype(BF16)

                        hop(way, u, step, block, c).start()

        over_parts(body)

    def gather_step(v, step, span):
        def body(c):
            for way, rank in ways:

                @pl.when((rank >= step) & (rank < 3))
                def _():
                    block = piece_at(way, step)
                    if step > 0:
                        relay(way, v, step - 1, block, c).wait_recv()
                    relay(way, v, step, block, c).start()

        over_parts(body, *span)

    def chip_sum(v):
        load_mine(v).wait()
        to_beside(v).wait()

        @pl.when(y == 1)
        def _():
            def body(c):
                total = mine[v, 1, part(c)].astype(F32) + theirs[v, 1, part(c)].astype(F32)
                mine[v, 1, part(c)] = total.astype(BF16)

            over_parts(body, 0, chunk - ready)
            to_below(v).start()

    def bring(v):
        def body(c, from_y):
            rows, out = part(c), part(c + ready)
            total = mine[v, 0, rows].astype(F32) + theirs[v, 0, rows].astype(F32)
            if from_y:
                total = total + below[v, rows].astype(F32)
            if v == 1:
                pieces[v, out] = total.astype(BF16)
            else:
                for head in range(feats // HD):
                    lanes = slice(head * HD, (head + 1) * HD)
                    pieces[v, out, lanes] = turn(
                        total[:, lanes], keep_ref[rows], -left_ref[rows], -right_ref[rows]
                    ).astype(BF16)

        @pl.when(y == 0)
        def _():
            to_below(v).wait_recv()
            over_parts(lambda c: body(c, True), 0, chunk - ready)

        @pl.when(y == 1)
        def _():
            over_parts(lambda c: body(c, False), 0, chunk - ready)

        keep(v).start()

    sum_step(0)
    for v in range(whole):
        load_done(v).wait()
        gather_step(v, 0, early)
    for v in range(whole):
        chip_sum(v)
    for w in range(count):
        second(w)
    for v in range(whole):
        bring(v)
        gather_step(v, 0, late)
    sum_step(1)
    for v in range(whole):
        gather_step(v, 1, early)
    for w in range(count):
        third(w)
    for v in range(whole):
        gather_step(v, 1, late)
    sum_step(2)
    for v in range(whole):
        gather_step(v, 2, early)

    def finish(c):
        for u in range(units):
            outs[u][part(c)] = held[u, z, part(c)].astype(F32)
            for way, rank in ways:

                @pl.when(rank > 0)
                def _():
                    hop(way, u, 2, z, c).wait_recv()
                    outs[u][part(c)] += got[way, u, 2, part(c)].astype(F32)

    for v in range(whole):
        gather_step(v, 2, late)
    over_parts(finish)
    for w in range(count):
        last(w)

    def drain(c):
        for way, rank in ways:

            @pl.when(rank == 3)
            def _():
                for v in range(whole):
                    for step in range(3):
                        relay(way, v, step, piece_at(way, step + 1), c).wait_recv()

        for step in range(3):
            for way, rank in ways:

                @pl.when(rank <= step)
                def _():
                    for u in range(units):
                        hop(way, u, step, block_at(way, step), c).wait_send()

                @pl.when((rank >= step) & (rank < 3))
                def _():
                    for v in range(whole):
                        relay(way, v, step, piece_at(way, step), c).wait_send()

    over_parts(drain)
    for v in range(whole):
        keep(v).wait()

        @pl.when(y == 1)
        def _():
            to_below(v).wait_send()


def exchange(partials, rows, shards_in, axes, collective_id, spread=0):
    units, count = len(partials), len(shards_in)
    grown = ((8, 1), (1, 8), (2, 4))
    shape = jax.ShapeDtypeStruct
    full = [
        shape(tuple(n * k for n, k in zip(w.shape, grown[axis])), BF16)
        for w, axis in zip(shards_in, axes)
    ]
    anywhere, local = pl.BlockSpec(memory_space=pl.ANY), pl.BlockSpec(memory_space=pltpu.VMEM)
    sems = pltpu.SemaphoreType.DMA
    out_specs, out_shape = [anywhere] * count, full
    in_specs = [anywhere] * (units + count)
    scratch = [sems((count,)), sems((count, 9)), sems((count, 9))]
    if units:
        tokens, feats = partials[0].shape[0], partials[0].shape[1] // 4
        chunk = 4
        in_specs = in_specs + [anywhere] * 4 + [local] * 3
        last = rows[2].shape[2]
        out_specs = [local] * units + [anywhere] * 2 + out_specs
        out_shape = (
            [shape((tokens, feats), F32)] * units + [shape((tokens, 4 * feats), BF16)] * 2 + out_shape
        )
        scratch = scratch + [
            pltpu.VMEM((units, 4, tokens, feats), BF16),
            pltpu.VMEM((2, units, 3, tokens, feats), BF16),
            sems((units, 4)),
            sems((2, units, 3, chunk)),
            sems((2, units, 3, chunk)),
            pltpu.VMEM((2, 2, last, feats), BF16),
            pltpu.VMEM((2, 2, last, feats), BF16),
            pltpu.VMEM((2, last, feats), BF16),
            pltpu.VMEM((2, tokens, feats), BF16),
            sems((2,)),
            sems((2, 2, 3, chunk)),
            sems((2, 2, 3, chunk)),
            sems((2,)),
            sems((2,)),
            sems((2,)),
            sems((2,)),
            sems((2,)),
            sems((2,)),
        ]
    if spread:
        out_specs = out_specs + [anywhere] * spread
        out_shape = out_shape + [
            shape((w.shape[0] // 4, w.shape[1] * 4), BF16) for w in shards_in[:spread]
        ]
        scratch = scratch + [sems((spread,))] + [sems((spread, 3))] * 2
    results = pl.pallas_call(
        functools.partial(exchange_kernel, units, spread, axes),
        in_specs=in_specs,
        out_specs=out_specs,
        out_shape=out_shape,
        scratch_shapes=scratch,
        compiler_params=pltpu.CompilerParams(
            collective_id=collective_id,
            has_side_effects=True,
            vmem_limit_bytes=(56 if units else 8) * 1024 * 1024,
        ),
        cost_estimate=pl.CostEstimate(
            flops=0, bytes_accessed=(600 if units else 240) * 1024 * 1024, transcendentals=0
        ),
        name="exchange",
    )(*partials, *shards_in, *rows)
    if not units:
        return results
    return results[:units], results[units : len(results) - count], results[len(results) - count :]


def head_sum_kernel(members, x_ref, out_ref, slots, send_sem, recv_sem):
    z = lax.axis_index("head")
    barrier = pltpu.get_barrier_semaphore()
    for k in range(1, members):
        pl.semaphore_signal(
            barrier,
            inc=1,
            device_id={"head": lax.rem(z + k, members)},
            device_id_type=pl.DeviceIdType.MESH,
        )
    pl.semaphore_wait(barrier, members - 1)
    copies = []
    for k in range(1, members):
        copy = pltpu.make_async_remote_copy(
            src_ref=x_ref,
            dst_ref=slots.at[z],
            send_sem=send_sem.at[k - 1],
            recv_sem=recv_sem.at[k - 1],
            device_id={"head": lax.rem(z + k, members)},
            device_id_type=pl.DeviceIdType.MESH,
        )
        copy.start()
        copies.append(copy)
    slots[z] = x_ref[...]
    for copy in copies:
        copy.wait()
    total = slots[0]
    for k in range(1, members):
        total = total + slots[k]
    out_ref[...] = total


def head_sum(x, collective_id):
    members = lax.axis_size("head")
    return pl.pallas_call(
        functools.partial(head_sum_kernel, members),
        out_shape=jax.ShapeDtypeStruct(x.shape, F32),
        in_specs=[pl.BlockSpec(memory_space=pltpu.VMEM)],
        out_specs=pl.BlockSpec(memory_space=pltpu.VMEM),
        scratch_shapes=[
            pltpu.VMEM((members,) + x.shape, F32),
            pltpu.SemaphoreType.DMA((members - 1,)),
            pltpu.SemaphoreType.DMA((members - 1,)),
        ],
        compiler_params=pltpu.CompilerParams(collective_id=collective_id, has_side_effects=True),
        name="sum_over_head",
    )(x)


def turn(v, keep, left, right):
    h = ROT // 2
    return v * keep + pltpu.roll(v, HD - h, 1) * left + pltpu.roll(v, h, 1) * right


def rotate_kernel(sign, v_ref, keep_ref, left_ref, right_ref, out_ref):
    for head in range(v_ref.shape[1] // HD):
        part = pl.ds(head * HD, HD)
        out_ref[:, part] = turn(
            v_ref[:, part], keep_ref[...], sign * left_ref[...], sign * right_ref[...]
        ).astype(BF16)


def rotate(values_in, tables, sign):
    tokens, feats = values_in.shape
    block = min(tokens, 256)
    table = pl.BlockSpec((block, HD), lambda i: (i, 0))
    wide = pl.BlockSpec((block, feats), lambda i: (i, 0))
    return pl.pallas_call(
        functools.partial(rotate_kernel, sign),
        grid=(tokens // block,),
        in_specs=[wide, table, table, table],
        out_specs=wide,
        out_shape=jax.ShapeDtypeStruct((tokens, feats), BF16),
        cost_estimate=pl.CostEstimate(
            flops=5 * tokens * feats, bytes_accessed=8 * tokens * feats, transcendentals=0
        ),
        name="rotate_heads",
    )(values_in, *tables)


def feed_kernel(x_ref, d_ref, up_ref, down_ref, gated_ref, d_up_ref, grad_up_ref, grad_down_ref):
    tokens, model_width = x_ref.shape
    step = min(256, tokens)
    for r in range(0, tokens, step):
        rows = slice(r, r + step)
        up_pre = dot(x_ref[rows], up_ref[...])
        d_gated = dot_nt(d_ref[rows], down_ref[...])
        below = 0.5 * (1.0 + lax.erf(up_pre * 0.5**0.5))
        density = jnp.exp(-0.5 * up_pre * up_pre) * (2.0 * jnp.pi) ** -0.5
        gated_ref[rows] = (up_pre * below).astype(BF16)
        d_up_ref[rows] = (d_gated * (below + up_pre * density)).astype(BF16)
    wide = min(512, model_width)
    for c in range(0, model_width, wide):
        part = slice(c, c + wide)
        grad_up_ref[part] = dot_tn(x_ref[:, part], d_up_ref[...]).astype(BF16)
        grad_down_ref[part] = dot_tn(d_ref[:, part], gated_ref[...]).astype(BF16)


def feed_forward(x, d_out, up, down):
    tokens, model_width = x.shape
    hidden = up.shape[1]
    block = min(512, hidden)
    fixed = pl.BlockSpec((tokens, model_width), lambda i: (0, 0), pipeline_mode=pl.Buffered(1))
    narrow = pl.BlockSpec((tokens, block), lambda i: (0, i))
    column = pl.BlockSpec((model_width, block), lambda i: (0, i))
    shape = lambda rows: jax.ShapeDtypeStruct((rows, hidden), BF16)
    return pl.pallas_call(
        feed_kernel,
        grid=(hidden // block,),
        in_specs=[fixed, fixed, column, pl.BlockSpec((block, model_width), lambda i: (i, 0))],
        out_specs=[narrow, narrow, column, column],
        out_shape=[shape(tokens), shape(tokens), shape(model_width), shape(model_width)],
        compiler_params=pltpu.CompilerParams(vmem_limit_bytes=56 * 1024 * 1024),
        cost_estimate=pl.CostEstimate(
            flops=8 * tokens * model_width * hidden,
            bytes_accessed=4 * model_width * (2 * hidden + tokens),
            transcendentals=0,
        ),
        name="feed_forward",
    )(x, d_out, up, down)


def attention_kernel(
    place_ref, q_ref, do_ref, start_ref, valid_ref, keep_ref, left_ref, right_ref, *refs
):
    blocks = (len(refs) - 6) // 2
    k_refs, v_refs = refs[:blocks], refs[blocks : 2 * blocks]
    o_ref, dq_ref, near_ref, beside_ref, s_ref, dp_ref = refs[2 * blocks :]
    grad_ref = lambda j: (beside_ref if j % 2 else near_ref).at[j // 2]
    rows = q_ref.shape[1]
    scale = HD ** (-0.5)
    member = place_ref[0]
    keep, left, right = keep_ref[0], left_ref[0], right_ref[0]
    q = turn(q_ref[0], keep, left, right).astype(BF16)
    d_out = do_ref[0]
    start = start_ref[0]
    top = jnp.full((rows, 1), MASKED, F32)
    t = member * rows + lax.broadcasted_iota(jnp.int32, (rows, rows), 0)
    for j in range(blocks):
        u = place_ref[j] * rows + lax.broadcasted_iota(jnp.int32, (rows, rows), 1)
        allowed = (u <= t) & (u >= start)
        s_ref[j] = jnp.where(allowed, dot_nt(q, k_refs[j][0]) * scale, MASKED)
        top = jnp.maximum(top, jnp.max(s_ref[j], axis=1, keepdims=True))
    total = jnp.zeros((rows, 1), F32)
    for j in range(blocks):
        e = jnp.exp(s_ref[j] - top)
        s_ref[j] = e
        total = total + jnp.sum(e, axis=1, keepdims=True)
    inverse = 1.0 / total
    out = jnp.zeros((rows, HD), F32)
    delta = jnp.zeros((rows, 1), F32)
    for j in range(blocks):
        p = s_ref[j] * inverse
        s_ref[j] = p
        p_bf = p.astype(BF16)
        out = out + dot(p_bf, v_refs[j][0])
        grad_ref(j)[1] = dot_tn(p_bf, d_out).astype(BF16)
        d_p = dot_nt(d_out, v_refs[j][0])
        dp_ref[j] = d_p
        delta = delta + jnp.sum(p * d_p, axis=1, keepdims=True)
    o_ref[0] = (out * valid_ref[0]).astype(BF16)
    d_q = jnp.zeros((rows, HD), F32)
    for j in range(blocks):
        d_s = (s_ref[j] * (dp_ref[j] - delta)).astype(BF16)
        d_q = d_q + dot(d_s, k_refs[j][0])
        grad_ref(j)[0] = (dot_tn(d_s, q) * scale).astype(BF16)
    dq_ref[0] = turn(d_q * scale, keep, -left, -right).astype(BF16)


def attention(index, places, queries, d_attended, starts, valid, tables, keys, values):
    _, rows, feats = queries.shape
    blocks = len(keys)
    tile = pl.BlockSpec((1, rows, HD), lambda h: (index, 0, h))
    fixed = lambda width: pl.BlockSpec((1, rows, width), lambda h: (index, 0, 0))
    out_tile = pl.BlockSpec((1, rows, HD), lambda h: (0, 0, h))
    grad_tile = pl.BlockSpec((blocks // 2, 2, rows, HD), lambda h: (0, 0, 0, h))
    shape = lambda *lead: jax.ShapeDtypeStruct(lead + (rows, feats), BF16)
    return pl.pallas_call(
        attention_kernel,
        grid=(feats // HD,),
        in_specs=[pl.BlockSpec(memory_space=pltpu.SMEM), tile, tile]
        + [fixed(1)] * 2
        + [fixed(HD)] * 3
        + [tile] * (2 * blocks),
        out_specs=[out_tile] * 2 + [grad_tile] * 2,
        out_shape=[shape(1)] * 2 + [shape(blocks // 2, 2)] * 2,
        scratch_shapes=[
            pltpu.VMEM((blocks, rows, rows), F32),
            pltpu.VMEM((blocks, rows, rows), F32),
        ],
        compiler_params=pltpu.CompilerParams(vmem_limit_bytes=40 * 1024 * 1024),
        cost_estimate=pl.CostEstimate(
            flops=6 * feats * rows * rows * blocks,
            bytes_accessed=rows * feats * 2 * (4 + 4 * blocks),
            transcendentals=0,
        ),
        name="attention_both_ways",
    )(places, queries, d_attended, starts, valid, *tables, *keys, *values)


def exchange_rows(local):
    if lax.axis_size("stream") != 4:
        raise ValueError("stream")
    across = lax.ppermute(local, "stream", [(0, 2), (1, 3)])
    beside = over_core(local)
    return (local, beside, across, over_core(across))


def add_f32(a, b):
    return a.astype(F32) + b.astype(F32)


def over_line(a):
    return lax.ppermute(a, "stream", [(2, 0), (3, 1)])


def columns_of(pieces, rows):
    lane = lax.broadcasted_iota(jnp.int32, (rows, 128), 1)
    out = jnp.zeros((rows, 128), F32)
    for index, piece in enumerate(pieces):
        out = jnp.where(lane == index, piece, out)
    return out


def row_sum(a):
    return jnp.sum(a, axis=1, keepdims=True)


def streams_kernel(weights_ref, history_ref, streams_ref, stats_ref):
    weights = weights_ref[...]
    layers = [history_ref[j].astype(F32) for j in range(HIST)]
    sums, squares = [], []
    for s in range(4):
        total = weights[:, s * HIST : s * HIST + 1] * layers[0]
        for j in range(1, HIST):
            total = total + weights[:, s * HIST + j : s * HIST + j + 1] * layers[j]
        streams_ref[s] = total
        sums.append(row_sum(total))
        squares.append(row_sum(total * total))
    stats_ref[...] = columns_of(sums + squares, weights.shape[0]).T[:8]


def mix_streams(weights, history):
    _, tokens, feats = history.shape
    block = min(128, tokens)
    return pl.pallas_call(
        streams_kernel,
        grid=(tokens // block,),
        in_specs=[
            pl.BlockSpec((block, weights.shape[1]), lambda i: (i, 0)),
            pl.BlockSpec((HIST, block, feats), lambda i: (0, i, 0)),
        ],
        out_specs=[
            pl.BlockSpec((4, block, feats), lambda i: (0, i, 0)),
            pl.BlockSpec((8, block), lambda i: (0, i)),
        ],
        out_shape=[
            jax.ShapeDtypeStruct((4, tokens, feats), F32),
            jax.ShapeDtypeStruct((8, tokens), F32),
        ],
        compiler_params=pltpu.CompilerParams(vmem_limit_bytes=40 * 1024 * 1024),
        cost_estimate=pl.CostEstimate(
            flops=80 * tokens * feats, bytes_accessed=34 * tokens * feats, transcendentals=0
        ),
        name="mix_streams",
    )(weights, history)


def early_kernel(streams_ref, cot_ref, history_ref, out_ref):
    cot = cot_ref[...].astype(F32)
    plain, crossed, direct = [], [], []
    layers = [history_ref[j].astype(F32) for j in range(HIST)]
    for layer in layers:
        plain.append(row_sum(layer))
        direct.append(row_sum(cot * layer))
    for s in range(4):
        for layer in layers:
            crossed.append(row_sum(streams_ref[s] * layer))
    out_ref[...] = columns_of(crossed + plain + direct, cot.shape[0]).T[:64].astype(BF16)


def early_sums(streams, cot, history):
    _, tokens, feats = streams.shape
    block = min(128, tokens)
    return pl.pallas_call(
        early_kernel,
        grid=(tokens // block,),
        in_specs=[
            pl.BlockSpec((4, block, feats), lambda i: (0, i, 0)),
            pl.BlockSpec((block, feats), lambda i: (i, 0)),
            pl.BlockSpec((HIST, block, feats), lambda i: (0, i, 0)),
        ],
        out_specs=pl.BlockSpec((64, block), lambda i: (0, i)),
        out_shape=jax.ShapeDtypeStruct((64, tokens), BF16),
        compiler_params=pltpu.CompilerParams(vmem_limit_bytes=40 * 1024 * 1024),
        cost_estimate=pl.CostEstimate(
            flops=110 * tokens * feats, bytes_accessed=36 * tokens * feats, transcendentals=0
        ),
        name="early_sums",
    )(streams, cot, history)


def sums_kernel(
    g0, g1, g2, g3, streams_ref, stats_ref, gain_ref, history_ref, dots_ref, out_ref, edge_ref
):
    stats = stats_ref[...]
    rows = stats.shape[0]

    @pl.when(pl.program_id(0) == 0)
    def _():
        edge_ref[...] = jnp.zeros_like(edge_ref)

    firsts, seconds, dots = [], [], []
    for s, g_ref in enumerate((g0, g1, g2, g3)):
        g = g_ref[...].astype(F32)
        centered = (streams_ref[s] - stats[:, s : s + 1]) * stats[:, 4 + s : 5 + s]
        edge_ref[s : s + 1] += jnp.sum(g * centered, axis=0, keepdims=True)
        edge_ref[4 + s : 5 + s] += jnp.sum(g, axis=0, keepdims=True)
        scaled = g * gain_ref[s : s + 1]
        firsts.append(row_sum(scaled))
        seconds.append(row_sum(scaled * centered))
        for j in range(HIST):
            dots.append(row_sum(scaled * history_ref[j].astype(F32)))
    dots_ref[...] = columns_of(dots, rows).T[:48].astype(BF16)
    out_ref[...] = columns_of(firsts + seconds, rows).T[:8]


def gradient_sums(grads, streams, stats, gain, history):
    _, tokens, feats = streams.shape
    block = min(128, tokens)
    wide = pl.BlockSpec((block, feats), lambda i: (i, 0))
    return pl.pallas_call(
        sums_kernel,
        grid=(tokens // block,),
        in_specs=[wide] * 4
        + [
            pl.BlockSpec((4, block, feats), lambda i: (0, i, 0)),
            pl.BlockSpec((block, 8), lambda i: (i, 0)),
            pl.BlockSpec((4, feats), lambda i: (0, 0)),
            pl.BlockSpec((HIST, block, feats), lambda i: (0, i, 0)),
        ],
        out_specs=[
            pl.BlockSpec((48, block), lambda i: (0, i)),
            pl.BlockSpec((8, block), lambda i: (0, i)),
            pl.BlockSpec((8, feats), lambda i: (0, 0)),
        ],
        out_shape=[
            jax.ShapeDtypeStruct((48, tokens), BF16),
            jax.ShapeDtypeStruct((8, tokens), F32),
            jax.ShapeDtypeStruct((8, feats), F32),
        ],
        compiler_params=pltpu.CompilerParams(vmem_limit_bytes=40 * 1024 * 1024),
        cost_estimate=pl.CostEstimate(
            flops=110 * tokens * feats, bytes_accessed=42 * tokens * feats, transcendentals=0
        ),
        name="gradient_sums",
    )(*grads, streams, stats, gain, history)


def small_kernel(
    members,
    plane,
    dots_ref,
    sums_ref,
    early_in,
    stats_ref,
    pre_ref,
    slope_ref,
    hidden_ref,
    rms_ref,
    w_ref,
    current_ref,
    edge_ref,
    small_ref,
    scaled_ref,
    coef_ref,
    dot_slots,
    early_slots,
    slots,
    got,
    d_mix_ref,
    early_ref,
    rows_ref,
    dot_send,
    dot_recv,
    early_send,
    early_recv,
    send_sem,
    recv_sem,
    plane_send,
    plane_recv,
):
    x, stream, z = lax.axis_index("dp"), lax.axis_index("stream"), lax.axis_index("head")
    line = [{"head": lax.rem(z + k, members)} for k in range(1, members)]
    near = (
        {"stream": stream + 1 - 2 * lax.rem(stream, 2)},
        {"stream": lax.rem(stream + 2, 4)},
        {"dp": 1 - x},
    )
    near = near if plane else ()
    barrier = pltpu.get_barrier_semaphore()
    for peer in line + list(near):
        pl.semaphore_signal(barrier, inc=1, device_id=peer, device_id_type=pl.DeviceIdType.MESH)
    pl.semaphore_wait(barrier, len(line) + len(near))
    copies = []
    for source, target, sends, receives in (
        (dots_ref, dot_slots, dot_send, dot_recv),
        (early_in, early_slots, early_send, early_recv),
        (sums_ref, slots, send_sem, recv_sem),
    ):
        for k, peer in enumerate(line):
            copy = pltpu.make_async_remote_copy(
                src_ref=source,
                dst_ref=target.at[z],
                send_sem=sends.at[k],
                recv_sem=receives.at[k],
                device_id=peer,
                device_id_type=pl.DeviceIdType.MESH,
            )
            copy.start()
            copies.append(copy)
        target[z] = source[...]
    for copy in copies:
        copy.wait()
    total, dots = slots[0], dot_slots[0].astype(F32)
    early_ref[...] = early_slots[0].astype(F32)
    for k in range(1, members):
        early_ref[...] += early_slots[k].astype(F32)
        total = total + slots[k]
        dots = dots + dot_slots[k].astype(F32)
    d_mix_ref[...] = dots[: 4 * HIST]
    n = 4 * HIST
    model_width = members * small_ref.shape[1]
    plain = early_ref[n : n + HIST]
    rows_ref[...] = jnp.zeros_like(rows_ref)
    rows_ref[0:8] = total / model_width
    for s in range(4):
        part = slice(s * HIST, (s + 1) * HIST)
        mean, inverse = stats_ref[s : s + 1], stats_ref[4 + s : 5 + s]
        crossed = (early_ref[part] - mean * plain) * inverse
        d_part = inverse * (
            d_mix_ref[part] - rows_ref[s : s + 1] * plain - rows_ref[4 + s : 5 + s] * crossed
        )
        if s == 3:
            d_part = d_part + early_ref[n + HIST : n + 2 * HIST]
        d_mix_ref[part] = d_part
    d_mix = d_mix_ref[...]
    high = dict(precision=HIGHEST, preferred_element_type=F32)
    d_pre = jnp.dot(w_ref[...], d_mix, **high) * slope_ref[...]
    rms = rms_ref[...]
    cross = jnp.sum(d_pre * pre_ref[...], axis=0, keepdims=True)
    rows_ref[8:9] = rms * rms * cross / model_width
    coef_ref[...] = rows_ref[...].T
    scaled = d_pre * rms
    scaled_ref[...] = scaled
    small_ref[...] = jnp.zeros_like(small_ref)
    small_ref[0:n] = jnp.dot(scaled, current_ref[...].astype(F32), **high)
    small_ref[n : n + 8] = edge_ref[...]
    small_ref[n + 8 : 2 * n + 8, 0:n] = lax.dot_general(
        hidden_ref[...], d_mix, (((1,), (1,)), ((), ())), **high
    )
    small_ref[n + 8 : 2 * n + 8, n : n + 1] = jnp.sum(d_mix, axis=1, keepdims=True)
    for step, peer in enumerate(near):
        copy = pltpu.make_async_remote_copy(
            src_ref=small_ref,
            dst_ref=got.at[step],
            send_sem=plane_send.at[step],
            recv_sem=plane_recv.at[step],
            device_id=peer,
            device_id_type=pl.DeviceIdType.MESH,
        )
        copy.start()
        copy.wait()
        small_ref[...] += got[step]


def small_gradients(dots, sums, early, stats, pre, slope, hidden, rms, w_out, current, edges):
    members, plane = lax.axis_size("head"), paired()
    tokens, feats = current.shape
    n = 4 * HIST
    shape = jax.ShapeDtypeStruct
    sems = pltpu.SemaphoreType.DMA
    small, scaled, coefs = pl.pallas_call(
        functools.partial(small_kernel, members, plane),
        in_specs=[pl.BlockSpec(memory_space=pltpu.VMEM)] * 11,
        out_specs=[pl.BlockSpec(memory_space=pltpu.VMEM)] * 3,
        out_shape=[shape((80, feats), F32), shape((n, tokens), F32), shape((tokens, 128), F32)],
        scratch_shapes=[
            pltpu.VMEM((members, 48, tokens), BF16),
            pltpu.VMEM((members, 64, tokens), BF16),
            pltpu.VMEM((members, 8, tokens), F32),
            pltpu.VMEM((3, 80, feats), F32),
            pltpu.VMEM((n, tokens), F32),
            pltpu.VMEM((64, tokens), F32),
            pltpu.VMEM((128, tokens), F32),
            sems((members - 1,)),
            sems((members - 1,)),
            sems((members - 1,)),
            sems((members - 1,)),
            sems((members - 1,)),
            sems((members - 1,)),
            sems((3,)),
            sems((3,)),
        ],
        compiler_params=pltpu.CompilerParams(
            collective_id=3, has_side_effects=True, vmem_limit_bytes=40 * 1024 * 1024
        ),
        name="small_gradients",
    )(dots, sums, early, stats, pre, slope, hidden, rms, w_out, current, edges)
    if not plane:
        small = lax.psum(small.astype(BF16), ("dp", "stream")).astype(F32)
    return small, scaled, coefs


def history_kernel(
    g0, g1, g2, g3, streams_ref, stats_ref, gain_ref, cot_ref, current_ref, weights_ref, coef_ref, d_ref, w_ref, out_ref
):
    stats, weights, coefs = stats_ref[...], weights_ref[...], coef_ref[...]
    d_streams = []
    for s, g_ref in enumerate((g0, g1, g2, g3)):
        inverse = stats[:, 4 + s : 5 + s]
        centered = (streams_ref[s] - stats[:, s : s + 1]) * inverse
        scaled = g_ref[...].astype(F32) * gain_ref[s : s + 1]
        d_streams.append(
            inverse * (scaled - coefs[:, s : s + 1] - centered * coefs[:, 4 + s : 5 + s])
        )
    d_streams[3] = d_streams[3] + cot_ref[...].astype(F32)
    for j in range(HIST):
        total = weights[:, j : j + 1] * d_streams[0]
        for s in range(1, 4):
            total = total + weights[:, s * HIST + j : s * HIST + j + 1] * d_streams[s]
        if j == HIST - 1:
            total = total + lax.dot_general(
                d_ref[...],
                w_ref[...],
                (((0,), (0,)), ((), ())),
                precision=HIGHEST,
                preferred_element_type=F32,
            )
            total = total - current_ref[...].astype(F32) * coefs[:, 8:9]
        out_ref[j] = total


def history_gradient(grads, streams, stats, gain, cot, current, weights, coefs, d_scaled, w_rows):
    _, tokens, feats = streams.shape
    block = min(128, tokens)
    wide = pl.BlockSpec((block, feats), lambda i: (i, 0))
    narrow = lambda a: pl.BlockSpec((block, a.shape[1]), lambda i: (i, 0))
    fixed = lambda a: pl.BlockSpec(a.shape, lambda i: (0, 0))
    return pl.pallas_call(
        history_kernel,
        grid=(tokens // block,),
        in_specs=[wide] * 4
        + [
            pl.BlockSpec((4, block, feats), lambda i: (0, i, 0)),
            narrow(stats),
            fixed(gain),
            wide,
            wide,
            narrow(weights),
            narrow(coefs),
            pl.BlockSpec((d_scaled.shape[0], block), lambda i: (0, i)),
            fixed(w_rows),
        ],
        out_specs=pl.BlockSpec((HIST, block, feats), lambda i: (0, i, 0)),
        out_shape=jax.ShapeDtypeStruct((HIST, tokens, feats), F32),
        compiler_params=pltpu.CompilerParams(vmem_limit_bytes=40 * 1024 * 1024),
        cost_estimate=pl.CostEstimate(
            flops=110 * tokens * feats, bytes_accessed=64 * tokens * feats, transcendentals=0
        ),
        name="history_gradient",
    )(*grads, streams, stats, gain, cot, current, weights, coefs, d_scaled, w_rows)


def shards(
    history,
    seq_lens,
    bucket_slot,
    w_mix_in,
    w_mix_out,
    mix_bias,
    ln_gain,
    ln_bias,
    w_qkv,
    w_attn_out,
    w_up,
    w_down,
    cotangent,
):
    member = lax.axis_index("stream")
    micro, quarter, feats = history.shape[1:]
    tokens = micro * quarter
    model_width = feats * lax.axis_size("head")
    slot_base = lax.axis_index("dp") * micro
    slot_ids = jnp.arange(bucket_slot.shape[0], dtype=jnp.int32)
    query_places = member * quarter + jnp.arange(quarter, dtype=jnp.int32)
    w_mix_in_f = w_mix_in.astype(F32)
    w_mix_out_f = w_mix_out.astype(F32)

    segments, starts = [], []
    for index in range(micro):
        bucket = jnp.sum(jnp.where(slot_ids == slot_base + index, bucket_slot, 0))
        lengths = jnp.sum(jnp.where(slot_ids[:, None] == bucket, seq_lens, 0), axis=0)
        bounds = jnp.cumsum(lengths)
        passed = (query_places[:, None] >= bounds[None, :]).astype(jnp.int32)
        segments.append(jnp.sum(passed, axis=1))
        starts.append(jnp.sum(passed * lengths[None, :], axis=1))
    valid = (jnp.concatenate(segments) < 3).astype(F32)[:, None]
    starts = jnp.concatenate(starts)
    position = jnp.tile(query_places, micro) - starts
    frequency = jnp.arange(ROT // 2, dtype=F32)
    phases = position.astype(F32)[:, None] * (10000.0 ** (-2.0 * frequency / ROT))
    cosine, sine = jnp.cos(phases), jnp.sin(phases)
    plain = jnp.zeros((tokens, HD - ROT), F32)
    none = jnp.zeros_like(sine)
    tables = (
        jnp.concatenate([cosine, cosine, plain + 1.0], axis=1),
        jnp.concatenate([-sine, none, plain], axis=1),
        jnp.concatenate([none, sine, plain], axis=1),
    )

    cot_rows = cotangent.reshape(tokens, feats).astype(F32) * valid
    cot_bf = cot_rows.astype(BF16)
    duplex = lined()

    history = history.reshape(HIST, tokens, feats)
    current = history[HIST - 1]
    current_f = current.astype(F32)
    mixed = lax.dot_general(w_mix_in, current, (((0,), (1,)), ((), ())), preferred_element_type=F32)
    square = jnp.sum(current_f * current_f, axis=1)[None]
    mixed = head_sum(jnp.concatenate([mixed, square]), 0).T
    mixed, cot_bf, w_up = lax.optimization_barrier((mixed, cot_bf, w_up))
    out_full = lax.all_gather(cot_bf, "head", axis=1, tiled=True)
    if duplex:
        (up_full,) = exchange([], (), [w_up], (0,), 4)
        mixed, up_full = lax.optimization_barrier((mixed, up_full))
    rms_scale = lax.rsqrt(mixed[:, 4 * HIST :] / model_width + EPSILON)
    mix_pre = mixed[:, : 4 * HIST] * rms_scale
    below_mix = 0.5 * (1.0 + lax.erf(mix_pre * 0.5**0.5))
    mix_hidden = gelu_exact(mix_pre)
    slope_mix = below_mix + mix_pre * jnp.exp(-0.5 * mix_pre * mix_pre) * (2.0 * jnp.pi) ** -0.5
    mix_weights = jnp.dot(mix_hidden, w_mix_out_f, precision=HIGHEST) + mix_bias.reshape(-1)
    streams, stats = mix_streams(mix_weights, history)
    stats = head_sum(stats, 1)
    stat_sum, stat_square = stats[:4], stats[4:]
    row_means = (stat_sum / model_width)[:, :, None]
    inv_std = lax.rsqrt(stat_square[:, :, None] / model_width - row_means * row_means + EPSILON)
    centered = (streams - row_means) * inv_std
    row_stats = jnp.concatenate([row_means[..., 0], inv_std[..., 0]]).T
    normed = (centered * ln_gain[:, None, :] + ln_bias[:, None, :]).astype(BF16)

    def all_features(a):
        return lax.all_gather(a, "head", axis=1, tiled=True)

    if duplex:
        w_down, normed = lax.optimization_barrier((w_down, normed))
        wk, wv, down_full, w_out_full, wq, *shares = exchange(
            [], (), [w_qkv[1], w_qkv[2], w_down, w_attn_out, w_qkv[0]], (0, 0, 1, 1, 0), 6, 2
        )
    else:
        wq, wk, wv = gather_weight(w_qkv, 1)
        w_out_full, down_full = gather_weight(w_attn_out, 1), gather_weight(w_down, 1)
        up_full = gather_weight(w_up, 0)

    def to_owner(partial):
        return lax.psum_scatter(
            partial.astype(BF16), "head", scatter_dimension=1, tiled=True
        ).astype(F32)

    up_out, out_full = lax.optimization_barrier((normed[3], out_full))
    up_in, k_out, down_full = lax.optimization_barrier(
        (all_features(up_out), normed[1], down_full)
    )
    k_in, v_out = lax.optimization_barrier((all_features(k_out), normed[2]))
    gated_up, d_up, product_up, product_down = feed_forward(up_in, out_full, up_full, down_full)
    feed_products = [product_up[None], product_down[None]]
    feed_parts = [chip_parts(a) if paired() else a for a in feed_products]
    v_out, d_up, feed_parts = lax.optimization_barrier((v_out, d_up, feed_parts))
    feed_lines = [line_parts(*a) for a in feed_parts] if paired() else feed_parts
    streams_late, feed_lines[0] = lax.optimization_barrier((streams, feed_lines[0]))
    early = early_sums(streams_late, cot_bf, history)
    feed = dot(gated_up, down_full).astype(BF16)
    d_attended = dot_nt(out_full, w_out_full).astype(BF16) * valid.astype(BF16)
    d_up_in = dot_nt(d_up, up_full).astype(BF16)
    keys = rotate(dot(k_in, wk), tables, 1.0)
    v_in, q_out, early, feed, d_attended, d_up_in, keys, wk, wv = lax.optimization_barrier(
        (all_features(v_out), normed[0], early, feed, d_attended, d_up_in, keys, wk, wv)
    )
    values = dot(v_in, wv).astype(BF16)
    by_micro = lambda a: a.reshape((micro, quarter) + a.shape[1:])
    key_blocks = exchange_rows(by_micro(keys))
    value_blocks = exchange_rows(by_micro(values))
    q_in, d_up_in, key_blocks, value_blocks, feed_lines[1], early = lax.optimization_barrier(
        (all_features(q_out), d_up_in, key_blocks, value_blocks, feed_lines[1], early)
    )
    g_up = to_owner(d_up_in)
    product = lambda a, b: dot_tn(a, b).astype(BF16)

    queries = dot(q_in, wq)
    places = member ^ jnp.arange(4, dtype=jnp.int32)
    attended, d_query_pre, d_rows = [], [], []
    queries = by_micro(queries)
    for index in range(micro):
        results = attention(
            index,
            places,
            queries,
            by_micro(d_attended),
            by_micro(starts[:, None]),
            by_micro(valid),
            tuple(by_micro(a) for a in tables),
            key_blocks,
            value_blocks,
        )
        attended.append(results[0][0])
        d_query_pre.append(results[1][0])
        if duplex and index == micro - 1:
            continue
        chip = add_f32(results[2], over_core(results[3]))
        across = chip[1].astype(BF16)
        queries, across = lax.optimization_barrier((queries, across))
        d_rows.append(add_f32(chip[0], over_line(across)))
    attended, d_query_pre = jnp.concatenate(attended), jnp.concatenate(d_query_pre)
    d_key_rows = jnp.concatenate([a[0] for a in d_rows])
    done = d_key_rows.shape[0]
    d_key_rows = rotate(d_key_rows, tuple(a[:done] for a in tables), -1.0)
    d_value_rows = jnp.concatenate([a[1] for a in d_rows]).astype(BF16)
    attended, d_query_pre, d_key_rows, d_value_rows = lax.optimization_barrier(
        (attended, d_query_pre, d_key_rows, d_value_rows)
    )

    products = jnp.stack([product(q_in, d_query_pre), product(out_full, attended)])
    if duplex:
        partials = [dot_nt(d_query_pre, wq).astype(BF16)]
        parts = chip_parts(products)
        partials, parts, g_up, feed_lines = lax.optimization_barrier(
            (partials, parts, g_up, feed_lines)
        )
        feed_terms = [last_parts(a) for a in feed_lines]
        (g_query,), (d_key_full, d_value_full), (wk_rows, wv_rows) = exchange(
            partials,
            [d_key_rows, d_value_rows, results[2], results[3], *(a[done:] for a in tables)],
            shares,
            (0, 0),
            5,
        )
        attended_late, g_query = lax.optimization_barrier((attended, g_query))
        pair = lambda a: (a[: tokens // 2], a[tokens // 2 :])
        halves = [
            (dot(a, w_out_full) + b).astype(BF16) for a, b in zip(pair(attended_late), pair(feed))
        ]
        branch = to_owner(halves[0])
        g_key, g_value = dot_nt(d_key_full, wk_rows), dot_nt(d_value_full, wv_rows)
        terms = plane_parts(*parts)
    else:
        g_query = to_owner(dot_nt(d_query_pre, wq))
        branch = to_owner(dot(attended, w_out_full) + feed)
        terms = scatter_parts(products)
        feed_terms = [scatter_parts(a) for a in feed_products]
        g_key = to_owner(dot_nt(d_key_rows, wk))
        g_value = to_owner(dot_nt(d_value_rows, wv))
        kv_terms = scatter_parts(
            jnp.stack([product(k_in, d_key_rows), product(v_in, d_value_rows)])
        )
    grad_up = add_terms(feed_terms[0][0][0], feed_terms[0][1][0], False)
    grad_down = add_terms(feed_terms[1][0][0], feed_terms[1][1][0], True)
    grad_attn_out = add_terms(terms[0][1], terms[1][1], True)

    grads = (g_query, g_key, g_value, g_up)
    dots, sums, edges = gradient_sums(grads, streams, row_stats, ln_gain, history)
    if duplex:
        sums, d_key_full, d_value_full = lax.optimization_barrier((sums, d_key_full, d_value_full))
        own = lambda a: lax.dynamic_slice_in_dim(a, lax.axis_index("head") * feats, feats, 1)
        kv = jnp.stack([product(k_in, own(d_key_full)), product(v_in, own(d_value_full))])
        kv_terms = scatter_parts(kv)
    grad_query = terms[0][:1].astype(F32) + terms[1][:1].astype(F32)
    small, d_scaled, coefs = small_gradients(
        dots, sums, early, row_stats.T, mix_pre.T, slope_mix.T, mix_hidden.T, rms_scale.T, w_mix_out_f, current, edges
    )
    if duplex:
        coefs, second_half = lax.optimization_barrier((coefs, halves[1]))
        branch = jnp.concatenate([branch, to_owner(second_half)])
    block_out = (valid * (streams[3] + branch)).astype(BF16)
    history_grad = history_gradient(
        grads, streams, row_stats, ln_gain, cot_bf, current, mix_weights, coefs, d_scaled, w_mix_in_f.T
    ).reshape(HIST, micro, quarter, feats)
    grad_qkv = jnp.concatenate([grad_query, kv_terms[0].astype(F32) + kv_terms[1].astype(F32)])
    n = 4 * HIST
    return (
        block_out.reshape(micro, quarter, feats),
        mix_weights.reshape(micro, quarter, 4 * HIST),
        history_grad,
        small[:n].T,
        small[n + 8 : 2 * n + 8, :n],
        small[n + 8 : 2 * n + 8, n].reshape(mix_bias.shape),
        small[n : n + 4],
        small[n + 4 : n + 8],
        grad_qkv,
        grad_attn_out,
        grad_up,
        grad_down,
    )


def solution(mesh):
    return jax.shard_map(
        shards,
        mesh=mesh,
        in_specs=(
            P(None, "dp", "stream", "head"),
            P(),
            P(),
            P("head", None),
            P(),
            P(),
            P(None, "head"),
            P(None, "head"),
            P(None, ("dp", "stream"), "head"),
            P("head", ("dp", "stream")),
            P(("dp", "stream"), "head"),
            P("head", ("dp", "stream")),
            P("dp", "stream", "head"),
        ),
        out_specs=(
            P("dp", "stream", "head"),
            P("dp", "stream", None),
            P(None, "dp", "stream", "head"),
            P("head", None),
            P(),
            P(),
            P(None, "head"),
            P(None, "head"),
            P(None, ("dp", "stream"), "head"),
            P("head", ("dp", "stream")),
            P(("dp", "stream"), "head"),
            P("head", ("dp", "stream")),
        ),
        check_vma=False,
    )
```

```python
import functools

import jax
import jax.numpy as jnp
from jax import lax
from jax.experimental import pallas as pl
from jax.experimental.pallas import tpu as pltpu
from jax.sharding import PartitionSpec as P

HD = 128
HIST = 9
ROT = 32

EPSILON = 1e-05
HIGHEST = lax.Precision.HIGHEST
MASKED = -1e30
F32 = jnp.float32
BF16 = jnp.bfloat16

SWAP_X = [(0, 1), (1, 0)]
SWAP_Y = [(0, 2), (2, 0), (1, 3), (3, 1)]
SWAP_CORE = [(0, 1), (1, 0), (2, 3), (3, 2)]


def dot(a, b):
    return jnp.dot(a, b, preferred_element_type=F32)


def dot_nt(a, b):
    return lax.dot_general(a, b, (((1,), (1,)), ((), ())), preferred_element_type=F32)


def dot_tn(a, b):
    return lax.dot_general(a, b, (((0,), (0,)), ((), ())), preferred_element_type=F32)


def gelu_exact(values_in):
    return jax.nn.gelu(values_in, approximate=False)


def over_x(a):
    return lax.ppermute(a, "dp", SWAP_X)


def over_y(a):
    return lax.ppermute(a, "stream", SWAP_Y)


def over_core(a):
    return lax.ppermute(a, "stream", SWAP_CORE)


def paired():
    return lax.axis_size("dp") == 2 and lax.axis_size("stream") == 4


def gather_weight(shard, axis):
    return lax.all_gather(shard, ("dp", "stream"), axis=axis, tiled=True)


def lined():
    return paired() and lax.axis_size("head") == 4


def take(a, index, axis):
    return lax.dynamic_index_in_dim(a, index, axis, keepdims=False)


def add_bf(a, b):
    return (a.astype(F32) + b.astype(F32)).astype(BF16)


def chip_parts(partial):
    count, rows, columns = partial.shape
    core, x = lax.axis_index("stream") % 2, lax.axis_index("dp")
    split = partial.reshape(count, 4, 2, rows // 8, columns)
    chip = add_bf(take(split, core, 2), over_core(take(split, 1 - core, 2)))
    chip = chip.reshape(count, 2, 2, rows // 8, columns)
    return take(chip, x, 1), take(chip, 1 - x, 1)


def line_parts(stays, leaves):
    return add_bf(stays, over_x(leaves))


def last_parts(line):
    y = lax.axis_index("stream") // 2
    return take(line, y, 1), over_y(take(line, 1 - y, 1))


def plane_parts(stays, leaves):
    return last_parts(line_parts(stays, leaves))


def scatter_parts(partial):
    if not paired():
        whole = lax.psum_scatter(partial, ("dp", "stream"), scatter_dimension=1, tiled=True)
        return whole, jnp.zeros_like(whole)
    return plane_parts(*chip_parts(partial))


def add_kernel(turned, a_ref, b_ref, out_ref):
    total = a_ref[...].astype(F32) + b_ref[...].astype(F32)
    out_ref[...] = total.T if turned else total


def add_terms(a, b, turned):
    rows, columns = a.shape
    block = min(512, columns)
    return pl.pallas_call(
        functools.partial(add_kernel, turned),
        grid=(columns // block,),
        in_specs=[pl.BlockSpec((rows, block), lambda i: (0, i))] * 2,
        out_specs=pl.BlockSpec((block, rows), lambda i: (i, 0))
        if turned
        else pl.BlockSpec((rows, block), lambda i: (0, i)),
        out_shape=jax.ShapeDtypeStruct((columns, rows) if turned else (rows, columns), F32),
        cost_estimate=pl.CostEstimate(
            flops=rows * columns, bytes_accessed=8 * rows * columns, transcendentals=0
        ),
        name="add_terms",
    )(a, b)


def exchange_kernel(units, spread, axes, *refs):
    count, whole = len(axes), 2 if units else 0
    inputs, refs = refs[: units + count], refs[units + count :]
    partials, shard_refs = inputs[:units], inputs[units:]
    if units:
        done_in, near_in, beside_in = refs[:2], refs[2], refs[3]
        keep_ref, left_ref, right_ref = refs[4:7]
        lines_in, stays_in, leaves_in, streams_in = refs[7:9], refs[9], refs[10], refs[11:13]
        refs = refs[13:]
    outputs, refs = refs[: units + whole + count], refs[units + whole + count :]
    outs, wides, fulls = outputs[:units], outputs[units : units + whole], outputs[units + whole :]
    shares, refs = refs[:spread], refs[spread:]
    if units:
        grad_refs, refs = refs[:6], refs[6:]
    own_sem, near_send, near_recv = refs[:3]
    if units:
        held, got, load_sem, send_sem, recv_sem = refs[3:8]
        mine, theirs, below, pieces, piece_own, piece_send, piece_recv = refs[8:15]
        mine_sem, done_sem, core_send, core_recv, y_send, y_recv = refs[15:21]
        feed_own, feed_got, pair_own, pair_x, pair_y, wide_in, full_grad, from_core = refs[21:29]
        job_load, job_send, job_recv = refs[29:]
    x, stream, z = lax.axis_index("dp"), lax.axis_index("stream"), lax.axis_index("head")
    core = lax.rem(stream, 2)
    other_x, other_y, other_core = 1 - x, lax.rem(stream + 2, 4), stream + 1 - 2 * core
    line = ({"head": lax.rem(z + 1, 4)}, {"head": lax.rem(z + 3, 4)})
    to_x, to_y, to_core = {"dp": other_x}, {"stream": other_y}, {"stream": other_core}
    place = x * 4 + stream
    place_x, place_y = other_x * 4 + stream, x * 4 + other_y
    place_far = other_x * 4 + other_y
    beside = lambda at: at + 1 - 2 * core

    barrier = pltpu.get_barrier_semaphore()
    peers = (line if units or spread else ()) + ((to_x, to_y, to_core) if count else ())
    peers = peers + (({"head": lax.rem(z + 2, 4)},) if spread else ())
    for peer in peers:
        pl.semaphore_signal(barrier, inc=1, device_id=peer, device_id_type=pl.DeviceIdType.MESH)
    pl.semaphore_wait(barrier, len(peers))

    def region(w, at, part=None):
        full, width = fulls[w], shard_refs[w].shape[min(axes[w], 1)]
        rows, columns = shard_refs[w].shape
        start, size = (0, rows) if part is None else (part * (rows // 2), rows // 2)
        if axes[w] == 0:
            return full.at[pl.ds(pl.multiple_of(at * width + start, size), size)]
        column = at * width
        if axes[w] == 2:
            start = lax.rem(at, 2) * rows + start
            start, column = pl.multiple_of(start, size), lax.div(at, 2) * width
        return full.at[pl.ds(start, size), pl.ds(pl.multiple_of(column, width), width)]

    def near(w, index, source, target, peer):
        return pltpu.make_async_remote_copy(
            src_ref=source,
            dst_ref=target,
            send_sem=near_send.at[w, index],
            recv_sem=near_recv.at[w, index],
            device_id=peer,
            device_id_type=pl.DeviceIdType.MESH,
        )

    def pass_on(w, index, at, peer, part=None):
        return near(w, index, region(w, at, part), region(w, at, part), peer)

    def first(w):
        target = region(w, place)
        pltpu.make_async_copy(shard_refs[w], target, own_sem.at[w]).start()
        for index, peer in enumerate((to_x, to_y, to_core)):
            near(w, index, shard_refs[w], target, peer).start()

    def second(w):
        pass_on(w, 0, place_x, to_x).wait_recv()
        pass_on(w, 4, place_x, to_y, 0).start()
        pass_on(w, 3, place_x, to_core).start()
        pass_on(w, 1, place_y, to_y).wait_recv()
        pass_on(w, 6, place_y, to_x, 1).start()
        pass_on(w, 5, place_y, to_core).start()

    def third(w):
        pass_on(w, 4, place_far, to_y, 0).wait_recv()
        pass_on(w, 7, place_far, to_core, 0).start()
        pass_on(w, 6, place_far, to_x, 1).wait_recv()
        pass_on(w, 8, place_far, to_core, 1).start()

    def last(w):
        for index, at, part in (
            (2, place, None),
            (3, place_x, None),
            (5, place_y, None),
            (7, place_far, 0),
            (8, place_far, 1),
        ):
            pass_on(w, index, beside(at), to_core, part).wait_recv()
        pltpu.make_async_copy(shard_refs[w], region(w, place), own_sem.at[w]).wait()
        for index in (0, 1, 2):
            near(w, index, shard_refs[w], region(w, place), to_core).wait_send()
        for index, at, part in (
            (3, place_x, None),
            (4, place_x, 0),
            (5, place_y, None),
            (6, place_y, 1),
            (7, place_far, 0),
            (8, place_far, 1),
        ):
            pass_on(w, index, at, to_core, part).wait_send()

    for w in range(count):
        first(w)
    if not units:
        moves = []
        for i in range(spread):
            second(i)
        for i in range(spread):
            third(i)
        for i in range(spread):
            last(i)
            spread_own, spread_send, spread_recv = refs[3:6]
            rows, columns = shares[i].shape[0], fulls[i].shape[1]
            target = shares[i].at[:, pl.ds(pl.multiple_of(z * columns, columns), columns)]

            def source(at):
                start = (at * 8 + place) * rows
                return fulls[i].at[pl.ds(pl.multiple_of(start, rows), rows)]

            moves.append(pltpu.make_async_copy(source(z), target, spread_own.at[i]))
            for k in range(1, 4):
                to = lax.rem(z + k, 4)
                moves.append(
                    pltpu.make_async_remote_copy(
                        src_ref=source(to),
                        dst_ref=target,
                        send_sem=spread_send.at[i, k - 1],
                        recv_sem=spread_recv.at[i, k - 1],
                        device_id={"head": to},
                        device_id_type=pl.DeviceIdType.MESH,
                    )
                )
        for move in moves:
            move.start()
        for w in range(spread, count):
            second(w)
        for w in range(spread, count):
            third(w)
        for w in range(spread, count):
            last(w)
        for move in moves:
            move.wait()
        return

    feats = held.shape[-1]
    chunk = send_sem.shape[-1]
    tokens = held.shape[2]
    step_rows = tokens // chunk
    y = lax.div(stream, 2)

    def load(u, b):
        return pltpu.make_async_copy(
            partials[u].at[:, b * feats : (b + 1) * feats], held.at[u, b], load_sem.at[u, b]
        )

    def to_beside(v):
        return pltpu.make_async_remote_copy(
            src_ref=beside_in.at[:, v],
            dst_ref=theirs.at[v],
            send_sem=core_send.at[v],
            recv_sem=core_recv.at[v],
            device_id=to_core,
            device_id_type=pl.DeviceIdType.MESH,
        )

    def load_done(v):
        return pltpu.make_async_copy(
            done_in[v], pieces.at[v, pl.ds(0, done_in[v].shape[0])], done_sem.at[v]
        )

    def load_mine(v):
        return pltpu.make_async_copy(near_in.at[:, v], mine.at[v], mine_sem.at[v])

    def to_below(v):
        return pltpu.make_async_remote_copy(
            src_ref=mine.at[v, 1],
            dst_ref=below.at[v],
            send_sem=y_send.at[v],
            recv_sem=y_recv.at[v],
            device_id=to_y,
            device_id_type=pl.DeviceIdType.MESH,
        )

    for v in range(2):
        to_beside(v).start()
        load_mine(v).start()
        load_done(v).start()
    for u in range(units):
        for b in range(4):
            load(u, b).start()
    for u in range(units):
        for b in range(4):
            load(u, b).wait()

    def columns(block):
        return pl.ds(pl.multiple_of(block * feats, feats), feats)

    def part(c):
        return pl.ds(pl.multiple_of(c * step_rows, step_rows), step_rows)

    def hop(way, u, step, block, c):
        return pltpu.make_async_remote_copy(
            src_ref=held.at[u, block, part(c)],
            dst_ref=got.at[way, u, step, part(c)],
            send_sem=send_sem.at[way, u, step, c],
            recv_sem=recv_sem.at[way, u, step, c],
            device_id=line[way],
            device_id_type=pl.DeviceIdType.MESH,
        )

    ways = ((0, z), (1, 3 - z))

    def relay(way, v, step, block, c):
        target = wides[v].at[part(c), columns(block)]
        return pltpu.make_async_remote_copy(
            src_ref=pieces.at[v, part(c)] if step == 0 else target,
            dst_ref=target,
            send_sem=piece_send.at[way, v, step, c],
            recv_sem=piece_recv.at[way, v, step, c],
            device_id=line[way],
            device_id_type=pl.DeviceIdType.MESH,
        )

    def piece_at(way, step):
        return z - step if way == 0 else z + step

    def block_at(way, step):
        return 3 - step + z if way == 0 else step + z - 3

    def keep(v):
        return pltpu.make_async_copy(pieces.at[v], wides[v].at[:, columns(z)], piece_own.at[v])

    def over_parts(body, start=0, stop=None):
        def step(c, carry):
            body(c)
            return carry

        lax.fori_loop(start, chunk if stop is None else stop, step, 0)

    ready = done_in[0].shape[0] // step_rows
    early, late = (0, ready), (ready, chunk)

    def sum_step(step):
        def body(c):
            for way, rank in ways:

                @pl.when(rank <= step)
                def _():
                    block = block_at(way, step)
                    for u in range(units):
                        if step > 0:

                            @pl.when(rank > 0)
                            def _():
                                hop(way, u, step - 1, block, c).wait_recv()
                                total = held[u, block, part(c)].astype(F32) + got[
                                    way, u, step - 1, part(c)
                                ].astype(F32)
                                held[u, block, part(c)] = total.astype(BF16)

                        hop(way, u, step, block, c).start()

        over_parts(body)

    def gather_step(v, step, span):
        def body(c):
            for way, rank in ways:

                @pl.when((rank >= step) & (rank < 3))
                def _():
                    block = piece_at(way, step)
                    if step > 0:
                        relay(way, v, step - 1, block, c).wait_recv()
                    relay(way, v, step, block, c).start()

        over_parts(body, *span)

    def chip_sum(v):
        load_mine(v).wait()
        to_beside(v).wait()

        @pl.when(y == 1)
        def _():
            def body(c):
                total = mine[v, 1, part(c)].astype(F32) + theirs[v, 1, part(c)].astype(F32)
                mine[v, 1, part(c)] = total.astype(BF16)

            over_parts(body, 0, chunk - ready)
            to_below(v).start()

    def bring(v):
        def body(c, from_y):
            rows, out = part(c), part(c + ready)
            total = mine[v, 0, rows].astype(F32) + theirs[v, 0, rows].astype(F32)
            if from_y:
                total = total + below[v, rows].astype(F32)
            if v == 1:
                pieces[v, out] = total.astype(BF16)
            else:
                for head in range(feats // HD):
                    lanes = slice(head * HD, (head + 1) * HD)
                    pieces[v, out, lanes] = turn(
                        total[:, lanes], keep_ref[rows], -left_ref[rows], -right_ref[rows]
                    ).astype(BF16)

        @pl.when(y == 0)
        def _():
            to_below(v).wait_recv()
            over_parts(lambda c: body(c, True), 0, chunk - ready)

        @pl.when(y == 1)
        def _():
            over_parts(lambda c: body(c, False), 0, chunk - ready)

        keep(v).start()

    def job(index, source, target, peer):
        return pltpu.make_async_remote_copy(
            src_ref=source,
            dst_ref=target,
            send_sem=job_send.at[index],
            recv_sem=job_recv.at[index],
            device_id=peer,
            device_id_type=pl.DeviceIdType.MESH,
        )

    def job_in(index):
        source, target = (
            (lines_in[index].at[y], feed_own.at[index])
            if index < 2
            else (stays_in, pair_own.at[0])
            if index == 2
            else (streams_in[index - 3], wide_in.at[index - 3])
        )
        return pltpu.make_async_copy(source, target, job_load.at[index])

    def feed_job(f):
        return job(f, lines_in[f].at[1 - y], feed_got.at[f], to_y)

    def pair_x_job(i):
        source = full_grad.at[:, pl.ds(other_x * 2, 2), core] if i else leaves_in
        return job(2 + 4 * i, source, pair_x.at[i], to_x)

    def pair_y_job(i):
        return job(3 + 4 * i, pair_own.at[i, :, 1 - y], pair_y.at[i], to_y)

    def core_job(i):
        return job(4 + i, full_grad.at[i, :, 1 - core], from_core.at[i], to_core)

    def product(i):
        job_in(3 + i).wait()
        rows = full_grad.shape[3]
        for b in range(4):
            part_in = wide_in[i, :, b * 2 * rows : (b + 1) * 2 * rows]
            block = dot_tn(part_in, pieces[i]).astype(BF16)
            full_grad[i, b, 0] = block[:rows]
            full_grad[i, b, 1] = block[rows:]
        core_job(i).start()

    def both(a, b):
        return a.astype(F32) + b.astype(F32)

    def chip_grad():
        for i in range(2):
            core_job(i).wait()
            for b in range(4):
                full_grad[i, b, core] = both(full_grad[i, b, core], from_core[i, b]).astype(BF16)
        pair_x_job(1).start()

    def pair_line(i):
        pair_x_job(i).wait()
        for n in range(2):
            for k in range(2):
                stays = pair_own[i, n, k] if i == 0 else full_grad[n, x * 2 + k, core]
                pair_own[i, n, k] = both(stays, pair_x[i, n, k]).astype(BF16)
        pair_y_job(i).start()

    def pair_finish(i):
        pair_y_job(i).wait()
        total = [both(pair_own[i, n, y], pair_y[i, n]) for n in range(2)]
        grad_refs[2 + 2 * i][...] = total[0]
        grad_refs[3 + 2 * i][...] = total[1].T if i == 0 else total[1]

    def feed_finish():
        wide = min(512, feed_own.shape[2])
        for f in range(2):
            feed_job(f).wait()
            for c in range(0, feed_own.shape[2], wide):
                span = slice(c, c + wide)
                total = both(feed_own[f, :, span], feed_got[f, :, span])
                if f == 0:
                    grad_refs[0][:, span] = total
                else:
                    grad_refs[1][span] = total.T

    pair_x_job(0).start()
    for index in range(5):
        job_in(index).start()
    sum_step(0)
    for v in range(whole):
        load_done(v).wait()
        gather_step(v, 0, early)
    for v in range(whole):
        chip_sum(v)
    for w in range(count):
        second(w)
    for v in range(whole):
        bring(v)
        gather_step(v, 0, late)
    for f in range(2):
        feed_job(f).start()
    sum_step(1)
    for v in range(whole):
        gather_step(v, 1, early)
    for w in range(count):
        third(w)
    for i in range(2):
        product(i)
    for v in range(whole):
        gather_step(v, 1, late)
    job_in(2).wait()
    pair_line(0)
    sum_step(2)
    for v in range(whole):
        gather_step(v, 2, early)
    chip_grad()
    for f in range(2):
        job_in(f).wait()
    feed_finish()
    pair_finish(0)

    def finish(c):
        for u in range(units):
            outs[u][part(c)] = held[u, z, part(c)].astype(F32)
            for way, rank in ways:

                @pl.when(rank > 0)
                def _():
                    hop(way, u, 2, z, c).wait_recv()
                    outs[u][part(c)] += got[way, u, 2, part(c)].astype(F32)

    for v in range(whole):
        gather_step(v, 2, late)
    pair_line(1)
    over_parts(finish)
    for w in range(count):
        last(w)
    pair_finish(1)

    def drain(c):
        for way, rank in ways:

            @pl.when(rank == 3)
            def _():
                for v in range(whole):
                    for step in range(3):
                        relay(way, v, step, piece_at(way, step + 1), c).wait_recv()

        for step in range(3):
            for way, rank in ways:

                @pl.when(rank <= step)
                def _():
                    for u in range(units):
                        hop(way, u, step, block_at(way, step), c).wait_send()

                @pl.when((rank >= step) & (rank < 3))
                def _():
                    for v in range(whole):
                        relay(way, v, step, piece_at(way, step), c).wait_send()

    over_parts(drain)
    for v in range(whole):
        keep(v).wait()

        @pl.when(y == 1)
        def _():
            to_below(v).wait_send()


def exchange(partials, rows, shards_in, axes, collective_id, spread=0):
    units, count = len(partials), len(shards_in)
    grown = ((8, 1), (1, 8), (2, 4))
    shape = jax.ShapeDtypeStruct
    full = [
        shape(tuple(n * k for n, k in zip(w.shape, grown[axis])), BF16)
        for w, axis in zip(shards_in, axes)
    ]
    anywhere, local = pl.BlockSpec(memory_space=pl.ANY), pl.BlockSpec(memory_space=pltpu.VMEM)
    sems = pltpu.SemaphoreType.DMA
    out_specs, out_shape = [anywhere] * count, full
    in_specs = [anywhere] * (units + count)
    scratch = [sems((count,)), sems((count, 9)), sems((count, 9))]
    if units:
        tokens, feats = partials[0].shape[0], partials[0].shape[1] // 4
        chunk = 4
        in_specs = in_specs + [anywhere] * 4 + [local] * 3 + [anywhere] * 6
        last = rows[2].shape[2]
        line, stays = rows[7], rows[9]
        out_specs = [local] * units + [anywhere] * 2 + out_specs
        out_shape = (
            [shape((tokens, feats), F32)] * units + [shape((tokens, 4 * feats), BF16)] * 2 + out_shape
        )
        scratch = scratch + [
            pltpu.VMEM((units, 4, tokens, feats), BF16),
            pltpu.VMEM((2, units, 3, tokens, feats), BF16),
            sems((units, 4)),
            sems((2, units, 3, chunk)),
            sems((2, units, 3, chunk)),
            pltpu.VMEM((2, 2, last, feats), BF16),
            pltpu.VMEM((2, 2, last, feats), BF16),
            pltpu.VMEM((2, last, feats), BF16),
            pltpu.VMEM((2, tokens, feats), BF16),
            sems((2,)),
            sems((2, 2, 3, chunk)),
            sems((2, 2, 3, chunk)),
            sems((2,)),
            sems((2,)),
            sems((2,)),
            sems((2,)),
            sems((2,)),
            sems((2,)),
            pltpu.VMEM((2,) + line.shape[1:], BF16),
            pltpu.VMEM((2,) + line.shape[1:], BF16),
            pltpu.VMEM((2,) + stays.shape, BF16),
            pltpu.VMEM((2,) + stays.shape, BF16),
            pltpu.VMEM((2, 2) + stays.shape[2:], BF16),
            pltpu.VMEM((2,) + rows[11].shape, BF16),
            pltpu.VMEM((2, 4, 2) + stays.shape[2:], BF16),
            pltpu.VMEM((2, 4) + stays.shape[2:], BF16),
            sems((5,)),
            sems((8,)),
            sems((8,)),
        ]
        wide, narrow = line.shape[1:], stays.shape[2:]
        out_specs = out_specs + [local] * 6
        out_shape = out_shape + [
            shape(s, F32) for s in (wide, wide[::-1], narrow, narrow[::-1], narrow, narrow)
        ]
    if spread:
        out_specs = out_specs + [anywhere] * spread
        out_shape = out_shape + [
            shape((w.shape[0] // 4, w.shape[1] * 4), BF16) for w in shards_in[:spread]
        ]
        scratch = scratch + [sems((spread,))] + [sems((spread, 3))] * 2
    results = pl.pallas_call(
        functools.partial(exchange_kernel, units, spread, axes),
        in_specs=in_specs,
        out_specs=out_specs,
        out_shape=out_shape,
        scratch_shapes=scratch,
        compiler_params=pltpu.CompilerParams(
            collective_id=collective_id,
            has_side_effects=True,
            vmem_limit_bytes=(56 if units else 8) * 1024 * 1024,
        ),
        cost_estimate=pl.CostEstimate(
            flops=0, bytes_accessed=(600 if units else 240) * 1024 * 1024, transcendentals=0
        ),
        name="exchange",
    )(*partials, *shards_in, *rows)
    if not units:
        return results
    end = units + 2 + count
    return results[:units], results[units : units + 2], results[units + 2 : end], results[end:]


def head_sum_kernel(members, x_ref, out_ref, slots, send_sem, recv_sem):
    z = lax.axis_index("head")
    barrier = pltpu.get_barrier_semaphore()
    for k in range(1, members):
        pl.semaphore_signal(
            barrier,
            inc=1,
            device_id={"head": lax.rem(z + k, members)},
            device_id_type=pl.DeviceIdType.MESH,
        )
    pl.semaphore_wait(barrier, members - 1)
    copies = []
    for k in range(1, members):
        copy = pltpu.make_async_remote_copy(
            src_ref=x_ref,
            dst_ref=slots.at[z],
            send_sem=send_sem.at[k - 1],
            recv_sem=recv_sem.at[k - 1],
            device_id={"head": lax.rem(z + k, members)},
            device_id_type=pl.DeviceIdType.MESH,
        )
        copy.start()
        copies.append(copy)
    slots[z] = x_ref[...]
    for copy in copies:
        copy.wait()
    total = slots[0]
    for k in range(1, members):
        total = total + slots[k]
    out_ref[...] = total


def head_sum(x, collective_id):
    members = lax.axis_size("head")
    return pl.pallas_call(
        functools.partial(head_sum_kernel, members),
        out_shape=jax.ShapeDtypeStruct(x.shape, F32),
        in_specs=[pl.BlockSpec(memory_space=pltpu.VMEM)],
        out_specs=pl.BlockSpec(memory_space=pltpu.VMEM),
        scratch_shapes=[
            pltpu.VMEM((members,) + x.shape, F32),
            pltpu.SemaphoreType.DMA((members - 1,)),
            pltpu.SemaphoreType.DMA((members - 1,)),
        ],
        compiler_params=pltpu.CompilerParams(collective_id=collective_id, has_side_effects=True),
        name="sum_over_head",
    )(x)


def turn(v, keep, left, right):
    h = ROT // 2
    return v * keep + pltpu.roll(v, HD - h, 1) * left + pltpu.roll(v, h, 1) * right


def rotate_kernel(sign, v_ref, keep_ref, left_ref, right_ref, out_ref):
    for head in range(v_ref.shape[1] // HD):
        part = pl.ds(head * HD, HD)
        out_ref[:, part] = turn(
            v_ref[:, part], keep_ref[...], sign * left_ref[...], sign * right_ref[...]
        ).astype(BF16)


def rotate(values_in, tables, sign):
    tokens, feats = values_in.shape
    block = min(tokens, 256)
    table = pl.BlockSpec((block, HD), lambda i: (i, 0))
    wide = pl.BlockSpec((block, feats), lambda i: (i, 0))
    return pl.pallas_call(
        functools.partial(rotate_kernel, sign),
        grid=(tokens // block,),
        in_specs=[wide, table, table, table],
        out_specs=wide,
        out_shape=jax.ShapeDtypeStruct((tokens, feats), BF16),
        cost_estimate=pl.CostEstimate(
            flops=5 * tokens * feats, bytes_accessed=8 * tokens * feats, transcendentals=0
        ),
        name="rotate_heads",
    )(values_in, *tables)


def feed_kernel(x_ref, d_ref, up_ref, down_ref, gated_ref, d_up_ref, grad_up_ref, grad_down_ref):
    tokens, model_width = x_ref.shape
    step = min(256, tokens)
    for r in range(0, tokens, step):
        rows = slice(r, r + step)
        up_pre = dot(x_ref[rows], up_ref[...])
        d_gated = dot_nt(d_ref[rows], down_ref[...])
        below = 0.5 * (1.0 + lax.erf(up_pre * 0.5**0.5))
        density = jnp.exp(-0.5 * up_pre * up_pre) * (2.0 * jnp.pi) ** -0.5
        gated_ref[rows] = (up_pre * below).astype(BF16)
        d_up_ref[rows] = (d_gated * (below + up_pre * density)).astype(BF16)
    wide = min(512, model_width)
    for c in range(0, model_width, wide):
        part = slice(c, c + wide)
        grad_up_ref[part] = dot_tn(x_ref[:, part], d_up_ref[...]).astype(BF16)
        grad_down_ref[part] = dot_tn(d_ref[:, part], gated_ref[...]).astype(BF16)


def feed_forward(x, d_out, up, down):
    tokens, model_width = x.shape
    hidden = up.shape[1]
    block = min(512, hidden)
    fixed = pl.BlockSpec((tokens, model_width), lambda i: (0, 0), pipeline_mode=pl.Buffered(1))
    narrow = pl.BlockSpec((tokens, block), lambda i: (0, i))
    column = pl.BlockSpec((model_width, block), lambda i: (0, i))
    shape = lambda rows: jax.ShapeDtypeStruct((rows, hidden), BF16)
    return pl.pallas_call(
        feed_kernel,
        grid=(hidden // block,),
        in_specs=[fixed, fixed, column, pl.BlockSpec((block, model_width), lambda i: (i, 0))],
        out_specs=[narrow, narrow, column, column],
        out_shape=[shape(tokens), shape(tokens), shape(model_width), shape(model_width)],
        compiler_params=pltpu.CompilerParams(vmem_limit_bytes=56 * 1024 * 1024),
        cost_estimate=pl.CostEstimate(
            flops=8 * tokens * model_width * hidden,
            bytes_accessed=4 * model_width * (2 * hidden + tokens),
            transcendentals=0,
        ),
        name="feed_forward",
    )(x, d_out, up, down)


def attention_kernel(
    place_ref, q_ref, do_ref, start_ref, valid_ref, keep_ref, left_ref, right_ref, *refs
):
    blocks = (len(refs) - 6) // 2
    k_refs, v_refs = refs[:blocks], refs[blocks : 2 * blocks]
    o_ref, dq_ref, near_ref, beside_ref, s_ref, dp_ref = refs[2 * blocks :]
    grad_ref = lambda j: (beside_ref if j % 2 else near_ref).at[j // 2]
    rows = q_ref.shape[1]
    scale = HD ** (-0.5)
    member = place_ref[0]
    keep, left, right = keep_ref[0], left_ref[0], right_ref[0]
    q = turn(q_ref[0], keep, left, right).astype(BF16)
    d_out = do_ref[0]
    start = start_ref[0]
    top = jnp.full((rows, 1), MASKED, F32)
    t = member * rows + lax.broadcasted_iota(jnp.int32, (rows, rows), 0)
    for j in range(blocks):
        u = place_ref[j] * rows + lax.broadcasted_iota(jnp.int32, (rows, rows), 1)
        allowed = (u <= t) & (u >= start)
        s_ref[j] = jnp.where(allowed, dot_nt(q, k_refs[j][0]) * scale, MASKED)
        top = jnp.maximum(top, jnp.max(s_ref[j], axis=1, keepdims=True))
    total = jnp.zeros((rows, 1), F32)
    for j in range(blocks):
        e = jnp.exp(s_ref[j] - top)
        s_ref[j] = e
        total = total + jnp.sum(e, axis=1, keepdims=True)
    inverse = 1.0 / total
    out = jnp.zeros((rows, HD), F32)
    delta = jnp.zeros((rows, 1), F32)
    for j in range(blocks):
        p = s_ref[j] * inverse
        s_ref[j] = p
        p_bf = p.astype(BF16)
        out = out + dot(p_bf, v_refs[j][0])
        grad_ref(j)[1] = dot_tn(p_bf, d_out).astype(BF16)
        d_p = dot_nt(d_out, v_refs[j][0])
        dp_ref[j] = d_p
        delta = delta + jnp.sum(p * d_p, axis=1, keepdims=True)
    o_ref[0] = (out * valid_ref[0]).astype(BF16)
    d_q = jnp.zeros((rows, HD), F32)
    for j in range(blocks):
        d_s = (s_ref[j] * (dp_ref[j] - delta)).astype(BF16)
        d_q = d_q + dot(d_s, k_refs[j][0])
        grad_ref(j)[0] = (dot_tn(d_s, q) * scale).astype(BF16)
    dq_ref[0] = turn(d_q * scale, keep, -left, -right).astype(BF16)


def attention(index, places, queries, d_attended, starts, valid, tables, keys, values):
    _, rows, feats = queries.shape
    blocks = len(keys)
    tile = pl.BlockSpec((1, rows, HD), lambda h: (index, 0, h))
    fixed = lambda width: pl.BlockSpec((1, rows, width), lambda h: (index, 0, 0))
    out_tile = pl.BlockSpec((1, rows, HD), lambda h: (0, 0, h))
    grad_tile = pl.BlockSpec((blocks // 2, 2, rows, HD), lambda h: (0, 0, 0, h))
    shape = lambda *lead: jax.ShapeDtypeStruct(lead + (rows, feats), BF16)
    return pl.pallas_call(
        attention_kernel,
        grid=(feats // HD,),
        in_specs=[pl.BlockSpec(memory_space=pltpu.SMEM), tile, tile]
        + [fixed(1)] * 2
        + [fixed(HD)] * 3
        + [tile] * (2 * blocks),
        out_specs=[out_tile] * 2 + [grad_tile] * 2,
        out_shape=[shape(1)] * 2 + [shape(blocks // 2, 2)] * 2,
        scratch_shapes=[
            pltpu.VMEM((blocks, rows, rows), F32),
            pltpu.VMEM((blocks, rows, rows), F32),
        ],
        compiler_params=pltpu.CompilerParams(vmem_limit_bytes=40 * 1024 * 1024),
        cost_estimate=pl.CostEstimate(
            flops=6 * feats * rows * rows * blocks,
            bytes_accessed=rows * feats * 2 * (4 + 4 * blocks),
            transcendentals=0,
        ),
        name="attention_both_ways",
    )(places, queries, d_attended, starts, valid, *tables, *keys, *values)


def exchange_rows(local):
    if lax.axis_size("stream") != 4:
        raise ValueError("stream")
    across = lax.ppermute(local, "stream", [(0, 2), (1, 3)])
    beside = over_core(local)
    return (local, beside, across, over_core(across))


def add_f32(a, b):
    return a.astype(F32) + b.astype(F32)


def over_line(a):
    return lax.ppermute(a, "stream", [(2, 0), (3, 1)])


def columns_of(pieces, rows):
    lane = lax.broadcasted_iota(jnp.int32, (rows, 128), 1)
    out = jnp.zeros((rows, 128), F32)
    for index, piece in enumerate(pieces):
        out = jnp.where(lane == index, piece, out)
    return out


def row_sum(a):
    return jnp.sum(a, axis=1, keepdims=True)


def streams_kernel(weights_ref, history_ref, streams_ref, stats_ref):
    weights = weights_ref[...]
    layers = [history_ref[j].astype(F32) for j in range(HIST)]
    sums, squares = [], []
    for s in range(4):
        total = weights[:, s * HIST : s * HIST + 1] * layers[0]
        for j in range(1, HIST):
            total = total + weights[:, s * HIST + j : s * HIST + j + 1] * layers[j]
        streams_ref[s] = total
        sums.append(row_sum(total))
        squares.append(row_sum(total * total))
    stats_ref[...] = columns_of(sums + squares, weights.shape[0]).T[:8]


def mix_streams(weights, history):
    _, tokens, feats = history.shape
    block = min(128, tokens)
    return pl.pallas_call(
        streams_kernel,
        grid=(tokens // block,),
        in_specs=[
            pl.BlockSpec((block, weights.shape[1]), lambda i: (i, 0)),
            pl.BlockSpec((HIST, block, feats), lambda i: (0, i, 0)),
        ],
        out_specs=[
            pl.BlockSpec((4, block, feats), lambda i: (0, i, 0)),
            pl.BlockSpec((8, block), lambda i: (0, i)),
        ],
        out_shape=[
            jax.ShapeDtypeStruct((4, tokens, feats), F32),
            jax.ShapeDtypeStruct((8, tokens), F32),
        ],
        compiler_params=pltpu.CompilerParams(vmem_limit_bytes=40 * 1024 * 1024),
        cost_estimate=pl.CostEstimate(
            flops=80 * tokens * feats, bytes_accessed=34 * tokens * feats, transcendentals=0
        ),
        name="mix_streams",
    )(weights, history)


def early_kernel(streams_ref, cot_ref, history_ref, out_ref):
    cot = cot_ref[...].astype(F32)
    plain, crossed, direct = [], [], []
    layers = [history_ref[j].astype(F32) for j in range(HIST)]
    for layer in layers:
        plain.append(row_sum(layer))
        direct.append(row_sum(cot * layer))
    for s in range(4):
        for layer in layers:
            crossed.append(row_sum(streams_ref[s] * layer))
    out_ref[...] = columns_of(crossed + plain + direct, cot.shape[0]).T[:64].astype(BF16)


def early_sums(streams, cot, history):
    _, tokens, feats = streams.shape
    block = min(128, tokens)
    return pl.pallas_call(
        early_kernel,
        grid=(tokens // block,),
        in_specs=[
            pl.BlockSpec((4, block, feats), lambda i: (0, i, 0)),
            pl.BlockSpec((block, feats), lambda i: (i, 0)),
            pl.BlockSpec((HIST, block, feats), lambda i: (0, i, 0)),
        ],
        out_specs=pl.BlockSpec((64, block), lambda i: (0, i)),
        out_shape=jax.ShapeDtypeStruct((64, tokens), BF16),
        compiler_params=pltpu.CompilerParams(vmem_limit_bytes=40 * 1024 * 1024),
        cost_estimate=pl.CostEstimate(
            flops=110 * tokens * feats, bytes_accessed=36 * tokens * feats, transcendentals=0
        ),
        name="early_sums",
    )(streams, cot, history)


def sums_kernel(
    g0, g1, g2, g3, streams_ref, stats_ref, gain_ref, history_ref, dots_ref, out_ref, edge_ref
):
    stats = stats_ref[...]
    rows = stats.shape[0]

    @pl.when(pl.program_id(0) == 0)
    def _():
        edge_ref[...] = jnp.zeros_like(edge_ref)

    firsts, seconds, dots = [], [], []
    for s, g_ref in enumerate((g0, g1, g2, g3)):
        g = g_ref[...].astype(F32)
        centered = (streams_ref[s] - stats[:, s : s + 1]) * stats[:, 4 + s : 5 + s]
        edge_ref[s : s + 1] += jnp.sum(g * centered, axis=0, keepdims=True)
        edge_ref[4 + s : 5 + s] += jnp.sum(g, axis=0, keepdims=True)
        scaled = g * gain_ref[s : s + 1]
        firsts.append(row_sum(scaled))
        seconds.append(row_sum(scaled * centered))
        for j in range(HIST):
            dots.append(row_sum(scaled * history_ref[j].astype(F32)))
    dots_ref[...] = columns_of(dots, rows).T[:48].astype(BF16)
    out_ref[...] = columns_of(firsts + seconds, rows).T[:8]


def gradient_sums(grads, streams, stats, gain, history):
    _, tokens, feats = streams.shape
    block = min(128, tokens)
    wide = pl.BlockSpec((block, feats), lambda i: (i, 0))
    return pl.pallas_call(
        sums_kernel,
        grid=(tokens // block,),
        in_specs=[wide] * 4
        + [
            pl.BlockSpec((4, block, feats), lambda i: (0, i, 0)),
            pl.BlockSpec((block, 8), lambda i: (i, 0)),
            pl.BlockSpec((4, feats), lambda i: (0, 0)),
            pl.BlockSpec((HIST, block, feats), lambda i: (0, i, 0)),
        ],
        out_specs=[
            pl.BlockSpec((48, block), lambda i: (0, i)),
            pl.BlockSpec((8, block), lambda i: (0, i)),
            pl.BlockSpec((8, feats), lambda i: (0, 0)),
        ],
        out_shape=[
            jax.ShapeDtypeStruct((48, tokens), BF16),
            jax.ShapeDtypeStruct((8, tokens), F32),
            jax.ShapeDtypeStruct((8, feats), F32),
        ],
        compiler_params=pltpu.CompilerParams(vmem_limit_bytes=40 * 1024 * 1024),
        cost_estimate=pl.CostEstimate(
            flops=110 * tokens * feats, bytes_accessed=42 * tokens * feats, transcendentals=0
        ),
        name="gradient_sums",
    )(*grads, streams, stats, gain, history)


def small_kernel(
    members,
    plane,
    dots_ref,
    sums_ref,
    early_in,
    stats_ref,
    pre_ref,
    slope_ref,
    hidden_ref,
    rms_ref,
    w_ref,
    current_ref,
    edge_ref,
    small_ref,
    scaled_ref,
    coef_ref,
    dot_slots,
    early_slots,
    slots,
    got,
    d_mix_ref,
    early_ref,
    rows_ref,
    dot_send,
    dot_recv,
    early_send,
    early_recv,
    send_sem,
    recv_sem,
    plane_send,
    plane_recv,
):
    x, stream, z = lax.axis_index("dp"), lax.axis_index("stream"), lax.axis_index("head")
    line = [{"head": lax.rem(z + k, members)} for k in range(1, members)]
    near = (
        {"stream": stream + 1 - 2 * lax.rem(stream, 2)},
        {"stream": lax.rem(stream + 2, 4)},
        {"dp": 1 - x},
    )
    near = near if plane else ()
    barrier = pltpu.get_barrier_semaphore()
    for peer in line + list(near):
        pl.semaphore_signal(barrier, inc=1, device_id=peer, device_id_type=pl.DeviceIdType.MESH)
    pl.semaphore_wait(barrier, len(line) + len(near))
    copies = []
    for source, target, sends, receives in (
        (dots_ref, dot_slots, dot_send, dot_recv),
        (early_in, early_slots, early_send, early_recv),
        (sums_ref, slots, send_sem, recv_sem),
    ):
        for k, peer in enumerate(line):
            copy = pltpu.make_async_remote_copy(
                src_ref=source,
                dst_ref=target.at[z],
                send_sem=sends.at[k],
                recv_sem=receives.at[k],
                device_id=peer,
                device_id_type=pl.DeviceIdType.MESH,
            )
            copy.start()
            copies.append(copy)
        target[z] = source[...]
    for copy in copies:
        copy.wait()
    total, dots = slots[0], dot_slots[0].astype(F32)
    early_ref[...] = early_slots[0].astype(F32)
    for k in range(1, members):
        early_ref[...] += early_slots[k].astype(F32)
        total = total + slots[k]
        dots = dots + dot_slots[k].astype(F32)
    d_mix_ref[...] = dots[: 4 * HIST]
    n = 4 * HIST
    model_width = members * small_ref.shape[1]
    plain = early_ref[n : n + HIST]
    rows_ref[...] = jnp.zeros_like(rows_ref)
    rows_ref[0:8] = total / model_width
    for s in range(4):
        part = slice(s * HIST, (s + 1) * HIST)
        mean, inverse = stats_ref[s : s + 1], stats_ref[4 + s : 5 + s]
        crossed = (early_ref[part] - mean * plain) * inverse
        d_part = inverse * (
            d_mix_ref[part] - rows_ref[s : s + 1] * plain - rows_ref[4 + s : 5 + s] * crossed
        )
        if s == 3:
            d_part = d_part + early_ref[n + HIST : n + 2 * HIST]
        d_mix_ref[part] = d_part
    d_mix = d_mix_ref[...]
    high = dict(precision=HIGHEST, preferred_element_type=F32)
    d_pre = jnp.dot(w_ref[...], d_mix, **high) * slope_ref[...]
    rms = rms_ref[...]
    cross = jnp.sum(d_pre * pre_ref[...], axis=0, keepdims=True)
    rows_ref[8:9] = rms * rms * cross / model_width
    coef_ref[...] = rows_ref[...].T
    scaled = d_pre * rms
    scaled_ref[...] = scaled
    small_ref[...] = jnp.zeros_like(small_ref)
    small_ref[0:n] = jnp.dot(scaled, current_ref[...].astype(F32), **high)
    small_ref[n : n + 8] = edge_ref[...]
    small_ref[n + 8 : 2 * n + 8, 0:n] = lax.dot_general(
        hidden_ref[...], d_mix, (((1,), (1,)), ((), ())), **high
    )
    small_ref[n + 8 : 2 * n + 8, n : n + 1] = jnp.sum(d_mix, axis=1, keepdims=True)
    for step, peer in enumerate(near):
        copy = pltpu.make_async_remote_copy(
            src_ref=small_ref,
            dst_ref=got.at[step],
            send_sem=plane_send.at[step],
            recv_sem=plane_recv.at[step],
            device_id=peer,
            device_id_type=pl.DeviceIdType.MESH,
        )
        copy.start()
        copy.wait()
        small_ref[...] += got[step]


def small_gradients(dots, sums, early, stats, pre, slope, hidden, rms, w_out, current, edges):
    members, plane = lax.axis_size("head"), paired()
    tokens, feats = current.shape
    n = 4 * HIST
    shape = jax.ShapeDtypeStruct
    sems = pltpu.SemaphoreType.DMA
    small, scaled, coefs = pl.pallas_call(
        functools.partial(small_kernel, members, plane),
        in_specs=[pl.BlockSpec(memory_space=pltpu.VMEM)] * 11,
        out_specs=[pl.BlockSpec(memory_space=pltpu.VMEM)] * 3,
        out_shape=[shape((80, feats), F32), shape((n, tokens), F32), shape((tokens, 128), F32)],
        scratch_shapes=[
            pltpu.VMEM((members, 48, tokens), BF16),
            pltpu.VMEM((members, 64, tokens), BF16),
            pltpu.VMEM((members, 8, tokens), F32),
            pltpu.VMEM((3, 80, feats), F32),
            pltpu.VMEM((n, tokens), F32),
            pltpu.VMEM((64, tokens), F32),
            pltpu.VMEM((128, tokens), F32),
            sems((members - 1,)),
            sems((members - 1,)),
            sems((members - 1,)),
            sems((members - 1,)),
            sems((members - 1,)),
            sems((members - 1,)),
            sems((3,)),
            sems((3,)),
        ],
        compiler_params=pltpu.CompilerParams(
            collective_id=3, has_side_effects=True, vmem_limit_bytes=40 * 1024 * 1024
        ),
        name="small_gradients",
    )(dots, sums, early, stats, pre, slope, hidden, rms, w_out, current, edges)
    if not plane:
        small = lax.psum(small.astype(BF16), ("dp", "stream")).astype(F32)
    return small, scaled, coefs


def history_kernel(
    g0, g1, g2, g3, streams_ref, stats_ref, gain_ref, cot_ref, current_ref, weights_ref, coef_ref, d_ref, w_ref, out_ref
):
    stats, weights, coefs = stats_ref[...], weights_ref[...], coef_ref[...]
    d_streams = []
    for s, g_ref in enumerate((g0, g1, g2, g3)):
        inverse = stats[:, 4 + s : 5 + s]
        centered = (streams_ref[s] - stats[:, s : s + 1]) * inverse
        scaled = g_ref[...].astype(F32) * gain_ref[s : s + 1]
        d_streams.append(
            inverse * (scaled - coefs[:, s : s + 1] - centered * coefs[:, 4 + s : 5 + s])
        )
    d_streams[3] = d_streams[3] + cot_ref[...].astype(F32)
    for j in range(HIST):
        total = weights[:, j : j + 1] * d_streams[0]
        for s in range(1, 4):
            total = total + weights[:, s * HIST + j : s * HIST + j + 1] * d_streams[s]
        if j == HIST - 1:
            total = total + lax.dot_general(
                d_ref[...],
                w_ref[...],
                (((0,), (0,)), ((), ())),
                precision=HIGHEST,
                preferred_element_type=F32,
            )
            total = total - current_ref[...].astype(F32) * coefs[:, 8:9]
        out_ref[j] = total


def history_gradient(grads, streams, stats, gain, cot, current, weights, coefs, d_scaled, w_rows):
    _, tokens, feats = streams.shape
    block = min(128, tokens)
    wide = pl.BlockSpec((block, feats), lambda i: (i, 0))
    narrow = lambda a: pl.BlockSpec((block, a.shape[1]), lambda i: (i, 0))
    fixed = lambda a: pl.BlockSpec(a.shape, lambda i: (0, 0))
    return pl.pallas_call(
        history_kernel,
        grid=(tokens // block,),
        in_specs=[wide] * 4
        + [
            pl.BlockSpec((4, block, feats), lambda i: (0, i, 0)),
            narrow(stats),
            fixed(gain),
            wide,
            wide,
            narrow(weights),
            narrow(coefs),
            pl.BlockSpec((d_scaled.shape[0], block), lambda i: (0, i)),
            fixed(w_rows),
        ],
        out_specs=pl.BlockSpec((HIST, block, feats), lambda i: (0, i, 0)),
        out_shape=jax.ShapeDtypeStruct((HIST, tokens, feats), F32),
        compiler_params=pltpu.CompilerParams(vmem_limit_bytes=40 * 1024 * 1024),
        cost_estimate=pl.CostEstimate(
            flops=110 * tokens * feats, bytes_accessed=64 * tokens * feats, transcendentals=0
        ),
        name="history_gradient",
    )(*grads, streams, stats, gain, cot, current, weights, coefs, d_scaled, w_rows)


def shards(
    history,
    seq_lens,
    bucket_slot,
    w_mix_in,
    w_mix_out,
    mix_bias,
    ln_gain,
    ln_bias,
    w_qkv,
    w_attn_out,
    w_up,
    w_down,
    cotangent,
):
    member = lax.axis_index("stream")
    micro, quarter, feats = history.shape[1:]
    tokens = micro * quarter
    model_width = feats * lax.axis_size("head")
    slot_base = lax.axis_index("dp") * micro
    slot_ids = jnp.arange(bucket_slot.shape[0], dtype=jnp.int32)
    query_places = member * quarter + jnp.arange(quarter, dtype=jnp.int32)
    w_mix_in_f = w_mix_in.astype(F32)
    w_mix_out_f = w_mix_out.astype(F32)

    segments, starts = [], []
    for index in range(micro):
        bucket = jnp.sum(jnp.where(slot_ids == slot_base + index, bucket_slot, 0))
        lengths = jnp.sum(jnp.where(slot_ids[:, None] == bucket, seq_lens, 0), axis=0)
        bounds = jnp.cumsum(lengths)
        passed = (query_places[:, None] >= bounds[None, :]).astype(jnp.int32)
        segments.append(jnp.sum(passed, axis=1))
        starts.append(jnp.sum(passed * lengths[None, :], axis=1))
    valid = (jnp.concatenate(segments) < 3).astype(F32)[:, None]
    starts = jnp.concatenate(starts)
    position = jnp.tile(query_places, micro) - starts
    frequency = jnp.arange(ROT // 2, dtype=F32)
    phases = position.astype(F32)[:, None] * (10000.0 ** (-2.0 * frequency / ROT))
    cosine, sine = jnp.cos(phases), jnp.sin(phases)
    plain = jnp.zeros((tokens, HD - ROT), F32)
    none = jnp.zeros_like(sine)
    tables = (
        jnp.concatenate([cosine, cosine, plain + 1.0], axis=1),
        jnp.concatenate([-sine, none, plain], axis=1),
        jnp.concatenate([none, sine, plain], axis=1),
    )

    cot_rows = cotangent.reshape(tokens, feats).astype(F32) * valid
    cot_bf = cot_rows.astype(BF16)
    duplex = lined()

    history = history.reshape(HIST, tokens, feats)
    current = history[HIST - 1]
    current_f = current.astype(F32)
    mixed = lax.dot_general(w_mix_in, current, (((0,), (1,)), ((), ())), preferred_element_type=F32)
    square = jnp.sum(current_f * current_f, axis=1)[None]
    mixed = head_sum(jnp.concatenate([mixed, square]), 0).T
    mixed, cot_bf, w_up = lax.optimization_barrier((mixed, cot_bf, w_up))
    out_full = lax.all_gather(cot_bf, "head", axis=1, tiled=True)
    if duplex:
        (up_full,) = exchange([], (), [w_up], (0,), 4)
        mixed, up_full = lax.optimization_barrier((mixed, up_full))
    rms_scale = lax.rsqrt(mixed[:, 4 * HIST :] / model_width + EPSILON)
    mix_pre = mixed[:, : 4 * HIST] * rms_scale
    below_mix = 0.5 * (1.0 + lax.erf(mix_pre * 0.5**0.5))
    mix_hidden = gelu_exact(mix_pre)
    slope_mix = below_mix + mix_pre * jnp.exp(-0.5 * mix_pre * mix_pre) * (2.0 * jnp.pi) ** -0.5
    mix_weights = jnp.dot(mix_hidden, w_mix_out_f, precision=HIGHEST) + mix_bias.reshape(-1)
    streams, stats = mix_streams(mix_weights, history)
    stats = head_sum(stats, 1)
    stat_sum, stat_square = stats[:4], stats[4:]
    row_means = (stat_sum / model_width)[:, :, None]
    inv_std = lax.rsqrt(stat_square[:, :, None] / model_width - row_means * row_means + EPSILON)
    centered = (streams - row_means) * inv_std
    row_stats = jnp.concatenate([row_means[..., 0], inv_std[..., 0]]).T
    normed = (centered * ln_gain[:, None, :] + ln_bias[:, None, :]).astype(BF16)

    def all_features(a):
        return lax.all_gather(a, "head", axis=1, tiled=True)

    if duplex:
        w_down, normed = lax.optimization_barrier((w_down, normed))
        wk, wv, down_full, w_out_full, wq, *shares = exchange(
            [], (), [w_qkv[1], w_qkv[2], w_down, w_attn_out, w_qkv[0]], (0, 0, 1, 1, 0), 6, 2
        )
    else:
        wq, wk, wv = gather_weight(w_qkv, 1)
        w_out_full, down_full = gather_weight(w_attn_out, 1), gather_weight(w_down, 1)
        up_full = gather_weight(w_up, 0)

    def to_owner(partial):
        return lax.psum_scatter(
            partial.astype(BF16), "head", scatter_dimension=1, tiled=True
        ).astype(F32)

    up_out, out_full = lax.optimization_barrier((normed[3], out_full))
    up_in, k_out, down_full = lax.optimization_barrier(
        (all_features(up_out), normed[1], down_full)
    )
    k_in, v_out = lax.optimization_barrier((all_features(k_out), normed[2]))
    gated_up, d_up, product_up, product_down = feed_forward(up_in, out_full, up_full, down_full)
    feed_products = [product_up[None], product_down[None]]
    feed_parts = [chip_parts(a) if paired() else a for a in feed_products]
    v_out, d_up, feed_parts = lax.optimization_barrier((v_out, d_up, feed_parts))
    feed_lines = [line_parts(*a) for a in feed_parts] if paired() else feed_parts
    streams_late, feed_lines[0] = lax.optimization_barrier((streams, feed_lines[0]))
    early = early_sums(streams_late, cot_bf, history)
    feed = dot(gated_up, down_full).astype(BF16)
    d_attended = dot_nt(out_full, w_out_full).astype(BF16) * valid.astype(BF16)
    d_up_in = dot_nt(d_up, up_full).astype(BF16)
    keys = rotate(dot(k_in, wk), tables, 1.0)
    v_in, q_out, early, feed, d_attended, d_up_in, keys, wk, wv = lax.optimization_barrier(
        (all_features(v_out), normed[0], early, feed, d_attended, d_up_in, keys, wk, wv)
    )
    values = dot(v_in, wv).astype(BF16)
    by_micro = lambda a: a.reshape((micro, quarter) + a.shape[1:])
    key_blocks = exchange_rows(by_micro(keys))
    value_blocks = exchange_rows(by_micro(values))
    q_in, d_up_in, key_blocks, value_blocks, feed_lines[1], early = lax.optimization_barrier(
        (all_features(q_out), d_up_in, key_blocks, value_blocks, feed_lines[1], early)
    )
    g_up = to_owner(d_up_in)
    product = lambda a, b: dot_tn(a, b).astype(BF16)

    queries = dot(q_in, wq)
    places = member ^ jnp.arange(4, dtype=jnp.int32)
    attended, d_query_pre, d_rows = [], [], []
    queries = by_micro(queries)
    for index in range(micro):
        results = attention(
            index,
            places,
            queries,
            by_micro(d_attended),
            by_micro(starts[:, None]),
            by_micro(valid),
            tuple(by_micro(a) for a in tables),
            key_blocks,
            value_blocks,
        )
        attended.append(results[0][0])
        d_query_pre.append(results[1][0])
        if duplex and index == micro - 1:
            continue
        chip = add_f32(results[2], over_core(results[3]))
        across = chip[1].astype(BF16)
        queries, across = lax.optimization_barrier((queries, across))
        d_rows.append(add_f32(chip[0], over_line(across)))
    attended, d_query_pre = jnp.concatenate(attended), jnp.concatenate(d_query_pre)
    d_key_rows = jnp.concatenate([a[0] for a in d_rows])
    done = d_key_rows.shape[0]
    d_key_rows = rotate(d_key_rows, tuple(a[:done] for a in tables), -1.0)
    d_value_rows = jnp.concatenate([a[1] for a in d_rows]).astype(BF16)
    attended, d_query_pre, d_key_rows, d_value_rows = lax.optimization_barrier(
        (attended, d_query_pre, d_key_rows, d_value_rows)
    )

    products = jnp.stack([product(q_in, d_query_pre), product(out_full, attended)])
    if duplex:
        partials = [dot_nt(d_query_pre, wq).astype(BF16)]
        parts = chip_parts(products)
        partials, parts, g_up, feed_lines = lax.optimization_barrier(
            (partials, parts, g_up, feed_lines)
        )
        (g_query,), (d_key_full, d_value_full), (wk_rows, wv_rows), plane_grads = exchange(
            partials,
            [d_key_rows, d_value_rows, results[2], results[3], *(a[done:] for a in tables)]
            + [a[0] for a in feed_lines]
            + [*parts, k_in, v_in],
            shares,
            (0, 0),
            5,
        )
        attended_late, g_query = lax.optimization_barrier((attended, g_query))
        pair = lambda a: (a[: tokens // 2], a[tokens // 2 :])
        halves = [
            (dot(a, w_out_full) + b).astype(BF16) for a, b in zip(pair(attended_late), pair(feed))
        ]
        branch = to_owner(halves[0])
        g_key, g_value = dot_nt(d_key_full, wk_rows), dot_nt(d_value_full, wv_rows)
    else:
        g_query = to_owner(dot_nt(d_query_pre, wq))
        branch = to_owner(dot(attended, w_out_full) + feed)
        terms = scatter_parts(products)
        feed_terms = [scatter_parts(a) for a in feed_products]
        g_key = to_owner(dot_nt(d_key_rows, wk))
        g_value = to_owner(dot_nt(d_value_rows, wv))
        kv_terms = scatter_parts(
            jnp.stack([product(k_in, d_key_rows), product(v_in, d_value_rows)])
        )
    grads = (g_query, g_key, g_value, g_up)
    dots, sums, edges = gradient_sums(grads, streams, row_stats, ln_gain, history)
    if duplex:
        grad_up, grad_down, grad_query, grad_attn_out, grad_key, grad_value = plane_grads
        grad_qkv = jnp.stack([grad_query, grad_key, grad_value])
    else:
        grad_up = add_terms(feed_terms[0][0][0], feed_terms[0][1][0], False)
        grad_down = add_terms(feed_terms[1][0][0], feed_terms[1][1][0], True)
        grad_attn_out = add_terms(terms[0][1], terms[1][1], True)
        grad_qkv = jnp.concatenate([add_f32(terms[0][:1], terms[1][:1]), add_f32(*kv_terms)])
    small, d_scaled, coefs = small_gradients(
        dots, sums, early, row_stats.T, mix_pre.T, slope_mix.T, mix_hidden.T, rms_scale.T, w_mix_out_f, current, edges
    )
    if duplex:
        coefs, second_half = lax.optimization_barrier((coefs, halves[1]))
        branch = jnp.concatenate([branch, to_owner(second_half)])
    block_out = (valid * (streams[3] + branch)).astype(BF16)
    history_grad = history_gradient(
        grads, streams, row_stats, ln_gain, cot_bf, current, mix_weights, coefs, d_scaled, w_mix_in_f.T
    ).reshape(HIST, micro, quarter, feats)
    n = 4 * HIST
    return (
        block_out.reshape(micro, quarter, feats),
        mix_weights.reshape(micro, quarter, 4 * HIST),
        history_grad,
        small[:n].T,
        small[n + 8 : 2 * n + 8, :n],
        small[n + 8 : 2 * n + 8, n].reshape(mix_bias.shape),
        small[n : n + 4],
        small[n + 4 : n + 8],
        grad_qkv,
        grad_attn_out,
        grad_up,
        grad_down,
    )


def solution(mesh):
    return jax.shard_map(
        shards,
        mesh=mesh,
        in_specs=(
            P(None, "dp", "stream", "head"),
            P(),
            P(),
            P("head", None),
            P(),
            P(),
            P(None, "head"),
            P(None, "head"),
            P(None, ("dp", "stream"), "head"),
            P("head", ("dp", "stream")),
            P(("dp", "stream"), "head"),
            P("head", ("dp", "stream")),
            P("dp", "stream", "head"),
        ),
        out_specs=(
            P("dp", "stream", "head"),
            P("dp", "stream", None),
            P(None, "dp", "stream", "head"),
            P("head", None),
            P(),
            P(),
            P(None, "head"),
            P(None, "head"),
            P(None, ("dp", "stream"), "head"),
            P("head", ("dp", "stream")),
            P(("dp", "stream"), "head"),
            P("head", ("dp", "stream")),
        ),
        check_vma=False,
    )
```

```python
import functools

import jax
import jax.numpy as jnp
from jax import lax
from jax.experimental import pallas as pl
from jax.experimental.pallas import tpu as pltpu
from jax.sharding import PartitionSpec as P

HD = 128
HIST = 9
ROT = 32

EPSILON = 1e-05
HIGHEST = lax.Precision.HIGHEST
MASKED = -1e30
F32 = jnp.float32
BF16 = jnp.bfloat16
VMEM_LIMIT = 60 * 1024 * 1024

SWAP_X = [(0, 1), (1, 0)]
SWAP_Y = [(0, 2), (2, 0), (1, 3), (3, 1)]
SWAP_CORE = [(0, 1), (1, 0), (2, 3), (3, 2)]


def dot(a, b):
    return jnp.dot(a, b, preferred_element_type=F32)


def dot_nt(a, b):
    return lax.dot_general(a, b, (((1,), (1,)), ((), ())), preferred_element_type=F32)


def dot_tn(a, b):
    return lax.dot_general(a, b, (((0,), (0,)), ((), ())), preferred_element_type=F32)


def gelu_exact(values_in):
    return jax.nn.gelu(values_in, approximate=False)


def over_x(a):
    return lax.ppermute(a, "dp", SWAP_X)


def over_y(a):
    return lax.ppermute(a, "stream", SWAP_Y)


def over_core(a):
    return lax.ppermute(a, "stream", SWAP_CORE)


def paired():
    return lax.axis_size("dp") == 2 and lax.axis_size("stream") == 4


def gather_weight(shard, axis):
    return lax.all_gather(shard, ("dp", "stream"), axis=axis, tiled=True)


def lined():
    return paired() and lax.axis_size("head") == 4


def take(a, index, axis):
    return lax.dynamic_index_in_dim(a, index, axis, keepdims=False)


def add_bf(a, b):
    return (a.astype(F32) + b.astype(F32)).astype(BF16)


def chip_parts(partial):
    count, rows, columns = partial.shape
    core, x = lax.axis_index("stream") % 2, lax.axis_index("dp")
    split = partial.reshape(count, 4, 2, rows // 8, columns)
    chip = add_bf(take(split, core, 2), over_core(take(split, 1 - core, 2)))
    chip = chip.reshape(count, 2, 2, rows // 8, columns)
    return take(chip, x, 1), take(chip, 1 - x, 1)


def line_parts(stays, leaves):
    return add_bf(stays, over_x(leaves))


def last_parts(line):
    y = lax.axis_index("stream") // 2
    return take(line, y, 1), over_y(take(line, 1 - y, 1))


def plane_parts(stays, leaves):
    return last_parts(line_parts(stays, leaves))


def scatter_parts(partial):
    if not paired():
        whole = lax.psum_scatter(partial, ("dp", "stream"), scatter_dimension=1, tiled=True)
        return whole, jnp.zeros_like(whole)
    return plane_parts(*chip_parts(partial))


def add_kernel(turned, a_ref, b_ref, out_ref):
    total = a_ref[...].astype(F32) + b_ref[...].astype(F32)
    out_ref[...] = total.T if turned else total


def add_terms(a, b, turned):
    rows, columns = a.shape
    block = min(512, columns)
    return pl.pallas_call(
        functools.partial(add_kernel, turned),
        grid=(columns // block,),
        in_specs=[pl.BlockSpec((rows, block), lambda i: (0, i))] * 2,
        out_specs=pl.BlockSpec((block, rows), lambda i: (i, 0))
        if turned
        else pl.BlockSpec((rows, block), lambda i: (0, i)),
        out_shape=jax.ShapeDtypeStruct((columns, rows) if turned else (rows, columns), F32),
        cost_estimate=pl.CostEstimate(
            flops=rows * columns, bytes_accessed=8 * rows * columns, transcendentals=0
        ),
        name="add_terms",
    )(a, b)


def exchange_kernel(units, spread, axes, *refs):
    count, whole = len(axes), 2 if units else 0
    inputs, refs = refs[: units + count], refs[units + count :]
    partials, shard_refs = inputs[:units], inputs[units:]
    if units:
        done_in, near_in, beside_in = refs[:2], refs[2], refs[3]
        keep_ref, left_ref, right_ref = refs[4:7]
        lines_in, stays_in, leaves_in, streams_in = refs[7:9], refs[9], refs[10], refs[11:13]
        refs = refs[13:]
    outputs, refs = refs[: units + whole + count], refs[units + whole + count :]
    outs, wides, fulls = outputs[:units], outputs[units : units + whole], outputs[units + whole :]
    shares, refs = refs[:spread], refs[spread:]
    if units:
        grad_refs, refs = refs[:6], refs[6:]
    own_sem, near_send, near_recv = refs[:3]
    if units:
        held, got, load_sem, send_sem, recv_sem = refs[3:8]
        mine, theirs, below, pieces, piece_own, piece_send, piece_recv = refs[8:15]
        mine_sem, done_sem, core_send, core_recv, y_send, y_recv = refs[15:21]
        feed_own, feed_got, pair_own, pair_x, pair_y, wide_in, full_grad, from_core = refs[21:29]
        job_load, job_send, job_recv = refs[29:]
    x, stream, z = lax.axis_index("dp"), lax.axis_index("stream"), lax.axis_index("head")
    core = lax.rem(stream, 2)
    other_x, other_y, other_core = 1 - x, lax.rem(stream + 2, 4), stream + 1 - 2 * core
    line = ({"head": lax.rem(z + 1, 4)}, {"head": lax.rem(z + 3, 4)})
    to_x, to_y, to_core = {"dp": other_x}, {"stream": other_y}, {"stream": other_core}
    place = x * 4 + stream
    place_x, place_y = other_x * 4 + stream, x * 4 + other_y
    place_far = other_x * 4 + other_y
    beside = lambda at: at + 1 - 2 * core

    barrier = pltpu.get_barrier_semaphore()
    peers = (line if units or spread else ()) + ((to_x, to_y, to_core) if count else ())
    peers = peers + (({"head": lax.rem(z + 2, 4)},) if spread else ())
    for peer in peers:
        pl.semaphore_signal(barrier, inc=1, device_id=peer, device_id_type=pl.DeviceIdType.MESH)
    pl.semaphore_wait(barrier, len(peers))

    def region(w, at, part=None):
        full, width = fulls[w], shard_refs[w].shape[min(axes[w], 1)]
        rows, columns = shard_refs[w].shape
        start, size = (0, rows) if part is None else (part * (rows // 2), rows // 2)
        if axes[w] == 0:
            return full.at[pl.ds(pl.multiple_of(at * width + start, size), size)]
        column = at * width
        if axes[w] == 2:
            start = lax.rem(at, 2) * rows + start
            start, column = pl.multiple_of(start, size), lax.div(at, 2) * width
        return full.at[pl.ds(start, size), pl.ds(pl.multiple_of(column, width), width)]

    def near(w, index, source, target, peer):
        return pltpu.make_async_remote_copy(
            src_ref=source,
            dst_ref=target,
            send_sem=near_send.at[w, index],
            recv_sem=near_recv.at[w, index],
            device_id=peer,
            device_id_type=pl.DeviceIdType.MESH,
        )

    def pass_on(w, index, at, peer, part=None):
        return near(w, index, region(w, at, part), region(w, at, part), peer)

    def first(w):
        target = region(w, place)
        pltpu.make_async_copy(shard_refs[w], target, own_sem.at[w]).start()
        for index, peer in enumerate((to_x, to_y, to_core)):
            near(w, index, shard_refs[w], target, peer).start()

    def second(w):
        pass_on(w, 0, place_x, to_x).wait_recv()
        pass_on(w, 4, place_x, to_y, 0).start()
        pass_on(w, 3, place_x, to_core).start()
        pass_on(w, 1, place_y, to_y).wait_recv()
        pass_on(w, 6, place_y, to_x, 1).start()
        pass_on(w, 5, place_y, to_core).start()

    def third(w):
        pass_on(w, 4, place_far, to_y, 0).wait_recv()
        pass_on(w, 7, place_far, to_core, 0).start()
        pass_on(w, 6, place_far, to_x, 1).wait_recv()
        pass_on(w, 8, place_far, to_core, 1).start()

    def last(w):
        for index, at, part in (
            (2, place, None),
            (3, place_x, None),
            (5, place_y, None),
            (7, place_far, 0),
            (8, place_far, 1),
        ):
            pass_on(w, index, beside(at), to_core, part).wait_recv()
        pltpu.make_async_copy(shard_refs[w], region(w, place), own_sem.at[w]).wait()
        for index in (0, 1, 2):
            near(w, index, shard_refs[w], region(w, place), to_core).wait_send()
        for index, at, part in (
            (3, place_x, None),
            (4, place_x, 0),
            (5, place_y, None),
            (6, place_y, 1),
            (7, place_far, 0),
            (8, place_far, 1),
        ):
            pass_on(w, index, at, to_core, part).wait_send()

    for w in range(count):
        first(w)
    if not units:
        moves = []
        for i in range(spread):
            second(i)
        for i in range(spread):
            third(i)
        for i in range(spread):
            last(i)
            spread_own, spread_send, spread_recv = refs[3:6]
            rows, columns = shares[i].shape[0], fulls[i].shape[1]
            target = shares[i].at[:, pl.ds(pl.multiple_of(z * columns, columns), columns)]

            def source(at):
                start = (at * 8 + place) * rows
                return fulls[i].at[pl.ds(pl.multiple_of(start, rows), rows)]

            moves.append(pltpu.make_async_copy(source(z), target, spread_own.at[i]))
            for k in range(1, 4):
                to = lax.rem(z + k, 4)
                moves.append(
                    pltpu.make_async_remote_copy(
                        src_ref=source(to),
                        dst_ref=target,
                        send_sem=spread_send.at[i, k - 1],
                        recv_sem=spread_recv.at[i, k - 1],
                        device_id={"head": to},
                        device_id_type=pl.DeviceIdType.MESH,
                    )
                )
        for move in moves:
            move.start()
        for w in range(spread, count):
            second(w)
        for w in range(spread, count):
            third(w)
        for w in range(spread, count):
            last(w)
        for move in moves:
            move.wait()
        return

    feats = held.shape[-1]
    chunk = send_sem.shape[-1]
    tokens = held.shape[2]
    step_rows = tokens // chunk
    y = lax.div(stream, 2)

    def load(u, b):
        return pltpu.make_async_copy(
            partials[u].at[:, b * feats : (b + 1) * feats], held.at[u, b], load_sem.at[u, b]
        )

    def to_beside(v):
        return pltpu.make_async_remote_copy(
            src_ref=beside_in.at[:, v],
            dst_ref=theirs.at[v],
            send_sem=core_send.at[v],
            recv_sem=core_recv.at[v],
            device_id=to_core,
            device_id_type=pl.DeviceIdType.MESH,
        )

    def load_done(v):
        return pltpu.make_async_copy(
            done_in[v], pieces.at[v, pl.ds(0, done_in[v].shape[0])], done_sem.at[v]
        )

    def load_mine(v):
        return pltpu.make_async_copy(near_in.at[:, v], mine.at[v], mine_sem.at[v])

    def to_below(v):
        return pltpu.make_async_remote_copy(
            src_ref=mine.at[v, 1],
            dst_ref=below.at[v],
            send_sem=y_send.at[v],
            recv_sem=y_recv.at[v],
            device_id=to_y,
            device_id_type=pl.DeviceIdType.MESH,
        )

    for v in range(2):
        to_beside(v).start()
        load_mine(v).start()
        load_done(v).start()
    for u in range(units):
        for b in range(4):
            load(u, b).start()
    for u in range(units):
        for b in range(4):
            load(u, b).wait()

    def columns(block):
        return pl.ds(pl.multiple_of(block * feats, feats), feats)

    def part(c):
        return pl.ds(pl.multiple_of(c * step_rows, step_rows), step_rows)

    def hop(way, u, step, block, c):
        return pltpu.make_async_remote_copy(
            src_ref=held.at[u, block, part(c)],
            dst_ref=got.at[way, u, step, part(c)],
            send_sem=send_sem.at[way, u, step, c],
            recv_sem=recv_sem.at[way, u, step, c],
            device_id=line[way],
            device_id_type=pl.DeviceIdType.MESH,
        )

    ways = ((0, z), (1, 3 - z))

    def relay(way, v, step, block, c):
        target = wides[v].at[part(c), columns(block)]
        return pltpu.make_async_remote_copy(
            src_ref=pieces.at[v, part(c)] if step == 0 else target,
            dst_ref=target,
            send_sem=piece_send.at[way, v, step, c],
            recv_sem=piece_recv.at[way, v, step, c],
            device_id=line[way],
            device_id_type=pl.DeviceIdType.MESH,
        )

    def piece_at(way, step):
        return z - step if way == 0 else z + step

    def block_at(way, step):
        return 3 - step + z if way == 0 else step + z - 3

    def keep(v):
        return pltpu.make_async_copy(pieces.at[v], wides[v].at[:, columns(z)], piece_own.at[v])

    def over_parts(body, start=0, stop=None):
        def step(c, carry):
            body(c)
            return carry

        lax.fori_loop(start, chunk if stop is None else stop, step, 0)

    ready = done_in[0].shape[0] // step_rows
    early, late = (0, ready), (ready, chunk)

    def sum_step(step):
        def body(c):
            for way, rank in ways:

                @pl.when(rank <= step)
                def _():
                    block = block_at(way, step)
                    for u in range(units):
                        if step > 0:

                            @pl.when(rank > 0)
                            def _():
                                hop(way, u, step - 1, block, c).wait_recv()
                                total = held[u, block, part(c)].astype(F32) + got[
                                    way, u, step - 1, part(c)
                                ].astype(F32)
                                held[u, block, part(c)] = total.astype(BF16)

                        hop(way, u, step, block, c).start()

        over_parts(body)

    def gather_step(v, step, span):
        def body(c):
            for way, rank in ways:

                @pl.when((rank >= step) & (rank < 3))
                def _():
                    block = piece_at(way, step)
                    if step > 0:
                        relay(way, v, step - 1, block, c).wait_recv()
                    relay(way, v, step, block, c).start()

        over_parts(body, *span)

    def chip_sum(v):
        load_mine(v).wait()
        to_beside(v).wait()

        @pl.when(y == 1)
        def _():
            def body(c):
                total = mine[v, 1, part(c)].astype(F32) + theirs[v, 1, part(c)].astype(F32)
                mine[v, 1, part(c)] = total.astype(BF16)

            over_parts(body, 0, chunk - ready)
            to_below(v).start()

    def bring(v):
        def body(c, from_y):
            rows, out = part(c), part(c + ready)
            total = mine[v, 0, rows].astype(F32) + theirs[v, 0, rows].astype(F32)
            if from_y:
                total = total + below[v, rows].astype(F32)
            if v == 1:
                pieces[v, out] = total.astype(BF16)
            else:
                for head in range(feats // HD):
                    lanes = slice(head * HD, (head + 1) * HD)
                    pieces[v, out, lanes] = turn(
                        total[:, lanes], keep_ref[rows], -left_ref[rows], -right_ref[rows]
                    ).astype(BF16)

        @pl.when(y == 0)
        def _():
            to_below(v).wait_recv()
            over_parts(lambda c: body(c, True), 0, chunk - ready)

        @pl.when(y == 1)
        def _():
            over_parts(lambda c: body(c, False), 0, chunk - ready)

        keep(v).start()

    def job(index, source, target, peer):
        return pltpu.make_async_remote_copy(
            src_ref=source,
            dst_ref=target,
            send_sem=job_send.at[index],
            recv_sem=job_recv.at[index],
            device_id=peer,
            device_id_type=pl.DeviceIdType.MESH,
        )

    def job_in(index):
        source, target = (
            (lines_in[index].at[y], feed_own.at[index])
            if index < 2
            else (stays_in, pair_own.at[0])
            if index == 2
            else (streams_in[index - 3], wide_in.at[index - 3])
        )
        return pltpu.make_async_copy(source, target, job_load.at[index])

    def feed_job(f):
        return job(f, lines_in[f].at[1 - y], feed_got.at[f], to_y)

    def pair_x_job(i):
        source = full_grad.at[:, pl.ds(other_x * 2, 2), core] if i else leaves_in
        return job(2 + 4 * i, source, pair_x.at[i], to_x)

    def pair_y_job(i):
        return job(3 + 4 * i, pair_own.at[i, :, 1 - y], pair_y.at[i], to_y)

    def core_job(i):
        return job(4 + i, full_grad.at[i, :, 1 - core], from_core.at[i], to_core)

    def product(i):
        job_in(3 + i).wait()
        rows = full_grad.shape[3]
        for b in range(4):
            part_in = wide_in[i, :, b * 2 * rows : (b + 1) * 2 * rows]
            block = dot_tn(part_in, pieces[i]).astype(BF16)
            full_grad[i, b, 0] = block[:rows]
            full_grad[i, b, 1] = block[rows:]
        core_job(i).start()

    def both(a, b):
        return a.astype(F32) + b.astype(F32)

    def chip_grad():
        for i in range(2):
            core_job(i).wait()
            for b in range(4):
                full_grad[i, b, core] = both(full_grad[i, b, core], from_core[i, b]).astype(BF16)
        pair_x_job(1).start()

    def pair_line(i):
        pair_x_job(i).wait()
        for n in range(2):
            for k in range(2):
                stays = pair_own[i, n, k] if i == 0 else full_grad[n, x * 2 + k, core]
                pair_own[i, n, k] = both(stays, pair_x[i, n, k]).astype(BF16)
        pair_y_job(i).start()

    def pair_finish(i):
        pair_y_job(i).wait()
        total = [both(pair_own[i, n, y], pair_y[i, n]) for n in range(2)]
        grad_refs[2 + 2 * i][...] = total[0]
        grad_refs[3 + 2 * i][...] = total[1].T if i == 0 else total[1]

    def feed_finish():
        wide = min(512, feed_own.shape[2])
        for f in range(2):
            feed_job(f).wait()
            for c in range(0, feed_own.shape[2], wide):
                span = slice(c, c + wide)
                total = both(feed_own[f, :, span], feed_got[f, :, span])
                if f == 0:
                    grad_refs[0][:, span] = total
                else:
                    grad_refs[1][span] = total.T

    pair_x_job(0).start()
    for index in range(5):
        job_in(index).start()
    sum_step(0)
    for v in range(whole):
        load_done(v).wait()
        gather_step(v, 0, early)
    for v in range(whole):
        chip_sum(v)
    for w in range(count):
        second(w)
    for v in range(whole):
        bring(v)
        gather_step(v, 0, late)
    for f in range(2):
        feed_job(f).start()
    sum_step(1)
    for v in range(whole):
        gather_step(v, 1, early)
    for w in range(count):
        third(w)
    for i in range(2):
        product(i)
    for v in range(whole):
        gather_step(v, 1, late)
    job_in(2).wait()
    pair_line(0)
    sum_step(2)
    for v in range(whole):
        gather_step(v, 2, early)
    chip_grad()
    for f in range(2):
        job_in(f).wait()
    feed_finish()
    pair_finish(0)

    def finish(c):
        for u in range(units):
            outs[u][part(c)] = held[u, z, part(c)].astype(F32)
            for way, rank in ways:

                @pl.when(rank > 0)
                def _():
                    hop(way, u, 2, z, c).wait_recv()
                    outs[u][part(c)] += got[way, u, 2, part(c)].astype(F32)

    for v in range(whole):
        gather_step(v, 2, late)
    pair_line(1)
    over_parts(finish)
    for w in range(count):
        last(w)
    pair_finish(1)

    def drain(c):
        for way, rank in ways:

            @pl.when(rank == 3)
            def _():
                for v in range(whole):
                    for step in range(3):
                        relay(way, v, step, piece_at(way, step + 1), c).wait_recv()

        for step in range(3):
            for way, rank in ways:

                @pl.when(rank <= step)
                def _():
                    for u in range(units):
                        hop(way, u, step, block_at(way, step), c).wait_send()

                @pl.when((rank >= step) & (rank < 3))
                def _():
                    for v in range(whole):
                        relay(way, v, step, piece_at(way, step), c).wait_send()

    over_parts(drain)
    for v in range(whole):
        keep(v).wait()

        @pl.when(y == 1)
        def _():
            to_below(v).wait_send()


def exchange(partials, rows, shards_in, axes, collective_id, spread=0):
    units, count = len(partials), len(shards_in)
    grown = ((8, 1), (1, 8), (2, 4))
    shape = jax.ShapeDtypeStruct
    full = [
        shape(tuple(n * k for n, k in zip(w.shape, grown[axis])), BF16)
        for w, axis in zip(shards_in, axes)
    ]
    anywhere, local = pl.BlockSpec(memory_space=pl.ANY), pl.BlockSpec(memory_space=pltpu.VMEM)
    sems = pltpu.SemaphoreType.DMA
    out_specs, out_shape = [anywhere] * count, full
    in_specs = [anywhere] * (units + count)
    scratch = [sems((count,)), sems((count, 9)), sems((count, 9))]
    if units:
        tokens, feats = partials[0].shape[0], partials[0].shape[1] // 4
        chunk = 4
        in_specs = in_specs + [anywhere] * 4 + [local] * 3 + [anywhere] * 6
        last = rows[2].shape[2]
        line, stays = rows[7], rows[9]
        out_specs = [local] * units + [anywhere] * 2 + out_specs
        out_shape = (
            [shape((tokens, feats), F32)] * units + [shape((tokens, 4 * feats), BF16)] * 2 + out_shape
        )
        scratch = scratch + [
            pltpu.VMEM((units, 4, tokens, feats), BF16),
            pltpu.VMEM((2, units, 3, tokens, feats), BF16),
            sems((units, 4)),
            sems((2, units, 3, chunk)),
            sems((2, units, 3, chunk)),
            pltpu.VMEM((2, 2, last, feats), BF16),
            pltpu.VMEM((2, 2, last, feats), BF16),
            pltpu.VMEM((2, last, feats), BF16),
            pltpu.VMEM((2, tokens, feats), BF16),
            sems((2,)),
            sems((2, 2, 3, chunk)),
            sems((2, 2, 3, chunk)),
            sems((2,)),
            sems((2,)),
            sems((2,)),
            sems((2,)),
            sems((2,)),
            sems((2,)),
            pltpu.VMEM((2,) + line.shape[1:], BF16),
            pltpu.VMEM((2,) + line.shape[1:], BF16),
            pltpu.VMEM((2,) + stays.shape, BF16),
            pltpu.VMEM((2,) + stays.shape, BF16),
            pltpu.VMEM((2, 2) + stays.shape[2:], BF16),
            pltpu.VMEM((2,) + rows[11].shape, BF16),
            pltpu.VMEM((2, 4, 2) + stays.shape[2:], BF16),
            pltpu.VMEM((2, 4) + stays.shape[2:], BF16),
            sems((5,)),
            sems((8,)),
            sems((8,)),
        ]
        wide, narrow = line.shape[1:], stays.shape[2:]
        out_specs = out_specs + [local] * 6
        out_shape = out_shape + [
            shape(s, F32) for s in (wide, wide[::-1], narrow, narrow[::-1], narrow, narrow)
        ]
    if spread:
        out_specs = out_specs + [anywhere] * spread
        out_shape = out_shape + [
            shape((w.shape[0] // 4, w.shape[1] * 4), BF16) for w in shards_in[:spread]
        ]
        scratch = scratch + [sems((spread,))] + [sems((spread, 3))] * 2
    results = pl.pallas_call(
        functools.partial(exchange_kernel, units, spread, axes),
        in_specs=in_specs,
        out_specs=out_specs,
        out_shape=out_shape,
        scratch_shapes=scratch,
        compiler_params=pltpu.CompilerParams(
            collective_id=collective_id,
            has_side_effects=True,
            vmem_limit_bytes=VMEM_LIMIT,
        ),
        cost_estimate=pl.CostEstimate(
            flops=0, bytes_accessed=(600 if units else 240) * 1024 * 1024, transcendentals=0
        ),
        name="exchange",
    )(*partials, *shards_in, *rows)
    if not units:
        return results
    end = units + 2 + count
    return results[:units], results[units : units + 2], results[units + 2 : end], results[end:]


def head_sum_kernel(members, x_ref, out_ref, slots, send_sem, recv_sem):
    z = lax.axis_index("head")
    barrier = pltpu.get_barrier_semaphore()
    for k in range(1, members):
        pl.semaphore_signal(
            barrier,
            inc=1,
            device_id={"head": lax.rem(z + k, members)},
            device_id_type=pl.DeviceIdType.MESH,
        )
    pl.semaphore_wait(barrier, members - 1)
    copies = []
    for k in range(1, members):
        copy = pltpu.make_async_remote_copy(
            src_ref=x_ref,
            dst_ref=slots.at[z],
            send_sem=send_sem.at[k - 1],
            recv_sem=recv_sem.at[k - 1],
            device_id={"head": lax.rem(z + k, members)},
            device_id_type=pl.DeviceIdType.MESH,
        )
        copy.start()
        copies.append(copy)
    slots[z] = x_ref[...]
    for copy in copies:
        copy.wait()
    total = slots[0]
    for k in range(1, members):
        total = total + slots[k]
    out_ref[...] = total


def head_sum(x, collective_id):
    members = lax.axis_size("head")
    return pl.pallas_call(
        functools.partial(head_sum_kernel, members),
        out_shape=jax.ShapeDtypeStruct(x.shape, F32),
        in_specs=[pl.BlockSpec(memory_space=pltpu.VMEM)],
        out_specs=pl.BlockSpec(memory_space=pltpu.VMEM),
        scratch_shapes=[
            pltpu.VMEM((members,) + x.shape, F32),
            pltpu.SemaphoreType.DMA((members - 1,)),
            pltpu.SemaphoreType.DMA((members - 1,)),
        ],
        compiler_params=pltpu.CompilerParams(
            collective_id=collective_id, has_side_effects=True, vmem_limit_bytes=VMEM_LIMIT
        ),
        name="sum_over_head",
    )(x)


def turn(v, keep, left, right):
    h = ROT // 2
    return v * keep + pltpu.roll(v, HD - h, 1) * left + pltpu.roll(v, h, 1) * right


def rotate_kernel(sign, v_ref, keep_ref, left_ref, right_ref, out_ref):
    for head in range(v_ref.shape[1] // HD):
        part = pl.ds(head * HD, HD)
        out_ref[:, part] = turn(
            v_ref[:, part], keep_ref[...], sign * left_ref[...], sign * right_ref[...]
        ).astype(BF16)


def rotate(values_in, tables, sign):
    tokens, feats = values_in.shape
    block = min(tokens, 256)
    table = pl.BlockSpec((block, HD), lambda i: (i, 0))
    wide = pl.BlockSpec((block, feats), lambda i: (i, 0))
    return pl.pallas_call(
        functools.partial(rotate_kernel, sign),
        grid=(tokens // block,),
        in_specs=[wide, table, table, table],
        out_specs=wide,
        out_shape=jax.ShapeDtypeStruct((tokens, feats), BF16),
        cost_estimate=pl.CostEstimate(
            flops=5 * tokens * feats, bytes_accessed=8 * tokens * feats, transcendentals=0
        ),
        name="rotate_heads",
    )(values_in, *tables)


def feed_kernel(x_ref, d_ref, up_ref, down_ref, gated_ref, d_up_ref, grad_up_ref, grad_down_ref):
    tokens, model_width = x_ref.shape
    step = min(256, tokens)
    for r in range(0, tokens, step):
        rows = slice(r, r + step)
        up_pre = dot(x_ref[rows], up_ref[...])
        d_gated = dot_nt(d_ref[rows], down_ref[...])
        below = 0.5 * (1.0 + lax.erf(up_pre * 0.5**0.5))
        density = jnp.exp(-0.5 * up_pre * up_pre) * (2.0 * jnp.pi) ** -0.5
        gated_ref[rows] = (up_pre * below).astype(BF16)
        d_up_ref[rows] = (d_gated * (below + up_pre * density)).astype(BF16)
    wide = min(512, model_width)
    for c in range(0, model_width, wide):
        part = slice(c, c + wide)
        grad_up_ref[part] = dot_tn(x_ref[:, part], d_up_ref[...]).astype(BF16)
        grad_down_ref[part] = dot_tn(d_ref[:, part], gated_ref[...]).astype(BF16)


def feed_forward(x, d_out, up, down):
    tokens, model_width = x.shape
    hidden = up.shape[1]
    block = min(512, hidden)
    fixed = pl.BlockSpec((tokens, model_width), lambda i: (0, 0), pipeline_mode=pl.Buffered(1))
    narrow = pl.BlockSpec((tokens, block), lambda i: (0, i))
    column = pl.BlockSpec((model_width, block), lambda i: (0, i))
    shape = lambda rows: jax.ShapeDtypeStruct((rows, hidden), BF16)
    return pl.pallas_call(
        feed_kernel,
        grid=(hidden // block,),
        in_specs=[fixed, fixed, column, pl.BlockSpec((block, model_width), lambda i: (i, 0))],
        out_specs=[narrow, narrow, column, column],
        out_shape=[shape(tokens), shape(tokens), shape(model_width), shape(model_width)],
        compiler_params=pltpu.CompilerParams(vmem_limit_bytes=VMEM_LIMIT),
        cost_estimate=pl.CostEstimate(
            flops=8 * tokens * model_width * hidden,
            bytes_accessed=4 * model_width * (2 * hidden + tokens),
            transcendentals=0,
        ),
        name="feed_forward",
    )(x, d_out, up, down)


def attention_kernel(
    place_ref, q_ref, do_ref, start_ref, valid_ref, keep_ref, left_ref, right_ref, *refs
):
    blocks = (len(refs) - 6) // 2
    k_refs, v_refs = refs[:blocks], refs[blocks : 2 * blocks]
    o_ref, dq_ref, near_ref, beside_ref, s_ref, dp_ref = refs[2 * blocks :]
    grad_ref = lambda j: (beside_ref if j % 2 else near_ref).at[j // 2]
    rows = q_ref.shape[1]
    scale = HD ** (-0.5)
    member = place_ref[0]
    keep, left, right = keep_ref[0], left_ref[0], right_ref[0]
    q = turn(q_ref[0], keep, left, right).astype(BF16)
    d_out = do_ref[0]
    start = start_ref[0]
    top = jnp.full((rows, 1), MASKED, F32)
    t = member * rows + lax.broadcasted_iota(jnp.int32, (rows, rows), 0)
    for j in range(blocks):
        u = place_ref[j] * rows + lax.broadcasted_iota(jnp.int32, (rows, rows), 1)
        allowed = (u <= t) & (u >= start)
        s_ref[j] = jnp.where(allowed, dot_nt(q, k_refs[j][0]) * scale, MASKED)
        top = jnp.maximum(top, jnp.max(s_ref[j], axis=1, keepdims=True))
    total = jnp.zeros((rows, 1), F32)
    for j in range(blocks):
        e = jnp.exp(s_ref[j] - top)
        s_ref[j] = e
        total = total + jnp.sum(e, axis=1, keepdims=True)
    inverse = 1.0 / total
    out = jnp.zeros((rows, HD), F32)
    delta = jnp.zeros((rows, 1), F32)
    for j in range(blocks):
        p = s_ref[j] * inverse
        s_ref[j] = p
        p_bf = p.astype(BF16)
        out = out + dot(p_bf, v_refs[j][0])
        grad_ref(j)[1] = dot_tn(p_bf, d_out).astype(BF16)
        d_p = dot_nt(d_out, v_refs[j][0])
        dp_ref[j] = d_p
        delta = delta + jnp.sum(p * d_p, axis=1, keepdims=True)
    o_ref[0] = (out * valid_ref[0]).astype(BF16)
    d_q = jnp.zeros((rows, HD), F32)
    for j in range(blocks):
        d_s = (s_ref[j] * (dp_ref[j] - delta)).astype(BF16)
        d_q = d_q + dot(d_s, k_refs[j][0])
        grad_ref(j)[0] = (dot_tn(d_s, q) * scale).astype(BF16)
    dq_ref[0] = turn(d_q * scale, keep, -left, -right).astype(BF16)


def attention(index, places, queries, d_attended, starts, valid, tables, keys, values):
    _, rows, feats = queries.shape
    blocks = len(keys)
    tile = pl.BlockSpec((1, rows, HD), lambda h: (index, 0, h))
    fixed = lambda width: pl.BlockSpec((1, rows, width), lambda h: (index, 0, 0))
    out_tile = pl.BlockSpec((1, rows, HD), lambda h: (0, 0, h))
    grad_tile = pl.BlockSpec((blocks // 2, 2, rows, HD), lambda h: (0, 0, 0, h))
    shape = lambda *lead: jax.ShapeDtypeStruct(lead + (rows, feats), BF16)
    return pl.pallas_call(
        attention_kernel,
        grid=(feats // HD,),
        in_specs=[pl.BlockSpec(memory_space=pltpu.SMEM), tile, tile]
        + [fixed(1)] * 2
        + [fixed(HD)] * 3
        + [tile] * (2 * blocks),
        out_specs=[out_tile] * 2 + [grad_tile] * 2,
        out_shape=[shape(1)] * 2 + [shape(blocks // 2, 2)] * 2,
        scratch_shapes=[
            pltpu.VMEM((blocks, rows, rows), F32),
            pltpu.VMEM((blocks, rows, rows), F32),
        ],
        compiler_params=pltpu.CompilerParams(vmem_limit_bytes=VMEM_LIMIT),
        cost_estimate=pl.CostEstimate(
            flops=0,
            bytes_accessed=1024,
            transcendentals=0,
        ),
        name="attention_both_ways",
    )(places, queries, d_attended, starts, valid, *tables, *keys, *values)


def exchange_rows(local):
    if lax.axis_size("stream") != 4:
        raise ValueError("stream")
    across = lax.ppermute(local, "stream", [(0, 2), (1, 3)])
    beside = over_core(local)
    return (local, beside, across, over_core(across))


def add_f32(a, b):
    return a.astype(F32) + b.astype(F32)


def over_line(a):
    return lax.ppermute(a, "stream", [(2, 0), (3, 1)])


def columns_of(pieces, rows):
    lane = lax.broadcasted_iota(jnp.int32, (rows, 128), 1)
    out = jnp.zeros((rows, 128), F32)
    for index, piece in enumerate(pieces):
        out = jnp.where(lane == index, piece, out)
    return out


def row_sum(a):
    return jnp.sum(a, axis=1, keepdims=True)


def streams_kernel(weights_ref, history_ref, streams_ref, stats_ref):
    weights = weights_ref[...]
    layers = [history_ref[j].astype(F32) for j in range(HIST)]
    sums, squares = [], []
    for s in range(4):
        total = weights[:, s * HIST : s * HIST + 1] * layers[0]
        for j in range(1, HIST):
            total = total + weights[:, s * HIST + j : s * HIST + j + 1] * layers[j]
        streams_ref[s] = total
        sums.append(row_sum(total))
        squares.append(row_sum(total * total))
    stats_ref[...] = columns_of(sums + squares, weights.shape[0]).T[:8]


def mix_streams(weights, history):
    _, tokens, feats = history.shape
    block = min(128, tokens)
    return pl.pallas_call(
        streams_kernel,
        grid=(tokens // block,),
        in_specs=[
            pl.BlockSpec((block, weights.shape[1]), lambda i: (i, 0)),
            pl.BlockSpec((HIST, block, feats), lambda i: (0, i, 0)),
        ],
        out_specs=[
            pl.BlockSpec((4, block, feats), lambda i: (0, i, 0)),
            pl.BlockSpec((8, block), lambda i: (0, i)),
        ],
        out_shape=[
            jax.ShapeDtypeStruct((4, tokens, feats), F32),
            jax.ShapeDtypeStruct((8, tokens), F32),
        ],
        compiler_params=pltpu.CompilerParams(vmem_limit_bytes=VMEM_LIMIT),
        cost_estimate=pl.CostEstimate(
            flops=80 * tokens * feats, bytes_accessed=34 * tokens * feats, transcendentals=0
        ),
        name="mix_streams",
    )(weights, history)


def early_kernel(streams_ref, cot_ref, history_ref, out_ref):
    cot = cot_ref[...].astype(F32)
    plain, crossed, direct = [], [], []
    layers = [history_ref[j].astype(F32) for j in range(HIST)]
    for layer in layers:
        plain.append(row_sum(layer))
        direct.append(row_sum(cot * layer))
    for s in range(4):
        for layer in layers:
            crossed.append(row_sum(streams_ref[s] * layer))
    out_ref[...] = columns_of(crossed + plain + direct, cot.shape[0]).T[:64].astype(BF16)


def early_sums(streams, cot, history):
    _, tokens, feats = streams.shape
    block = min(128, tokens)
    return pl.pallas_call(
        early_kernel,
        grid=(tokens // block,),
        in_specs=[
            pl.BlockSpec((4, block, feats), lambda i: (0, i, 0)),
            pl.BlockSpec((block, feats), lambda i: (i, 0)),
            pl.BlockSpec((HIST, block, feats), lambda i: (0, i, 0)),
        ],
        out_specs=pl.BlockSpec((64, block), lambda i: (0, i)),
        out_shape=jax.ShapeDtypeStruct((64, tokens), BF16),
        compiler_params=pltpu.CompilerParams(vmem_limit_bytes=VMEM_LIMIT),
        cost_estimate=pl.CostEstimate(
            flops=110 * tokens * feats, bytes_accessed=36 * tokens * feats, transcendentals=0
        ),
        name="early_sums",
    )(streams, cot, history)


def sums_kernel(
    g0, g1, g2, g3, streams_ref, stats_ref, gain_ref, history_ref, dots_ref, out_ref, edge_ref
):
    stats = stats_ref[...]
    rows = stats.shape[0]

    @pl.when(pl.program_id(0) == 0)
    def _():
        edge_ref[...] = jnp.zeros_like(edge_ref)

    firsts, seconds, dots = [], [], []
    for s, g_ref in enumerate((g0, g1, g2, g3)):
        g = g_ref[...].astype(F32)
        centered = (streams_ref[s] - stats[:, s : s + 1]) * stats[:, 4 + s : 5 + s]
        edge_ref[s : s + 1] += jnp.sum(g * centered, axis=0, keepdims=True)
        edge_ref[4 + s : 5 + s] += jnp.sum(g, axis=0, keepdims=True)
        scaled = g * gain_ref[s : s + 1]
        firsts.append(row_sum(scaled))
        seconds.append(row_sum(scaled * centered))
        for j in range(HIST):
            dots.append(row_sum(scaled * history_ref[j].astype(F32)))
    dots_ref[...] = columns_of(dots, rows).T[:48].astype(BF16)
    out_ref[...] = columns_of(firsts + seconds, rows).T[:8]


def gradient_sums(grads, streams, stats, gain, history):
    _, tokens, feats = streams.shape
    block = min(128, tokens)
    wide = pl.BlockSpec((block, feats), lambda i: (i, 0))
    return pl.pallas_call(
        sums_kernel,
        grid=(tokens // block,),
        in_specs=[wide] * 4
        + [
            pl.BlockSpec((4, block, feats), lambda i: (0, i, 0)),
            pl.BlockSpec((block, 8), lambda i: (i, 0)),
            pl.BlockSpec((4, feats), lambda i: (0, 0)),
            pl.BlockSpec((HIST, block, feats), lambda i: (0, i, 0)),
        ],
        out_specs=[
            pl.BlockSpec((48, block), lambda i: (0, i)),
            pl.BlockSpec((8, block), lambda i: (0, i)),
            pl.BlockSpec((8, feats), lambda i: (0, 0)),
        ],
        out_shape=[
            jax.ShapeDtypeStruct((48, tokens), BF16),
            jax.ShapeDtypeStruct((8, tokens), F32),
            jax.ShapeDtypeStruct((8, feats), F32),
        ],
        compiler_params=pltpu.CompilerParams(vmem_limit_bytes=VMEM_LIMIT),
        cost_estimate=pl.CostEstimate(
            flops=110 * tokens * feats, bytes_accessed=42 * tokens * feats, transcendentals=0
        ),
        name="gradient_sums",
    )(*grads, streams, stats, gain, history)


def totals_kernel(members, *refs):
    ins, outs, slots, sems = refs[:3], refs[3:6], refs[6:9], refs[9:]
    z = lax.axis_index("head")
    line = [{"head": lax.rem(z + k, members)} for k in range(1, members)]
    barrier = pltpu.get_barrier_semaphore()
    for peer in line:
        pl.semaphore_signal(barrier, inc=1, device_id=peer, device_id_type=pl.DeviceIdType.MESH)
    pl.semaphore_wait(barrier, len(line))
    copies = []
    for index in range(3):
        for k, peer in enumerate(line):
            copy = pltpu.make_async_remote_copy(
                src_ref=ins[index],
                dst_ref=slots[index].at[z],
                send_sem=sems[2 * index].at[k],
                recv_sem=sems[2 * index + 1].at[k],
                device_id=peer,
                device_id_type=pl.DeviceIdType.MESH,
            )
            copy.start()
            copies.append(copy)
        slots[index][z] = ins[index][...]
    for copy in copies:
        copy.wait()
    for index in range(3):
        total = slots[index][0].astype(F32)
        for k in range(1, members):
            total = total + slots[index][k].astype(F32)
        outs[index][...] = total


def head_totals(arrays, collective_id):
    members = lax.axis_size("head")
    local = pl.BlockSpec(memory_space=pltpu.VMEM)
    return pl.pallas_call(
        functools.partial(totals_kernel, members),
        in_specs=[local] * 3,
        out_specs=[local] * 3,
        out_shape=[jax.ShapeDtypeStruct(a.shape, F32) for a in arrays],
        scratch_shapes=[pltpu.VMEM((members,) + a.shape, a.dtype) for a in arrays]
        + [pltpu.SemaphoreType.DMA((members - 1,))] * 6,
        compiler_params=pltpu.CompilerParams(
            collective_id=collective_id, has_side_effects=True, vmem_limit_bytes=VMEM_LIMIT
        ),
        name="totals_over_head",
    )(*arrays)


def small_kernel(
    members,
    plane,
    dots_ref,
    early_ref,
    sums_ref,
    stats_ref,
    pre_ref,
    slope_ref,
    hidden_ref,
    rms_ref,
    w_ref,
    current_ref,
    edge_ref,
    small_ref,
    scaled_ref,
    coef_ref,
    got,
    d_mix_ref,
    rows_ref,
    plane_send,
    plane_recv,
):
    x, stream = lax.axis_index("dp"), lax.axis_index("stream")
    near = (
        {"stream": stream + 1 - 2 * lax.rem(stream, 2)},
        {"stream": lax.rem(stream + 2, 4)},
        {"dp": 1 - x},
    )
    near = near if plane else ()
    if plane:
        barrier = pltpu.get_barrier_semaphore()
        for peer in near:
            pl.semaphore_signal(
                barrier, inc=1, device_id=peer, device_id_type=pl.DeviceIdType.MESH
            )
        pl.semaphore_wait(barrier, len(near))
    n = 4 * HIST
    model_width = members * small_ref.shape[1]
    plain = early_ref[n : n + HIST]
    rows_ref[...] = jnp.zeros_like(rows_ref)
    rows_ref[0:8] = sums_ref[...] / model_width
    for s in range(4):
        part = slice(s * HIST, (s + 1) * HIST)
        mean, inverse = stats_ref[s : s + 1], stats_ref[4 + s : 5 + s]
        crossed = (early_ref[part] - mean * plain) * inverse
        d_part = inverse * (
            dots_ref[part] - rows_ref[s : s + 1] * plain - rows_ref[4 + s : 5 + s] * crossed
        )
        if s == 3:
            d_part = d_part + early_ref[n + HIST : n + 2 * HIST]
        d_mix_ref[part] = d_part
    d_mix = d_mix_ref[...]
    high = dict(precision=HIGHEST, preferred_element_type=F32)
    d_pre = jnp.dot(w_ref[...], d_mix, **high) * slope_ref[...]
    rms = rms_ref[...]
    cross = jnp.sum(d_pre * pre_ref[...], axis=0, keepdims=True)
    rows_ref[8:9] = rms * rms * cross / model_width
    coef_ref[...] = rows_ref[...].T
    scaled = d_pre * rms
    scaled_ref[...] = scaled
    small_ref[...] = jnp.zeros_like(small_ref)
    small_ref[0:n] = jnp.dot(scaled, current_ref[...].astype(F32), **high)
    small_ref[n : n + 8] = edge_ref[...]
    small_ref[n + 8 : 2 * n + 8, 0:n] = lax.dot_general(
        hidden_ref[...], d_mix, (((1,), (1,)), ((), ())), **high
    )
    small_ref[n + 8 : 2 * n + 8, n : n + 1] = jnp.sum(d_mix, axis=1, keepdims=True)
    for step, peer in enumerate(near):
        copy = pltpu.make_async_remote_copy(
            src_ref=small_ref,
            dst_ref=got.at[step],
            send_sem=plane_send.at[step],
            recv_sem=plane_recv.at[step],
            device_id=peer,
            device_id_type=pl.DeviceIdType.MESH,
        )
        copy.start()
        copy.wait()
        small_ref[...] += got[step]


def small_gradients(dots, early, sums, stats, pre, slope, hidden, rms, w_out, current, edges):
    members, plane = lax.axis_size("head"), paired()
    tokens, feats = current.shape
    n = 4 * HIST
    shape = jax.ShapeDtypeStruct
    sems = pltpu.SemaphoreType.DMA
    small, scaled, coefs = pl.pallas_call(
        functools.partial(small_kernel, members, plane),
        in_specs=[pl.BlockSpec(memory_space=pltpu.VMEM)] * 11,
        out_specs=[pl.BlockSpec(memory_space=pltpu.VMEM)] * 3,
        out_shape=[shape((80, feats), F32), shape((n, tokens), F32), shape((tokens, 128), F32)],
        scratch_shapes=[
            pltpu.VMEM((3, 80, feats), F32),
            pltpu.VMEM((n, tokens), F32),
            pltpu.VMEM((128, tokens), F32),
            sems((3,)),
            sems((3,)),
        ],
        compiler_params=pltpu.CompilerParams(
            collective_id=3 if plane else None,
            has_side_effects=plane,
            vmem_limit_bytes=VMEM_LIMIT,
        ),
        name="small_gradients",
    )(dots, early, sums, stats, pre, slope, hidden, rms, w_out, current, edges)
    if not plane:
        small = lax.psum(small.astype(BF16), ("dp", "stream")).astype(F32)
    return small, scaled, coefs


def history_kernel(
    g0, g1, g2, g3, streams_ref, stats_ref, gain_ref, cot_ref, current_ref, weights_ref, coef_ref, d_ref, w_ref, out_ref
):
    stats, weights, coefs = stats_ref[...], weights_ref[...], coef_ref[...]
    d_streams = []
    for s, g_ref in enumerate((g0, g1, g2, g3)):
        inverse = stats[:, 4 + s : 5 + s]
        centered = (streams_ref[s] - stats[:, s : s + 1]) * inverse
        scaled = g_ref[...].astype(F32) * gain_ref[s : s + 1]
        d_streams.append(
            inverse * (scaled - coefs[:, s : s + 1] - centered * coefs[:, 4 + s : 5 + s])
        )
    d_streams[3] = d_streams[3] + cot_ref[...].astype(F32)
    for j in range(HIST):
        total = weights[:, j : j + 1] * d_streams[0]
        for s in range(1, 4):
            total = total + weights[:, s * HIST + j : s * HIST + j + 1] * d_streams[s]
        if j == HIST - 1:
            total = total + lax.dot_general(
                d_ref[...],
                w_ref[...],
                (((0,), (0,)), ((), ())),
                precision=HIGHEST,
                preferred_element_type=F32,
            )
            total = total - current_ref[...].astype(F32) * coefs[:, 8:9]
        out_ref[j] = total


def history_gradient(grads, streams, stats, gain, cot, current, weights, coefs, d_scaled, w_rows):
    _, tokens, feats = streams.shape
    block = min(128, tokens)
    wide = pl.BlockSpec((block, feats), lambda i: (i, 0))
    narrow = lambda a: pl.BlockSpec((block, a.shape[1]), lambda i: (i, 0))
    fixed = lambda a: pl.BlockSpec(a.shape, lambda i: (0, 0))
    return pl.pallas_call(
        history_kernel,
        grid=(tokens // block,),
        in_specs=[wide] * 4
        + [
            pl.BlockSpec((4, block, feats), lambda i: (0, i, 0)),
            narrow(stats),
            fixed(gain),
            wide,
            wide,
            narrow(weights),
            narrow(coefs),
            pl.BlockSpec((d_scaled.shape[0], block), lambda i: (0, i)),
            fixed(w_rows),
        ],
        out_specs=pl.BlockSpec((HIST, block, feats), lambda i: (0, i, 0)),
        out_shape=jax.ShapeDtypeStruct((HIST, tokens, feats), F32),
        compiler_params=pltpu.CompilerParams(vmem_limit_bytes=VMEM_LIMIT),
        cost_estimate=pl.CostEstimate(
            flops=110 * tokens * feats, bytes_accessed=64 * tokens * feats, transcendentals=0
        ),
        name="history_gradient",
    )(*grads, streams, stats, gain, cot, current, weights, coefs, d_scaled, w_rows)


def shards(
    history,
    seq_lens,
    bucket_slot,
    w_mix_in,
    w_mix_out,
    mix_bias,
    ln_gain,
    ln_bias,
    w_qkv,
    w_attn_out,
    w_up,
    w_down,
    cotangent,
):
    member = lax.axis_index("stream")
    micro, quarter, feats = history.shape[1:]
    tokens = micro * quarter
    model_width = feats * lax.axis_size("head")
    slot_base = lax.axis_index("dp") * micro
    slot_ids = jnp.arange(bucket_slot.shape[0], dtype=jnp.int32)
    query_places = member * quarter + jnp.arange(quarter, dtype=jnp.int32)
    w_mix_in_f = w_mix_in.astype(F32)
    w_mix_out_f = w_mix_out.astype(F32)

    segments, starts = [], []
    for index in range(micro):
        bucket = jnp.sum(jnp.where(slot_ids == slot_base + index, bucket_slot, 0))
        lengths = jnp.sum(jnp.where(slot_ids[:, None] == bucket, seq_lens, 0), axis=0)
        bounds = jnp.cumsum(lengths)
        passed = (query_places[:, None] >= bounds[None, :]).astype(jnp.int32)
        segments.append(jnp.sum(passed, axis=1))
        starts.append(jnp.sum(passed * lengths[None, :], axis=1))
    valid = (jnp.concatenate(segments) < 3).astype(F32)[:, None]
    starts = jnp.concatenate(starts)
    position = jnp.tile(query_places, micro) - starts
    frequency = jnp.arange(ROT // 2, dtype=F32)
    phases = position.astype(F32)[:, None] * (10000.0 ** (-2.0 * frequency / ROT))
    cosine, sine = jnp.cos(phases), jnp.sin(phases)
    plain = jnp.zeros((tokens, HD - ROT), F32)
    none = jnp.zeros_like(sine)
    tables = (
        jnp.concatenate([cosine, cosine, plain + 1.0], axis=1),
        jnp.concatenate([-sine, none, plain], axis=1),
        jnp.concatenate([none, sine, plain], axis=1),
    )

    cot_rows = cotangent.reshape(tokens, feats).astype(F32) * valid
    cot_bf = cot_rows.astype(BF16)
    duplex = lined()

    history = history.reshape(HIST, tokens, feats)
    current = history[HIST - 1]
    current_f = current.astype(F32)
    mixed = lax.dot_general(w_mix_in, current, (((0,), (1,)), ((), ())), preferred_element_type=F32)
    square = jnp.sum(current_f * current_f, axis=1)[None]
    mixed = head_sum(jnp.concatenate([mixed, square]), 0).T
    mixed, cot_bf, w_up = lax.optimization_barrier((mixed, cot_bf, w_up))
    out_full = lax.all_gather(cot_bf, "head", axis=1, tiled=True)
    if duplex:
        (up_full,) = exchange([], (), [w_up], (0,), 4)
        mixed, up_full = lax.optimization_barrier((mixed, up_full))
    rms_scale = lax.rsqrt(mixed[:, 4 * HIST :] / model_width + EPSILON)
    mix_pre = mixed[:, : 4 * HIST] * rms_scale
    below_mix = 0.5 * (1.0 + lax.erf(mix_pre * 0.5**0.5))
    mix_hidden = gelu_exact(mix_pre)
    slope_mix = below_mix + mix_pre * jnp.exp(-0.5 * mix_pre * mix_pre) * (2.0 * jnp.pi) ** -0.5
    mix_weights = jnp.dot(mix_hidden, w_mix_out_f, precision=HIGHEST) + mix_bias.reshape(-1)
    streams, stats = mix_streams(mix_weights, history)
    stats = head_sum(stats, 1)
    stat_sum, stat_square = stats[:4], stats[4:]
    row_means = (stat_sum / model_width)[:, :, None]
    inv_std = lax.rsqrt(stat_square[:, :, None] / model_width - row_means * row_means + EPSILON)
    centered = (streams - row_means) * inv_std
    row_stats = jnp.concatenate([row_means[..., 0], inv_std[..., 0]]).T
    normed = (centered * ln_gain[:, None, :] + ln_bias[:, None, :]).astype(BF16)

    def all_features(a):
        return lax.all_gather(a, "head", axis=1, tiled=True)

    if duplex:
        w_down, normed = lax.optimization_barrier((w_down, normed))
        wk, wv, down_full, w_out_full, wq, *shares = exchange(
            [], (), [w_qkv[1], w_qkv[2], w_down, w_attn_out, w_qkv[0]], (0, 0, 1, 1, 0), 6, 2
        )
    else:
        wq, wk, wv = gather_weight(w_qkv, 1)
        w_out_full, down_full = gather_weight(w_attn_out, 1), gather_weight(w_down, 1)
        up_full = gather_weight(w_up, 0)

    def to_owner(partial):
        return lax.psum_scatter(
            partial.astype(BF16), "head", scatter_dimension=1, tiled=True
        ).astype(F32)

    up_out, out_full = lax.optimization_barrier((normed[3], out_full))
    up_in, k_out, down_full = lax.optimization_barrier(
        (all_features(up_out), normed[1], down_full)
    )
    k_in, v_out = lax.optimization_barrier((all_features(k_out), normed[2]))
    gated_up, d_up, product_up, product_down = feed_forward(up_in, out_full, up_full, down_full)
    feed_products = [product_up[None], product_down[None]]
    feed_parts = [chip_parts(a) if paired() else a for a in feed_products]
    v_out, d_up, feed_parts = lax.optimization_barrier((v_out, d_up, feed_parts))
    feed_lines = [line_parts(*a) for a in feed_parts] if paired() else feed_parts
    streams_late, feed_lines[0] = lax.optimization_barrier((streams, feed_lines[0]))
    early = early_sums(streams_late, cot_bf, history)
    feed = dot(gated_up, down_full).astype(BF16)
    d_attended = dot_nt(out_full, w_out_full).astype(BF16) * valid.astype(BF16)
    d_up_in = dot_nt(d_up, up_full).astype(BF16)
    keys = rotate(dot(k_in, wk), tables, 1.0)
    v_in, q_out, early, feed, d_attended, d_up_in, keys, wk, wv = lax.optimization_barrier(
        (all_features(v_out), normed[0], early, feed, d_attended, d_up_in, keys, wk, wv)
    )
    values = dot(v_in, wv).astype(BF16)
    by_micro = lambda a: a.reshape((micro, quarter) + a.shape[1:])
    key_blocks = exchange_rows(by_micro(keys))
    value_blocks = exchange_rows(by_micro(values))
    q_in, d_up_in, key_blocks, value_blocks, feed_lines[1], early = lax.optimization_barrier(
        (all_features(q_out), d_up_in, key_blocks, value_blocks, feed_lines[1], early)
    )
    g_up = to_owner(d_up_in)
    product = lambda a, b: dot_tn(a, b).astype(BF16)

    queries = dot(q_in, wq)
    places = member ^ jnp.arange(4, dtype=jnp.int32)
    attended, d_query_pre, d_rows = [], [], []
    queries = by_micro(queries)
    for index in range(micro):
        results = attention(
            index,
            places,
            queries,
            by_micro(d_attended),
            by_micro(starts[:, None]),
            by_micro(valid),
            tuple(by_micro(a) for a in tables),
            key_blocks,
            value_blocks,
        )
        attended.append(results[0][0])
        d_query_pre.append(results[1][0])
        if duplex and index == micro - 1:
            continue
        chip = add_f32(results[2], over_core(results[3]))
        across = chip[1].astype(BF16)
        queries, across = lax.optimization_barrier((queries, across))
        d_rows.append(add_f32(chip[0], over_line(across)))
    attended, d_query_pre = jnp.concatenate(attended), jnp.concatenate(d_query_pre)
    d_key_rows = jnp.concatenate([a[0] for a in d_rows])
    done = d_key_rows.shape[0]
    d_key_rows = rotate(d_key_rows, tuple(a[:done] for a in tables), -1.0)
    d_value_rows = jnp.concatenate([a[1] for a in d_rows]).astype(BF16)
    attended, d_query_pre, d_key_rows, d_value_rows = lax.optimization_barrier(
        (attended, d_query_pre, d_key_rows, d_value_rows)
    )

    products = jnp.stack([product(q_in, d_query_pre), product(out_full, attended)])
    if duplex:
        partials = [dot_nt(d_query_pre, wq).astype(BF16)]
        parts = chip_parts(products)
        partials, parts, g_up, feed_lines = lax.optimization_barrier(
            (partials, parts, g_up, feed_lines)
        )
        (g_query,), (d_key_full, d_value_full), (wk_rows, wv_rows), plane_grads = exchange(
            partials,
            [d_key_rows, d_value_rows, results[2], results[3], *(a[done:] for a in tables)]
            + [a[0] for a in feed_lines]
            + [*parts, k_in, v_in],
            shares,
            (0, 0),
            5,
        )
        attended_late, g_query = lax.optimization_barrier((attended, g_query))
        cut = 3 * tokens // 8
        pair = lambda a: (a[:cut], a[cut:])
        halves = [
            (dot(a, w_out_full) + b).astype(BF16) for a, b in zip(pair(attended_late), pair(feed))
        ]
        branch = to_owner(halves[0])
        g_key, g_value = dot_nt(d_key_full, wk_rows), dot_nt(d_value_full, wv_rows)
    else:
        g_query = to_owner(dot_nt(d_query_pre, wq))
        branch = to_owner(dot(attended, w_out_full) + feed)
        terms = scatter_parts(products)
        feed_terms = [scatter_parts(a) for a in feed_products]
        g_key = to_owner(dot_nt(d_key_rows, wk))
        g_value = to_owner(dot_nt(d_value_rows, wv))
        kv_terms = scatter_parts(
            jnp.stack([product(k_in, d_key_rows), product(v_in, d_value_rows)])
        )
    grads = (g_query, g_key, g_value, g_up)
    dots, sums, edges = gradient_sums(grads, streams, row_stats, ln_gain, history)
    dots, early, sums = head_totals((dots, early, sums), 7)
    if duplex:
        sums, second_half = lax.optimization_barrier((sums, halves[1]))
        branch = jnp.concatenate([branch, to_owner(second_half)])
        grad_up, grad_down, grad_query, grad_attn_out, grad_key, grad_value = plane_grads
        grad_qkv = jnp.stack([grad_query, grad_key, grad_value])
    else:
        grad_up = add_terms(feed_terms[0][0][0], feed_terms[0][1][0], False)
        grad_down = add_terms(feed_terms[1][0][0], feed_terms[1][1][0], True)
        grad_attn_out = add_terms(terms[0][1], terms[1][1], True)
        grad_qkv = jnp.concatenate([add_f32(terms[0][:1], terms[1][:1]), add_f32(*kv_terms)])
    small, d_scaled, coefs = small_gradients(
        dots, early, sums, row_stats.T, mix_pre.T, slope_mix.T, mix_hidden.T, rms_scale.T, w_mix_out_f, current, edges
    )
    block_out = (valid * (streams[3] + branch)).astype(BF16)
    history_grad = history_gradient(
        grads, streams, row_stats, ln_gain, cot_bf, current, mix_weights, coefs, d_scaled, w_mix_in_f.T
    ).reshape(HIST, micro, quarter, feats)
    n = 4 * HIST
    return (
        block_out.reshape(micro, quarter, feats),
        mix_weights.reshape(micro, quarter, 4 * HIST),
        history_grad,
        small[:n].T,
        small[n + 8 : 2 * n + 8, :n],
        small[n + 8 : 2 * n + 8, n].reshape(mix_bias.shape),
        small[n : n + 4],
        small[n + 4 : n + 8],
        grad_qkv,
        grad_attn_out,
        grad_up,
        grad_down,
    )


def solution(mesh):
    return jax.shard_map(
        shards,
        mesh=mesh,
        in_specs=(
            P(None, "dp", "stream", "head"),
            P(),
            P(),
            P("head", None),
            P(),
            P(),
            P(None, "head"),
            P(None, "head"),
            P(None, ("dp", "stream"), "head"),
            P("head", ("dp", "stream")),
            P(("dp", "stream"), "head"),
            P("head", ("dp", "stream")),
            P("dp", "stream", "head"),
        ),
        out_specs=(
            P("dp", "stream", "head"),
            P("dp", "stream", None),
            P(None, "dp", "stream", "head"),
            P("head", None),
            P(),
            P(),
            P(None, "head"),
            P(None, "head"),
            P(None, ("dp", "stream"), "head"),
            P("head", ("dp", "stream")),
            P(("dp", "stream"), "head"),
            P("head", ("dp", "stream")),
        ),
        check_vma=False,
    )
```

```python
import functools

import jax
import jax.numpy as jnp
from jax import lax
from jax.experimental import pallas as pl
from jax.experimental.pallas import tpu as pltpu
from jax.sharding import PartitionSpec as P

HD = 128
HIST = 9
ROT = 32

EPSILON = 1e-05
HIGHEST = lax.Precision.HIGHEST
MASKED = -1e30
F32 = jnp.float32
BF16 = jnp.bfloat16
VMEM_LIMIT = 60 * 1024 * 1024

SWAP_X = [(0, 1), (1, 0)]
SWAP_Y = [(0, 2), (2, 0), (1, 3), (3, 1)]
SWAP_CORE = [(0, 1), (1, 0), (2, 3), (3, 2)]


def dot(a, b):
    return jnp.dot(a, b, preferred_element_type=F32)


def dot_nt(a, b):
    return lax.dot_general(a, b, (((1,), (1,)), ((), ())), preferred_element_type=F32)


def dot_tn(a, b):
    return lax.dot_general(a, b, (((0,), (0,)), ((), ())), preferred_element_type=F32)


def gelu_exact(values_in):
    return jax.nn.gelu(values_in, approximate=False)


def over_x(a):
    return lax.ppermute(a, "dp", SWAP_X)


def over_y(a):
    return lax.ppermute(a, "stream", SWAP_Y)


def over_core(a):
    return lax.ppermute(a, "stream", SWAP_CORE)


def paired():
    return lax.axis_size("dp") == 2 and lax.axis_size("stream") == 4


def gather_weight(shard, axis):
    return lax.all_gather(shard, ("dp", "stream"), axis=axis, tiled=True)


def lined():
    return paired() and lax.axis_size("head") == 4


def take(a, index, axis):
    return lax.dynamic_index_in_dim(a, index, axis, keepdims=False)


def add_bf(a, b):
    return (a.astype(F32) + b.astype(F32)).astype(BF16)


def chip_parts(partial):
    count, rows, columns = partial.shape
    core, x = lax.axis_index("stream") % 2, lax.axis_index("dp")
    split = partial.reshape(count, 4, 2, rows // 8, columns)
    chip = add_bf(take(split, core, 2), over_core(take(split, 1 - core, 2)))
    chip = chip.reshape(count, 2, 2, rows // 8, columns)
    return take(chip, x, 1), take(chip, 1 - x, 1)


def line_parts(stays, leaves):
    return add_bf(stays, over_x(leaves))


def last_parts(line):
    y = lax.axis_index("stream") // 2
    return take(line, y, 1), over_y(take(line, 1 - y, 1))


def plane_parts(stays, leaves):
    return last_parts(line_parts(stays, leaves))


def scatter_parts(partial):
    if not paired():
        whole = lax.psum_scatter(partial, ("dp", "stream"), scatter_dimension=1, tiled=True)
        return whole, jnp.zeros_like(whole)
    return plane_parts(*chip_parts(partial))


def add_kernel(turned, a_ref, b_ref, out_ref):
    total = a_ref[...].astype(F32) + b_ref[...].astype(F32)
    out_ref[...] = total.T if turned else total


def add_terms(a, b, turned):
    rows, columns = a.shape
    block = min(512, columns)
    return pl.pallas_call(
        functools.partial(add_kernel, turned),
        grid=(columns // block,),
        in_specs=[pl.BlockSpec((rows, block), lambda i: (0, i))] * 2,
        out_specs=pl.BlockSpec((block, rows), lambda i: (i, 0))
        if turned
        else pl.BlockSpec((rows, block), lambda i: (0, i)),
        out_shape=jax.ShapeDtypeStruct((columns, rows) if turned else (rows, columns), F32),
        cost_estimate=pl.CostEstimate(
            flops=rows * columns, bytes_accessed=8 * rows * columns, transcendentals=0
        ),
        name="add_terms",
    )(a, b)


def exchange_kernel(units, spread, axes, *refs):
    count, whole = len(axes), 2 if units else 0
    inputs, refs = refs[: units + count], refs[units + count :]
    partials, shard_refs = inputs[:units], inputs[units:]
    if units:
        done_in, near_in, beside_in = refs[:2], refs[2], refs[3]
        keep_ref, left_ref, right_ref = refs[4:7]
        lines_in, stays_in, leaves_in, streams_in = refs[7:9], refs[9], refs[10], refs[11:13]
        refs = refs[13:]
    outputs, refs = refs[: units + whole + count], refs[units + whole + count :]
    outs, wides, fulls = outputs[:units], outputs[units : units + whole], outputs[units + whole :]
    shares, refs = refs[:spread], refs[spread:]
    if units:
        grad_refs, refs = refs[:6], refs[6:]
    own_sem, near_send, near_recv = refs[:3]
    if units:
        held, got, load_sem, send_sem, recv_sem = refs[3:8]
        mine, theirs, below, pieces, piece_own, piece_send, piece_recv = refs[8:15]
        mine_sem, done_sem, core_send, core_recv, y_send, y_recv = refs[15:21]
        feed_own, feed_got, pair_own, pair_x, pair_y, wide_in, full_grad, from_core = refs[21:29]
        job_load, job_send, job_recv = refs[29:]
    x, stream, z = lax.axis_index("dp"), lax.axis_index("stream"), lax.axis_index("head")
    core = lax.rem(stream, 2)
    other_x, other_y, other_core = 1 - x, lax.rem(stream + 2, 4), stream + 1 - 2 * core
    line = ({"head": lax.rem(z + 1, 4)}, {"head": lax.rem(z + 3, 4)})
    to_x, to_y, to_core = {"dp": other_x}, {"stream": other_y}, {"stream": other_core}
    place = x * 4 + stream
    place_x, place_y = other_x * 4 + stream, x * 4 + other_y
    place_far = other_x * 4 + other_y
    beside = lambda at: at + 1 - 2 * core

    barrier = pltpu.get_barrier_semaphore()
    peers = (line if units or spread else ()) + ((to_x, to_y, to_core) if count else ())
    peers = peers + (({"head": lax.rem(z + 2, 4)},) if spread else ())
    for peer in peers:
        pl.semaphore_signal(barrier, inc=1, device_id=peer, device_id_type=pl.DeviceIdType.MESH)
    pl.semaphore_wait(barrier, len(peers))

    def region(w, at, part=None):
        full, width = fulls[w], shard_refs[w].shape[min(axes[w], 1)]
        rows, columns = shard_refs[w].shape
        start, size = (0, rows) if part is None else (part * (rows // 2), rows // 2)
        if axes[w] == 0:
            return full.at[pl.ds(pl.multiple_of(at * width + start, size), size)]
        column = at * width
        if axes[w] == 2:
            start = lax.rem(at, 2) * rows + start
            start, column = pl.multiple_of(start, size), lax.div(at, 2) * width
        return full.at[pl.ds(start, size), pl.ds(pl.multiple_of(column, width), width)]

    def near(w, index, source, target, peer):
        return pltpu.make_async_remote_copy(
            src_ref=source,
            dst_ref=target,
            send_sem=near_send.at[w, index],
            recv_sem=near_recv.at[w, index],
            device_id=peer,
            device_id_type=pl.DeviceIdType.MESH,
        )

    def pass_on(w, index, at, peer, part=None):
        return near(w, index, region(w, at, part), region(w, at, part), peer)

    def first(w):
        target = region(w, place)
        pltpu.make_async_copy(shard_refs[w], target, own_sem.at[w]).start()
        for index, peer in enumerate((to_x, to_y, to_core)):
            near(w, index, shard_refs[w], target, peer).start()

    def second(w):
        pass_on(w, 0, place_x, to_x).wait_recv()
        pass_on(w, 4, place_x, to_y, 0).start()
        pass_on(w, 3, place_x, to_core).start()
        pass_on(w, 1, place_y, to_y).wait_recv()
        pass_on(w, 6, place_y, to_x, 1).start()
        pass_on(w, 5, place_y, to_core).start()

    def third(w):
        pass_on(w, 4, place_far, to_y, 0).wait_recv()
        pass_on(w, 7, place_far, to_core, 0).start()
        pass_on(w, 6, place_far, to_x, 1).wait_recv()
        pass_on(w, 8, place_far, to_core, 1).start()

    def last(w):
        for index, at, part in (
            (2, place, None),
            (3, place_x, None),
            (5, place_y, None),
            (7, place_far, 0),
            (8, place_far, 1),
        ):
            pass_on(w, index, beside(at), to_core, part).wait_recv()
        pltpu.make_async_copy(shard_refs[w], region(w, place), own_sem.at[w]).wait()
        for index in (0, 1, 2):
            near(w, index, shard_refs[w], region(w, place), to_core).wait_send()
        for index, at, part in (
            (3, place_x, None),
            (4, place_x, 0),
            (5, place_y, None),
            (6, place_y, 1),
            (7, place_far, 0),
            (8, place_far, 1),
        ):
            pass_on(w, index, at, to_core, part).wait_send()

    for w in range(count):
        first(w)
    if not units:
        moves = []
        for i in range(spread):
            second(i)
        for i in range(spread):
            third(i)
        for i in range(spread):
            last(i)
            spread_own, spread_send, spread_recv = refs[3:6]
            rows, columns = shares[i].shape[0], fulls[i].shape[1]
            target = shares[i].at[:, pl.ds(pl.multiple_of(z * columns, columns), columns)]

            def source(at):
                start = (at * 8 + place) * rows
                return fulls[i].at[pl.ds(pl.multiple_of(start, rows), rows)]

            moves.append(pltpu.make_async_copy(source(z), target, spread_own.at[i]))
            for k in range(1, 4):
                to = lax.rem(z + k, 4)
                moves.append(
                    pltpu.make_async_remote_copy(
                        src_ref=source(to),
                        dst_ref=target,
                        send_sem=spread_send.at[i, k - 1],
                        recv_sem=spread_recv.at[i, k - 1],
                        device_id={"head": to},
                        device_id_type=pl.DeviceIdType.MESH,
                    )
                )
        for move in moves:
            move.start()
        for w in range(spread, count):
            second(w)
        for w in range(spread, count):
            third(w)
        for w in range(spread, count):
            last(w)
        for move in moves:
            move.wait()
        return

    feats = held.shape[-1]
    chunk = send_sem.shape[-1]
    tokens = held.shape[2]
    step_rows = tokens // chunk
    y = lax.div(stream, 2)

    def load(u, b):
        return pltpu.make_async_copy(
            partials[u].at[:, b * feats : (b + 1) * feats], held.at[u, b], load_sem.at[u, b]
        )

    def to_beside(v):
        return pltpu.make_async_remote_copy(
            src_ref=beside_in.at[:, v],
            dst_ref=theirs.at[v],
            send_sem=core_send.at[v],
            recv_sem=core_recv.at[v],
            device_id=to_core,
            device_id_type=pl.DeviceIdType.MESH,
        )

    def load_done(v):
        return pltpu.make_async_copy(
            done_in[v], pieces.at[v, pl.ds(0, done_in[v].shape[0])], done_sem.at[v]
        )

    def load_mine(v):
        return pltpu.make_async_copy(near_in.at[:, v], mine.at[v], mine_sem.at[v])

    def to_below(v):
        return pltpu.make_async_remote_copy(
            src_ref=mine.at[v, 1],
            dst_ref=below.at[v],
            send_sem=y_send.at[v],
            recv_sem=y_recv.at[v],
            device_id=to_y,
            device_id_type=pl.DeviceIdType.MESH,
        )

    for v in range(2):
        to_beside(v).start()
        load_mine(v).start()
        load_done(v).start()
    for u in range(units):
        for b in range(4):
            load(u, b).start()
    for u in range(units):
        for b in range(4):
            load(u, b).wait()

    def columns(block):
        return pl.ds(pl.multiple_of(block * feats, feats), feats)

    def part(c):
        return pl.ds(pl.multiple_of(c * step_rows, step_rows), step_rows)

    def hop(way, u, step, block, c):
        return pltpu.make_async_remote_copy(
            src_ref=held.at[u, block, part(c)],
            dst_ref=got.at[way, u, step, part(c)],
            send_sem=send_sem.at[way, u, step, c],
            recv_sem=recv_sem.at[way, u, step, c],
            device_id=line[way],
            device_id_type=pl.DeviceIdType.MESH,
        )

    ways = ((0, z), (1, 3 - z))

    def relay(way, v, step, block, c):
        target = wides[v].at[part(c), columns(block)]
        return pltpu.make_async_remote_copy(
            src_ref=pieces.at[v, part(c)] if step == 0 else target,
            dst_ref=target,
            send_sem=piece_send.at[way, v, step, c],
            recv_sem=piece_recv.at[way, v, step, c],
            device_id=line[way],
            device_id_type=pl.DeviceIdType.MESH,
        )

    def piece_at(way, step):
        return z - step if way == 0 else z + step

    def block_at(way, step):
        return 3 - step + z if way == 0 else step + z - 3

    def keep(v):
        return pltpu.make_async_copy(pieces.at[v], wides[v].at[:, columns(z)], piece_own.at[v])

    def over_parts(body, start=0, stop=None):
        def step(c, carry):
            body(c)
            return carry

        lax.fori_loop(start, chunk if stop is None else stop, step, 0)

    ready = done_in[0].shape[0] // step_rows
    early, late = (0, ready), (ready, chunk)

    def sum_step(step):
        def body(c):
            for way, rank in ways:

                @pl.when(rank <= step)
                def _():
                    block = block_at(way, step)
                    for u in range(units):
                        if step > 0:

                            @pl.when(rank > 0)
                            def _():
                                hop(way, u, step - 1, block, c).wait_recv()
                                total = held[u, block, part(c)].astype(F32) + got[
                                    way, u, step - 1, part(c)
                                ].astype(F32)
                                held[u, block, part(c)] = total.astype(BF16)

                        hop(way, u, step, block, c).start()

        over_parts(body)

    def gather_step(v, step, span):
        def body(c):
            for way, rank in ways:

                @pl.when((rank >= step) & (rank < 3))
                def _():
                    block = piece_at(way, step)
                    if step > 0:
                        relay(way, v, step - 1, block, c).wait_recv()
                    relay(way, v, step, block, c).start()

        over_parts(body, *span)

    def chip_sum(v):
        load_mine(v).wait()
        to_beside(v).wait()

        @pl.when(y == 1)
        def _():
            def body(c):
                total = mine[v, 1, part(c)].astype(F32) + theirs[v, 1, part(c)].astype(F32)
                mine[v, 1, part(c)] = total.astype(BF16)

            over_parts(body, 0, chunk - ready)
            to_below(v).start()

    def bring(v):
        def body(c, from_y):
            rows, out = part(c), part(c + ready)
            total = mine[v, 0, rows].astype(F32) + theirs[v, 0, rows].astype(F32)
            if from_y:
                total = total + below[v, rows].astype(F32)
            if v == 1:
                pieces[v, out] = total.astype(BF16)
            else:
                for head in range(feats // HD):
                    lanes = slice(head * HD, (head + 1) * HD)
                    pieces[v, out, lanes] = turn(
                        total[:, lanes], keep_ref[rows], -left_ref[rows], -right_ref[rows]
                    ).astype(BF16)

        @pl.when(y == 0)
        def _():
            to_below(v).wait_recv()
            over_parts(lambda c: body(c, True), 0, chunk - ready)

        @pl.when(y == 1)
        def _():
            over_parts(lambda c: body(c, False), 0, chunk - ready)

        keep(v).start()

    def job(index, source, target, peer):
        return pltpu.make_async_remote_copy(
            src_ref=source,
            dst_ref=target,
            send_sem=job_send.at[index],
            recv_sem=job_recv.at[index],
            device_id=peer,
            device_id_type=pl.DeviceIdType.MESH,
        )

    def job_in(index):
        source, target = (
            (lines_in[index].at[y], feed_own.at[index])
            if index < 2
            else (stays_in, pair_own.at[0])
            if index == 2
            else (streams_in[index - 3], wide_in.at[index - 3])
        )
        return pltpu.make_async_copy(source, target, job_load.at[index])

    def feed_job(f):
        return job(f, lines_in[f].at[1 - y], feed_got.at[f], to_y)

    def pair_x_job(i):
        source = full_grad.at[:, pl.ds(other_x * 2, 2), core] if i else leaves_in
        return job(2 + 4 * i, source, pair_x.at[i], to_x)

    def pair_y_job(i):
        return job(3 + 4 * i, pair_own.at[i, :, 1 - y], pair_y.at[i], to_y)

    def core_job(i):
        return job(4 + i, full_grad.at[i, :, 1 - core], from_core.at[i], to_core)

    def product(i):
        job_in(3 + i).wait()
        rows = full_grad.shape[3]
        for b in range(4):
            part_in = wide_in[i, :, b * 2 * rows : (b + 1) * 2 * rows]
            block = dot_tn(part_in, pieces[i]).astype(BF16)
            full_grad[i, b, 0] = block[:rows]
            full_grad[i, b, 1] = block[rows:]
        core_job(i).start()

    def both(a, b):
        return a.astype(F32) + b.astype(F32)

    def chip_grad():
        for i in range(2):
            core_job(i).wait()
            for b in range(4):
                full_grad[i, b, core] = both(full_grad[i, b, core], from_core[i, b]).astype(BF16)
        pair_x_job(1).start()

    def pair_line(i):
        pair_x_job(i).wait()
        for n in range(2):
            for k in range(2):
                stays = pair_own[i, n, k] if i == 0 else full_grad[n, x * 2 + k, core]
                pair_own[i, n, k] = both(stays, pair_x[i, n, k]).astype(BF16)
        pair_y_job(i).start()

    def pair_finish(i):
        pair_y_job(i).wait()
        total = [both(pair_own[i, n, y], pair_y[i, n]) for n in range(2)]
        grad_refs[2 + 2 * i][...] = total[0]
        grad_refs[3 + 2 * i][...] = total[1].T if i == 0 else total[1]

    def feed_finish():
        wide = min(512, feed_own.shape[2])
        for f in range(2):
            feed_job(f).wait()
            for c in range(0, feed_own.shape[2], wide):
                span = slice(c, c + wide)
                total = both(feed_own[f, :, span], feed_got[f, :, span])
                if f == 0:
                    grad_refs[0][:, span] = total
                else:
                    grad_refs[1][span] = total.T

    pair_x_job(0).start()
    for index in range(5):
        job_in(index).start()
    sum_step(0)
    for v in range(whole):
        load_done(v).wait()
        gather_step(v, 0, early)
    for v in range(whole):
        chip_sum(v)
    for w in range(count):
        second(w)
    for v in range(whole):
        bring(v)
        gather_step(v, 0, late)
    for f in range(2):
        feed_job(f).start()
    sum_step(1)
    for v in range(whole):
        gather_step(v, 1, early)
    for w in range(count):
        third(w)
    for i in range(2):
        product(i)
    for v in range(whole):
        gather_step(v, 1, late)
    job_in(2).wait()
    pair_line(0)
    sum_step(2)
    for v in range(whole):
        gather_step(v, 2, early)
    chip_grad()
    for f in range(2):
        job_in(f).wait()
    feed_finish()
    pair_finish(0)

    def finish(c):
        for u in range(units):
            outs[u][part(c)] = held[u, z, part(c)].astype(F32)
            for way, rank in ways:

                @pl.when(rank > 0)
                def _():
                    hop(way, u, 2, z, c).wait_recv()
                    outs[u][part(c)] += got[way, u, 2, part(c)].astype(F32)

    for v in range(whole):
        gather_step(v, 2, late)
    pair_line(1)
    over_parts(finish)
    for w in range(count):
        last(w)
    pair_finish(1)

    def drain(c):
        for way, rank in ways:

            @pl.when(rank == 3)
            def _():
                for v in range(whole):
                    for step in range(3):
                        relay(way, v, step, piece_at(way, step + 1), c).wait_recv()

        for step in range(3):
            for way, rank in ways:

                @pl.when(rank <= step)
                def _():
                    for u in range(units):
                        hop(way, u, step, block_at(way, step), c).wait_send()

                @pl.when((rank >= step) & (rank < 3))
                def _():
                    for v in range(whole):
                        relay(way, v, step, piece_at(way, step), c).wait_send()

    over_parts(drain)
    for v in range(whole):
        keep(v).wait()

        @pl.when(y == 1)
        def _():
            to_below(v).wait_send()


def exchange(partials, rows, shards_in, axes, collective_id, spread=0):
    units, count = len(partials), len(shards_in)
    grown = ((8, 1), (1, 8), (2, 4))
    shape = jax.ShapeDtypeStruct
    full = [
        shape(tuple(n * k for n, k in zip(w.shape, grown[axis])), BF16)
        for w, axis in zip(shards_in, axes)
    ]
    anywhere, local = pl.BlockSpec(memory_space=pl.ANY), pl.BlockSpec(memory_space=pltpu.VMEM)
    sems = pltpu.SemaphoreType.DMA
    out_specs, out_shape = [anywhere] * count, full
    in_specs = [anywhere] * (units + count)
    scratch = [sems((count,)), sems((count, 9)), sems((count, 9))]
    if units:
        tokens, feats = partials[0].shape[0], partials[0].shape[1] // 4
        chunk = 4
        in_specs = in_specs + [anywhere] * 4 + [local] * 3 + [anywhere] * 6
        last = rows[2].shape[2]
        line, stays = rows[7], rows[9]
        out_specs = [local] * units + [anywhere] * 2 + out_specs
        out_shape = (
            [shape((tokens, feats), F32)] * units + [shape((tokens, 4 * feats), BF16)] * 2 + out_shape
        )
        scratch = scratch + [
            pltpu.VMEM((units, 4, tokens, feats), BF16),
            pltpu.VMEM((2, units, 3, tokens, feats), BF16),
            sems((units, 4)),
            sems((2, units, 3, chunk)),
            sems((2, units, 3, chunk)),
            pltpu.VMEM((2, 2, last, feats), BF16),
            pltpu.VMEM((2, 2, last, feats), BF16),
            pltpu.VMEM((2, last, feats), BF16),
            pltpu.VMEM((2, tokens, feats), BF16),
            sems((2,)),
            sems((2, 2, 3, chunk)),
            sems((2, 2, 3, chunk)),
            sems((2,)),
            sems((2,)),
            sems((2,)),
            sems((2,)),
            sems((2,)),
            sems((2,)),
            pltpu.VMEM((2,) + line.shape[1:], BF16),
            pltpu.VMEM((2,) + line.shape[1:], BF16),
            pltpu.VMEM((2,) + stays.shape, BF16),
            pltpu.VMEM((2,) + stays.shape, BF16),
            pltpu.VMEM((2, 2) + stays.shape[2:], BF16),
            pltpu.VMEM((2,) + rows[11].shape, BF16),
            pltpu.VMEM((2, 4, 2) + stays.shape[2:], BF16),
            pltpu.VMEM((2, 4) + stays.shape[2:], BF16),
            sems((5,)),
            sems((8,)),
            sems((8,)),
        ]
        wide, narrow = line.shape[1:], stays.shape[2:]
        out_specs = out_specs + [local] * 6
        out_shape = out_shape + [
            shape(s, F32) for s in (wide, wide[::-1], narrow, narrow[::-1], narrow, narrow)
        ]
    if spread:
        out_specs = out_specs + [anywhere] * spread
        out_shape = out_shape + [
            shape((w.shape[0] // 4, w.shape[1] * 4), BF16) for w in shards_in[:spread]
        ]
        scratch = scratch + [sems((spread,))] + [sems((spread, 3))] * 2
    results = pl.pallas_call(
        functools.partial(exchange_kernel, units, spread, axes),
        in_specs=in_specs,
        out_specs=out_specs,
        out_shape=out_shape,
        scratch_shapes=scratch,
        compiler_params=pltpu.CompilerParams(
            collective_id=collective_id,
            has_side_effects=True,
            vmem_limit_bytes=VMEM_LIMIT,
        ),
        cost_estimate=pl.CostEstimate(
            flops=0, bytes_accessed=(600 if units else 240) * 1024 * 1024, transcendentals=0
        ),
        name="exchange",
    )(*partials, *shards_in, *rows)
    if not units:
        return results
    end = units + 2 + count
    return results[:units], results[units : units + 2], results[units + 2 : end], results[end:]


def head_sum_kernel(members, x_ref, out_ref, slots, send_sem, recv_sem):
    z = lax.axis_index("head")
    barrier = pltpu.get_barrier_semaphore()
    for k in range(1, members):
        pl.semaphore_signal(
            barrier,
            inc=1,
            device_id={"head": lax.rem(z + k, members)},
            device_id_type=pl.DeviceIdType.MESH,
        )
    pl.semaphore_wait(barrier, members - 1)
    copies = []
    for k in range(1, members):
        copy = pltpu.make_async_remote_copy(
            src_ref=x_ref,
            dst_ref=slots.at[z],
            send_sem=send_sem.at[k - 1],
            recv_sem=recv_sem.at[k - 1],
            device_id={"head": lax.rem(z + k, members)},
            device_id_type=pl.DeviceIdType.MESH,
        )
        copy.start()
        copies.append(copy)
    slots[z] = x_ref[...]
    for copy in copies:
        copy.wait()
    total = slots[0]
    for k in range(1, members):
        total = total + slots[k]
    out_ref[...] = total


def head_sum(x, collective_id):
    members = lax.axis_size("head")
    return pl.pallas_call(
        functools.partial(head_sum_kernel, members),
        out_shape=jax.ShapeDtypeStruct(x.shape, F32),
        in_specs=[pl.BlockSpec(memory_space=pltpu.VMEM)],
        out_specs=pl.BlockSpec(memory_space=pltpu.VMEM),
        scratch_shapes=[
            pltpu.VMEM((members,) + x.shape, F32),
            pltpu.SemaphoreType.DMA((members - 1,)),
            pltpu.SemaphoreType.DMA((members - 1,)),
        ],
        compiler_params=pltpu.CompilerParams(
            collective_id=collective_id, has_side_effects=True, vmem_limit_bytes=VMEM_LIMIT
        ),
        name="sum_over_head",
    )(x)


def turn(v, keep, left, right):
    h = ROT // 2
    return v * keep + pltpu.roll(v, HD - h, 1) * left + pltpu.roll(v, h, 1) * right


def rotate_kernel(sign, v_ref, keep_ref, left_ref, right_ref, out_ref):
    for head in range(v_ref.shape[1] // HD):
        part = pl.ds(head * HD, HD)
        out_ref[:, part] = turn(
            v_ref[:, part], keep_ref[...], sign * left_ref[...], sign * right_ref[...]
        ).astype(BF16)


def rotate(values_in, tables, sign):
    tokens, feats = values_in.shape
    block = min(tokens, 256)
    table = pl.BlockSpec((block, HD), lambda i: (i, 0))
    wide = pl.BlockSpec((block, feats), lambda i: (i, 0))
    return pl.pallas_call(
        functools.partial(rotate_kernel, sign),
        grid=(tokens // block,),
        in_specs=[wide, table, table, table],
        out_specs=wide,
        out_shape=jax.ShapeDtypeStruct((tokens, feats), BF16),
        cost_estimate=pl.CostEstimate(
            flops=5 * tokens * feats, bytes_accessed=8 * tokens * feats, transcendentals=0
        ),
        name="rotate_heads",
    )(values_in, *tables)


def feed_kernel(x_ref, d_ref, up_ref, down_ref, gated_ref, d_up_ref, grad_up_ref, grad_down_ref):
    tokens, model_width = x_ref.shape
    step = min(256, tokens)
    for r in range(0, tokens, step):
        rows = slice(r, r + step)
        up_pre = dot(x_ref[rows], up_ref[...])
        d_gated = dot_nt(d_ref[rows], down_ref[...])
        below = 0.5 * (1.0 + lax.erf(up_pre * 0.5**0.5))
        density = jnp.exp(-0.5 * up_pre * up_pre) * (2.0 * jnp.pi) ** -0.5
        gated_ref[rows] = (up_pre * below).astype(BF16)
        d_up_ref[rows] = (d_gated * (below + up_pre * density)).astype(BF16)
    wide = min(512, model_width)
    for c in range(0, model_width, wide):
        part = slice(c, c + wide)
        grad_up_ref[part] = dot_tn(x_ref[:, part], d_up_ref[...]).astype(BF16)
        grad_down_ref[part] = dot_tn(d_ref[:, part], gated_ref[...]).astype(BF16)


def feed_forward(x, d_out, up, down):
    tokens, model_width = x.shape
    hidden = up.shape[1]
    block = min(512, hidden)
    fixed = pl.BlockSpec((tokens, model_width), lambda i: (0, 0), pipeline_mode=pl.Buffered(1))
    narrow = pl.BlockSpec((tokens, block), lambda i: (0, i))
    column = pl.BlockSpec((model_width, block), lambda i: (0, i))
    shape = lambda rows: jax.ShapeDtypeStruct((rows, hidden), BF16)
    return pl.pallas_call(
        feed_kernel,
        grid=(hidden // block,),
        in_specs=[fixed, fixed, column, pl.BlockSpec((block, model_width), lambda i: (i, 0))],
        out_specs=[narrow, narrow, column, column],
        out_shape=[shape(tokens), shape(tokens), shape(model_width), shape(model_width)],
        compiler_params=pltpu.CompilerParams(vmem_limit_bytes=VMEM_LIMIT),
        cost_estimate=pl.CostEstimate(
            flops=8 * tokens * model_width * hidden,
            bytes_accessed=4 * model_width * (2 * hidden + tokens),
            transcendentals=0,
        ),
        name="feed_forward",
    )(x, d_out, up, down)


def attention_kernel(
    extra, place_ref, q_ref, do_ref, start_ref, valid_ref, keep_ref, left_ref, right_ref, *refs
):
    blocks = (len(refs) - 6 - extra) // 2
    k_refs, v_refs = refs[:blocks], refs[blocks : 2 * blocks]
    o_ref, dq_ref, near_ref, beside_ref, s_ref, dp_ref = refs[2 * blocks + extra :]
    grad_ref = lambda j: (beside_ref if j % 2 else near_ref).at[j // 2]
    rows = q_ref.shape[1]
    scale = HD ** (-0.5)
    member = place_ref[0]
    keep, left, right = keep_ref[0], left_ref[0], right_ref[0]
    q = turn(q_ref[0], keep, left, right).astype(BF16)
    d_out = do_ref[0]
    start = start_ref[0]
    top = jnp.full((rows, 1), MASKED, F32)
    t = member * rows + lax.broadcasted_iota(jnp.int32, (rows, rows), 0)
    for j in range(blocks):
        u = place_ref[j] * rows + lax.broadcasted_iota(jnp.int32, (rows, rows), 1)
        allowed = (u <= t) & (u >= start)
        s_ref[j] = jnp.where(allowed, dot_nt(q, k_refs[j][0]) * scale, MASKED)
        top = jnp.maximum(top, jnp.max(s_ref[j], axis=1, keepdims=True))
    total = jnp.zeros((rows, 1), F32)
    for j in range(blocks):
        e = jnp.exp(s_ref[j] - top)
        s_ref[j] = e
        total = total + jnp.sum(e, axis=1, keepdims=True)
    inverse = 1.0 / total
    out = jnp.zeros((rows, HD), F32)
    delta = jnp.zeros((rows, 1), F32)
    for j in range(blocks):
        p = s_ref[j] * inverse
        s_ref[j] = p
        p_bf = p.astype(BF16)
        out = out + dot(p_bf, v_refs[j][0])
        grad_ref(j)[1] = dot_tn(p_bf, d_out).astype(BF16)
        d_p = dot_nt(d_out, v_refs[j][0])
        dp_ref[j] = d_p
        delta = delta + jnp.sum(p * d_p, axis=1, keepdims=True)
    o_ref[0] = (out * valid_ref[0]).astype(BF16)
    d_q = jnp.zeros((rows, HD), F32)
    for j in range(blocks):
        d_s = (s_ref[j] * (dp_ref[j] - delta)).astype(BF16)
        d_q = d_q + dot(d_s, k_refs[j][0])
        grad_ref(j)[0] = (dot_tn(d_s, q) * scale).astype(BF16)
    dq_ref[0] = turn(d_q * scale, keep, -left, -right).astype(BF16)


def attention(index, places, queries, d_attended, starts, valid, tables, keys, values, earlier):
    micro, rows, feats = queries.shape
    blocks = len(keys)
    tile = pl.BlockSpec((1, rows, HD), lambda h: (index, 0, h))
    fixed = lambda width: pl.BlockSpec((1, rows, width), lambda h: (index, 0, 0))
    grad_tile = pl.BlockSpec((blocks // 2, 2, rows, HD), lambda h: (0, 0, 0, h))
    shape = lambda *lead: jax.ShapeDtypeStruct(lead + (rows, feats), BF16)
    return pl.pallas_call(
        functools.partial(attention_kernel, len(earlier)),
        grid=(feats // HD,),
        in_specs=[pl.BlockSpec(memory_space=pltpu.SMEM), tile, tile]
        + [fixed(1)] * 2
        + [fixed(HD)] * 3
        + [tile] * (2 * blocks)
        + [pl.BlockSpec(memory_space=pl.ANY)] * len(earlier),
        out_specs=[tile] * 2 + [grad_tile] * 2,
        out_shape=[shape(micro)] * 2 + [shape(blocks // 2, 2)] * 2,
        input_output_aliases={8 + 2 * blocks + i: i for i in range(len(earlier))},
        scratch_shapes=[
            pltpu.VMEM((blocks, rows, rows), F32),
            pltpu.VMEM((blocks, rows, rows), F32),
        ],
        compiler_params=pltpu.CompilerParams(vmem_limit_bytes=VMEM_LIMIT),
        cost_estimate=pl.CostEstimate(
            flops=0,
            bytes_accessed=1024,
            transcendentals=0,
        ),
        name="attention_both_ways",
    )(places, queries, d_attended, starts, valid, *tables, *keys, *values, *earlier)


def exchange_rows(local):
    if lax.axis_size("stream") != 4:
        raise ValueError("stream")
    across = lax.ppermute(local, "stream", [(0, 2), (1, 3)])
    beside = over_core(local)
    return (local, beside, across, over_core(across))


def add_f32(a, b):
    return a.astype(F32) + b.astype(F32)


def over_line(a):
    return lax.ppermute(a, "stream", [(2, 0), (3, 1)])


def columns_of(pieces, rows):
    lane = lax.broadcasted_iota(jnp.int32, (rows, 128), 1)
    out = jnp.zeros((rows, 128), F32)
    for index, piece in enumerate(pieces):
        out = jnp.where(lane == index, piece, out)
    return out


def row_sum(a):
    return jnp.sum(a, axis=1, keepdims=True)


def streams_kernel(weights_ref, history_ref, streams_ref, stats_ref):
    weights = weights_ref[...]
    layers = [history_ref[j].astype(F32) for j in range(HIST)]
    sums, squares = [], []
    for s in range(4):
        total = weights[:, s * HIST : s * HIST + 1] * layers[0]
        for j in range(1, HIST):
            total = total + weights[:, s * HIST + j : s * HIST + j + 1] * layers[j]
        streams_ref[s] = total
        sums.append(row_sum(total))
        squares.append(row_sum(total * total))
    stats_ref[...] = columns_of(sums + squares, weights.shape[0]).T[:8]


def mix_streams(weights, history):
    _, tokens, feats = history.shape
    block = min(128, tokens)
    return pl.pallas_call(
        streams_kernel,
        grid=(tokens // block,),
        in_specs=[
            pl.BlockSpec((block, weights.shape[1]), lambda i: (i, 0)),
            pl.BlockSpec((HIST, block, feats), lambda i: (0, i, 0)),
        ],
        out_specs=[
            pl.BlockSpec((4, block, feats), lambda i: (0, i, 0)),
            pl.BlockSpec((8, block), lambda i: (0, i)),
        ],
        out_shape=[
            jax.ShapeDtypeStruct((4, tokens, feats), F32),
            jax.ShapeDtypeStruct((8, tokens), F32),
        ],
        compiler_params=pltpu.CompilerParams(vmem_limit_bytes=VMEM_LIMIT),
        cost_estimate=pl.CostEstimate(
            flops=80 * tokens * feats, bytes_accessed=34 * tokens * feats, transcendentals=0
        ),
        name="mix_streams",
    )(weights, history)


def early_kernel(streams_ref, cot_ref, history_ref, out_ref):
    cot = cot_ref[...].astype(F32)
    plain, crossed, direct = [], [], []
    layers = [history_ref[j].astype(F32) for j in range(HIST)]
    for layer in layers:
        plain.append(row_sum(layer))
        direct.append(row_sum(cot * layer))
    for s in range(4):
        for layer in layers:
            crossed.append(row_sum(streams_ref[s] * layer))
    out_ref[...] = columns_of(crossed + plain + direct, cot.shape[0]).T[:64].astype(BF16)


def early_sums(streams, cot, history):
    _, tokens, feats = streams.shape
    block = min(128, tokens)
    return pl.pallas_call(
        early_kernel,
        grid=(tokens // block,),
        in_specs=[
            pl.BlockSpec((4, block, feats), lambda i: (0, i, 0)),
            pl.BlockSpec((block, feats), lambda i: (i, 0)),
            pl.BlockSpec((HIST, block, feats), lambda i: (0, i, 0)),
        ],
        out_specs=pl.BlockSpec((64, block), lambda i: (0, i)),
        out_shape=jax.ShapeDtypeStruct((64, tokens), BF16),
        compiler_params=pltpu.CompilerParams(vmem_limit_bytes=VMEM_LIMIT),
        cost_estimate=pl.CostEstimate(
            flops=110 * tokens * feats, bytes_accessed=36 * tokens * feats, transcendentals=0
        ),
        name="early_sums",
    )(streams, cot, history)


def sums_kernel(
    g0, g1, g2, g3, streams_ref, stats_ref, gain_ref, history_ref, dots_ref, out_ref, edge_ref
):
    stats = stats_ref[...]
    rows = stats.shape[0]

    @pl.when(pl.program_id(0) == 0)
    def _():
        edge_ref[...] = jnp.zeros_like(edge_ref)

    firsts, seconds, dots = [], [], []
    for s, g_ref in enumerate((g0, g1, g2, g3)):
        g = g_ref[...].astype(F32)
        centered = (streams_ref[s] - stats[:, s : s + 1]) * stats[:, 4 + s : 5 + s]
        edge_ref[s : s + 1] += jnp.sum(g * centered, axis=0, keepdims=True)
        edge_ref[4 + s : 5 + s] += jnp.sum(g, axis=0, keepdims=True)
        scaled = g * gain_ref[s : s + 1]
        firsts.append(row_sum(scaled))
        seconds.append(row_sum(scaled * centered))
        for j in range(HIST):
            dots.append(row_sum(scaled * history_ref[j].astype(F32)))
    dots_ref[...] = columns_of(dots, rows).T[:48].astype(BF16)
    out_ref[...] = columns_of(firsts + seconds, rows).T[:8]


def gradient_sums(grads, streams, stats, gain, history):
    _, tokens, feats = streams.shape
    block = min(128, tokens)
    wide = pl.BlockSpec((block, feats), lambda i: (i, 0))
    return pl.pallas_call(
        sums_kernel,
        grid=(tokens // block,),
        in_specs=[wide] * 4
        + [
            pl.BlockSpec((4, block, feats), lambda i: (0, i, 0)),
            pl.BlockSpec((block, 8), lambda i: (i, 0)),
            pl.BlockSpec((4, feats), lambda i: (0, 0)),
            pl.BlockSpec((HIST, block, feats), lambda i: (0, i, 0)),
        ],
        out_specs=[
            pl.BlockSpec((48, block), lambda i: (0, i)),
            pl.BlockSpec((8, block), lambda i: (0, i)),
            pl.BlockSpec((8, feats), lambda i: (0, 0)),
        ],
        out_shape=[
            jax.ShapeDtypeStruct((48, tokens), BF16),
            jax.ShapeDtypeStruct((8, tokens), F32),
            jax.ShapeDtypeStruct((8, feats), F32),
        ],
        compiler_params=pltpu.CompilerParams(vmem_limit_bytes=VMEM_LIMIT),
        cost_estimate=pl.CostEstimate(
            flops=110 * tokens * feats, bytes_accessed=42 * tokens * feats, transcendentals=0
        ),
        name="gradient_sums",
    )(*grads, streams, stats, gain, history)


def totals_kernel(members, *refs):
    ins, outs, slots, sems = refs[:3], refs[3:6], refs[6:9], refs[9:]
    z = lax.axis_index("head")
    line = [{"head": lax.rem(z + k, members)} for k in range(1, members)]
    barrier = pltpu.get_barrier_semaphore()
    for peer in line:
        pl.semaphore_signal(barrier, inc=1, device_id=peer, device_id_type=pl.DeviceIdType.MESH)
    pl.semaphore_wait(barrier, len(line))
    copies = []
    for index in range(3):
        for k, peer in enumerate(line):
            copy = pltpu.make_async_remote_copy(
                src_ref=ins[index],
                dst_ref=slots[index].at[z],
                send_sem=sems[2 * index].at[k],
                recv_sem=sems[2 * index + 1].at[k],
                device_id=peer,
                device_id_type=pl.DeviceIdType.MESH,
            )
            copy.start()
            copies.append(copy)
        slots[index][z] = ins[index][...]
    for copy in copies:
        copy.wait()
    for index in range(3):
        total = slots[index][0].astype(F32)
        for k in range(1, members):
            total = total + slots[index][k].astype(F32)
        outs[index][...] = total


def head_totals(arrays, collective_id):
    members = lax.axis_size("head")
    local = pl.BlockSpec(memory_space=pltpu.VMEM)
    return pl.pallas_call(
        functools.partial(totals_kernel, members),
        in_specs=[local] * 3,
        out_specs=[local] * 3,
        out_shape=[jax.ShapeDtypeStruct(a.shape, F32) for a in arrays],
        scratch_shapes=[pltpu.VMEM((members,) + a.shape, a.dtype) for a in arrays]
        + [pltpu.SemaphoreType.DMA((members - 1,))] * 6,
        compiler_params=pltpu.CompilerParams(
            collective_id=collective_id, has_side_effects=True, vmem_limit_bytes=VMEM_LIMIT
        ),
        name="totals_over_head",
    )(*arrays)


def small_kernel(
    members,
    plane,
    dots_ref,
    early_ref,
    sums_ref,
    stats_ref,
    pre_ref,
    slope_ref,
    hidden_ref,
    rms_ref,
    w_ref,
    current_ref,
    edge_ref,
    small_ref,
    scaled_ref,
    coef_ref,
    got,
    d_mix_ref,
    rows_ref,
    plane_send,
    plane_recv,
):
    x, stream = lax.axis_index("dp"), lax.axis_index("stream")
    near = (
        {"stream": stream + 1 - 2 * lax.rem(stream, 2)},
        {"stream": lax.rem(stream + 2, 4)},
        {"dp": 1 - x},
    )
    near = near if plane else ()
    if plane:
        barrier = pltpu.get_barrier_semaphore()
        for peer in near:
            pl.semaphore_signal(
                barrier, inc=1, device_id=peer, device_id_type=pl.DeviceIdType.MESH
            )
        pl.semaphore_wait(barrier, len(near))
    n = 4 * HIST
    model_width = members * small_ref.shape[1]
    plain = early_ref[n : n + HIST]
    rows_ref[...] = jnp.zeros_like(rows_ref)
    rows_ref[0:8] = sums_ref[...] / model_width
    for s in range(4):
        part = slice(s * HIST, (s + 1) * HIST)
        mean, inverse = stats_ref[s : s + 1], stats_ref[4 + s : 5 + s]
        crossed = (early_ref[part] - mean * plain) * inverse
        d_part = inverse * (
            dots_ref[part] - rows_ref[s : s + 1] * plain - rows_ref[4 + s : 5 + s] * crossed
        )
        if s == 3:
            d_part = d_part + early_ref[n + HIST : n + 2 * HIST]
        d_mix_ref[part] = d_part
    d_mix = d_mix_ref[...]
    high = dict(precision=HIGHEST, preferred_element_type=F32)
    d_pre = jnp.dot(w_ref[...], d_mix, **high) * slope_ref[...]
    rms = rms_ref[...]
    cross = jnp.sum(d_pre * pre_ref[...], axis=0, keepdims=True)
    rows_ref[8:9] = rms * rms * cross / model_width
    coef_ref[...] = rows_ref[...].T
    scaled = d_pre * rms
    scaled_ref[...] = scaled
    small_ref[...] = jnp.zeros_like(small_ref)
    small_ref[0:n] = jnp.dot(scaled, current_ref[...].astype(F32), **high)
    small_ref[n : n + 8] = edge_ref[...]
    small_ref[n + 8 : 2 * n + 8, 0:n] = lax.dot_general(
        hidden_ref[...], d_mix, (((1,), (1,)), ((), ())), **high
    )
    small_ref[n + 8 : 2 * n + 8, n : n + 1] = jnp.sum(d_mix, axis=1, keepdims=True)
    for step, peer in enumerate(near):
        copy = pltpu.make_async_remote_copy(
            src_ref=small_ref,
            dst_ref=got.at[step],
            send_sem=plane_send.at[step],
            recv_sem=plane_recv.at[step],
            device_id=peer,
            device_id_type=pl.DeviceIdType.MESH,
        )
        copy.start()
        copy.wait()
        small_ref[...] += got[step]


def small_gradients(dots, early, sums, stats, pre, slope, hidden, rms, w_out, current, edges):
    members, plane = lax.axis_size("head"), paired()
    tokens, feats = current.shape
    n = 4 * HIST
    shape = jax.ShapeDtypeStruct
    sems = pltpu.SemaphoreType.DMA
    small, scaled, coefs = pl.pallas_call(
        functools.partial(small_kernel, members, plane),
        in_specs=[pl.BlockSpec(memory_space=pltpu.VMEM)] * 11,
        out_specs=[pl.BlockSpec(memory_space=pltpu.VMEM)] * 3,
        out_shape=[shape((80, feats), F32), shape((n, tokens), F32), shape((tokens, 128), F32)],
        scratch_shapes=[
            pltpu.VMEM((3, 80, feats), F32),
            pltpu.VMEM((n, tokens), F32),
            pltpu.VMEM((128, tokens), F32),
            sems((3,)),
            sems((3,)),
        ],
        compiler_params=pltpu.CompilerParams(
            collective_id=3 if plane else None,
            has_side_effects=plane,
            vmem_limit_bytes=VMEM_LIMIT,
        ),
        name="small_gradients",
    )(dots, early, sums, stats, pre, slope, hidden, rms, w_out, current, edges)
    if not plane:
        small = lax.psum(small.astype(BF16), ("dp", "stream")).astype(F32)
    return small, scaled, coefs


def history_kernel(
    g0, g1, g2, g3, streams_ref, stats_ref, gain_ref, cot_ref, current_ref, weights_ref, coef_ref, d_ref, w_ref, out_ref
):
    stats, weights, coefs = stats_ref[...], weights_ref[...], coef_ref[...]
    d_streams = []
    for s, g_ref in enumerate((g0, g1, g2, g3)):
        inverse = stats[:, 4 + s : 5 + s]
        centered = (streams_ref[s] - stats[:, s : s + 1]) * inverse
        scaled = g_ref[...].astype(F32) * gain_ref[s : s + 1]
        d_streams.append(
            inverse * (scaled - coefs[:, s : s + 1] - centered * coefs[:, 4 + s : 5 + s])
        )
    d_streams[3] = d_streams[3] + cot_ref[...].astype(F32)
    for j in range(HIST):
        total = weights[:, j : j + 1] * d_streams[0]
        for s in range(1, 4):
            total = total + weights[:, s * HIST + j : s * HIST + j + 1] * d_streams[s]
        if j == HIST - 1:
            total = total + lax.dot_general(
                d_ref[...],
                w_ref[...],
                (((0,), (0,)), ((), ())),
                precision=HIGHEST,
                preferred_element_type=F32,
            )
            total = total - current_ref[...].astype(F32) * coefs[:, 8:9]
        out_ref[j] = total


def history_gradient(grads, streams, stats, gain, cot, current, weights, coefs, d_scaled, w_rows):
    _, tokens, feats = streams.shape
    block = min(128, tokens)
    wide = pl.BlockSpec((block, feats), lambda i: (i, 0))
    narrow = lambda a: pl.BlockSpec((block, a.shape[1]), lambda i: (i, 0))
    fixed = lambda a: pl.BlockSpec(a.shape, lambda i: (0, 0))
    return pl.pallas_call(
        history_kernel,
        grid=(tokens // block,),
        in_specs=[wide] * 4
        + [
            pl.BlockSpec((4, block, feats), lambda i: (0, i, 0)),
            narrow(stats),
            fixed(gain),
            wide,
            wide,
            narrow(weights),
            narrow(coefs),
            pl.BlockSpec((d_scaled.shape[0], block), lambda i: (0, i)),
            fixed(w_rows),
        ],
        out_specs=pl.BlockSpec((HIST, block, feats), lambda i: (0, i, 0)),
        out_shape=jax.ShapeDtypeStruct((HIST, tokens, feats), F32),
        compiler_params=pltpu.CompilerParams(vmem_limit_bytes=VMEM_LIMIT),
        cost_estimate=pl.CostEstimate(
            flops=110 * tokens * feats, bytes_accessed=64 * tokens * feats, transcendentals=0
        ),
        name="history_gradient",
    )(*grads, streams, stats, gain, cot, current, weights, coefs, d_scaled, w_rows)


def shards(
    history,
    seq_lens,
    bucket_slot,
    w_mix_in,
    w_mix_out,
    mix_bias,
    ln_gain,
    ln_bias,
    w_qkv,
    w_attn_out,
    w_up,
    w_down,
    cotangent,
):
    member = lax.axis_index("stream")
    micro, quarter, feats = history.shape[1:]
    tokens = micro * quarter
    model_width = feats * lax.axis_size("head")
    slot_base = lax.axis_index("dp") * micro
    slot_ids = jnp.arange(bucket_slot.shape[0], dtype=jnp.int32)
    query_places = member * quarter + jnp.arange(quarter, dtype=jnp.int32)
    w_mix_in_f = w_mix_in.astype(F32)
    w_mix_out_f = w_mix_out.astype(F32)

    segments, starts = [], []
    for index in range(micro):
        bucket = jnp.sum(jnp.where(slot_ids == slot_base + index, bucket_slot, 0))
        lengths = jnp.sum(jnp.where(slot_ids[:, None] == bucket, seq_lens, 0), axis=0)
        bounds = jnp.cumsum(lengths)
        passed = (query_places[:, None] >= bounds[None, :]).astype(jnp.int32)
        segments.append(jnp.sum(passed, axis=1))
        starts.append(jnp.sum(passed * lengths[None, :], axis=1))
    valid = (jnp.concatenate(segments) < 3).astype(F32)[:, None]
    starts = jnp.concatenate(starts)
    position = jnp.tile(query_places, micro) - starts
    frequency = jnp.arange(ROT // 2, dtype=F32)
    phases = position.astype(F32)[:, None] * (10000.0 ** (-2.0 * frequency / ROT))
    cosine, sine = jnp.cos(phases), jnp.sin(phases)
    plain = jnp.zeros((tokens, HD - ROT), F32)
    none = jnp.zeros_like(sine)
    tables = (
        jnp.concatenate([cosine, cosine, plain + 1.0], axis=1),
        jnp.concatenate([-sine, none, plain], axis=1),
        jnp.concatenate([none, sine, plain], axis=1),
    )

    cot_rows = cotangent.reshape(tokens, feats).astype(F32) * valid
    cot_bf = cot_rows.astype(BF16)
    duplex = lined()

    history = history.reshape(HIST, tokens, feats)
    current = history[HIST - 1]
    current_f = current.astype(F32)
    mixed = lax.dot_general(w_mix_in, current, (((0,), (1,)), ((), ())), preferred_element_type=F32)
    square = jnp.sum(current_f * current_f, axis=1)[None]
    mixed = head_sum(jnp.concatenate([mixed, square]), 0).T
    mixed, cot_bf, w_up = lax.optimization_barrier((mixed, cot_bf, w_up))
    out_full = lax.all_gather(cot_bf, "head", axis=1, tiled=True)
    if duplex:
        (up_full,) = exchange([], (), [w_up], (0,), 4)
        mixed, up_full = lax.optimization_barrier((mixed, up_full))
    rms_scale = lax.rsqrt(mixed[:, 4 * HIST :] / model_width + EPSILON)
    mix_pre = mixed[:, : 4 * HIST] * rms_scale
    below_mix = 0.5 * (1.0 + lax.erf(mix_pre * 0.5**0.5))
    mix_hidden = gelu_exact(mix_pre)
    slope_mix = below_mix + mix_pre * jnp.exp(-0.5 * mix_pre * mix_pre) * (2.0 * jnp.pi) ** -0.5
    mix_weights = jnp.dot(mix_hidden, w_mix_out_f, precision=HIGHEST) + mix_bias.reshape(-1)
    streams, stats = mix_streams(mix_weights, history)
    stats = head_sum(stats, 1)
    stat_sum, stat_square = stats[:4], stats[4:]
    row_means = (stat_sum / model_width)[:, :, None]
    inv_std = lax.rsqrt(stat_square[:, :, None] / model_width - row_means * row_means + EPSILON)
    centered = (streams - row_means) * inv_std
    row_stats = jnp.concatenate([row_means[..., 0], inv_std[..., 0]]).T
    normed = (centered * ln_gain[:, None, :] + ln_bias[:, None, :]).astype(BF16)

    def all_features(a):
        return lax.all_gather(a, "head", axis=1, tiled=True)

    if duplex:
        w_down, normed = lax.optimization_barrier((w_down, normed))
        wk, wv, down_full, w_out_full, wq, *shares = exchange(
            [], (), [w_qkv[1], w_qkv[2], w_down, w_attn_out, w_qkv[0]], (0, 0, 1, 1, 0), 6, 2
        )
    else:
        wq, wk, wv = gather_weight(w_qkv, 1)
        w_out_full, down_full = gather_weight(w_attn_out, 1), gather_weight(w_down, 1)
        up_full = gather_weight(w_up, 0)

    def to_owner(partial):
        return lax.psum_scatter(
            partial.astype(BF16), "head", scatter_dimension=1, tiled=True
        ).astype(F32)

    up_out, out_full = lax.optimization_barrier((normed[3], out_full))
    up_in, k_out, down_full = lax.optimization_barrier(
        (all_features(up_out), normed[1], down_full)
    )
    k_in, v_out = lax.optimization_barrier((all_features(k_out), normed[2]))
    gated_up, d_up, product_up, product_down = feed_forward(up_in, out_full, up_full, down_full)
    feed_products = [product_up[None], product_down[None]]
    feed_parts = [chip_parts(a) if paired() else a for a in feed_products]
    v_out, d_up, feed_parts = lax.optimization_barrier((v_out, d_up, feed_parts))
    feed_lines = [line_parts(*a) for a in feed_parts] if paired() else feed_parts
    streams_late, feed_lines[0] = lax.optimization_barrier((streams, feed_lines[0]))
    early = early_sums(streams_late, cot_bf, history)
    feed = dot(gated_up, down_full).astype(BF16)
    d_attended = dot_nt(out_full, w_out_full).astype(BF16) * valid.astype(BF16)
    d_up_in = dot_nt(d_up, up_full).astype(BF16)
    keys = rotate(dot(k_in, wk), tables, 1.0)
    v_in, q_out, early, feed, d_attended, d_up_in, keys, wk, wv = lax.optimization_barrier(
        (all_features(v_out), normed[0], early, feed, d_attended, d_up_in, keys, wk, wv)
    )
    values = dot(v_in, wv).astype(BF16)
    by_micro = lambda a: a.reshape((micro, quarter) + a.shape[1:])
    key_blocks = exchange_rows(by_micro(keys))
    value_blocks = exchange_rows(by_micro(values))
    d_up_in, key_blocks, value_blocks = lax.optimization_barrier(
        (d_up_in, key_blocks, value_blocks)
    )
    q_in, key_blocks, value_blocks, feed_lines[1], early = lax.optimization_barrier(
        (all_features(q_out), key_blocks, value_blocks, feed_lines[1], early)
    )
    g_up = to_owner(d_up_in)
    product = lambda a, b: dot_tn(a, b).astype(BF16)

    queries = dot(q_in, wq)
    places = member ^ jnp.arange(4, dtype=jnp.int32)
    earlier, d_rows = (), []
    queries = by_micro(queries)
    for index in range(micro):
        results = attention(
            index,
            places,
            queries,
            by_micro(d_attended),
            by_micro(starts[:, None]),
            by_micro(valid),
            tuple(by_micro(a) for a in tables),
            key_blocks,
            value_blocks,
            earlier,
        )
        earlier = results[:2]
        if duplex and index == micro - 1:
            continue
        chip = add_f32(results[2], over_core(results[3]))
        across = chip[1].astype(BF16)
        queries, across = lax.optimization_barrier((queries, across))
        d_rows.append(add_f32(chip[0], over_line(across)))
    attended, d_query_pre = (a.reshape(tokens, feats) for a in earlier)
    d_key_rows = jnp.concatenate([a[0] for a in d_rows])
    done = d_key_rows.shape[0]
    d_key_rows = rotate(d_key_rows, tuple(a[:done] for a in tables), -1.0)
    d_value_rows = jnp.concatenate([a[1] for a in d_rows]).astype(BF16)
    attended, d_query_pre, d_key_rows, d_value_rows = lax.optimization_barrier(
        (attended, d_query_pre, d_key_rows, d_value_rows)
    )

    products = jnp.stack([product(q_in, d_query_pre), product(out_full, attended)])
    if duplex:
        partials = [dot_nt(d_query_pre, wq).astype(BF16)]
        parts = chip_parts(products)
        partials, parts, g_up, feed_lines = lax.optimization_barrier(
            (partials, parts, g_up, feed_lines)
        )
        (g_query,), (d_key_full, d_value_full), (wk_rows, wv_rows), plane_grads = exchange(
            partials,
            [d_key_rows, d_value_rows, results[2], results[3], *(a[done:] for a in tables)]
            + [a[0] for a in feed_lines]
            + [*parts, k_in, v_in],
            shares,
            (0, 0),
            5,
        )
        attended_late, g_query = lax.optimization_barrier((attended, g_query))
        cut = 3 * tokens // 8
        pair = lambda a: (a[:cut], a[cut:])
        halves = [
            (dot(a, w_out_full) + b).astype(BF16) for a, b in zip(pair(attended_late), pair(feed))
        ]
        branch = to_owner(halves[0])
        g_key, g_value = dot_nt(d_key_full, wk_rows), dot_nt(d_value_full, wv_rows)
    else:
        g_query = to_owner(dot_nt(d_query_pre, wq))
        branch = to_owner(dot(attended, w_out_full) + feed)
        terms = scatter_parts(products)
        feed_terms = [scatter_parts(a) for a in feed_products]
        g_key = to_owner(dot_nt(d_key_rows, wk))
        g_value = to_owner(dot_nt(d_value_rows, wv))
        kv_terms = scatter_parts(
            jnp.stack([product(k_in, d_key_rows), product(v_in, d_value_rows)])
        )
    grads = (g_query, g_key, g_value, g_up)
    dots, sums, edges = gradient_sums(grads, streams, row_stats, ln_gain, history)
    dots, early, sums = head_totals((dots, early, sums), 7)
    if duplex:
        sums, second_half = lax.optimization_barrier((sums, halves[1]))
        branch = jnp.concatenate([branch, to_owner(second_half)])
        grad_up, grad_down, grad_query, grad_attn_out, grad_key, grad_value = plane_grads
        grad_qkv = jnp.stack([grad_query, grad_key, grad_value])
    else:
        grad_up = add_terms(feed_terms[0][0][0], feed_terms[0][1][0], False)
        grad_down = add_terms(feed_terms[1][0][0], feed_terms[1][1][0], True)
        grad_attn_out = add_terms(terms[0][1], terms[1][1], True)
        grad_qkv = jnp.concatenate([add_f32(terms[0][:1], terms[1][:1]), add_f32(*kv_terms)])
    small, d_scaled, coefs = small_gradients(
        dots, early, sums, row_stats.T, mix_pre.T, slope_mix.T, mix_hidden.T, rms_scale.T, w_mix_out_f, current, edges
    )
    block_out = (valid * (streams[3] + branch)).astype(BF16)
    history_grad = history_gradient(
        grads, streams, row_stats, ln_gain, cot_bf, current, mix_weights, coefs, d_scaled, w_mix_in_f.T
    ).reshape(HIST, micro, quarter, feats)
    n = 4 * HIST
    return (
        block_out.reshape(micro, quarter, feats),
        mix_weights.reshape(micro, quarter, 4 * HIST),
        history_grad,
        small[:n].T,
        small[n + 8 : 2 * n + 8, :n],
        small[n + 8 : 2 * n + 8, n].reshape(mix_bias.shape),
        small[n : n + 4],
        small[n + 4 : n + 8],
        grad_qkv,
        grad_attn_out,
        grad_up,
        grad_down,
    )


def solution(mesh):
    return jax.shard_map(
        shards,
        mesh=mesh,
        in_specs=(
            P(None, "dp", "stream", "head"),
            P(),
            P(),
            P("head", None),
            P(),
            P(),
            P(None, "head"),
            P(None, "head"),
            P(None, ("dp", "stream"), "head"),
            P("head", ("dp", "stream")),
            P(("dp", "stream"), "head"),
            P("head", ("dp", "stream")),
            P("dp", "stream", "head"),
        ),
        out_specs=(
            P("dp", "stream", "head"),
            P("dp", "stream", None),
            P(None, "dp", "stream", "head"),
            P("head", None),
            P(),
            P(),
            P(None, "head"),
            P(None, "head"),
            P(None, ("dp", "stream"), "head"),
            P("head", ("dp", "stream")),
            P(("dp", "stream"), "head"),
            P("head", ("dp", "stream")),
        ),
        check_vma=False,
    )
```

```python
import functools

import jax
import jax.numpy as jnp
from jax import lax
from jax.experimental import pallas as pl
from jax.experimental.pallas import tpu as pltpu
from jax.sharding import PartitionSpec as P

HD = 128
HIST = 9
ROT = 32

EPSILON = 1e-05
HIGHEST = lax.Precision.HIGHEST
MASKED = -1e30
F32 = jnp.float32
BF16 = jnp.bfloat16
VMEM_LIMIT = 60 * 1024 * 1024

SWAP_X = [(0, 1), (1, 0)]
SWAP_Y = [(0, 2), (2, 0), (1, 3), (3, 1)]
SWAP_CORE = [(0, 1), (1, 0), (2, 3), (3, 2)]


def dot(a, b):
    return jnp.dot(a, b, preferred_element_type=F32)


def dot_nt(a, b):
    return lax.dot_general(a, b, (((1,), (1,)), ((), ())), preferred_element_type=F32)


def dot_tn(a, b):
    return lax.dot_general(a, b, (((0,), (0,)), ((), ())), preferred_element_type=F32)


def gelu_exact(values_in):
    return jax.nn.gelu(values_in, approximate=False)


def over_x(a):
    return lax.ppermute(a, "dp", SWAP_X)


def over_y(a):
    return lax.ppermute(a, "stream", SWAP_Y)


def over_core(a):
    return lax.ppermute(a, "stream", SWAP_CORE)


def paired():
    return lax.axis_size("dp") == 2 and lax.axis_size("stream") == 4


def gather_weight(shard, axis):
    return lax.all_gather(shard, ("dp", "stream"), axis=axis, tiled=True)


def lined():
    return paired() and lax.axis_size("head") == 4


def take(a, index, axis):
    return lax.dynamic_index_in_dim(a, index, axis, keepdims=False)


def add_bf(a, b):
    return (a.astype(F32) + b.astype(F32)).astype(BF16)


def chip_parts(partial):
    count, rows, columns = partial.shape
    core, x = lax.axis_index("stream") % 2, lax.axis_index("dp")
    split = partial.reshape(count, 4, 2, rows // 8, columns)
    chip = add_bf(take(split, core, 2), over_core(take(split, 1 - core, 2)))
    chip = chip.reshape(count, 2, 2, rows // 8, columns)
    return take(chip, x, 1), take(chip, 1 - x, 1)


def line_parts(stays, leaves):
    return add_bf(stays, over_x(leaves))


def last_parts(line):
    y = lax.axis_index("stream") // 2
    return take(line, y, 1), over_y(take(line, 1 - y, 1))


def plane_parts(stays, leaves):
    return last_parts(line_parts(stays, leaves))


def scatter_parts(partial):
    if not paired():
        whole = lax.psum_scatter(partial, ("dp", "stream"), scatter_dimension=1, tiled=True)
        return whole, jnp.zeros_like(whole)
    return plane_parts(*chip_parts(partial))


def add_kernel(turned, a_ref, b_ref, out_ref):
    total = a_ref[...].astype(F32) + b_ref[...].astype(F32)
    out_ref[...] = total.T if turned else total


def add_terms(a, b, turned):
    rows, columns = a.shape
    block = min(512, columns)
    return pl.pallas_call(
        functools.partial(add_kernel, turned),
        grid=(columns // block,),
        in_specs=[pl.BlockSpec((rows, block), lambda i: (0, i))] * 2,
        out_specs=pl.BlockSpec((block, rows), lambda i: (i, 0))
        if turned
        else pl.BlockSpec((rows, block), lambda i: (0, i)),
        out_shape=jax.ShapeDtypeStruct((columns, rows) if turned else (rows, columns), F32),
        cost_estimate=pl.CostEstimate(
            flops=rows * columns, bytes_accessed=8 * rows * columns, transcendentals=0
        ),
        name="add_terms",
    )(a, b)


def exchange_kernel(units, spread, axes, *refs):
    count, whole = len(axes), 2 if units else 0
    inputs, refs = refs[: units + count], refs[units + count :]
    partials, shard_refs = inputs[:units], inputs[units:]
    if units:
        done_in, near_in, beside_in = refs[:2], refs[2], refs[3]
        keep_ref, left_ref, right_ref = refs[4:7]
        lines_in, stays_in, leaves_in, streams_in = refs[7:9], refs[9], refs[10], refs[11:13]
        refs = refs[13:]
    outputs, refs = refs[: units + whole + count], refs[units + whole + count :]
    outs, wides, fulls = outputs[:units], outputs[units : units + whole], outputs[units + whole :]
    shares, refs = refs[:spread], refs[spread:]
    if units:
        grad_refs, refs = refs[:6], refs[6:]
    own_sem, near_send, near_recv = refs[:3]
    if units:
        held, got, load_sem, send_sem, recv_sem = refs[3:8]
        mine, theirs, below, pieces, piece_own, piece_send, piece_recv = refs[8:15]
        mine_sem, done_sem, core_send, core_recv, y_send, y_recv = refs[15:21]
        feed_own, feed_got, pair_own, pair_x, pair_y, wide_in, full_grad, from_core = refs[21:29]
        job_load, job_send, job_recv = refs[29:]
    x, stream, z = lax.axis_index("dp"), lax.axis_index("stream"), lax.axis_index("head")
    core = lax.rem(stream, 2)
    other_x, other_y, other_core = 1 - x, lax.rem(stream + 2, 4), stream + 1 - 2 * core
    line = ({"head": lax.rem(z + 1, 4)}, {"head": lax.rem(z + 3, 4)})
    to_x, to_y, to_core = {"dp": other_x}, {"stream": other_y}, {"stream": other_core}
    place = x * 4 + stream
    place_x, place_y = other_x * 4 + stream, x * 4 + other_y
    place_far = other_x * 4 + other_y
    beside = lambda at: at + 1 - 2 * core

    barrier = pltpu.get_barrier_semaphore()
    peers = (line if units or spread else ()) + ((to_x, to_y, to_core) if count else ())
    peers = peers + (({"head": lax.rem(z + 2, 4)},) if spread else ())
    for peer in peers:
        pl.semaphore_signal(barrier, inc=1, device_id=peer, device_id_type=pl.DeviceIdType.MESH)
    pl.semaphore_wait(barrier, len(peers))

    def region(w, at, part=None):
        full, width = fulls[w], shard_refs[w].shape[min(axes[w], 1)]
        rows, columns = shard_refs[w].shape
        start, size = (0, rows) if part is None else (part * (rows // 2), rows // 2)
        if axes[w] == 0:
            return full.at[pl.ds(pl.multiple_of(at * width + start, size), size)]
        column = at * width
        if axes[w] == 2:
            start = lax.rem(at, 2) * rows + start
            start, column = pl.multiple_of(start, size), lax.div(at, 2) * width
        return full.at[pl.ds(start, size), pl.ds(pl.multiple_of(column, width), width)]

    def near(w, index, source, target, peer):
        return pltpu.make_async_remote_copy(
            src_ref=source,
            dst_ref=target,
            send_sem=near_send.at[w, index],
            recv_sem=near_recv.at[w, index],
            device_id=peer,
            device_id_type=pl.DeviceIdType.MESH,
        )

    def pass_on(w, index, at, peer, part=None):
        return near(w, index, region(w, at, part), region(w, at, part), peer)

    def first(w):
        target = region(w, place)
        pltpu.make_async_copy(shard_refs[w], target, own_sem.at[w]).start()
        for index, peer in enumerate((to_x, to_y, to_core)):
            near(w, index, shard_refs[w], target, peer).start()

    def second(w):
        pass_on(w, 0, place_x, to_x).wait_recv()
        pass_on(w, 4, place_x, to_y, 0).start()
        pass_on(w, 3, place_x, to_core).start()
        pass_on(w, 1, place_y, to_y).wait_recv()
        pass_on(w, 6, place_y, to_x, 1).start()
        pass_on(w, 5, place_y, to_core).start()

    def third(w):
        pass_on(w, 4, place_far, to_y, 0).wait_recv()
        pass_on(w, 7, place_far, to_core, 0).start()
        pass_on(w, 6, place_far, to_x, 1).wait_recv()
        pass_on(w, 8, place_far, to_core, 1).start()

    def last(w):
        for index, at, part in (
            (2, place, None),
            (3, place_x, None),
            (5, place_y, None),
            (7, place_far, 0),
            (8, place_far, 1),
        ):
            pass_on(w, index, beside(at), to_core, part).wait_recv()
        pltpu.make_async_copy(shard_refs[w], region(w, place), own_sem.at[w]).wait()
        for index in (0, 1, 2):
            near(w, index, shard_refs[w], region(w, place), to_core).wait_send()
        for index, at, part in (
            (3, place_x, None),
            (4, place_x, 0),
            (5, place_y, None),
            (6, place_y, 1),
            (7, place_far, 0),
            (8, place_far, 1),
        ):
            pass_on(w, index, at, to_core, part).wait_send()

    for w in range(count):
        first(w)
    if not units:
        moves = []
        for i in range(spread):
            second(i)
        for i in range(spread):
            third(i)
        for i in range(spread):
            last(i)
            spread_own, spread_send, spread_recv = refs[3:6]
            rows, columns = shares[i].shape[0], fulls[i].shape[1]
            target = shares[i].at[:, pl.ds(pl.multiple_of(z * columns, columns), columns)]

            def source(at):
                start = (at * 8 + place) * rows
                return fulls[i].at[pl.ds(pl.multiple_of(start, rows), rows)]

            moves.append(pltpu.make_async_copy(source(z), target, spread_own.at[i]))
            for k in range(1, 4):
                to = lax.rem(z + k, 4)
                moves.append(
                    pltpu.make_async_remote_copy(
                        src_ref=source(to),
                        dst_ref=target,
                        send_sem=spread_send.at[i, k - 1],
                        recv_sem=spread_recv.at[i, k - 1],
                        device_id={"head": to},
                        device_id_type=pl.DeviceIdType.MESH,
                    )
                )
        for move in moves:
            move.start()
        for w in range(spread, count):
            second(w)
        for w in range(spread, count):
            third(w)
        for w in range(spread, count):
            last(w)
        for move in moves:
            move.wait()
        return

    feats = held.shape[-1]
    chunk = send_sem.shape[-1]
    tokens = held.shape[2]
    step_rows = tokens // chunk
    y = lax.div(stream, 2)

    def load(u, b):
        return pltpu.make_async_copy(
            partials[u].at[:, b * feats : (b + 1) * feats], held.at[u, b], load_sem.at[u, b]
        )

    def to_beside(v):
        return pltpu.make_async_remote_copy(
            src_ref=beside_in.at[:, v],
            dst_ref=theirs.at[v],
            send_sem=core_send.at[v],
            recv_sem=core_recv.at[v],
            device_id=to_core,
            device_id_type=pl.DeviceIdType.MESH,
        )

    def load_done(v):
        return pltpu.make_async_copy(
            done_in[v], pieces.at[v, pl.ds(0, done_in[v].shape[0])], done_sem.at[v]
        )

    def load_mine(v):
        return pltpu.make_async_copy(near_in.at[:, v], mine.at[v], mine_sem.at[v])

    def to_below(v):
        return pltpu.make_async_remote_copy(
            src_ref=mine.at[v, 1],
            dst_ref=below.at[v],
            send_sem=y_send.at[v],
            recv_sem=y_recv.at[v],
            device_id=to_y,
            device_id_type=pl.DeviceIdType.MESH,
        )

    for v in range(2):
        to_beside(v).start()
        load_mine(v).start()
        load_done(v).start()
    for u in range(units):
        for b in range(4):
            load(u, b).start()
    for u in range(units):
        for b in range(4):
            load(u, b).wait()

    def columns(block):
        return pl.ds(pl.multiple_of(block * feats, feats), feats)

    def part(c):
        return pl.ds(pl.multiple_of(c * step_rows, step_rows), step_rows)

    def hop(way, u, step, block, c):
        return pltpu.make_async_remote_copy(
            src_ref=held.at[u, block, part(c)],
            dst_ref=got.at[way, u, step, part(c)],
            send_sem=send_sem.at[way, u, step, c],
            recv_sem=recv_sem.at[way, u, step, c],
            device_id=line[way],
            device_id_type=pl.DeviceIdType.MESH,
        )

    ways = ((0, z), (1, 3 - z))

    def relay(way, v, step, block, c):
        target = wides[v].at[part(c), columns(block)]
        return pltpu.make_async_remote_copy(
            src_ref=pieces.at[v, part(c)] if step == 0 else target,
            dst_ref=target,
            send_sem=piece_send.at[way, v, step, c],
            recv_sem=piece_recv.at[way, v, step, c],
            device_id=line[way],
            device_id_type=pl.DeviceIdType.MESH,
        )

    def piece_at(way, step):
        return z - step if way == 0 else z + step

    def block_at(way, step):
        return 3 - step + z if way == 0 else step + z - 3

    def keep(v):
        return pltpu.make_async_copy(pieces.at[v], wides[v].at[:, columns(z)], piece_own.at[v])

    def over_parts(body, start=0, stop=None):
        def step(c, carry):
            body(c)
            return carry

        lax.fori_loop(start, chunk if stop is None else stop, step, 0)

    ready = done_in[0].shape[0] // step_rows
    early, late = (0, ready), (ready, chunk)

    def sum_step(step):
        def body(c):
            for way, rank in ways:

                @pl.when(rank <= step)
                def _():
                    block = block_at(way, step)
                    for u in range(units):
                        if step > 0:

                            @pl.when(rank > 0)
                            def _():
                                hop(way, u, step - 1, block, c).wait_recv()
                                total = held[u, block, part(c)].astype(F32) + got[
                                    way, u, step - 1, part(c)
                                ].astype(F32)
                                held[u, block, part(c)] = total.astype(BF16)

                        hop(way, u, step, block, c).start()

        over_parts(body)

    def gather_step(v, step, span):
        def body(c):
            for way, rank in ways:

                @pl.when((rank >= step) & (rank < 3))
                def _():
                    block = piece_at(way, step)
                    if step > 0:
                        relay(way, v, step - 1, block, c).wait_recv()
                    relay(way, v, step, block, c).start()

        over_parts(body, *span)

    def chip_sum(v):
        load_mine(v).wait()
        to_beside(v).wait()

        @pl.when(y == 1)
        def _():
            def body(c):
                total = mine[v, 1, part(c)].astype(F32) + theirs[v, 1, part(c)].astype(F32)
                mine[v, 1, part(c)] = total.astype(BF16)

            over_parts(body, 0, chunk - ready)
            to_below(v).start()

    def bring(v):
        def body(c, from_y):
            rows, out = part(c), part(c + ready)
            total = mine[v, 0, rows].astype(F32) + theirs[v, 0, rows].astype(F32)
            if from_y:
                total = total + below[v, rows].astype(F32)
            if v == 1:
                pieces[v, out] = total.astype(BF16)
            else:
                for head in range(feats // HD):
                    lanes = slice(head * HD, (head + 1) * HD)
                    pieces[v, out, lanes] = turn(
                        total[:, lanes], keep_ref[rows], -left_ref[rows], -right_ref[rows]
                    ).astype(BF16)

        @pl.when(y == 0)
        def _():
            to_below(v).wait_recv()
            over_parts(lambda c: body(c, True), 0, chunk - ready)

        @pl.when(y == 1)
        def _():
            over_parts(lambda c: body(c, False), 0, chunk - ready)

        keep(v).start()

    def job(index, source, target, peer):
        return pltpu.make_async_remote_copy(
            src_ref=source,
            dst_ref=target,
            send_sem=job_send.at[index],
            recv_sem=job_recv.at[index],
            device_id=peer,
            device_id_type=pl.DeviceIdType.MESH,
        )

    def job_in(index):
        source, target = (
            (lines_in[index].at[y], feed_own.at[index])
            if index < 2
            else (stays_in, pair_own.at[0])
            if index == 2
            else (streams_in[index - 3], wide_in.at[index - 3])
        )
        return pltpu.make_async_copy(source, target, job_load.at[index])

    def feed_job(f):
        return job(f, lines_in[f].at[1 - y], feed_got.at[f], to_y)

    def pair_x_job(i):
        source = full_grad.at[:, pl.ds(other_x * 2, 2), core] if i else leaves_in
        return job(2 + 4 * i, source, pair_x.at[i], to_x)

    def pair_y_job(i):
        return job(3 + 4 * i, pair_own.at[i, :, 1 - y], pair_y.at[i], to_y)

    def core_job(i):
        return job(4 + i, full_grad.at[i, :, 1 - core], from_core.at[i], to_core)

    def product(i):
        job_in(3 + i).wait()
        rows = full_grad.shape[3]
        for b in range(4):
            part_in = wide_in[i, :, b * 2 * rows : (b + 1) * 2 * rows]
            block = dot_tn(part_in, pieces[i]).astype(BF16)
            full_grad[i, b, 0] = block[:rows]
            full_grad[i, b, 1] = block[rows:]
        core_job(i).start()

    def both(a, b):
        return a.astype(F32) + b.astype(F32)

    def chip_grad():
        for i in range(2):
            core_job(i).wait()
            for b in range(4):
                full_grad[i, b, core] = both(full_grad[i, b, core], from_core[i, b]).astype(BF16)
        pair_x_job(1).start()

    def pair_line(i):
        pair_x_job(i).wait()
        for n in range(2):
            for k in range(2):
                stays = pair_own[i, n, k] if i == 0 else full_grad[n, x * 2 + k, core]
                pair_own[i, n, k] = both(stays, pair_x[i, n, k]).astype(BF16)
        pair_y_job(i).start()

    def pair_finish(i):
        pair_y_job(i).wait()
        total = [both(pair_own[i, n, y], pair_y[i, n]) for n in range(2)]
        grad_refs[2 + 2 * i][...] = total[0]
        grad_refs[3 + 2 * i][...] = total[1].T if i == 0 else total[1]

    def feed_finish():
        wide = min(512, feed_own.shape[2])
        for f in range(2):
            feed_job(f).wait()
            for c in range(0, feed_own.shape[2], wide):
                span = slice(c, c + wide)
                total = both(feed_own[f, :, span], feed_got[f, :, span])
                if f == 0:
                    grad_refs[0][:, span] = total
                else:
                    grad_refs[1][span] = total.T

    pair_x_job(0).start()
    for index in range(5):
        job_in(index).start()
    sum_step(0)
    for v in range(whole):
        load_done(v).wait()
        gather_step(v, 0, early)
    for v in range(whole):
        chip_sum(v)
    for w in range(count):
        second(w)
    for v in range(whole):
        bring(v)
        gather_step(v, 0, late)
    for f in range(2):
        feed_job(f).start()
    sum_step(1)
    for v in range(whole):
        gather_step(v, 1, early)
    for w in range(count):
        third(w)
    for i in range(2):
        product(i)
    for v in range(whole):
        gather_step(v, 1, late)
    job_in(2).wait()
    pair_line(0)
    sum_step(2)
    for v in range(whole):
        gather_step(v, 2, early)
    chip_grad()
    for f in range(2):
        job_in(f).wait()
    feed_finish()
    pair_finish(0)

    def finish(c):
        for u in range(units):
            outs[u][part(c)] = held[u, z, part(c)].astype(F32)
            for way, rank in ways:

                @pl.when(rank > 0)
                def _():
                    hop(way, u, 2, z, c).wait_recv()
                    outs[u][part(c)] += got[way, u, 2, part(c)].astype(F32)

    for v in range(whole):
        gather_step(v, 2, late)
    pair_line(1)
    over_parts(finish)
    for w in range(count):
        last(w)
    pair_finish(1)

    def drain(c):
        for way, rank in ways:

            @pl.when(rank == 3)
            def _():
                for v in range(whole):
                    for step in range(3):
                        relay(way, v, step, piece_at(way, step + 1), c).wait_recv()

        for step in range(3):
            for way, rank in ways:

                @pl.when(rank <= step)
                def _():
                    for u in range(units):
                        hop(way, u, step, block_at(way, step), c).wait_send()

                @pl.when((rank >= step) & (rank < 3))
                def _():
                    for v in range(whole):
                        relay(way, v, step, piece_at(way, step), c).wait_send()

    over_parts(drain)
    for v in range(whole):
        keep(v).wait()

        @pl.when(y == 1)
        def _():
            to_below(v).wait_send()


def exchange(partials, rows, shards_in, axes, collective_id, spread=0):
    units, count = len(partials), len(shards_in)
    grown = ((8, 1), (1, 8), (2, 4))
    shape = jax.ShapeDtypeStruct
    full = [
        shape(tuple(n * k for n, k in zip(w.shape, grown[axis])), BF16)
        for w, axis in zip(shards_in, axes)
    ]
    anywhere, local = pl.BlockSpec(memory_space=pl.ANY), pl.BlockSpec(memory_space=pltpu.VMEM)
    sems = pltpu.SemaphoreType.DMA
    out_specs, out_shape = [anywhere] * count, full
    in_specs = [anywhere] * (units + count)
    scratch = [sems((count,)), sems((count, 9)), sems((count, 9))]
    if units:
        tokens, feats = partials[0].shape[0], partials[0].shape[1] // 4
        chunk = 4
        in_specs = in_specs + [anywhere] * 4 + [local] * 3 + [anywhere] * 6
        last = rows[2].shape[2]
        line, stays = rows[7], rows[9]
        out_specs = [local] * units + [anywhere] * 2 + out_specs
        out_shape = (
            [shape((tokens, feats), F32)] * units + [shape((tokens, 4 * feats), BF16)] * 2 + out_shape
        )
        scratch = scratch + [
            pltpu.VMEM((units, 4, tokens, feats), BF16),
            pltpu.VMEM((2, units, 3, tokens, feats), BF16),
            sems((units, 4)),
            sems((2, units, 3, chunk)),
            sems((2, units, 3, chunk)),
            pltpu.VMEM((2, 2, last, feats), BF16),
            pltpu.VMEM((2, 2, last, feats), BF16),
            pltpu.VMEM((2, last, feats), BF16),
            pltpu.VMEM((2, tokens, feats), BF16),
            sems((2,)),
            sems((2, 2, 3, chunk)),
            sems((2, 2, 3, chunk)),
            sems((2,)),
            sems((2,)),
            sems((2,)),
            sems((2,)),
            sems((2,)),
            sems((2,)),
            pltpu.VMEM((2,) + line.shape[1:], BF16),
            pltpu.VMEM((2,) + line.shape[1:], BF16),
            pltpu.VMEM((2,) + stays.shape, BF16),
            pltpu.VMEM((2,) + stays.shape, BF16),
            pltpu.VMEM((2, 2) + stays.shape[2:], BF16),
            pltpu.VMEM((2,) + rows[11].shape, BF16),
            pltpu.VMEM((2, 4, 2) + stays.shape[2:], BF16),
            pltpu.VMEM((2, 4) + stays.shape[2:], BF16),
            sems((5,)),
            sems((8,)),
            sems((8,)),
        ]
        wide, narrow = line.shape[1:], stays.shape[2:]
        out_specs = out_specs + [local] * 6
        out_shape = out_shape + [
            shape(s, F32) for s in (wide, wide[::-1], narrow, narrow[::-1], narrow, narrow)
        ]
    if spread:
        out_specs = out_specs + [anywhere] * spread
        out_shape = out_shape + [
            shape((w.shape[0] // 4, w.shape[1] * 4), BF16) for w in shards_in[:spread]
        ]
        scratch = scratch + [sems((spread,))] + [sems((spread, 3))] * 2
    results = pl.pallas_call(
        functools.partial(exchange_kernel, units, spread, axes),
        in_specs=in_specs,
        out_specs=out_specs,
        out_shape=out_shape,
        scratch_shapes=scratch,
        compiler_params=pltpu.CompilerParams(
            collective_id=collective_id,
            has_side_effects=True,
            vmem_limit_bytes=VMEM_LIMIT,
        ),
        cost_estimate=pl.CostEstimate(
            flops=0, bytes_accessed=(600 if units else 240) * 1024 * 1024, transcendentals=0
        ),
        name="exchange",
    )(*partials, *shards_in, *rows)
    if not units:
        return results
    end = units + 2 + count
    return results[:units], results[units : units + 2], results[units + 2 : end], results[end:]


def head_sum_kernel(members, x_ref, out_ref, slots, send_sem, recv_sem):
    z = lax.axis_index("head")
    barrier = pltpu.get_barrier_semaphore()
    for k in range(1, members):
        pl.semaphore_signal(
            barrier,
            inc=1,
            device_id={"head": lax.rem(z + k, members)},
            device_id_type=pl.DeviceIdType.MESH,
        )
    pl.semaphore_wait(barrier, members - 1)
    copies = []
    for k in range(1, members):
        copy = pltpu.make_async_remote_copy(
            src_ref=x_ref,
            dst_ref=slots.at[z],
            send_sem=send_sem.at[k - 1],
            recv_sem=recv_sem.at[k - 1],
            device_id={"head": lax.rem(z + k, members)},
            device_id_type=pl.DeviceIdType.MESH,
        )
        copy.start()
        copies.append(copy)
    slots[z] = x_ref[...]
    for copy in copies:
        copy.wait()
    total = slots[0]
    for k in range(1, members):
        total = total + slots[k]
    out_ref[...] = total


def head_sum(x, collective_id):
    members = lax.axis_size("head")
    return pl.pallas_call(
        functools.partial(head_sum_kernel, members),
        out_shape=jax.ShapeDtypeStruct(x.shape, F32),
        in_specs=[pl.BlockSpec(memory_space=pltpu.VMEM)],
        out_specs=pl.BlockSpec(memory_space=pltpu.VMEM),
        scratch_shapes=[
            pltpu.VMEM((members,) + x.shape, F32),
            pltpu.SemaphoreType.DMA((members - 1,)),
            pltpu.SemaphoreType.DMA((members - 1,)),
        ],
        compiler_params=pltpu.CompilerParams(
            collective_id=collective_id, has_side_effects=True, vmem_limit_bytes=VMEM_LIMIT
        ),
        name="sum_over_head",
    )(x)


def turn(v, keep, left, right):
    h = ROT // 2
    return v * keep + pltpu.roll(v, HD - h, 1) * left + pltpu.roll(v, h, 1) * right


def rotate_kernel(sign, v_ref, keep_ref, left_ref, right_ref, out_ref):
    for head in range(v_ref.shape[1] // HD):
        part = pl.ds(head * HD, HD)
        out_ref[:, part] = turn(
            v_ref[:, part], keep_ref[...], sign * left_ref[...], sign * right_ref[...]
        ).astype(BF16)


def rotate(values_in, tables, sign):
    tokens, feats = values_in.shape
    block = min(tokens, 256)
    table = pl.BlockSpec((block, HD), lambda i: (i, 0))
    wide = pl.BlockSpec((block, feats), lambda i: (i, 0))
    return pl.pallas_call(
        functools.partial(rotate_kernel, sign),
        grid=(tokens // block,),
        in_specs=[wide, table, table, table],
        out_specs=wide,
        out_shape=jax.ShapeDtypeStruct((tokens, feats), BF16),
        cost_estimate=pl.CostEstimate(
            flops=5 * tokens * feats, bytes_accessed=8 * tokens * feats, transcendentals=0
        ),
        name="rotate_heads",
    )(values_in, *tables)


def feed_kernel(x_ref, d_ref, up_ref, down_ref, gated_ref, d_up_ref, grad_up_ref, grad_down_ref):
    tokens, model_width = x_ref.shape
    step = min(256, tokens)
    for r in range(0, tokens, step):
        rows = slice(r, r + step)
        up_pre = dot(x_ref[rows], up_ref[...])
        d_gated = dot_nt(d_ref[rows], down_ref[...])
        below = 0.5 * (1.0 + lax.erf(up_pre * 0.5**0.5))
        density = jnp.exp(-0.5 * up_pre * up_pre) * (2.0 * jnp.pi) ** -0.5
        gated_ref[rows] = (up_pre * below).astype(BF16)
        d_up_ref[rows] = (d_gated * (below + up_pre * density)).astype(BF16)
    wide = min(512, model_width)
    for c in range(0, model_width, wide):
        part = slice(c, c + wide)
        grad_up_ref[part] = dot_tn(x_ref[:, part], d_up_ref[...]).astype(BF16)
        grad_down_ref[part] = dot_tn(d_ref[:, part], gated_ref[...]).astype(BF16)


def feed_forward(x, d_out, up, down):
    tokens, model_width = x.shape
    hidden = up.shape[1]
    block = min(512, hidden)
    fixed = pl.BlockSpec((tokens, model_width), lambda i: (0, 0), pipeline_mode=pl.Buffered(1))
    narrow = pl.BlockSpec((tokens, block), lambda i: (0, i))
    column = pl.BlockSpec((model_width, block), lambda i: (0, i))
    shape = lambda rows: jax.ShapeDtypeStruct((rows, hidden), BF16)
    return pl.pallas_call(
        feed_kernel,
        grid=(hidden // block,),
        in_specs=[fixed, fixed, column, pl.BlockSpec((block, model_width), lambda i: (i, 0))],
        out_specs=[narrow, narrow, column, column],
        out_shape=[shape(tokens), shape(tokens), shape(model_width), shape(model_width)],
        compiler_params=pltpu.CompilerParams(vmem_limit_bytes=VMEM_LIMIT),
        cost_estimate=pl.CostEstimate(
            flops=8 * tokens * model_width * hidden,
            bytes_accessed=4 * model_width * (2 * hidden + tokens),
            transcendentals=0,
        ),
        name="feed_forward",
    )(x, d_out, up, down)


def attention_kernel(
    extra, place_ref, q_ref, do_ref, start_ref, valid_ref, keep_ref, left_ref, right_ref, *refs
):
    blocks = (len(refs) - 6 - extra) // 2
    k_refs, v_refs = refs[:blocks], refs[blocks : 2 * blocks]
    o_ref, dq_ref, near_ref, beside_ref, s_ref, dp_ref = refs[2 * blocks + extra :]
    grad_ref = lambda j: (beside_ref if j % 2 else near_ref).at[j // 2]
    rows = q_ref.shape[1]
    scale = HD ** (-0.5)
    member = place_ref[0]
    keep, left, right = keep_ref[0], left_ref[0], right_ref[0]
    q = turn(q_ref[0], keep, left, right).astype(BF16)
    d_out = do_ref[0]
    start = start_ref[0]
    top = jnp.full((rows, 1), MASKED, F32)
    t = member * rows + lax.broadcasted_iota(jnp.int32, (rows, rows), 0)
    for j in range(blocks):
        u = place_ref[j] * rows + lax.broadcasted_iota(jnp.int32, (rows, rows), 1)
        allowed = (u <= t) & (u >= start)
        s_ref[j] = jnp.where(allowed, dot_nt(q, k_refs[j][0]) * scale, MASKED)
        top = jnp.maximum(top, jnp.max(s_ref[j], axis=1, keepdims=True))
    total = jnp.zeros((rows, 1), F32)
    for j in range(blocks):
        e = jnp.exp(s_ref[j] - top)
        s_ref[j] = e
        total = total + jnp.sum(e, axis=1, keepdims=True)
    inverse = 1.0 / total
    out = jnp.zeros((rows, HD), F32)
    delta = jnp.zeros((rows, 1), F32)
    for j in range(blocks):
        p = s_ref[j] * inverse
        s_ref[j] = p
        p_bf = p.astype(BF16)
        out = out + dot(p_bf, v_refs[j][0])
        grad_ref(j)[1] = dot_tn(p_bf, d_out).astype(BF16)
        d_p = dot_nt(d_out, v_refs[j][0])
        dp_ref[j] = d_p
        delta = delta + jnp.sum(p * d_p, axis=1, keepdims=True)
    o_ref[0] = (out * valid_ref[0]).astype(BF16)
    d_q = jnp.zeros((rows, HD), F32)
    for j in range(blocks):
        d_s = (s_ref[j] * (dp_ref[j] - delta)).astype(BF16)
        d_q = d_q + dot(d_s, k_refs[j][0])
        grad_ref(j)[0] = (dot_tn(d_s, q) * scale).astype(BF16)
    dq_ref[0] = turn(d_q * scale, keep, -left, -right).astype(BF16)


def attention(index, places, queries, d_attended, starts, valid, tables, keys, values, earlier):
    micro, rows, feats = queries.shape
    blocks = len(keys)
    tile = pl.BlockSpec((1, rows, HD), lambda h: (index, 0, h))
    fixed = lambda width: pl.BlockSpec((1, rows, width), lambda h: (index, 0, 0))
    grad_tile = pl.BlockSpec((blocks // 2, 2, rows, HD), lambda h: (0, 0, 0, h))
    shape = lambda *lead: jax.ShapeDtypeStruct(lead + (rows, feats), BF16)
    return pl.pallas_call(
        functools.partial(attention_kernel, len(earlier)),
        grid=(feats // HD,),
        in_specs=[pl.BlockSpec(memory_space=pltpu.SMEM), tile, tile]
        + [fixed(1)] * 2
        + [fixed(HD)] * 3
        + [tile] * (2 * blocks)
        + [pl.BlockSpec(memory_space=pl.ANY)] * len(earlier),
        out_specs=[tile] * 2 + [grad_tile] * 2,
        out_shape=[shape(micro)] * 2 + [shape(blocks // 2, 2)] * 2,
        input_output_aliases={8 + 2 * blocks + i: i for i in range(len(earlier))},
        scratch_shapes=[
            pltpu.VMEM((blocks, rows, rows), F32),
            pltpu.VMEM((blocks, rows, rows), F32),
        ],
        compiler_params=pltpu.CompilerParams(vmem_limit_bytes=VMEM_LIMIT),
        cost_estimate=pl.CostEstimate(
            flops=0,
            bytes_accessed=1024,
            transcendentals=0,
        ),
        name="attention_both_ways",
    )(places, queries, d_attended, starts, valid, *tables, *keys, *values, *earlier)


def exchange_rows(local):
    if lax.axis_size("stream") != 4:
        raise ValueError("stream")
    across = lax.ppermute(local, "stream", [(0, 2), (1, 3)])
    beside = over_core(local)
    return (local, beside, across, over_core(across))


def add_f32(a, b):
    return a.astype(F32) + b.astype(F32)


def over_line(a):
    return lax.ppermute(a, "stream", [(2, 0), (3, 1)])


def columns_of(pieces, rows):
    lane = lax.broadcasted_iota(jnp.int32, (rows, 128), 1)
    out = jnp.zeros((rows, 128), F32)
    for index, piece in enumerate(pieces):
        out = jnp.where(lane == index, piece, out)
    return out


def row_sum(a):
    return jnp.sum(a, axis=1, keepdims=True)


def streams_kernel(weights_ref, history_ref, streams_ref, stats_ref):
    weights = weights_ref[...]
    layers = [history_ref[j].astype(F32) for j in range(HIST)]
    sums, squares = [], []
    for s in range(4):
        total = weights[:, s * HIST : s * HIST + 1] * layers[0]
        for j in range(1, HIST):
            total = total + weights[:, s * HIST + j : s * HIST + j + 1] * layers[j]
        streams_ref[s] = total
        sums.append(row_sum(total))
        squares.append(row_sum(total * total))
    stats_ref[...] = columns_of(sums + squares, weights.shape[0]).T[:8]


def mix_streams(weights, history):
    _, tokens, feats = history.shape
    block = min(256, tokens)
    return pl.pallas_call(
        streams_kernel,
        grid=(tokens // block,),
        in_specs=[
            pl.BlockSpec((block, weights.shape[1]), lambda i: (i, 0)),
            pl.BlockSpec((HIST, block, feats), lambda i: (0, i, 0)),
        ],
        out_specs=[
            pl.BlockSpec((4, block, feats), lambda i: (0, i, 0)),
            pl.BlockSpec((8, block), lambda i: (0, i)),
        ],
        out_shape=[
            jax.ShapeDtypeStruct((4, tokens, feats), F32),
            jax.ShapeDtypeStruct((8, tokens), F32),
        ],
        compiler_params=pltpu.CompilerParams(vmem_limit_bytes=VMEM_LIMIT),
        cost_estimate=pl.CostEstimate(
            flops=80 * tokens * feats, bytes_accessed=34 * tokens * feats, transcendentals=0
        ),
        name="mix_streams",
    )(weights, history)


def early_kernel(streams_ref, cot_ref, history_ref, out_ref):
    cot = cot_ref[...].astype(F32)
    plain, crossed, direct = [], [], []
    layers = [history_ref[j].astype(F32) for j in range(HIST)]
    for layer in layers:
        plain.append(row_sum(layer))
        direct.append(row_sum(cot * layer))
    for s in range(4):
        for layer in layers:
            crossed.append(row_sum(streams_ref[s] * layer))
    out_ref[...] = columns_of(crossed + plain + direct, cot.shape[0]).T[:64].astype(BF16)


def early_sums(streams, cot, history):
    _, tokens, feats = streams.shape
    block = min(256, tokens)
    return pl.pallas_call(
        early_kernel,
        grid=(tokens // block,),
        in_specs=[
            pl.BlockSpec((4, block, feats), lambda i: (0, i, 0)),
            pl.BlockSpec((block, feats), lambda i: (i, 0)),
            pl.BlockSpec((HIST, block, feats), lambda i: (0, i, 0)),
        ],
        out_specs=pl.BlockSpec((64, block), lambda i: (0, i)),
        out_shape=jax.ShapeDtypeStruct((64, tokens), BF16),
        compiler_params=pltpu.CompilerParams(vmem_limit_bytes=VMEM_LIMIT),
        cost_estimate=pl.CostEstimate(
            flops=110 * tokens * feats, bytes_accessed=36 * tokens * feats, transcendentals=0
        ),
        name="early_sums",
    )(streams, cot, history)


def sums_kernel(
    g0, g1, g2, g3, streams_ref, stats_ref, gain_ref, history_ref, dots_ref, out_ref, edge_ref
):
    stats = stats_ref[...]
    rows = stats.shape[0]

    @pl.when(pl.program_id(0) == 0)
    def _():
        edge_ref[...] = jnp.zeros_like(edge_ref)

    firsts, seconds, dots = [], [], []
    for s, g_ref in enumerate((g0, g1, g2, g3)):
        g = g_ref[...].astype(F32)
        centered = (streams_ref[s] - stats[:, s : s + 1]) * stats[:, 4 + s : 5 + s]
        edge_ref[s : s + 1] += jnp.sum(g * centered, axis=0, keepdims=True)
        edge_ref[4 + s : 5 + s] += jnp.sum(g, axis=0, keepdims=True)
        scaled = g * gain_ref[s : s + 1]
        firsts.append(row_sum(scaled))
        seconds.append(row_sum(scaled * centered))
        for j in range(HIST):
            dots.append(row_sum(scaled * history_ref[j].astype(F32)))
    dots_ref[...] = columns_of(dots, rows).T[:48].astype(BF16)
    out_ref[...] = columns_of(firsts + seconds, rows).T[:8]


def gradient_sums(grads, streams, stats, gain, history):
    _, tokens, feats = streams.shape
    block = min(256, tokens)
    wide = pl.BlockSpec((block, feats), lambda i: (i, 0))
    return pl.pallas_call(
        sums_kernel,
        grid=(tokens // block,),
        in_specs=[wide] * 4
        + [
            pl.BlockSpec((4, block, feats), lambda i: (0, i, 0)),
            pl.BlockSpec((block, 8), lambda i: (i, 0)),
            pl.BlockSpec((4, feats), lambda i: (0, 0)),
            pl.BlockSpec((HIST, block, feats), lambda i: (0, i, 0)),
        ],
        out_specs=[
            pl.BlockSpec((48, block), lambda i: (0, i)),
            pl.BlockSpec((8, block), lambda i: (0, i)),
            pl.BlockSpec((8, feats), lambda i: (0, 0)),
        ],
        out_shape=[
            jax.ShapeDtypeStruct((48, tokens), BF16),
            jax.ShapeDtypeStruct((8, tokens), F32),
            jax.ShapeDtypeStruct((8, feats), F32),
        ],
        compiler_params=pltpu.CompilerParams(vmem_limit_bytes=VMEM_LIMIT),
        cost_estimate=pl.CostEstimate(
            flops=110 * tokens * feats, bytes_accessed=42 * tokens * feats, transcendentals=0
        ),
        name="gradient_sums",
    )(*grads, streams, stats, gain, history)


def totals_kernel(members, *refs):
    ins, outs, slots, sems = refs[:3], refs[3:6], refs[6:9], refs[9:]
    z = lax.axis_index("head")
    line = [{"head": lax.rem(z + k, members)} for k in range(1, members)]
    barrier = pltpu.get_barrier_semaphore()
    for peer in line:
        pl.semaphore_signal(barrier, inc=1, device_id=peer, device_id_type=pl.DeviceIdType.MESH)
    pl.semaphore_wait(barrier, len(line))
    copies = []
    for index in range(3):
        for k, peer in enumerate(line):
            copy = pltpu.make_async_remote_copy(
                src_ref=ins[index],
                dst_ref=slots[index].at[z],
                send_sem=sems[2 * index].at[k],
                recv_sem=sems[2 * index + 1].at[k],
                device_id=peer,
                device_id_type=pl.DeviceIdType.MESH,
            )
            copy.start()
            copies.append(copy)
        slots[index][z] = ins[index][...]
    for copy in copies:
        copy.wait()
    for index in range(3):
        total = slots[index][0].astype(F32)
        for k in range(1, members):
            total = total + slots[index][k].astype(F32)
        outs[index][...] = total


def head_totals(arrays, collective_id):
    members = lax.axis_size("head")
    local = pl.BlockSpec(memory_space=pltpu.VMEM)
    return pl.pallas_call(
        functools.partial(totals_kernel, members),
        in_specs=[local] * 3,
        out_specs=[local] * 3,
        out_shape=[jax.ShapeDtypeStruct(a.shape, F32) for a in arrays],
        scratch_shapes=[pltpu.VMEM((members,) + a.shape, a.dtype) for a in arrays]
        + [pltpu.SemaphoreType.DMA((members - 1,))] * 6,
        compiler_params=pltpu.CompilerParams(
            collective_id=collective_id, has_side_effects=True, vmem_limit_bytes=VMEM_LIMIT
        ),
        name="totals_over_head",
    )(*arrays)


def small_kernel(
    members,
    plane,
    dots_ref,
    early_ref,
    sums_ref,
    stats_ref,
    pre_ref,
    slope_ref,
    hidden_ref,
    rms_ref,
    w_ref,
    current_ref,
    edge_ref,
    small_ref,
    scaled_ref,
    coef_ref,
    got,
    d_mix_ref,
    rows_ref,
    plane_send,
    plane_recv,
):
    x, stream = lax.axis_index("dp"), lax.axis_index("stream")
    near = (
        {"stream": stream + 1 - 2 * lax.rem(stream, 2)},
        {"stream": lax.rem(stream + 2, 4)},
        {"dp": 1 - x},
    )
    near = near if plane else ()
    if plane:
        barrier = pltpu.get_barrier_semaphore()
        for peer in near:
            pl.semaphore_signal(
                barrier, inc=1, device_id=peer, device_id_type=pl.DeviceIdType.MESH
            )
        pl.semaphore_wait(barrier, len(near))
    n = 4 * HIST
    model_width = members * small_ref.shape[1]
    plain = early_ref[n : n + HIST]
    rows_ref[...] = jnp.zeros_like(rows_ref)
    rows_ref[0:8] = sums_ref[...] / model_width
    for s in range(4):
        part = slice(s * HIST, (s + 1) * HIST)
        mean, inverse = stats_ref[s : s + 1], stats_ref[4 + s : 5 + s]
        crossed = (early_ref[part] - mean * plain) * inverse
        d_part = inverse * (
            dots_ref[part] - rows_ref[s : s + 1] * plain - rows_ref[4 + s : 5 + s] * crossed
        )
        if s == 3:
            d_part = d_part + early_ref[n + HIST : n + 2 * HIST]
        d_mix_ref[part] = d_part
    d_mix = d_mix_ref[...]
    high = dict(precision=HIGHEST, preferred_element_type=F32)
    d_pre = jnp.dot(w_ref[...], d_mix, **high) * slope_ref[...]
    rms = rms_ref[...]
    cross = jnp.sum(d_pre * pre_ref[...], axis=0, keepdims=True)
    rows_ref[8:9] = rms * rms * cross / model_width
    coef_ref[...] = rows_ref[...].T
    scaled = d_pre * rms
    scaled_ref[...] = scaled
    small_ref[...] = jnp.zeros_like(small_ref)
    small_ref[0:n] = jnp.dot(scaled, current_ref[...].astype(F32), **high)
    small_ref[n : n + 8] = edge_ref[...]
    small_ref[n + 8 : 2 * n + 8, 0:n] = lax.dot_general(
        hidden_ref[...], d_mix, (((1,), (1,)), ((), ())), **high
    )
    small_ref[n + 8 : 2 * n + 8, n : n + 1] = jnp.sum(d_mix, axis=1, keepdims=True)
    for step, peer in enumerate(near):
        copy = pltpu.make_async_remote_copy(
            src_ref=small_ref,
            dst_ref=got.at[step],
            send_sem=plane_send.at[step],
            recv_sem=plane_recv.at[step],
            device_id=peer,
            device_id_type=pl.DeviceIdType.MESH,
        )
        copy.start()
        copy.wait()
        small_ref[...] += got[step]


def small_gradients(dots, early, sums, stats, pre, slope, hidden, rms, w_out, current, edges):
    members, plane = lax.axis_size("head"), paired()
    tokens, feats = current.shape
    n = 4 * HIST
    shape = jax.ShapeDtypeStruct
    sems = pltpu.SemaphoreType.DMA
    small, scaled, coefs = pl.pallas_call(
        functools.partial(small_kernel, members, plane),
        in_specs=[pl.BlockSpec(memory_space=pltpu.VMEM)] * 11,
        out_specs=[pl.BlockSpec(memory_space=pltpu.VMEM)] * 3,
        out_shape=[shape((80, feats), F32), shape((n, tokens), F32), shape((tokens, 128), F32)],
        scratch_shapes=[
            pltpu.VMEM((3, 80, feats), F32),
            pltpu.VMEM((n, tokens), F32),
            pltpu.VMEM((128, tokens), F32),
            sems((3,)),
            sems((3,)),
        ],
        compiler_params=pltpu.CompilerParams(
            collective_id=3 if plane else None,
            has_side_effects=plane,
            vmem_limit_bytes=VMEM_LIMIT,
        ),
        name="small_gradients",
    )(dots, early, sums, stats, pre, slope, hidden, rms, w_out, current, edges)
    if not plane:
        small = lax.psum(small.astype(BF16), ("dp", "stream")).astype(F32)
    return small, scaled, coefs


def history_kernel(
    g0, g1, g2, g3, streams_ref, stats_ref, gain_ref, cot_ref, current_ref, weights_ref, coef_ref, d_ref, w_ref, out_ref
):
    stats, weights, coefs = stats_ref[...], weights_ref[...], coef_ref[...]
    d_streams = []
    for s, g_ref in enumerate((g0, g1, g2, g3)):
        inverse = stats[:, 4 + s : 5 + s]
        centered = (streams_ref[s] - stats[:, s : s + 1]) * inverse
        scaled = g_ref[...].astype(F32) * gain_ref[s : s + 1]
        d_streams.append(
            inverse * (scaled - coefs[:, s : s + 1] - centered * coefs[:, 4 + s : 5 + s])
        )
    d_streams[3] = d_streams[3] + cot_ref[...].astype(F32)
    for j in range(HIST):
        total = weights[:, j : j + 1] * d_streams[0]
        for s in range(1, 4):
            total = total + weights[:, s * HIST + j : s * HIST + j + 1] * d_streams[s]
        if j == HIST - 1:
            total = total + lax.dot_general(
                d_ref[...],
                w_ref[...],
                (((0,), (0,)), ((), ())),
                precision=HIGHEST,
                preferred_element_type=F32,
            )
            total = total - current_ref[...].astype(F32) * coefs[:, 8:9]
        out_ref[j] = total


def history_gradient(grads, streams, stats, gain, cot, current, weights, coefs, d_scaled, w_rows):
    _, tokens, feats = streams.shape
    block = min(256, tokens)
    wide = pl.BlockSpec((block, feats), lambda i: (i, 0))
    narrow = lambda a: pl.BlockSpec((block, a.shape[1]), lambda i: (i, 0))
    fixed = lambda a: pl.BlockSpec(a.shape, lambda i: (0, 0))
    return pl.pallas_call(
        history_kernel,
        grid=(tokens // block,),
        in_specs=[wide] * 4
        + [
            pl.BlockSpec((4, block, feats), lambda i: (0, i, 0)),
            narrow(stats),
            fixed(gain),
            wide,
            wide,
            narrow(weights),
            narrow(coefs),
            pl.BlockSpec((d_scaled.shape[0], block), lambda i: (0, i)),
            fixed(w_rows),
        ],
        out_specs=pl.BlockSpec((HIST, block, feats), lambda i: (0, i, 0)),
        out_shape=jax.ShapeDtypeStruct((HIST, tokens, feats), F32),
        compiler_params=pltpu.CompilerParams(vmem_limit_bytes=VMEM_LIMIT),
        cost_estimate=pl.CostEstimate(
            flops=110 * tokens * feats, bytes_accessed=64 * tokens * feats, transcendentals=0
        ),
        name="history_gradient",
    )(*grads, streams, stats, gain, cot, current, weights, coefs, d_scaled, w_rows)


def shards(
    history,
    seq_lens,
    bucket_slot,
    w_mix_in,
    w_mix_out,
    mix_bias,
    ln_gain,
    ln_bias,
    w_qkv,
    w_attn_out,
    w_up,
    w_down,
    cotangent,
):
    member = lax.axis_index("stream")
    micro, quarter, feats = history.shape[1:]
    tokens = micro * quarter
    model_width = feats * lax.axis_size("head")
    slot_base = lax.axis_index("dp") * micro
    slot_ids = jnp.arange(bucket_slot.shape[0], dtype=jnp.int32)
    query_places = member * quarter + jnp.arange(quarter, dtype=jnp.int32)
    w_mix_in_f = w_mix_in.astype(F32)
    w_mix_out_f = w_mix_out.astype(F32)

    segments, starts = [], []
    for index in range(micro):
        bucket = jnp.sum(jnp.where(slot_ids == slot_base + index, bucket_slot, 0))
        lengths = jnp.sum(jnp.where(slot_ids[:, None] == bucket, seq_lens, 0), axis=0)
        bounds = jnp.cumsum(lengths)
        passed = (query_places[:, None] >= bounds[None, :]).astype(jnp.int32)
        segments.append(jnp.sum(passed, axis=1))
        starts.append(jnp.sum(passed * lengths[None, :], axis=1))
    valid = (jnp.concatenate(segments) < 3).astype(F32)[:, None]
    starts = jnp.concatenate(starts)
    position = jnp.tile(query_places, micro) - starts
    frequency = jnp.arange(ROT // 2, dtype=F32)
    phases = position.astype(F32)[:, None] * (10000.0 ** (-2.0 * frequency / ROT))
    cosine, sine = jnp.cos(phases), jnp.sin(phases)
    plain = jnp.zeros((tokens, HD - ROT), F32)
    none = jnp.zeros_like(sine)
    tables = (
        jnp.concatenate([cosine, cosine, plain + 1.0], axis=1),
        jnp.concatenate([-sine, none, plain], axis=1),
        jnp.concatenate([none, sine, plain], axis=1),
    )

    cot_rows = cotangent.reshape(tokens, feats).astype(F32) * valid
    cot_bf = cot_rows.astype(BF16)
    duplex = lined()

    history = history.reshape(HIST, tokens, feats)
    current = history[HIST - 1]
    current_f = current.astype(F32)
    mixed = lax.dot_general(w_mix_in, current, (((0,), (1,)), ((), ())), preferred_element_type=F32)
    square = jnp.sum(current_f * current_f, axis=1)[None]
    mixed = head_sum(jnp.concatenate([mixed, square]), 0).T
    mixed, cot_bf, w_up = lax.optimization_barrier((mixed, cot_bf, w_up))
    out_full = lax.all_gather(cot_bf, "head", axis=1, tiled=True)
    if duplex:
        (up_full,) = exchange([], (), [w_up], (0,), 4)
        mixed, up_full = lax.optimization_barrier((mixed, up_full))
    rms_scale = lax.rsqrt(mixed[:, 4 * HIST :] / model_width + EPSILON)
    mix_pre = mixed[:, : 4 * HIST] * rms_scale
    below_mix = 0.5 * (1.0 + lax.erf(mix_pre * 0.5**0.5))
    mix_hidden = gelu_exact(mix_pre)
    slope_mix = below_mix + mix_pre * jnp.exp(-0.5 * mix_pre * mix_pre) * (2.0 * jnp.pi) ** -0.5
    mix_weights = jnp.dot(mix_hidden, w_mix_out_f, precision=HIGHEST) + mix_bias.reshape(-1)
    streams, stats = mix_streams(mix_weights, history)
    stats = head_sum(stats, 1)
    stat_sum, stat_square = stats[:4], stats[4:]
    row_means = (stat_sum / model_width)[:, :, None]
    inv_std = lax.rsqrt(stat_square[:, :, None] / model_width - row_means * row_means + EPSILON)
    centered = (streams - row_means) * inv_std
    row_stats = jnp.concatenate([row_means[..., 0], inv_std[..., 0]]).T
    normed = (centered * ln_gain[:, None, :] + ln_bias[:, None, :]).astype(BF16)

    def all_features(a):
        return lax.all_gather(a, "head", axis=1, tiled=True)

    if duplex:
        w_down, normed = lax.optimization_barrier((w_down, normed))
        wk, wv, down_full, w_out_full, wq, *shares = exchange(
            [], (), [w_qkv[1], w_qkv[2], w_down, w_attn_out, w_qkv[0]], (0, 0, 1, 1, 0), 6, 2
        )
    else:
        wq, wk, wv = gather_weight(w_qkv, 1)
        w_out_full, down_full = gather_weight(w_attn_out, 1), gather_weight(w_down, 1)
        up_full = gather_weight(w_up, 0)

    def to_owner(partial):
        return lax.psum_scatter(
            partial.astype(BF16), "head", scatter_dimension=1, tiled=True
        ).astype(F32)

    up_out, out_full = lax.optimization_barrier((normed[3], out_full))
    up_in, k_out, down_full = lax.optimization_barrier(
        (all_features(up_out), normed[1], down_full)
    )
    k_in, v_out = lax.optimization_barrier((all_features(k_out), normed[2]))
    gated_up, d_up, product_up, product_down = feed_forward(up_in, out_full, up_full, down_full)
    feed_products = [product_up[None], product_down[None]]
    feed_parts = [chip_parts(a) if paired() else a for a in feed_products]
    v_out, d_up, feed_parts = lax.optimization_barrier((v_out, d_up, feed_parts))
    feed_lines = [line_parts(*a) for a in feed_parts] if paired() else feed_parts
    streams_late, feed_lines[0] = lax.optimization_barrier((streams, feed_lines[0]))
    early = early_sums(streams_late, cot_bf, history)
    feed = dot(gated_up, down_full).astype(BF16)
    d_attended = dot_nt(out_full, w_out_full).astype(BF16) * valid.astype(BF16)
    d_up_in = dot_nt(d_up, up_full).astype(BF16)
    keys = rotate(dot(k_in, wk), tables, 1.0)
    v_in, q_out, early, feed, d_attended, d_up_in, keys, wk, wv = lax.optimization_barrier(
        (all_features(v_out), normed[0], early, feed, d_attended, d_up_in, keys, wk, wv)
    )
    values = dot(v_in, wv).astype(BF16)
    by_micro = lambda a: a.reshape((micro, quarter) + a.shape[1:])
    key_blocks = exchange_rows(by_micro(keys))
    value_blocks = exchange_rows(by_micro(values))
    d_up_in, key_blocks, value_blocks = lax.optimization_barrier(
        (d_up_in, key_blocks, value_blocks)
    )
    q_in, key_blocks, value_blocks, feed_lines[1], early = lax.optimization_barrier(
        (all_features(q_out), key_blocks, value_blocks, feed_lines[1], early)
    )
    g_up = to_owner(d_up_in)
    product = lambda a, b: dot_tn(a, b).astype(BF16)

    queries = dot(q_in, wq)
    places = member ^ jnp.arange(4, dtype=jnp.int32)
    earlier, d_rows = (), []
    queries = by_micro(queries)
    for index in range(micro):
        results = attention(
            index,
            places,
            queries,
            by_micro(d_attended),
            by_micro(starts[:, None]),
            by_micro(valid),
            tuple(by_micro(a) for a in tables),
            key_blocks,
            value_blocks,
            earlier,
        )
        earlier = results[:2]
        if duplex and index == micro - 1:
            continue
        chip = add_f32(results[2], over_core(results[3]))
        across = chip[1].astype(BF16)
        queries, across = lax.optimization_barrier((queries, across))
        d_rows.append(add_f32(chip[0], over_line(across)))
    attended, d_query_pre = (a.reshape(tokens, feats) for a in earlier)
    d_key_rows = jnp.concatenate([a[0] for a in d_rows])
    done = d_key_rows.shape[0]
    d_key_rows = rotate(d_key_rows, tuple(a[:done] for a in tables), -1.0)
    d_value_rows = jnp.concatenate([a[1] for a in d_rows]).astype(BF16)
    attended, d_query_pre, d_key_rows, d_value_rows = lax.optimization_barrier(
        (attended, d_query_pre, d_key_rows, d_value_rows)
    )

    products = jnp.stack([product(q_in, d_query_pre), product(out_full, attended)])
    if duplex:
        partials = [dot_nt(d_query_pre, wq).astype(BF16)]
        parts = chip_parts(products)
        partials, parts, g_up, feed_lines = lax.optimization_barrier(
            (partials, parts, g_up, feed_lines)
        )
        (g_query,), (d_key_full, d_value_full), (wk_rows, wv_rows), plane_grads = exchange(
            partials,
            [d_key_rows, d_value_rows, results[2], results[3], *(a[done:] for a in tables)]
            + [a[0] for a in feed_lines]
            + [*parts, k_in, v_in],
            shares,
            (0, 0),
            5,
        )
        attended_late, g_query = lax.optimization_barrier((attended, g_query))
        cut = 3 * tokens // 8
        pair = lambda a: (a[:cut], a[cut:])
        halves = [
            (dot(a, w_out_full) + b).astype(BF16) for a, b in zip(pair(attended_late), pair(feed))
        ]
        branch = to_owner(halves[0])
        g_key, g_value = dot_nt(d_key_full, wk_rows), dot_nt(d_value_full, wv_rows)
    else:
        g_query = to_owner(dot_nt(d_query_pre, wq))
        branch = to_owner(dot(attended, w_out_full) + feed)
        terms = scatter_parts(products)
        feed_terms = [scatter_parts(a) for a in feed_products]
        g_key = to_owner(dot_nt(d_key_rows, wk))
        g_value = to_owner(dot_nt(d_value_rows, wv))
        kv_terms = scatter_parts(
            jnp.stack([product(k_in, d_key_rows), product(v_in, d_value_rows)])
        )
    grads = (g_query, g_key, g_value, g_up)
    dots, sums, edges = gradient_sums(grads, streams, row_stats, ln_gain, history)
    dots, early, sums = head_totals((dots, early, sums), 7)
    if duplex:
        sums, second_half = lax.optimization_barrier((sums, halves[1]))
        branch = jnp.concatenate([branch, to_owner(second_half)])
        grad_up, grad_down, grad_query, grad_attn_out, grad_key, grad_value = plane_grads
        grad_qkv = jnp.stack([grad_query, grad_key, grad_value])
    else:
        grad_up = add_terms(feed_terms[0][0][0], feed_terms[0][1][0], False)
        grad_down = add_terms(feed_terms[1][0][0], feed_terms[1][1][0], True)
        grad_attn_out = add_terms(terms[0][1], terms[1][1], True)
        grad_qkv = jnp.concatenate([add_f32(terms[0][:1], terms[1][:1]), add_f32(*kv_terms)])
    small, d_scaled, coefs = small_gradients(
        dots, early, sums, row_stats.T, mix_pre.T, slope_mix.T, mix_hidden.T, rms_scale.T, w_mix_out_f, current, edges
    )
    block_out = (valid * (streams[3] + branch)).astype(BF16)
    history_grad = history_gradient(
        grads, streams, row_stats, ln_gain, cot_bf, current, mix_weights, coefs, d_scaled, w_mix_in_f.T
    ).reshape(HIST, micro, quarter, feats)
    n = 4 * HIST
    return (
        block_out.reshape(micro, quarter, feats),
        mix_weights.reshape(micro, quarter, 4 * HIST),
        history_grad,
        small[:n].T,
        small[n + 8 : 2 * n + 8, :n],
        small[n + 8 : 2 * n + 8, n].reshape(mix_bias.shape),
        small[n : n + 4],
        small[n + 4 : n + 8],
        grad_qkv,
        grad_attn_out,
        grad_up,
        grad_down,
    )


def solution(mesh):
    return jax.shard_map(
        shards,
        mesh=mesh,
        in_specs=(
            P(None, "dp", "stream", "head"),
            P(),
            P(),
            P("head", None),
            P(),
            P(),
            P(None, "head"),
            P(None, "head"),
            P(None, ("dp", "stream"), "head"),
            P("head", ("dp", "stream")),
            P(("dp", "stream"), "head"),
            P("head", ("dp", "stream")),
            P("dp", "stream", "head"),
        ),
        out_specs=(
            P("dp", "stream", "head"),
            P("dp", "stream", None),
            P(None, "dp", "stream", "head"),
            P("head", None),
            P(),
            P(),
            P(None, "head"),
            P(None, "head"),
            P(None, ("dp", "stream"), "head"),
            P("head", ("dp", "stream")),
            P(("dp", "stream"), "head"),
            P("head", ("dp", "stream")),
        ),
        check_vma=False,
    )
```

```python
import functools

import jax
import jax.numpy as jnp
from jax import lax
from jax.experimental import pallas as pl
from jax.experimental.pallas import tpu as pltpu
from jax.sharding import PartitionSpec as P

HD = 128
HIST = 9
ROT = 32

EPSILON = 1e-05
HIGHEST = lax.Precision.HIGHEST
MASKED = -1e30
F32 = jnp.float32
BF16 = jnp.bfloat16
VMEM_LIMIT = 60 * 1024 * 1024

SWAP_X = [(0, 1), (1, 0)]
SWAP_Y = [(0, 2), (2, 0), (1, 3), (3, 1)]
SWAP_CORE = [(0, 1), (1, 0), (2, 3), (3, 2)]


def dot(a, b):
    return jnp.dot(a, b, preferred_element_type=F32)


def dot_nt(a, b):
    return lax.dot_general(a, b, (((1,), (1,)), ((), ())), preferred_element_type=F32)


def dot_tn(a, b):
    return lax.dot_general(a, b, (((0,), (0,)), ((), ())), preferred_element_type=F32)


def gelu_exact(values_in):
    return jax.nn.gelu(values_in, approximate=False)


def over_x(a):
    return lax.ppermute(a, "dp", SWAP_X)


def over_y(a):
    return lax.ppermute(a, "stream", SWAP_Y)


def over_core(a):
    return lax.ppermute(a, "stream", SWAP_CORE)


def paired():
    return lax.axis_size("dp") == 2 and lax.axis_size("stream") == 4


def gather_weight(shard, axis):
    return lax.all_gather(shard, ("dp", "stream"), axis=axis, tiled=True)


def lined():
    return paired() and lax.axis_size("head") == 4


def take(a, index, axis):
    return lax.dynamic_index_in_dim(a, index, axis, keepdims=False)


def add_bf(a, b):
    return (a.astype(F32) + b.astype(F32)).astype(BF16)


def chip_parts(partial):
    count, rows, columns = partial.shape
    core, x = lax.axis_index("stream") % 2, lax.axis_index("dp")
    split = partial.reshape(count, 4, 2, rows // 8, columns)
    chip = add_bf(take(split, core, 2), over_core(take(split, 1 - core, 2)))
    chip = chip.reshape(count, 2, 2, rows // 8, columns)
    return take(chip, x, 1), take(chip, 1 - x, 1)


def line_parts(stays, leaves):
    return add_bf(stays, over_x(leaves))


def last_parts(line):
    y = lax.axis_index("stream") // 2
    return take(line, y, 1), over_y(take(line, 1 - y, 1))


def plane_parts(stays, leaves):
    return last_parts(line_parts(stays, leaves))


def scatter_parts(partial):
    if not paired():
        whole = lax.psum_scatter(partial, ("dp", "stream"), scatter_dimension=1, tiled=True)
        return whole, jnp.zeros_like(whole)
    return plane_parts(*chip_parts(partial))


def add_kernel(turned, a_ref, b_ref, out_ref):
    total = a_ref[...].astype(F32) + b_ref[...].astype(F32)
    out_ref[...] = total.T if turned else total


def add_terms(a, b, turned):
    rows, columns = a.shape
    block = min(512, columns)
    return pl.pallas_call(
        functools.partial(add_kernel, turned),
        grid=(columns // block,),
        in_specs=[pl.BlockSpec((rows, block), lambda i: (0, i))] * 2,
        out_specs=pl.BlockSpec((block, rows), lambda i: (i, 0))
        if turned
        else pl.BlockSpec((rows, block), lambda i: (0, i)),
        out_shape=jax.ShapeDtypeStruct((columns, rows) if turned else (rows, columns), F32),
        cost_estimate=pl.CostEstimate(
            flops=rows * columns, bytes_accessed=8 * rows * columns, transcendentals=0
        ),
        name="add_terms",
    )(a, b)


def exchange_kernel(units, spread, axes, *refs):
    count, whole = len(axes), 2 if units else 0
    inputs, refs = refs[: units + count], refs[units + count :]
    partials, shard_refs = inputs[:units], inputs[units:]
    if units:
        done_in, near_in, beside_in = refs[:2], refs[2], refs[3]
        keep_ref, left_ref, right_ref = refs[4:7]
        lines_in, stays_in, leaves_in, streams_in = refs[7:9], refs[9], refs[10], refs[11:13]
        refs = refs[13:]
    outputs, refs = refs[: units + whole + count], refs[units + whole + count :]
    outs, wides, fulls = outputs[:units], outputs[units : units + whole], outputs[units + whole :]
    shares, refs = refs[:spread], refs[spread:]
    if units:
        grad_refs, refs = refs[:6], refs[6:]
    own_sem, near_send, near_recv = refs[:3]
    if units:
        held, got, load_sem, send_sem, recv_sem = refs[3:8]
        mine, theirs, below, pieces, piece_own, piece_send, piece_recv = refs[8:15]
        mine_sem, done_sem, core_send, core_recv, y_send, y_recv = refs[15:21]
        feed_own, feed_got, pair_own, pair_x, pair_y, wide_in, full_grad, from_core = refs[21:29]
        job_load, job_send, job_recv = refs[29:]
    x, stream, z = lax.axis_index("dp"), lax.axis_index("stream"), lax.axis_index("head")
    core = lax.rem(stream, 2)
    other_x, other_y, other_core = 1 - x, lax.rem(stream + 2, 4), stream + 1 - 2 * core
    line = ({"head": lax.rem(z + 1, 4)}, {"head": lax.rem(z + 3, 4)})
    to_x, to_y, to_core = {"dp": other_x}, {"stream": other_y}, {"stream": other_core}
    place = x * 4 + stream
    place_x, place_y = other_x * 4 + stream, x * 4 + other_y
    place_far = other_x * 4 + other_y
    beside = lambda at: at + 1 - 2 * core

    barrier = pltpu.get_barrier_semaphore()
    peers = (line if units or spread else ()) + ((to_x, to_y, to_core) if count else ())
    peers = peers + (({"head": lax.rem(z + 2, 4)},) if spread else ())
    for peer in peers:
        pl.semaphore_signal(barrier, inc=1, device_id=peer, device_id_type=pl.DeviceIdType.MESH)
    pl.semaphore_wait(barrier, len(peers))

    def region(w, at, part=None):
        full, width = fulls[w], shard_refs[w].shape[min(axes[w], 1)]
        rows, columns = shard_refs[w].shape
        start, size = (0, rows) if part is None else (part * (rows // 2), rows // 2)
        if axes[w] == 0:
            return full.at[pl.ds(pl.multiple_of(at * width + start, size), size)]
        column = at * width
        if axes[w] == 2:
            start = lax.rem(at, 2) * rows + start
            start, column = pl.multiple_of(start, size), lax.div(at, 2) * width
        return full.at[pl.ds(start, size), pl.ds(pl.multiple_of(column, width), width)]

    def near(w, index, source, target, peer):
        return pltpu.make_async_remote_copy(
            src_ref=source,
            dst_ref=target,
            send_sem=near_send.at[w, index],
            recv_sem=near_recv.at[w, index],
            device_id=peer,
            device_id_type=pl.DeviceIdType.MESH,
        )

    def pass_on(w, index, at, peer, part=None):
        return near(w, index, region(w, at, part), region(w, at, part), peer)

    def first(w):
        target = region(w, place)
        pltpu.make_async_copy(shard_refs[w], target, own_sem.at[w]).start()
        for index, peer in enumerate((to_x, to_y, to_core)):
            near(w, index, shard_refs[w], target, peer).start()

    def second(w):
        pass_on(w, 0, place_x, to_x).wait_recv()
        pass_on(w, 4, place_x, to_y, 0).start()
        pass_on(w, 3, place_x, to_core).start()
        pass_on(w, 1, place_y, to_y).wait_recv()
        pass_on(w, 6, place_y, to_x, 1).start()
        pass_on(w, 5, place_y, to_core).start()

    def third(w):
        pass_on(w, 4, place_far, to_y, 0).wait_recv()
        pass_on(w, 7, place_far, to_core, 0).start()
        pass_on(w, 6, place_far, to_x, 1).wait_recv()
        pass_on(w, 8, place_far, to_core, 1).start()

    def last(w):
        for index, at, part in (
            (2, place, None),
            (3, place_x, None),
            (5, place_y, None),
            (7, place_far, 0),
            (8, place_far, 1),
        ):
            pass_on(w, index, beside(at), to_core, part).wait_recv()
        pltpu.make_async_copy(shard_refs[w], region(w, place), own_sem.at[w]).wait()
        for index in (0, 1, 2):
            near(w, index, shard_refs[w], region(w, place), to_core).wait_send()
        for index, at, part in (
            (3, place_x, None),
            (4, place_x, 0),
            (5, place_y, None),
            (6, place_y, 1),
            (7, place_far, 0),
            (8, place_far, 1),
        ):
            pass_on(w, index, at, to_core, part).wait_send()

    for w in range(count):
        first(w)
    if not units:
        moves = []
        for i in range(spread):
            second(i)
        for i in range(spread):
            third(i)
        for i in range(spread):
            last(i)
            spread_own, spread_send, spread_recv = refs[3:6]
            rows, columns = shares[i].shape[0], fulls[i].shape[1]
            target = shares[i].at[:, pl.ds(pl.multiple_of(z * columns, columns), columns)]

            def source(at):
                start = (at * 8 + place) * rows
                return fulls[i].at[pl.ds(pl.multiple_of(start, rows), rows)]

            moves.append(pltpu.make_async_copy(source(z), target, spread_own.at[i]))
            for k in range(1, 4):
                to = lax.rem(z + k, 4)
                moves.append(
                    pltpu.make_async_remote_copy(
                        src_ref=source(to),
                        dst_ref=target,
                        send_sem=spread_send.at[i, k - 1],
                        recv_sem=spread_recv.at[i, k - 1],
                        device_id={"head": to},
                        device_id_type=pl.DeviceIdType.MESH,
                    )
                )
        for move in moves:
            move.start()
        for w in range(spread, count):
            second(w)
        for w in range(spread, count):
            third(w)
        for w in range(spread, count):
            last(w)
        for move in moves:
            move.wait()
        return

    feats = held.shape[-1]
    chunk = send_sem.shape[-1]
    tokens = held.shape[2]
    step_rows = tokens // chunk
    y = lax.div(stream, 2)

    def load(u, b):
        return pltpu.make_async_copy(
            partials[u].at[:, b * feats : (b + 1) * feats], held.at[u, b], load_sem.at[u, b]
        )

    def to_beside(v):
        return pltpu.make_async_remote_copy(
            src_ref=beside_in.at[:, v],
            dst_ref=theirs.at[v],
            send_sem=core_send.at[v],
            recv_sem=core_recv.at[v],
            device_id=to_core,
            device_id_type=pl.DeviceIdType.MESH,
        )

    def load_done(v):
        return pltpu.make_async_copy(
            done_in[v], pieces.at[v, pl.ds(0, done_in[v].shape[0])], done_sem.at[v]
        )

    def load_mine(v):
        return pltpu.make_async_copy(near_in.at[:, v], mine.at[v], mine_sem.at[v])

    def to_below(v):
        return pltpu.make_async_remote_copy(
            src_ref=mine.at[v, 1],
            dst_ref=below.at[v],
            send_sem=y_send.at[v],
            recv_sem=y_recv.at[v],
            device_id=to_y,
            device_id_type=pl.DeviceIdType.MESH,
        )

    for v in range(2):
        to_beside(v).start()
        load_mine(v).start()
        load_done(v).start()
    for u in range(units):
        for b in range(4):
            load(u, b).start()
    for u in range(units):
        for b in range(4):
            load(u, b).wait()

    def columns(block):
        return pl.ds(pl.multiple_of(block * feats, feats), feats)

    def part(c):
        return pl.ds(pl.multiple_of(c * step_rows, step_rows), step_rows)

    def hop(way, u, step, block, c):
        return pltpu.make_async_remote_copy(
            src_ref=held.at[u, block, part(c)],
            dst_ref=got.at[way, u, step, part(c)],
            send_sem=send_sem.at[way, u, step, c],
            recv_sem=recv_sem.at[way, u, step, c],
            device_id=line[way],
            device_id_type=pl.DeviceIdType.MESH,
        )

    ways = ((0, z), (1, 3 - z))

    def relay(way, v, step, block, c):
        target = wides[v].at[part(c), columns(block)]
        return pltpu.make_async_remote_copy(
            src_ref=pieces.at[v, part(c)] if step == 0 else target,
            dst_ref=target,
            send_sem=piece_send.at[way, v, step, c],
            recv_sem=piece_recv.at[way, v, step, c],
            device_id=line[way],
            device_id_type=pl.DeviceIdType.MESH,
        )

    def piece_at(way, step):
        return z - step if way == 0 else z + step

    def block_at(way, step):
        return 3 - step + z if way == 0 else step + z - 3

    def keep(v):
        return pltpu.make_async_copy(pieces.at[v], wides[v].at[:, columns(z)], piece_own.at[v])

    def over_parts(body, start=0, stop=None):
        def step(c, carry):
            body(c)
            return carry

        lax.fori_loop(start, chunk if stop is None else stop, step, 0)

    ready = done_in[0].shape[0] // step_rows
    early, late = (0, ready), (ready, chunk)

    def sum_step(step):
        def body(c):
            for way, rank in ways:

                @pl.when(rank <= step)
                def _():
                    block = block_at(way, step)
                    for u in range(units):
                        if step > 0:

                            @pl.when(rank > 0)
                            def _():
                                hop(way, u, step - 1, block, c).wait_recv()
                                total = held[u, block, part(c)].astype(F32) + got[
                                    way, u, step - 1, part(c)
                                ].astype(F32)
                                held[u, block, part(c)] = total.astype(BF16)

                        hop(way, u, step, block, c).start()

        over_parts(body)

    def gather_step(v, step, span):
        def body(c):
            for way, rank in ways:

                @pl.when((rank >= step) & (rank < 3))
                def _():
                    block = piece_at(way, step)
                    if step > 0:
                        relay(way, v, step - 1, block, c).wait_recv()
                    relay(way, v, step, block, c).start()

        over_parts(body, *span)

    def chip_sum(v):
        load_mine(v).wait()
        to_beside(v).wait()

        @pl.when(y == 1)
        def _():
            def body(c):
                total = mine[v, 1, part(c)].astype(F32) + theirs[v, 1, part(c)].astype(F32)
                mine[v, 1, part(c)] = total.astype(BF16)

            over_parts(body, 0, chunk - ready)
            to_below(v).start()

    def bring(v):
        def body(c, from_y):
            rows, out = part(c), part(c + ready)
            total = mine[v, 0, rows].astype(F32) + theirs[v, 0, rows].astype(F32)
            if from_y:
                total = total + below[v, rows].astype(F32)
            if v == 1:
                pieces[v, out] = total.astype(BF16)
            else:
                for head in range(feats // HD):
                    lanes = slice(head * HD, (head + 1) * HD)
                    pieces[v, out, lanes] = turn(
                        total[:, lanes], keep_ref[rows], -left_ref[rows], -right_ref[rows]
                    ).astype(BF16)

        @pl.when(y == 0)
        def _():
            to_below(v).wait_recv()
            over_parts(lambda c: body(c, True), 0, chunk - ready)

        @pl.when(y == 1)
        def _():
            over_parts(lambda c: body(c, False), 0, chunk - ready)

        keep(v).start()

    def job(index, source, target, peer):
        return pltpu.make_async_remote_copy(
            src_ref=source,
            dst_ref=target,
            send_sem=job_send.at[index],
            recv_sem=job_recv.at[index],
            device_id=peer,
            device_id_type=pl.DeviceIdType.MESH,
        )

    def job_in(index):
        source, target = (
            (lines_in[index].at[y], feed_own.at[index])
            if index < 2
            else (stays_in, pair_own.at[0])
            if index == 2
            else (streams_in[index - 3], wide_in.at[index - 3])
        )
        return pltpu.make_async_copy(source, target, job_load.at[index])

    def feed_job(f):
        return job(f, lines_in[f].at[1 - y], feed_got.at[f], to_y)

    def pair_x_job(i):
        source = full_grad.at[:, pl.ds(other_x * 2, 2), core] if i else leaves_in
        return job(2 + 4 * i, source, pair_x.at[i], to_x)

    def pair_y_job(i):
        return job(3 + 4 * i, pair_own.at[i, :, 1 - y], pair_y.at[i], to_y)

    def core_job(i):
        return job(4 + i, full_grad.at[i, :, 1 - core], from_core.at[i], to_core)

    def product(i):
        job_in(3 + i).wait()
        rows = full_grad.shape[3]
        for b in range(4):
            part_in = wide_in[i, :, b * 2 * rows : (b + 1) * 2 * rows]
            block = dot_tn(part_in, pieces[i]).astype(BF16)
            full_grad[i, b, 0] = block[:rows]
            full_grad[i, b, 1] = block[rows:]
        core_job(i).start()

    def both(a, b):
        return a.astype(F32) + b.astype(F32)

    def chip_grad():
        for i in range(2):
            core_job(i).wait()
            for b in range(4):
                full_grad[i, b, core] = both(full_grad[i, b, core], from_core[i, b]).astype(BF16)
        pair_x_job(1).start()

    def pair_line(i):
        pair_x_job(i).wait()
        for n in range(2):
            for k in range(2):
                stays = pair_own[i, n, k] if i == 0 else full_grad[n, x * 2 + k, core]
                pair_own[i, n, k] = both(stays, pair_x[i, n, k]).astype(BF16)
        pair_y_job(i).start()

    def pair_finish(i):
        pair_y_job(i).wait()
        total = [both(pair_own[i, n, y], pair_y[i, n]) for n in range(2)]
        grad_refs[2 + 2 * i][...] = total[0]
        grad_refs[3 + 2 * i][...] = total[1].T if i == 0 else total[1]

    def feed_finish():
        wide = min(512, feed_own.shape[2])
        for f in range(2):
            feed_job(f).wait()
            for c in range(0, feed_own.shape[2], wide):
                span = slice(c, c + wide)
                total = both(feed_own[f, :, span], feed_got[f, :, span])
                if f == 0:
                    grad_refs[0][:, span] = total
                else:
                    grad_refs[1][span] = total.T

    pair_x_job(0).start()
    for index in range(5):
        job_in(index).start()
    sum_step(0)
    for v in range(whole):
        load_done(v).wait()
        gather_step(v, 0, early)
    for v in range(whole):
        chip_sum(v)
    for w in range(count):
        second(w)
    for v in range(whole):
        bring(v)
        gather_step(v, 0, late)
    for f in range(2):
        feed_job(f).start()
    sum_step(1)
    for v in range(whole):
        gather_step(v, 1, early)
    for w in range(count):
        third(w)
    for i in range(2):
        product(i)
    for v in range(whole):
        gather_step(v, 1, late)
    job_in(2).wait()
    pair_line(0)
    sum_step(2)
    for v in range(whole):
        gather_step(v, 2, early)
    chip_grad()
    for f in range(2):
        job_in(f).wait()
    feed_finish()
    pair_finish(0)

    def finish(c):
        for u in range(units):
            outs[u][part(c)] = held[u, z, part(c)].astype(F32)
            for way, rank in ways:

                @pl.when(rank > 0)
                def _():
                    hop(way, u, 2, z, c).wait_recv()
                    outs[u][part(c)] += got[way, u, 2, part(c)].astype(F32)

    for v in range(whole):
        gather_step(v, 2, late)
    pair_line(1)
    over_parts(finish)
    for w in range(count):
        last(w)
    pair_finish(1)

    def drain(c):
        for way, rank in ways:

            @pl.when(rank == 3)
            def _():
                for v in range(whole):
                    for step in range(3):
                        relay(way, v, step, piece_at(way, step + 1), c).wait_recv()

        for step in range(3):
            for way, rank in ways:

                @pl.when(rank <= step)
                def _():
                    for u in range(units):
                        hop(way, u, step, block_at(way, step), c).wait_send()

                @pl.when((rank >= step) & (rank < 3))
                def _():
                    for v in range(whole):
                        relay(way, v, step, piece_at(way, step), c).wait_send()

    over_parts(drain)
    for v in range(whole):
        keep(v).wait()

        @pl.when(y == 1)
        def _():
            to_below(v).wait_send()


def exchange(partials, rows, shards_in, axes, collective_id, spread=0):
    units, count = len(partials), len(shards_in)
    grown = ((8, 1), (1, 8), (2, 4))
    shape = jax.ShapeDtypeStruct
    full = [
        shape(tuple(n * k for n, k in zip(w.shape, grown[axis])), BF16)
        for w, axis in zip(shards_in, axes)
    ]
    anywhere, local = pl.BlockSpec(memory_space=pl.ANY), pl.BlockSpec(memory_space=pltpu.VMEM)
    sems = pltpu.SemaphoreType.DMA
    out_specs, out_shape = [anywhere] * count, full
    in_specs = [anywhere] * (units + count)
    scratch = [sems((count,)), sems((count, 9)), sems((count, 9))]
    if units:
        tokens, feats = partials[0].shape[0], partials[0].shape[1] // 4
        chunk = 4
        in_specs = in_specs + [anywhere] * 4 + [local] * 3 + [anywhere] * 6
        last = rows[2].shape[2]
        line, stays = rows[7], rows[9]
        out_specs = [local] * units + [anywhere] * 2 + out_specs
        out_shape = (
            [shape((tokens, feats), F32)] * units + [shape((tokens, 4 * feats), BF16)] * 2 + out_shape
        )
        scratch = scratch + [
            pltpu.VMEM((units, 4, tokens, feats), BF16),
            pltpu.VMEM((2, units, 3, tokens, feats), BF16),
            sems((units, 4)),
            sems((2, units, 3, chunk)),
            sems((2, units, 3, chunk)),
            pltpu.VMEM((2, 2, last, feats), BF16),
            pltpu.VMEM((2, 2, last, feats), BF16),
            pltpu.VMEM((2, last, feats), BF16),
            pltpu.VMEM((2, tokens, feats), BF16),
            sems((2,)),
            sems((2, 2, 3, chunk)),
            sems((2, 2, 3, chunk)),
            sems((2,)),
            sems((2,)),
            sems((2,)),
            sems((2,)),
            sems((2,)),
            sems((2,)),
            pltpu.VMEM((2,) + line.shape[1:], BF16),
            pltpu.VMEM((2,) + line.shape[1:], BF16),
            pltpu.VMEM((2,) + stays.shape, BF16),
            pltpu.VMEM((2,) + stays.shape, BF16),
            pltpu.VMEM((2, 2) + stays.shape[2:], BF16),
            pltpu.VMEM((2,) + rows[11].shape, BF16),
            pltpu.VMEM((2, 4, 2) + stays.shape[2:], BF16),
            pltpu.VMEM((2, 4) + stays.shape[2:], BF16),
            sems((5,)),
            sems((8,)),
            sems((8,)),
        ]
        wide, narrow = line.shape[1:], stays.shape[2:]
        out_specs = out_specs + [local] * 6
        out_shape = out_shape + [
            shape(s, F32) for s in (wide, wide[::-1], narrow, narrow[::-1], narrow, narrow)
        ]
    if spread:
        out_specs = out_specs + [anywhere] * spread
        out_shape = out_shape + [
            shape((w.shape[0] // 4, w.shape[1] * 4), BF16) for w in shards_in[:spread]
        ]
        scratch = scratch + [sems((spread,))] + [sems((spread, 3))] * 2
    results = pl.pallas_call(
        functools.partial(exchange_kernel, units, spread, axes),
        in_specs=in_specs,
        out_specs=out_specs,
        out_shape=out_shape,
        scratch_shapes=scratch,
        compiler_params=pltpu.CompilerParams(
            collective_id=collective_id,
            has_side_effects=True,
            vmem_limit_bytes=VMEM_LIMIT,
        ),
        cost_estimate=pl.CostEstimate(
            flops=0, bytes_accessed=(600 if units else 240) * 1024 * 1024, transcendentals=0
        ),
        name="exchange",
    )(*partials, *shards_in, *rows)
    if not units:
        return results
    end = units + 2 + count
    return results[:units], results[units : units + 2], results[units + 2 : end], results[end:]


def head_sum_kernel(members, x_ref, out_ref, slots, send_sem, recv_sem):
    z = lax.axis_index("head")
    barrier = pltpu.get_barrier_semaphore()
    for k in range(1, members):
        pl.semaphore_signal(
            barrier,
            inc=1,
            device_id={"head": lax.rem(z + k, members)},
            device_id_type=pl.DeviceIdType.MESH,
        )
    pl.semaphore_wait(barrier, members - 1)
    copies = []
    for k in range(1, members):
        copy = pltpu.make_async_remote_copy(
            src_ref=x_ref,
            dst_ref=slots.at[z],
            send_sem=send_sem.at[k - 1],
            recv_sem=recv_sem.at[k - 1],
            device_id={"head": lax.rem(z + k, members)},
            device_id_type=pl.DeviceIdType.MESH,
        )
        copy.start()
        copies.append(copy)
    slots[z] = x_ref[...]
    for copy in copies:
        copy.wait()
    total = slots[0]
    for k in range(1, members):
        total = total + slots[k]
    out_ref[...] = total


def head_sum(x, collective_id):
    members = lax.axis_size("head")
    return pl.pallas_call(
        functools.partial(head_sum_kernel, members),
        out_shape=jax.ShapeDtypeStruct(x.shape, F32),
        in_specs=[pl.BlockSpec(memory_space=pltpu.VMEM)],
        out_specs=pl.BlockSpec(memory_space=pltpu.VMEM),
        scratch_shapes=[
            pltpu.VMEM((members,) + x.shape, F32),
            pltpu.SemaphoreType.DMA((members - 1,)),
            pltpu.SemaphoreType.DMA((members - 1,)),
        ],
        compiler_params=pltpu.CompilerParams(
            collective_id=collective_id, has_side_effects=True, vmem_limit_bytes=VMEM_LIMIT
        ),
        name="sum_over_head",
    )(x)


def turn(v, keep, left, right):
    h = ROT // 2
    return v * keep + pltpu.roll(v, HD - h, 1) * left + pltpu.roll(v, h, 1) * right


def rotate_kernel(sign, v_ref, keep_ref, left_ref, right_ref, out_ref):
    for head in range(v_ref.shape[1] // HD):
        part = pl.ds(head * HD, HD)
        out_ref[:, part] = turn(
            v_ref[:, part], keep_ref[...], sign * left_ref[...], sign * right_ref[...]
        ).astype(BF16)


def rotate(values_in, tables, sign):
    tokens, feats = values_in.shape
    block = min(tokens, 256)
    table = pl.BlockSpec((block, HD), lambda i: (i, 0))
    wide = pl.BlockSpec((block, feats), lambda i: (i, 0))
    return pl.pallas_call(
        functools.partial(rotate_kernel, sign),
        grid=(tokens // block,),
        in_specs=[wide, table, table, table],
        out_specs=wide,
        out_shape=jax.ShapeDtypeStruct((tokens, feats), BF16),
        cost_estimate=pl.CostEstimate(
            flops=5 * tokens * feats, bytes_accessed=8 * tokens * feats, transcendentals=0
        ),
        name="rotate_heads",
    )(values_in, *tables)


def feed_kernel(x_ref, d_ref, up_ref, down_ref, gated_ref, d_up_ref, grad_up_ref, grad_down_ref):
    tokens, model_width = x_ref.shape
    step = min(256, tokens)
    for r in range(0, tokens, step):
        rows = slice(r, r + step)
        up_pre = dot(x_ref[rows], up_ref[...])
        d_gated = dot_nt(d_ref[rows], down_ref[...])
        below = 0.5 * (1.0 + lax.erf(up_pre * 0.5**0.5))
        density = jnp.exp(-0.5 * up_pre * up_pre) * (2.0 * jnp.pi) ** -0.5
        gated_ref[rows] = (up_pre * below).astype(BF16)
        d_up_ref[rows] = (d_gated * (below + up_pre * density)).astype(BF16)
    wide = min(512, model_width)
    for c in range(0, model_width, wide):
        part = slice(c, c + wide)
        grad_up_ref[part] = dot_tn(x_ref[:, part], d_up_ref[...]).astype(BF16)
        grad_down_ref[part] = dot_tn(d_ref[:, part], gated_ref[...]).astype(BF16)


def feed_forward(x, d_out, up, down):
    tokens, model_width = x.shape
    hidden = up.shape[1]
    block = min(512, hidden)
    fixed = pl.BlockSpec((tokens, model_width), lambda i: (0, 0), pipeline_mode=pl.Buffered(1))
    narrow = pl.BlockSpec((tokens, block), lambda i: (0, i))
    column = pl.BlockSpec((model_width, block), lambda i: (0, i))
    shape = lambda rows: jax.ShapeDtypeStruct((rows, hidden), BF16)
    return pl.pallas_call(
        feed_kernel,
        grid=(hidden // block,),
        in_specs=[fixed, fixed, column, pl.BlockSpec((block, model_width), lambda i: (i, 0))],
        out_specs=[narrow, narrow, column, column],
        out_shape=[shape(tokens), shape(tokens), shape(model_width), shape(model_width)],
        compiler_params=pltpu.CompilerParams(vmem_limit_bytes=VMEM_LIMIT),
        cost_estimate=pl.CostEstimate(
            flops=8 * tokens * model_width * hidden,
            bytes_accessed=4 * model_width * (2 * hidden + tokens),
            transcendentals=0,
        ),
        name="feed_forward",
    )(x, d_out, up, down)


def attention_kernel(
    extra, place_ref, q_ref, do_ref, start_ref, valid_ref, keep_ref, left_ref, right_ref, *refs
):
    blocks = (len(refs) - 6 - extra) // 2
    k_refs, v_refs = refs[:blocks], refs[blocks : 2 * blocks]
    o_ref, dq_ref, near_ref, beside_ref, s_ref, dp_ref = refs[2 * blocks + extra :]
    grad_ref = lambda j: (beside_ref if j % 2 else near_ref).at[j // 2]
    rows = q_ref.shape[1]
    scale = HD ** (-0.5)
    member = place_ref[0]
    keep, left, right = keep_ref[0], left_ref[0], right_ref[0]
    q = turn(q_ref[0], keep, left, right).astype(BF16)
    d_out = do_ref[0]
    start = start_ref[0]
    top = jnp.full((rows, 1), MASKED, F32)
    t = member * rows + lax.broadcasted_iota(jnp.int32, (rows, rows), 0)
    for j in range(blocks):
        u = place_ref[j] * rows + lax.broadcasted_iota(jnp.int32, (rows, rows), 1)
        allowed = (u <= t) & (u >= start)
        s_ref[j] = jnp.where(allowed, dot_nt(q, k_refs[j][0]) * scale, MASKED)
        top = jnp.maximum(top, jnp.max(s_ref[j], axis=1, keepdims=True))
    total = jnp.zeros((rows, 1), F32)
    for j in range(blocks):
        e = jnp.exp(s_ref[j] - top)
        s_ref[j] = e
        total = total + jnp.sum(e, axis=1, keepdims=True)
    inverse = 1.0 / total
    out = jnp.zeros((rows, HD), F32)
    delta = jnp.zeros((rows, 1), F32)
    for j in range(blocks):
        p = s_ref[j] * inverse
        s_ref[j] = p
        p_bf = p.astype(BF16)
        out = out + dot(p_bf, v_refs[j][0])
        grad_ref(j)[1] = dot_tn(p_bf, d_out).astype(BF16)
        d_p = dot_nt(d_out, v_refs[j][0])
        dp_ref[j] = d_p
        delta = delta + jnp.sum(p * d_p, axis=1, keepdims=True)
    o_ref[0] = (out * valid_ref[0]).astype(BF16)
    d_q = jnp.zeros((rows, HD), F32)
    for j in range(blocks):
        d_s = (s_ref[j] * (dp_ref[j] - delta)).astype(BF16)
        d_q = d_q + dot(d_s, k_refs[j][0])
        grad_ref(j)[0] = (dot_tn(d_s, q) * scale).astype(BF16)
    dq_ref[0] = turn(d_q * scale, keep, -left, -right).astype(BF16)


def attention(index, places, queries, d_attended, starts, valid, tables, keys, values, earlier):
    micro, rows, feats = queries.shape
    blocks = len(keys)
    tile = pl.BlockSpec((1, rows, HD), lambda h: (index, 0, h))
    fixed = lambda width: pl.BlockSpec((1, rows, width), lambda h: (index, 0, 0))
    grad_tile = pl.BlockSpec((blocks // 2, 2, rows, HD), lambda h: (0, 0, 0, h))
    shape = lambda *lead: jax.ShapeDtypeStruct(lead + (rows, feats), BF16)
    return pl.pallas_call(
        functools.partial(attention_kernel, len(earlier)),
        grid=(feats // HD,),
        in_specs=[pl.BlockSpec(memory_space=pltpu.SMEM), tile, tile]
        + [fixed(1)] * 2
        + [fixed(HD)] * 3
        + [tile] * (2 * blocks)
        + [pl.BlockSpec(memory_space=pl.ANY)] * len(earlier),
        out_specs=[tile] * 2 + [grad_tile] * 2,
        out_shape=[shape(micro)] * 2 + [shape(blocks // 2, 2)] * 2,
        input_output_aliases={8 + 2 * blocks + i: i for i in range(len(earlier))},
        scratch_shapes=[
            pltpu.VMEM((blocks, rows, rows), F32),
            pltpu.VMEM((blocks, rows, rows), F32),
        ],
        compiler_params=pltpu.CompilerParams(vmem_limit_bytes=VMEM_LIMIT),
        cost_estimate=pl.CostEstimate(
            flops=0,
            bytes_accessed=1024,
            transcendentals=0,
        ),
        name="attention_both_ways",
    )(places, queries, d_attended, starts, valid, *tables, *keys, *values, *earlier)


def exchange_rows(local):
    if lax.axis_size("stream") != 4:
        raise ValueError("stream")
    across = lax.ppermute(local, "stream", [(0, 2), (1, 3)])
    beside = over_core(local)
    return (local, beside, across, over_core(across))


def add_f32(a, b):
    return a.astype(F32) + b.astype(F32)


def over_line(a):
    return lax.ppermute(a, "stream", [(2, 0), (3, 1)])


def columns_of(pieces, rows):
    lane = lax.broadcasted_iota(jnp.int32, (rows, 128), 1)
    out = jnp.zeros((rows, 128), F32)
    for index, piece in enumerate(pieces):
        out = jnp.where(lane == index, piece, out)
    return out


def row_sum(a):
    return jnp.sum(a, axis=1, keepdims=True)


def streams_kernel(weights_ref, history_ref, streams_ref, stats_ref):
    weights = weights_ref[...]
    layers = [history_ref[j].astype(F32) for j in range(HIST)]
    sums, squares = [], []
    for s in range(4):
        total = weights[:, s * HIST : s * HIST + 1] * layers[0]
        for j in range(1, HIST):
            total = total + weights[:, s * HIST + j : s * HIST + j + 1] * layers[j]
        streams_ref[s] = total
        sums.append(row_sum(total))
        squares.append(row_sum(total * total))
    stats_ref[...] = columns_of(sums + squares, weights.shape[0]).T[:8]


def mix_streams(weights, history):
    _, tokens, feats = history.shape
    block = min(256, tokens)
    return pl.pallas_call(
        streams_kernel,
        grid=(tokens // block,),
        in_specs=[
            pl.BlockSpec((block, weights.shape[1]), lambda i: (i, 0)),
            pl.BlockSpec((HIST, block, feats), lambda i: (0, i, 0)),
        ],
        out_specs=[
            pl.BlockSpec((4, block, feats), lambda i: (0, i, 0)),
            pl.BlockSpec((8, block), lambda i: (0, i)),
        ],
        out_shape=[
            jax.ShapeDtypeStruct((4, tokens, feats), F32),
            jax.ShapeDtypeStruct((8, tokens), F32),
        ],
        compiler_params=pltpu.CompilerParams(vmem_limit_bytes=VMEM_LIMIT),
        cost_estimate=pl.CostEstimate(
            flops=80 * tokens * feats, bytes_accessed=34 * tokens * feats, transcendentals=0
        ),
        name="mix_streams",
    )(weights, history)


def early_kernel(streams_ref, cot_ref, history_ref, out_ref):
    cot = cot_ref[...].astype(F32)
    plain, crossed, direct = [], [], []
    layers = [history_ref[j].astype(F32) for j in range(HIST)]
    for layer in layers:
        plain.append(row_sum(layer))
        direct.append(row_sum(cot * layer))
    for s in range(4):
        for layer in layers:
            crossed.append(row_sum(streams_ref[s] * layer))
    out_ref[...] = columns_of(crossed + plain + direct, cot.shape[0]).T[:64].astype(BF16)


def early_sums(streams, cot, history):
    _, tokens, feats = streams.shape
    block = min(256, tokens)
    return pl.pallas_call(
        early_kernel,
        grid=(tokens // block,),
        in_specs=[
            pl.BlockSpec((4, block, feats), lambda i: (0, i, 0)),
            pl.BlockSpec((block, feats), lambda i: (i, 0)),
            pl.BlockSpec((HIST, block, feats), lambda i: (0, i, 0)),
        ],
        out_specs=pl.BlockSpec((64, block), lambda i: (0, i)),
        out_shape=jax.ShapeDtypeStruct((64, tokens), BF16),
        compiler_params=pltpu.CompilerParams(vmem_limit_bytes=VMEM_LIMIT),
        cost_estimate=pl.CostEstimate(
            flops=110 * tokens * feats, bytes_accessed=36 * tokens * feats, transcendentals=0
        ),
        name="early_sums",
    )(streams, cot, history)


def sums_kernel(
    g0, g1, g2, g3, streams_ref, stats_ref, gain_ref, history_ref, dots_ref, out_ref, edge_ref
):
    stats = stats_ref[...]
    rows = stats.shape[0]

    @pl.when(pl.program_id(0) == 0)
    def _():
        edge_ref[...] = jnp.zeros_like(edge_ref)

    firsts, seconds, dots = [], [], []
    for s, g_ref in enumerate((g0, g1, g2, g3)):
        g = g_ref[...].astype(F32)
        centered = (streams_ref[s] - stats[:, s : s + 1]) * stats[:, 4 + s : 5 + s]
        edge_ref[s : s + 1] += jnp.sum(g * centered, axis=0, keepdims=True)
        edge_ref[4 + s : 5 + s] += jnp.sum(g, axis=0, keepdims=True)
        scaled = g * gain_ref[s : s + 1]
        firsts.append(row_sum(scaled))
        seconds.append(row_sum(scaled * centered))
        for j in range(HIST):
            dots.append(row_sum(scaled * history_ref[j].astype(F32)))
    dots_ref[...] = columns_of(dots, rows).T[:48].astype(BF16)
    out_ref[...] = columns_of(firsts + seconds, rows).T[:8]


def gradient_sums(grads, streams, stats, gain, history):
    _, tokens, feats = streams.shape
    block = min(256, tokens)
    wide = pl.BlockSpec((block, feats), lambda i: (i, 0))
    return pl.pallas_call(
        sums_kernel,
        grid=(tokens // block,),
        in_specs=[wide] * 4
        + [
            pl.BlockSpec((4, block, feats), lambda i: (0, i, 0)),
            pl.BlockSpec((block, 8), lambda i: (i, 0)),
            pl.BlockSpec((4, feats), lambda i: (0, 0)),
            pl.BlockSpec((HIST, block, feats), lambda i: (0, i, 0)),
        ],
        out_specs=[
            pl.BlockSpec((48, block), lambda i: (0, i)),
            pl.BlockSpec((8, block), lambda i: (0, i)),
            pl.BlockSpec((8, feats), lambda i: (0, 0)),
        ],
        out_shape=[
            jax.ShapeDtypeStruct((48, tokens), BF16),
            jax.ShapeDtypeStruct((8, tokens), F32),
            jax.ShapeDtypeStruct((8, feats), F32),
        ],
        compiler_params=pltpu.CompilerParams(vmem_limit_bytes=VMEM_LIMIT),
        cost_estimate=pl.CostEstimate(
            flops=110 * tokens * feats, bytes_accessed=42 * tokens * feats, transcendentals=0
        ),
        name="gradient_sums",
    )(*grads, streams, stats, gain, history)


def totals_kernel(members, *refs):
    ins, outs, slots, sems = refs[:3], refs[3:6], refs[6:9], refs[9:]
    z = lax.axis_index("head")
    line = [{"head": lax.rem(z + k, members)} for k in range(1, members)]
    barrier = pltpu.get_barrier_semaphore()
    for peer in line:
        pl.semaphore_signal(barrier, inc=1, device_id=peer, device_id_type=pl.DeviceIdType.MESH)
    pl.semaphore_wait(barrier, len(line))
    copies = []
    for index in range(3):
        for k, peer in enumerate(line):
            copy = pltpu.make_async_remote_copy(
                src_ref=ins[index],
                dst_ref=slots[index].at[z],
                send_sem=sems[2 * index].at[k],
                recv_sem=sems[2 * index + 1].at[k],
                device_id=peer,
                device_id_type=pl.DeviceIdType.MESH,
            )
            copy.start()
            copies.append(copy)
        slots[index][z] = ins[index][...]
    for copy in copies:
        copy.wait()
    for index in range(3):
        total = slots[index][0].astype(F32)
        for k in range(1, members):
            total = total + slots[index][k].astype(F32)
        outs[index][...] = total


def head_totals(arrays, collective_id):
    members = lax.axis_size("head")
    local = pl.BlockSpec(memory_space=pltpu.VMEM)
    return pl.pallas_call(
        functools.partial(totals_kernel, members),
        in_specs=[local] * 3,
        out_specs=[local] * 3,
        out_shape=[jax.ShapeDtypeStruct(a.shape, F32) for a in arrays],
        scratch_shapes=[pltpu.VMEM((members,) + a.shape, a.dtype) for a in arrays]
        + [pltpu.SemaphoreType.DMA((members - 1,))] * 6,
        compiler_params=pltpu.CompilerParams(
            collective_id=collective_id, has_side_effects=True, vmem_limit_bytes=VMEM_LIMIT
        ),
        name="totals_over_head",
    )(*arrays)


def small_kernel(
    members,
    plane,
    dots_ref,
    early_ref,
    sums_ref,
    stats_ref,
    pre_ref,
    slope_ref,
    hidden_ref,
    rms_ref,
    w_ref,
    current_ref,
    edge_ref,
    small_ref,
    scaled_ref,
    coef_ref,
    got,
    d_mix_ref,
    rows_ref,
    plane_send,
    plane_recv,
):
    x, stream = lax.axis_index("dp"), lax.axis_index("stream")
    near = (
        {"stream": stream + 1 - 2 * lax.rem(stream, 2)},
        {"stream": lax.rem(stream + 2, 4)},
        {"dp": 1 - x},
    )
    near = near if plane else ()
    if plane:
        barrier = pltpu.get_barrier_semaphore()
        for peer in near:
            pl.semaphore_signal(
                barrier, inc=1, device_id=peer, device_id_type=pl.DeviceIdType.MESH
            )
        pl.semaphore_wait(barrier, len(near))
    n = 4 * HIST
    model_width = members * small_ref.shape[1]
    plain = early_ref[n : n + HIST]
    rows_ref[...] = jnp.zeros_like(rows_ref)
    rows_ref[0:8] = sums_ref[...] / model_width
    for s in range(4):
        part = slice(s * HIST, (s + 1) * HIST)
        mean, inverse = stats_ref[s : s + 1], stats_ref[4 + s : 5 + s]
        crossed = (early_ref[part] - mean * plain) * inverse
        d_part = inverse * (
            dots_ref[part] - rows_ref[s : s + 1] * plain - rows_ref[4 + s : 5 + s] * crossed
        )
        if s == 3:
            d_part = d_part + early_ref[n + HIST : n + 2 * HIST]
        d_mix_ref[part] = d_part
    d_mix = d_mix_ref[...]
    high = dict(precision=HIGHEST, preferred_element_type=F32)
    d_pre = jnp.dot(w_ref[...], d_mix, **high) * slope_ref[...]
    rms = rms_ref[...]
    cross = jnp.sum(d_pre * pre_ref[...], axis=0, keepdims=True)
    rows_ref[8:9] = rms * rms * cross / model_width
    coef_ref[...] = rows_ref[...].T
    scaled = d_pre * rms
    scaled_ref[...] = scaled
    small_ref[...] = jnp.zeros_like(small_ref)
    small_ref[0:n] = jnp.dot(scaled, current_ref[...].astype(F32), **high)
    small_ref[n : n + 8] = edge_ref[...]
    small_ref[n + 8 : 2 * n + 8, 0:n] = lax.dot_general(
        hidden_ref[...], d_mix, (((1,), (1,)), ((), ())), **high
    )
    small_ref[n + 8 : 2 * n + 8, n : n + 1] = jnp.sum(d_mix, axis=1, keepdims=True)
    for step, peer in enumerate(near):
        copy = pltpu.make_async_remote_copy(
            src_ref=small_ref,
            dst_ref=got.at[step],
            send_sem=plane_send.at[step],
            recv_sem=plane_recv.at[step],
            device_id=peer,
            device_id_type=pl.DeviceIdType.MESH,
        )
        copy.start()
        copy.wait()
        small_ref[...] += got[step]


def small_gradients(dots, early, sums, stats, pre, slope, hidden, rms, w_out, current, edges):
    members, plane = lax.axis_size("head"), paired()
    tokens, feats = current.shape
    n = 4 * HIST
    shape = jax.ShapeDtypeStruct
    sems = pltpu.SemaphoreType.DMA
    small, scaled, coefs = pl.pallas_call(
        functools.partial(small_kernel, members, plane),
        in_specs=[pl.BlockSpec(memory_space=pltpu.VMEM)] * 11,
        out_specs=[pl.BlockSpec(memory_space=pltpu.VMEM)] * 3,
        out_shape=[shape((80, feats), F32), shape((n, tokens), F32), shape((tokens, 128), F32)],
        scratch_shapes=[
            pltpu.VMEM((3, 80, feats), F32),
            pltpu.VMEM((n, tokens), F32),
            pltpu.VMEM((128, tokens), F32),
            sems((3,)),
            sems((3,)),
        ],
        compiler_params=pltpu.CompilerParams(
            collective_id=3 if plane else None,
            has_side_effects=plane,
            vmem_limit_bytes=VMEM_LIMIT,
        ),
        name="small_gradients",
    )(dots, early, sums, stats, pre, slope, hidden, rms, w_out, current, edges)
    if not plane:
        small = lax.psum(small.astype(BF16), ("dp", "stream")).astype(F32)
    return small, scaled, coefs


def history_kernel(
    g0, g1, g2, g3, streams_ref, stats_ref, gain_ref, cot_ref, current_ref, weights_ref, coef_ref, d_ref, w_ref, out_ref
):
    stats, weights, coefs = stats_ref[...], weights_ref[...], coef_ref[...]
    d_streams = []
    for s, g_ref in enumerate((g0, g1, g2, g3)):
        inverse = stats[:, 4 + s : 5 + s]
        centered = (streams_ref[s] - stats[:, s : s + 1]) * inverse
        scaled = g_ref[...].astype(F32) * gain_ref[s : s + 1]
        d_streams.append(
            inverse * (scaled - coefs[:, s : s + 1] - centered * coefs[:, 4 + s : 5 + s])
        )
    d_streams[3] = d_streams[3] + cot_ref[...].astype(F32)
    for j in range(HIST):
        total = weights[:, j : j + 1] * d_streams[0]
        for s in range(1, 4):
            total = total + weights[:, s * HIST + j : s * HIST + j + 1] * d_streams[s]
        if j == HIST - 1:
            total = total + lax.dot_general(
                d_ref[...],
                w_ref[...],
                (((0,), (0,)), ((), ())),
                precision=HIGHEST,
                preferred_element_type=F32,
            )
            total = total - current_ref[...].astype(F32) * coefs[:, 8:9]
        out_ref[j] = total


def history_gradient(grads, streams, stats, gain, cot, current, weights, coefs, d_scaled, w_rows):
    _, tokens, feats = streams.shape
    block = min(256, tokens)
    wide = pl.BlockSpec((block, feats), lambda i: (i, 0))
    narrow = lambda a: pl.BlockSpec((block, a.shape[1]), lambda i: (i, 0))
    fixed = lambda a: pl.BlockSpec(a.shape, lambda i: (0, 0))
    return pl.pallas_call(
        history_kernel,
        grid=(tokens // block,),
        in_specs=[wide] * 4
        + [
            pl.BlockSpec((4, block, feats), lambda i: (0, i, 0)),
            narrow(stats),
            fixed(gain),
            wide,
            wide,
            narrow(weights),
            narrow(coefs),
            pl.BlockSpec((d_scaled.shape[0], block), lambda i: (0, i)),
            fixed(w_rows),
        ],
        out_specs=pl.BlockSpec((HIST, block, feats), lambda i: (0, i, 0)),
        out_shape=jax.ShapeDtypeStruct((HIST, tokens, feats), F32),
        compiler_params=pltpu.CompilerParams(vmem_limit_bytes=VMEM_LIMIT),
        cost_estimate=pl.CostEstimate(
            flops=110 * tokens * feats, bytes_accessed=64 * tokens * feats, transcendentals=0
        ),
        name="history_gradient",
    )(*grads, streams, stats, gain, cot, current, weights, coefs, d_scaled, w_rows)


def shards(
    history,
    seq_lens,
    bucket_slot,
    w_mix_in,
    w_mix_out,
    mix_bias,
    ln_gain,
    ln_bias,
    w_qkv,
    w_attn_out,
    w_up,
    w_down,
    cotangent,
):
    member = lax.axis_index("stream")
    micro, quarter, feats = history.shape[1:]
    tokens = micro * quarter
    model_width = feats * lax.axis_size("head")
    slot_base = lax.axis_index("dp") * micro
    slot_ids = jnp.arange(bucket_slot.shape[0], dtype=jnp.int32)
    query_places = member * quarter + jnp.arange(quarter, dtype=jnp.int32)
    w_mix_in_f = w_mix_in.astype(F32)
    w_mix_out_f = w_mix_out.astype(F32)

    segments, starts = [], []
    for index in range(micro):
        bucket = jnp.sum(jnp.where(slot_ids == slot_base + index, bucket_slot, 0))
        lengths = jnp.sum(jnp.where(slot_ids[:, None] == bucket, seq_lens, 0), axis=0)
        bounds = jnp.cumsum(lengths)
        passed = (query_places[:, None] >= bounds[None, :]).astype(jnp.int32)
        segments.append(jnp.sum(passed, axis=1))
        starts.append(jnp.sum(passed * lengths[None, :], axis=1))
    valid = (jnp.concatenate(segments) < 3).astype(F32)[:, None]
    starts = jnp.concatenate(starts)
    position = jnp.tile(query_places, micro) - starts
    frequency = jnp.arange(ROT // 2, dtype=F32)
    phases = position.astype(F32)[:, None] * (10000.0 ** (-2.0 * frequency / ROT))
    cosine, sine = jnp.cos(phases), jnp.sin(phases)
    plain = jnp.zeros((tokens, HD - ROT), F32)
    none = jnp.zeros_like(sine)
    tables = (
        jnp.concatenate([cosine, cosine, plain + 1.0], axis=1),
        jnp.concatenate([-sine, none, plain], axis=1),
        jnp.concatenate([none, sine, plain], axis=1),
    )

    cot_rows = cotangent.reshape(tokens, feats).astype(F32) * valid
    cot_bf = cot_rows.astype(BF16)
    duplex = lined()

    history = history.reshape(HIST, tokens, feats)
    current = history[HIST - 1]
    current_f = current.astype(F32)
    mixed = lax.dot_general(w_mix_in, current, (((0,), (1,)), ((), ())), preferred_element_type=F32)
    square = jnp.sum(current_f * current_f, axis=1)[None]
    mixed = head_sum(jnp.concatenate([mixed, square]), 0).T
    mixed, cot_bf, w_up = lax.optimization_barrier((mixed, cot_bf, w_up))
    out_full = lax.all_gather(cot_bf, "head", axis=1, tiled=True)
    if duplex:
        (up_full,) = exchange([], (), [w_up], (0,), 4)
        mixed, up_full = lax.optimization_barrier((mixed, up_full))
    rms_scale = lax.rsqrt(mixed[:, 4 * HIST :] / model_width + EPSILON)
    mix_pre = mixed[:, : 4 * HIST] * rms_scale
    below_mix = 0.5 * (1.0 + lax.erf(mix_pre * 0.5**0.5))
    mix_hidden = gelu_exact(mix_pre)
    slope_mix = below_mix + mix_pre * jnp.exp(-0.5 * mix_pre * mix_pre) * (2.0 * jnp.pi) ** -0.5
    mix_weights = jnp.dot(mix_hidden, w_mix_out_f, precision=HIGHEST) + mix_bias.reshape(-1)
    streams, stats = mix_streams(mix_weights, history)
    stats = head_sum(stats, 1)
    stat_sum, stat_square = stats[:4], stats[4:]
    row_means = (stat_sum / model_width)[:, :, None]
    inv_std = lax.rsqrt(stat_square[:, :, None] / model_width - row_means * row_means + EPSILON)
    centered = (streams - row_means) * inv_std
    row_stats = jnp.concatenate([row_means[..., 0], inv_std[..., 0]]).T
    normed = (centered * ln_gain[:, None, :] + ln_bias[:, None, :]).astype(BF16)

    def all_features(a):
        return lax.all_gather(a, "head", axis=1, tiled=True)

    if duplex:
        w_down, normed = lax.optimization_barrier((w_down, normed))
        wk, wv, down_full, w_out_full, wq, *shares = exchange(
            [], (), [w_qkv[1], w_qkv[2], w_down, w_attn_out, w_qkv[0]], (0, 0, 1, 1, 0), 6, 2
        )
    else:
        wq, wk, wv = gather_weight(w_qkv, 1)
        w_out_full, down_full = gather_weight(w_attn_out, 1), gather_weight(w_down, 1)
        up_full = gather_weight(w_up, 0)

    def to_owner(partial):
        return lax.psum_scatter(
            partial.astype(BF16), "head", scatter_dimension=1, tiled=True
        ).astype(F32)

    up_out, out_full = lax.optimization_barrier((normed[3], out_full))
    up_in, k_out, down_full = lax.optimization_barrier(
        (all_features(up_out), normed[1], down_full)
    )
    k_in, v_out = lax.optimization_barrier((all_features(k_out), normed[2]))
    gated_up, d_up, product_up, product_down = feed_forward(up_in, out_full, up_full, down_full)
    feed_products = [product_up[None], product_down[None]]
    feed_parts = [chip_parts(a) if paired() else a for a in feed_products]
    v_out, d_up, feed_parts = lax.optimization_barrier((v_out, d_up, feed_parts))
    feed_lines = [line_parts(*a) for a in feed_parts] if paired() else feed_parts
    streams_late, feed_lines[0] = lax.optimization_barrier((streams, feed_lines[0]))
    early = early_sums(streams_late, cot_bf, history)
    feed = dot(gated_up, down_full).astype(BF16)
    d_attended = dot_nt(out_full, w_out_full).astype(BF16) * valid.astype(BF16)
    d_up_in = dot_nt(d_up, up_full).astype(BF16)
    keys = rotate(dot(k_in, wk), tables, 1.0)
    v_in, q_out, early, feed, d_attended, d_up_in, keys, wk, wv = lax.optimization_barrier(
        (all_features(v_out), normed[0], early, feed, d_attended, d_up_in, keys, wk, wv)
    )
    values = dot(v_in, wv).astype(BF16)
    by_micro = lambda a: a.reshape((micro, quarter) + a.shape[1:])
    key_blocks = exchange_rows(by_micro(keys))
    value_blocks = exchange_rows(by_micro(values))
    d_up_in, key_blocks, value_blocks = lax.optimization_barrier(
        (d_up_in, key_blocks, value_blocks)
    )
    q_in, key_blocks, value_blocks, feed_lines[1], early = lax.optimization_barrier(
        (all_features(q_out), key_blocks, value_blocks, feed_lines[1], early)
    )
    g_up = to_owner(d_up_in)
    product = lambda a, b: dot_tn(a, b).astype(BF16)

    queries = dot(q_in, wq)
    places = member ^ jnp.arange(4, dtype=jnp.int32)
    earlier, d_rows = (), []
    queries = by_micro(queries)
    for index in range(micro):
        results = attention(
            index,
            places,
            queries,
            by_micro(d_attended),
            by_micro(starts[:, None]),
            by_micro(valid),
            tuple(by_micro(a) for a in tables),
            key_blocks,
            value_blocks,
            earlier,
        )
        earlier = results[:2]
        if duplex and index == micro - 1:
            continue
        chip = add_f32(results[2], over_core(results[3]))
        across = chip[1].astype(BF16)
        queries, across = lax.optimization_barrier((queries, across))
        d_rows.append(add_f32(chip[0], over_line(across)))
    attended, d_query_pre = (a.reshape(tokens, feats) for a in earlier)
    d_key_rows = jnp.concatenate([a[0] for a in d_rows])
    done = d_key_rows.shape[0]
    d_key_rows = rotate(d_key_rows, tuple(a[:done] for a in tables), -1.0)
    d_value_rows = jnp.concatenate([a[1] for a in d_rows]).astype(BF16)
    attended, d_query_pre, d_key_rows, d_value_rows = lax.optimization_barrier(
        (attended, d_query_pre, d_key_rows, d_value_rows)
    )

    products = jnp.stack([product(q_in, d_query_pre), product(out_full, attended)])
    if duplex:
        partials = [dot_nt(d_query_pre, wq).astype(BF16)]
        parts = chip_parts(products)
        partials, parts, g_up, feed_lines = lax.optimization_barrier(
            (partials, parts, g_up, feed_lines)
        )
        (g_query,), (d_key_full, d_value_full), (wk_rows, wv_rows), plane_grads = exchange(
            partials,
            [d_key_rows, d_value_rows, results[2], results[3], *(a[done:] for a in tables)]
            + [a[0] for a in feed_lines]
            + [*parts, k_in, v_in],
            shares,
            (0, 0),
            5,
        )
        attended_late, g_query = lax.optimization_barrier((attended, g_query))
        cut = 5 * tokens // 16
        pair = lambda a: (a[:cut], a[cut:])
        halves = [
            (dot(a, w_out_full) + b).astype(BF16) for a, b in zip(pair(attended_late), pair(feed))
        ]
        branch = to_owner(halves[0])
        g_key, g_value = dot_nt(d_key_full, wk_rows), dot_nt(d_value_full, wv_rows)
    else:
        g_query = to_owner(dot_nt(d_query_pre, wq))
        branch = to_owner(dot(attended, w_out_full) + feed)
        terms = scatter_parts(products)
        feed_terms = [scatter_parts(a) for a in feed_products]
        g_key = to_owner(dot_nt(d_key_rows, wk))
        g_value = to_owner(dot_nt(d_value_rows, wv))
        kv_terms = scatter_parts(
            jnp.stack([product(k_in, d_key_rows), product(v_in, d_value_rows)])
        )
    grads = (g_query, g_key, g_value, g_up)
    dots, sums, edges = gradient_sums(grads, streams, row_stats, ln_gain, history)
    dots, early, sums = head_totals((dots, early, sums), 7)
    if duplex:
        sums, second_half = lax.optimization_barrier((sums, halves[1]))
        branch = jnp.concatenate([branch, to_owner(second_half)])
        grad_up, grad_down, grad_query, grad_attn_out, grad_key, grad_value = plane_grads
        grad_qkv = jnp.stack([grad_query, grad_key, grad_value])
    else:
        grad_up = add_terms(feed_terms[0][0][0], feed_terms[0][1][0], False)
        grad_down = add_terms(feed_terms[1][0][0], feed_terms[1][1][0], True)
        grad_attn_out = add_terms(terms[0][1], terms[1][1], True)
        grad_qkv = jnp.concatenate([add_f32(terms[0][:1], terms[1][:1]), add_f32(*kv_terms)])
    small, d_scaled, coefs = small_gradients(
        dots, early, sums, row_stats.T, mix_pre.T, slope_mix.T, mix_hidden.T, rms_scale.T, w_mix_out_f, current, edges
    )
    block_out = (valid * (streams[3] + branch)).astype(BF16)
    history_grad = history_gradient(
        grads, streams, row_stats, ln_gain, cot_bf, current, mix_weights, coefs, d_scaled, w_mix_in_f.T
    ).reshape(HIST, micro, quarter, feats)
    n = 4 * HIST
    return (
        block_out.reshape(micro, quarter, feats),
        mix_weights.reshape(micro, quarter, 4 * HIST),
        history_grad,
        small[:n].T,
        small[n + 8 : 2 * n + 8, :n],
        small[n + 8 : 2 * n + 8, n].reshape(mix_bias.shape),
        small[n : n + 4],
        small[n + 4 : n + 8],
        grad_qkv,
        grad_attn_out,
        grad_up,
        grad_down,
    )


def solution(mesh):
    return jax.shard_map(
        shards,
        mesh=mesh,
        in_specs=(
            P(None, "dp", "stream", "head"),
            P(),
            P(),
            P("head", None),
            P(),
            P(),
            P(None, "head"),
            P(None, "head"),
            P(None, ("dp", "stream"), "head"),
            P("head", ("dp", "stream")),
            P(("dp", "stream"), "head"),
            P("head", ("dp", "stream")),
            P("dp", "stream", "head"),
        ),
        out_specs=(
            P("dp", "stream", "head"),
            P("dp", "stream", None),
            P(None, "dp", "stream", "head"),
            P("head", None),
            P(),
            P(),
            P(None, "head"),
            P(None, "head"),
            P(None, ("dp", "stream"), "head"),
            P("head", ("dp", "stream")),
            P(("dp", "stream"), "head"),
            P("head", ("dp", "stream")),
        ),
        check_vma=False,
    )
```
